32 devices in a mesh: group: 2 (over y), seq: 16 (over z, x, core).
Axes of the slice: x: 2, y: 2, z: 4, core: 2. Of those that a mesh axis runs over, the one named last changes fastest.
Arguments:
- prompt_raw: bfloat16 [32, 512, 576], P(('group', 'seq')), parts along dimension 0, may hold values from -6 to 6
- lengths: int32 [32], P('group'), parts along dimension 0, may hold values from 1 to 512, 6144 in all
- owners: int32 [32], P('group'), parts along dimension 0, may hold values from 0 to 15, as said below
- resident: bfloat16 [64, 1024, 576], P(('group', 'seq')), parts along dimension 0, may hold values from -6 to 6
- new_raw: bfloat16 [32, 2, 576], P('group'), parts along dimension 0, may hold values from -6 to 6
- queries: bfloat16 [32, 2, 16, 192], P('group', None, 'seq'), parts along dimension 0, may hold values from -100 to 100
- kv_gain: bfloat16 [512], replicated, may hold values from 0.099609375 to 1.8984375
- w_uk: bfloat16 [16, 128, 512], P('seq'), may hold values from -0.5 to 0.5
- w_uv: bfloat16 [16, 512, 128], P('seq'), may hold values from -3 to 3
- w_o: bfloat16 [16, 128, 7168], P('seq'), may hold values from -0.125 to 0.125
Outputs:
- layer_out: bfloat16 [32, 2, 7168], P(('group', 'seq')), parts along dimension 0
The draws below stay inside these ranges and needn't reach their ends.
There are 2 independent parts, one for each index of `group`. The reference program is written for one: setup_inputs(seed, part) draws one part's arguments, and reference() takes and returns one part's arrays. A program takes and returns all parts, laid end to end along the dimension named above; an argument that names none is the same for every part. Nothing has to cross between parts.
Inputs may be any that keep to these rules, and one draw needn't show every extreme that they name: `owners`: no device is the owner of more than 2 sequences, and some device owns exactly 2.
All inputs are finite; a program needn't handle non-finite values.
Results may differ from the reference program's by a relative error of at most 0.0096.
Values may be sent and summed in bfloat16 or wider, within the bound.
No kernel may reach another device: no remote copies, remote signals or barrier semaphores. Data moves between devices by JAX's collectives and lax.ppermute only.
A program may use at most 64 MiB of HBM per device.

```python
import math
import jax
import jax.numpy as jnp
import numpy as np
from jax import lax

LATENT = 512
ROPE = 64
NOPE = 128
VHEAD = 128
MODEL_WIDTH = 7168
SLOTS = 2
MOST = 512
RES = 1024
HEADS = 16
SEQS = 16
KVW = 576
N_SEQ = 16


def draw_owners(key, part):
    key = jax.random.fold_in(key, 11)
    first, second = jax.random.split(key)
    order = jax.random.permutation(first, SEQS)
    pairs = SEQS // 4
    index = jnp.arange(SEQS, dtype=jnp.int32)
    placed = jnp.where(index < 2 * pairs, index // 2, index - pairs)
    relabel = jax.random.permutation(second, SEQS).astype(jnp.int32)
    owner_at = relabel[placed]
    return jnp.zeros((SEQS,), jnp.int32).at[order].set(owner_at)


def draw_queries(key, part):
    key = jax.random.fold_in(key, 23)
    first = jax.random.fold_in(key, 0)
    shape = (SEQS, 2, HEADS, NOPE + ROPE)
    values = jnp.clip(jax.random.normal(first, shape, jnp.float32), -4.0, 4.0)
    return values.astype(jnp.bfloat16)


def shard_levels(own_key, dims, shards, smallest, largest):
    def one(dim, shards_of):
        heights = jax.random.uniform(jax.random.fold_in(jax.random.fold_in(own_key, 6), dim), (shards_of,), jnp.float32, smallest / len(shards), largest / len(shards))
        return jnp.repeat(jnp.exp(heights), dims[dim] // shards_of).reshape((-1,) + (1,) * (len(dims) - dim - 1))

    factor_of = one(*shards[0])
    for cut in shards[1:]:
        factor_of = factor_of * one(*cut)
    return factor_of


def profile(amount, total, reach, slope):
    portions = [(1 << 20) // math.isqrt(grade ** slope) + 1 for grade in range(2, amount + 1)]
    spare, given = total - reach - (amount - 1), [1] * (amount - 1)
    while spare > 0:
        movable = [i for i in range(amount - 1) if given[i] < reach]
        mass, budget = sum([portions[i] for i in movable]), spare
        for i in movable:
            more = min(reach - given[i], max(1, budget * portions[i] // mass), spare)
            given[i] = given[i] + more
            spare = spare - more
    return np.array([reach] + given)


def ragged_sizes(rng, number_of, total, reach, slope):
    if number_of == 2:
        one = jax.random.randint(rng, (), max(1, total - reach), min(reach, total - 1) + 1)
        return jnp.stack([one, total - one])
    sizes = jnp.asarray(profile(number_of, total, reach, slope), jnp.int32)
    couples = (number_of - 1) // 2
    giver, receiver = sizes[1:1 + 2 * couples:2], sizes[2:2 + 2 * couples:2]
    slack = jnp.minimum(giver - 1, reach - receiver)
    moved = jax.random.randint(jax.random.fold_in(rng, 1), (couples,), 0, 1 << 20) % (slack + 1)
    sizes = sizes.at[1:1 + 2 * couples:2].set(giver - moved).at[2:2 + 2 * couples:2].set(receiver + moved)
    return sizes[jax.random.permutation(jax.random.fold_in(rng, 2), number_of)]


def bell_draw(key, dims, spread, most, shards=(), kind=jnp.bfloat16):
    values = jax.random.normal(key, dims, jnp.float32) * spread
    if len(shards) > 0:
        values = shard_levels(key, dims, shards, -0.22, 0.18) * values
    return jnp.clip(values, min=-most, max=most).astype(kind)


def setup_inputs(seed: int = 0, part: int = 0) -> dict:
    seeds = jax.random.split(jax.random.key(seed), 11)
    part_keys = jax.random.split(jax.random.fold_in(seeds[10], part), 11)
    return {
        "prompt_raw": bell_draw(part_keys[0], (SEQS, MOST, KVW), 1.0, 6.0, ((0, 16),)),
        "lengths": ragged_sizes(part_keys[1], SEQS, SEQS * MOST * 3 // 4, MOST, 1).astype(jnp.int32),
        "owners": draw_owners(jax.random.fold_in(jax.random.fold_in(seeds[10], part), 71), part),
        "resident": bell_draw(part_keys[3], (SLOTS * N_SEQ, RES, KVW), 1.0, 6.0, ((0, 16),)),
        "new_raw": bell_draw(part_keys[4], (SEQS, 2, KVW), 1.0, 6.0),
        "queries": draw_queries(jax.random.fold_in(jax.random.fold_in(seeds[10], part), 71), part),
        "kv_gain": jnp.clip(1.0 + 0.18 * jax.random.normal(seeds[6], (LATENT,), jnp.float32), 0.099609375, 1.8984375).astype(jnp.bfloat16),
        "w_uk": bell_draw(seeds[7], (HEADS, NOPE, LATENT), NOPE ** -0.5, 0.5, ((0, 16),)),
        "w_uv": bell_draw(seeds[8], (HEADS, LATENT, VHEAD), 4 ** -0.5, 3.0, ((0, 16),)),
        "w_o": bell_draw(seeds[9], (HEADS, VHEAD, MODEL_WIDTH), (HEADS * VHEAD) ** -0.5, 0.125, ((0, 16),)),
    }


def slot_table(owners):
    count = owners.shape[0]
    index = jnp.arange(count, dtype=jnp.int32)
    same = owners[:, None] == owners[None, :]
    earlier = index[None, :] < index[:, None]
    return lax.optimization_barrier(jnp.sum((same & earlier).astype(jnp.int32), axis=1)).astype(jnp.int32)

def rotate(values, position):
    width = values.shape[-1]
    half = width // 2
    freqs = 10000.0 ** (-(jnp.arange(half, dtype=jnp.float32) * 2.0) / width)
    angle = position[..., None] * freqs
    cosine = jnp.cos(angle)
    sine = jnp.sin(angle)
    first = values[..., :half]
    second = values[..., half:]
    return jnp.concatenate([first * cosine - second * sine, second * cosine + first * sine], axis=-1)

def compress(raw, gain, position):
    latent_width = gain.shape[0]
    values = raw.astype(jnp.float32)
    latent = values[..., :latent_width]
    meansq = lax.optimization_barrier(jnp.mean(latent * latent, axis=-1, keepdims=True))
    latent = latent * lax.rsqrt(meansq + 1e-06) * gain.astype(jnp.float32)
    rotated = rotate(values[..., latent_width:], position)
    return jnp.concatenate([latent, rotated], axis=-1).astype(jnp.bfloat16)

def attend(query, keys, visible, heads, latent_width, scale):
    scores = lax.dot_general(query, keys, (((1,), (1,)), ((), ())), preferred_element_type=jnp.float32) * scale
    mask = jnp.repeat(visible, heads, axis=0)
    scores = jnp.where(mask, scores, -1e+30)
    top = lax.optimization_barrier(jnp.max(scores, axis=1, keepdims=True))
    weights = jnp.where(mask, jnp.exp(scores - top), 0.0)
    total = lax.optimization_barrier(jnp.sum(weights, axis=1, keepdims=True))
    numer = jnp.dot(weights.astype(jnp.bfloat16), keys[:, :latent_width], preferred_element_type=jnp.float32)
    return (numer / total).astype(jnp.bfloat16)

def reference(prompt_raw, lengths, owners, resident, new_raw, queries, kv_gain, w_uk, w_uv, w_o):
    seqs = lengths.shape[0]
    most = prompt_raw.shape[1]
    res_rows = resident.shape[1]
    heads = queries.shape[2]
    nope = w_uk.shape[1]
    latent_width = kv_gain.shape[0]
    scale = 1.0 / queries.shape[-1] ** 0.5
    slot = slot_table(owners)
    key_id = (owners * SLOTS + slot).astype(jnp.int32)
    absorbed = jnp.einsum('sthd,hdl->sthl', queries[..., :nope].astype(jnp.float32), w_uk.astype(jnp.float32)).astype(jnp.bfloat16)
    qpos = (res_rows + lengths[:, None] + jnp.arange(2, dtype=jnp.int32)[None, :]).astype(jnp.float32)
    qrot = rotate(queries[..., nope:].astype(jnp.float32), qpos[:, :, None]).astype(jnp.bfloat16)
    qcat = jnp.concatenate([absorbed, qrot], axis=-1)
    prompt_pos = (res_rows + jnp.arange(most, dtype=jnp.int32)).astype(jnp.float32)
    causal = jnp.arange(2, dtype=jnp.int32)[None, :] <= jnp.arange(2, dtype=jnp.int32)[:, None]

    def one_sequence(index):
        prompt_rows = compress(prompt_raw[index], kv_gain, prompt_pos)
        new_rows = compress(new_raw[index], kv_gain, qpos[index])
        keys = jnp.concatenate([resident[key_id[index]], prompt_rows, new_rows], axis=0)
        prompt_seen = jnp.broadcast_to(jnp.arange(most, dtype=jnp.int32)[None, :] < lengths[index], (2, most))
        visible = jnp.concatenate([jnp.ones((2, res_rows), dtype=bool), prompt_seen, causal], axis=1)
        query = qcat[index].reshape(2 * heads, -1)
        return attend(query, keys, visible, heads, latent_width, scale).reshape(2, heads, latent_width)
    latent_out = lax.map(one_sequence, jnp.arange(seqs, dtype=jnp.int32))
    head_out = jnp.einsum('sthl,hlv->sthv', latent_out.astype(jnp.float32), w_uv.astype(jnp.float32)).astype(jnp.bfloat16)
    flat_out = jnp.dot(head_out.reshape(seqs * 2, -1), w_o.reshape(-1, w_o.shape[-1]), preferred_element_type=jnp.float32)
    return flat_out.reshape(seqs, 2, -1).astype(jnp.bfloat16)
```

```python
import functools

import jax
import jax.numpy as jnp
import numpy as np
from jax import lax
from jax.experimental import pallas as pl
from jax.experimental.pallas import tpu as pltpu
from jax.sharding import PartitionSpec as P

F32 = jnp.float32
BF16 = jnp.bfloat16
I32 = jnp.int32
VMEM = pl.BlockSpec(memory_space=pltpu.VMEM)
SMEM = pl.BlockSpec(memory_space=pltpu.SMEM)
LANES = 128
PACK = 16
PART = 6
BITS = 14.0


def iota(shape, dim):
    return lax.broadcasted_iota(I32, shape, dim)


def dot(a, b, dims=((1,), (0,))):
    return lax.dot_general(a, b, (dims, ((), ())), preferred_element_type=F32)


def column_of(row, picks):
    n, width = picks.shape[0], row.shape[1]
    hit = iota((n, width), 1) == picks
    return jnp.sum(jnp.where(hit, row, 0), axis=1, keepdims=True)


def slots_of(owners_row):
    seqs = owners_row.shape[1]
    owners_col = column_of(owners_row, iota((seqs, 1), 0))
    earlier = iota((seqs, seqs), 0) < iota((seqs, seqs), 1)
    same = (owners_col == owners_row) & earlier
    return jnp.sum(jnp.where(same, 1, 0), axis=0, keepdims=True)


def doubled(row):
    seqs = row.shape[1]
    col = column_of(row, iota((seqs, 1), 0))
    hit = iota((seqs, 2 * seqs), 1) // 2 == iota((seqs, 2 * seqs), 0)
    return jnp.sum(jnp.where(hit, col, 0), axis=0, keepdims=True)


def turn(x, angle):
    half = x.shape[1] // 2
    swapped = jnp.concatenate([x[:, half:], x[:, :half]], axis=1)
    sine = jnp.sin(angle)
    sine = jnp.where(iota(x.shape, 1) < half, -sine, sine)
    return x * jnp.cos(angle) + swapped * sine


def query_kernel(res_rows, owners_ref, lengths_ref, freq_ref, queries_ref, uk_ref, out_ref, flat):
    seqs = owners_ref.shape[1]
    nope, latent = uk_ref.shape
    rope = freq_ref.shape[1]
    half = latent // 2
    rows = 2 * seqs
    for s in range(seqs):
        for t in range(2):
            flat[2 * s + t : 2 * s + t + 1, : nope + rope] = queries_ref[s, t].astype(F32)
    values = flat[:, : nope + rope]
    absorbed = dot(values[:, :nope].astype(BF16), uk_ref[...]).astype(BF16)
    row = iota((rows, 1), 0)
    lengths = column_of(lengths_ref[...], row // 2)
    position = (res_rows + lengths + row % 2).astype(F32)
    turned = turn(values[:, nope:], position * freq_ref[...])
    zero = jnp.zeros((rows, rope), F32)
    pieces = [absorbed[:, :half], absorbed[:, half:]]
    for k in range(3):
        blocks = [turned if j == k else zero for j in range(half // rope)]
        pieces.append(jnp.concatenate(blocks, axis=1).astype(BF16))
    owners = owners_ref[...]
    owner = doubled(owners)
    slot = doubled(slots_of(owners))
    count = out_ref.shape[0]
    total = count * PACK
    shape = (total, rows)
    dest, r = iota(shape, 0) // PACK, iota(shape, 0) % PACK
    seq, tok = iota(shape, 1) // 2, iota(shape, 1) % 2
    here = jnp.where(owner == dest, slot + 1, -1)

    result = None
    for p in range(2):
        q = r - PART * p
        wanted = ((q // 2 == 0) & (seq == dest)) | (here == q // 2)
        hit = (q >= 0) & (q < PART) & (tok == q % 2) & wanted
        one = dot(jnp.where(hit, 1.0, 0.0).astype(BF16), pieces[p])
        result = one if result is None else result + one
    for k in range(3):
        match = (seq == dest) if k == 0 else (here == k)
        hit = (r == 2 * PART + tok) & match
        result = result + dot(jnp.where(hit, 1.0, 0.0).astype(BF16), pieces[2 + k])
    out_ref[...] = result.astype(BF16).reshape(out_ref.shape)


def compress_kernel(res_rows, lengths_ref, freq_ref, gain_ref, prompt_ref, new_ref, out_ref):
    latent = gain_ref.shape[1]
    most = prompt_ref.shape[1]
    width = prompt_ref.shape[2]
    pad = out_ref.shape[0] - most
    device = lax.axis_index("seq")
    gain = gain_ref[...].astype(F32)
    freq = freq_ref[...]

    def compress(raw, position):
        values = raw.astype(F32)
        lat = values[:, :latent]
        meansq = jnp.sum(lat * lat, axis=1, keepdims=True) * (1.0 / latent)
        lat = lat * lax.rsqrt(meansq + 1e-06) * gain
        return lat.astype(BF16), turn(values[:, latent:], position * freq).astype(BF16)

    step = 64
    for i in range(most // step):
        position = (res_rows + i * step + iota((step, 1), 0)).astype(F32)
        lat, rot = compress(prompt_ref[0, i * step : (i + 1) * step, :], position)
        out_ref[i * step : (i + 1) * step, :latent] = lat
        out_ref[i * step : (i + 1) * step, latent:] = rot
    fresh = new_ref[device].astype(F32)
    fresh = jnp.concatenate([fresh, jnp.zeros((pad - 2, width), F32)], axis=0)
    position = (res_rows + lengths_ref[device] + iota((pad, 1), 0)).astype(F32)
    lat, rot = compress(fresh, position)
    out_ref[most:, :latent] = lat
    out_ref[most:, latent:] = rot


def score_kernel(most, scale, lengths_ref, q_ref, keys_ref, resident_ref, sp_ref, sr_ref, stat_ref):
    heads = q_ref.shape[0]
    half = q_ref.shape[2]
    width = keys_ref.shape[1]
    rope = width - 2 * half
    device = lax.axis_index("seq")
    rows = 2 * heads
    total = heads * PACK
    flat = q_ref[...].reshape(total, half)
    shape = (rows, total)
    head, tok = iota(shape, 0) // 2, iota(shape, 0) % 2
    source = iota(shape, 1) - head * PACK

    def picked(r):
        hit = source == r + tok
        return dot(jnp.where(hit, 1.0, 0.0).astype(BF16), flat)

    turned = picked(2 * PART)
    tops, sums = [], []
    for k in range(3):
        query = jnp.concatenate(
            [picked(2 * k), picked(PART + 2 * k), turned[:, k * rope : (k + 1) * rope]], axis=1
        ).astype(BF16)
        keys = keys_ref[...] if k == 0 else resident_ref[k - 1]
        scores = dot(query, keys, ((1,), (1,))) * scale
        if k == 0:
            at = iota(scores.shape, 1)
            token = iota(scores.shape, 0) % 2
            seen = (at < lengths_ref[device]) | ((at >= most) & (at <= most + token))
            scores = jnp.where(seen, scores, -1e30)
            sp_ref[...] = scores
        else:
            sr_ref[k - 1] = scores
        top = jnp.max(scores, axis=1, keepdims=True)
        tops.append(top)
        sums.append(jnp.sum(jnp.exp(scores - top), axis=1, keepdims=True))
    lanes = stat_ref.shape[2]
    here = iota((3 * rows, lanes), 0) == iota((3 * rows, lanes), 1)
    top = jnp.sum(jnp.where(here, jnp.concatenate(tops, axis=0), 0.0), axis=0, keepdims=True)
    total = jnp.sum(jnp.where(here, jnp.concatenate(sums, axis=0), 0.0), axis=0, keepdims=True)
    both = jnp.concatenate([top, total], axis=0)
    stat_ref[...] = jnp.broadcast_to(both[None], stat_ref.shape)


def attend_kernel(owners_ref, stat_ref, sp_ref, sr_ref, keys_ref, resident_ref, out_ref):
    heads = out_ref.shape[0]
    latent = out_ref.shape[1] // PART * LANES
    seqs = owners_ref.shape[0]
    rows = 2 * heads
    device = lax.axis_index("seq")
    lanes = stat_ref.shape[2]
    my_owner = owners_ref[device]
    my_slot = jnp.int32(0)
    seen = jnp.int32(0)
    first = jnp.int32(0)
    second = jnp.int32(0)
    for s in range(seqs):
        owner = owners_ref[s]
        my_slot = my_slot + jnp.where((owner == my_owner) & (s < device), 1, 0)
        mine = owner == device
        first = jnp.where(mine & (seen == 0), s, first)
        second = jnp.where(mine & (seen == 1), s, second)
        seen = seen + jnp.where(mine, 1, 0)

    def column(row, segment):
        picks = iota((rows, 1), 0) + segment * rows
        hit = iota((rows, lanes), 1) == picks
        return jnp.sum(jnp.where(hit, row, 0.0), axis=1, keepdims=True)

    mine = stat_ref[device]
    others = [(stat_ref[my_owner], 1 + my_slot), (stat_ref[first], 0), (stat_ref[second], 0)]
    for k in range(3):
        other, segment = others[k]
        top0, sum0 = column(mine[0:1], k), column(mine[1:2], k)
        top1, sum1 = column(other[0:1], segment), column(other[1:2], segment)
        top = jnp.maximum(top0, top1)
        total = sum0 * jnp.exp(top0 - top) + sum1 * jnp.exp(top1 - top)
        scores = sp_ref[...] if k == 0 else sr_ref[k - 1]
        keys = keys_ref[...] if k == 0 else resident_ref[k - 1]
        weights = jnp.exp(scores - top).astype(BF16)
        part = dot(weights, keys[:, :latent]) / total
        for h in range(heads):
            for c in range(latent // LANES):
                at = c * PART + 2 * k
                out_ref[h, at : at + 2, :] = part[2 * h : 2 * h + 2, c * LANES : (c + 1) * LANES]


def project_kernel(owners_ref, part_ref, uv_ref, wo_ref, out_ref):
    count, each, lanes = part_ref.shape
    seqs = owners_ref.shape[1]
    cuts = each // PART
    rows = 2 * seqs
    width = wo_ref.shape[2]
    owners = owners_ref[...]
    shape = (cuts * rows, 1)
    cut = iota(shape, 0) // rows
    seq, tok = iota(shape, 0) % rows // 2, iota(shape, 0) % 2
    owner = column_of(owners, seq)
    slot = column_of(slots_of(owners), seq)
    first = seq * each + cut * PART + tok
    second = owner * each + cut * PART + 2 + 2 * slot + tok
    at = iota((cuts * rows, count * each), 1)
    hit = jnp.where((at == first) | (at == second), 1.0, 0.0).astype(BF16)
    rest = part_ref[...].reshape(count * each, lanes)
    latent = None
    for _ in range(3):
        piece = rest.astype(BF16)
        rest = rest - piece.astype(F32)
        one = dot(hit, piece)
        latent = one if latent is None else latent + one
    latent = latent.astype(BF16)
    latent = jnp.concatenate([latent[c * rows : (c + 1) * rows] for c in range(cuts)], axis=1)
    head_out = dot(latent, uv_ref[0]).astype(BF16)
    product = dot(head_out, wo_ref[0])
    top = jnp.max(jnp.abs(product), axis=1, keepdims=True)
    power = jnp.clip(jnp.floor(jnp.log2(jnp.maximum(top, 1e-35))) + 1.0, -100.0, 100.0)
    coded = jnp.round(product * jnp.exp2(BITS - power)).astype(I32).astype(jnp.int16)
    power = jnp.broadcast_to(power, (rows, LANES)).astype(I32).astype(jnp.int16)
    for s in range(seqs):
        out_ref[s, :, :width] = coded[2 * s : 2 * s + 2]
        out_ref[s, :, width:] = power[2 * s : 2 * s + 2]


def add_kernel(coded_ref, out_ref):
    count = coded_ref.shape[0]
    width = out_ref.shape[2]
    total = None
    for s in range(count):
        power = coded_ref[s, :, width : width + 1].astype(I32).astype(F32)
        one = coded_ref[s, :, :width].astype(I32).astype(F32) * jnp.exp2(power - BITS)
        total = one if total is None else total + one
    out_ref[0] = total.astype(BF16)


def swap(x):
    return lax.all_to_all(x, "seq", split_axis=0, concat_axis=0, tiled=True)


def call(kernel, shapes, specs, scratch=(), cost=None):
    single = not isinstance(shapes, (list, tuple))
    return pl.pallas_call(
        kernel,
        out_shape=shapes,
        in_specs=specs,
        out_specs=VMEM if single else [VMEM] * len(shapes),
        scratch_shapes=list(scratch),
        cost_estimate=cost,
        compiler_params=pltpu.CompilerParams(vmem_limit_bytes=48 * 1024 * 1024),
    )


def on_device(prompt_raw, lengths, owners, resident, new_raw, queries, kv_gain, w_uk, w_uv, w_o):
    count = lax.axis_size("seq")
    seqs = lengths.shape[0]
    most, width = prompt_raw.shape[1:]
    latent = kv_gain.shape[0]
    res_rows = resident.shape[1]
    nope = w_uk.shape[1]
    rope = width - latent
    heads = count
    out_width = w_o.shape[2]
    scale = 1.0 / queries.shape[-1] ** 0.5
    half = np.arange(rope // 2, dtype=np.float32)
    freq = np.float32(10000.0) ** (-(half * np.float32(2.0)) / np.float32(rope))
    freq = jnp.asarray(np.concatenate([freq, freq]).astype(np.float32)[None])
    owners_row, lengths_row = owners.reshape(1, seqs), lengths.reshape(1, seqs)
    keys_rows = most + 16

    query = call(
        functools.partial(query_kernel, res_rows),
        jax.ShapeDtypeStruct((count, PACK, latent // 2), BF16),
        [VMEM] * 5,
        [pltpu.VMEM((2 * seqs, 2 * LANES), F32)],
    )(owners_row, lengths_row, freq, queries, w_uk[0])
    received = swap(query)
    keys = call(
        functools.partial(compress_kernel, res_rows),
        jax.ShapeDtypeStruct((keys_rows, width), BF16),
        [SMEM] + [VMEM] * 4,
        cost=pl.CostEstimate(flops=10**7, bytes_accessed=10**7, transcendentals=10**5),
    )(lengths, freq, kv_gain.reshape(1, latent), prompt_raw, new_raw)
    lanes = -(-6 * heads // LANES) * LANES
    scores_p, scores_r, stat = call(
        functools.partial(score_kernel, most, scale),
        [
            jax.ShapeDtypeStruct((2 * heads, keys_rows), F32),
            jax.ShapeDtypeStruct((2, 2 * heads, res_rows), F32),
            jax.ShapeDtypeStruct((count, 2, lanes), F32),
        ],
        [SMEM] + [VMEM] * 3,
    )(lengths, received, keys, resident)
    stats = swap(stat)
    part = call(
        attend_kernel,
        jax.ShapeDtypeStruct((heads, PART * (latent // LANES), LANES), F32),
        [SMEM] + [VMEM] * 5,
    )(owners, stats, scores_p, scores_r, keys, resident)
    parts = swap(part)
    coded = call(
        project_kernel,
        jax.ShapeDtypeStruct((seqs, 2, out_width + LANES), jnp.int16),
        [VMEM] * 4,
    )(owners_row, parts, w_uv, w_o)
    return call(add_kernel, jax.ShapeDtypeStruct((1, 2, out_width), BF16), [VMEM])(swap(coded))


def solution(mesh):
    in_specs = (
        P(("group", "seq"), None, None),
        P("group"),
        P("group"),
        P(("group", "seq"), None, None),
        P("group", None, None),
        P("group", None, "seq", None),
        P(),
        P("seq", None, None),
        P("seq", None, None),
        P("seq", None, None),
    )
    out_specs = P(("group", "seq"), None, None)
    return jax.shard_map(
        on_device, mesh=mesh, in_specs=in_specs, out_specs=out_specs, check_vma=False
    )
```

```python
import functools

import jax
import jax.numpy as jnp
import numpy as np
from jax import lax
from jax.experimental import pallas as pl
from jax.experimental.pallas import tpu as pltpu
from jax.sharding import PartitionSpec as P

F32 = jnp.float32
BF16 = jnp.bfloat16
I32 = jnp.int32
I16 = jnp.int16
VMEM = pl.BlockSpec(memory_space=pltpu.VMEM)
SMEM = pl.BlockSpec(memory_space=pltpu.SMEM)
HBM = pl.BlockSpec(memory_space=pltpu.HBM)
LANES = 128
PACK = 16
PART = 6
BITS = 14.0
NEAR = 4


def iota(shape, dim):
    return lax.broadcasted_iota(I32, shape, dim)


def dot(a, b, dims=((1,), (0,))):
    return lax.dot_general(a, b, (dims, ((), ())), preferred_element_type=F32)


def column_of(row, picks):
    n, width = picks.shape[0], row.shape[1]
    hit = iota((n, width), 1) == picks
    return jnp.sum(jnp.where(hit, row, 0), axis=1, keepdims=True)


def slots_of(owners_row):
    seqs = owners_row.shape[1]
    owners_col = column_of(owners_row, iota((seqs, 1), 0))
    earlier = iota((seqs, seqs), 0) < iota((seqs, seqs), 1)
    same = (owners_col == owners_row) & earlier
    return jnp.sum(jnp.where(same, 1, 0), axis=0, keepdims=True)


def doubled(row):
    seqs = row.shape[1]
    col = column_of(row, iota((seqs, 1), 0))
    hit = iota((seqs, 2 * seqs), 1) // 2 == iota((seqs, 2 * seqs), 0)
    return jnp.sum(jnp.where(hit, col, 0), axis=0, keepdims=True)


def relative(n, device, count):
    far = count // NEAR
    return ((device // NEAR) ^ (n % far)) * NEAR + ((device % NEAR) ^ (n // far))


def query_kernel(
    res_rows, owners_hbm, lengths_hbm, freq_hbm, queries_hbm, uk_hbm, out_ref, owners_ref, lengths_ref, freq_ref, queries_ref, uk_ref, flat, sems
):
    copies = []
    pairs = [
        (owners_hbm, owners_ref),
        (lengths_hbm, lengths_ref),
        (freq_hbm, freq_ref),
        (queries_hbm, queries_ref),
        (uk_hbm, uk_ref),
    ]
    for n, (source, target) in enumerate(pairs):
        copies.append(pltpu.make_async_copy(source, target, sems.at[n]))
        copies[-1].start()
    for copy in copies:
        copy.wait()
    seqs = owners_ref.shape[1]
    nope, latent = uk_ref.shape
    rope = freq_ref.shape[1]
    half = latent // 2
    rows = 2 * seqs
    for s in range(seqs):
        flat[2 * s : 2 * s + 2, : nope + rope] = queries_ref[s, 0].astype(F32)
    values = flat[:, : nope + rope]
    absorbed = dot(values[:, :nope].astype(BF16), uk_ref[...]).astype(BF16)
    row = iota((rows, 1), 0)
    lengths = column_of(lengths_ref[...], row // 2)
    angle = (res_rows + lengths + row % 2).astype(F32) * freq_ref[...]
    x = values[:, nope:]
    swapped = jnp.concatenate([x[:, rope // 2 :], x[:, : rope // 2]], axis=1)
    sine = jnp.sin(angle)
    sine = jnp.where(iota(x.shape, 1) < rope // 2, -sine, sine)
    turned = x * jnp.cos(angle) + swapped * sine
    zero = jnp.zeros((rows, rope), F32)
    pieces = [absorbed[:, :half], absorbed[:, half:]]
    for k in range(3):
        blocks = [turned if j == k else zero for j in range(half // rope)]
        pieces.append(jnp.concatenate(blocks, axis=1).astype(BF16))
    owners = owners_ref[...]
    owner = doubled(owners)
    slot = doubled(slots_of(owners))
    count = out_ref.shape[0]
    total = count * PACK
    shape = (total, rows)
    dest, r = iota(shape, 0) // PACK, iota(shape, 0) % PACK
    seq, tok = iota(shape, 1) // 2, iota(shape, 1) % 2
    here = jnp.where(owner == dest, slot + 1, -1)
    result = None
    for p in range(2):
        q = r - PART * p
        wanted = ((q // 2 == 0) & (seq == dest)) | (here == q // 2)
        hit = (q >= 0) & (q < PART) & (tok == q % 2) & wanted
        one = dot(jnp.where(hit, 1.0, 0.0).astype(BF16), pieces[p])
        result = one if result is None else result + one
    for k in range(3):
        match = (seq == dest) if k == 0 else (here == k)
        hit = (r == 2 * PART + tok) & match
        result = result + dot(jnp.where(hit, 1.0, 0.0).astype(BF16), pieces[2 + k])
    out_ref[...] = result.astype(BF16).reshape(out_ref.shape)


def compress_kernel(res_rows, lengths_ref, freq_ref, gain_ref, prompt_ref, new_ref, out_ref):
    latent = gain_ref.shape[1]
    width, most = prompt_ref.shape[1:]
    half = (width - latent) // 2
    device = lax.axis_index("seq")
    fresh = new_ref[device].astype(F32)
    fresh = jnp.concatenate([fresh, jnp.zeros((PACK - 2, width), F32)], axis=0).astype(BF16)
    pick = jnp.where(iota((PACK, LANES), 0) == iota((PACK, LANES), 1), 1.0, 0.0).astype(BF16)
    fresh = dot(fresh, pick, ((0,), (0,)))
    gain = jnp.broadcast_to(gain_ref[...].astype(F32), (PACK, latent))
    top = jnp.where(iota((PACK, LANES), 0) == 0, 1.0, 0.0).astype(BF16)
    gain = dot(gain.astype(BF16), top, ((0,), (0,)))
    freq = freq_ref[...]
    for i in range(most // LANES + 1):
        at = slice(i * LANES, (i + 1) * LANES)
        lane = iota((1, LANES), 1)
        if i * LANES < most:
            raw = prompt_ref[0, :, at].astype(F32)
            position = res_rows + i * LANES + lane
        else:
            raw = fresh
            position = res_rows + lengths_ref[device] + lane
        lat = raw[:latent]
        meansq = jnp.sum(lat * lat, axis=0, keepdims=True) * (1.0 / latent)
        out_ref[:latent, at] = (lat * lax.rsqrt(meansq + 1e-06) * gain).astype(BF16)
        angle = position.astype(F32) * freq
        cosine, sine = jnp.cos(angle), jnp.sin(angle)
        x1, x2 = raw[latent : latent + half], raw[latent + half :]
        out_ref[latent : latent + half, at] = (x1 * cosine - x2 * sine).astype(BF16)
        out_ref[latent + half :, at] = (x2 * cosine + x1 * sine).astype(BF16)


def score_kernel(most, scale, lengths_ref, q_ref, keys_ref, resident_ref, sp_ref, sr_ref, stat_ref):
    heads = q_ref.shape[0]
    half = q_ref.shape[2]
    width = keys_ref.shape[0]
    rope = width - 2 * half
    device = lax.axis_index("seq")
    rows = 2 * heads
    total = heads * PACK
    flat = q_ref[...].reshape(total, half)
    shape = (rows, total)
    head, tok = iota(shape, 0) // 2, iota(shape, 0) % 2
    source = iota(shape, 1) - head * PACK

    def picked(r):
        hit = source == r + tok
        return dot(jnp.where(hit, 1.0, 0.0).astype(BF16), flat)

    turned = picked(2 * PART)
    tops, sums = [], []
    for k in range(3):
        query = jnp.concatenate(
            [picked(2 * k), picked(PART + 2 * k), turned[:, k * rope : (k + 1) * rope]], axis=1
        ).astype(BF16)
        keys = keys_ref[...] if k == 0 else resident_ref[k - 1]
        scores = dot(query, keys) * scale
        if k == 0:
            at = iota(scores.shape, 1)
            token = iota(scores.shape, 0) % 2
            seen = (at < lengths_ref[device]) | ((at >= most) & (at <= most + token))
            scores = jnp.where(seen, scores, -1e30)
            sp_ref[...] = scores
        else:
            sr_ref[k - 1] = scores
        top = jnp.max(scores, axis=1, keepdims=True)
        tops.append(top)
        sums.append(jnp.sum(jnp.exp(scores - top), axis=1, keepdims=True))
    lanes = stat_ref.shape[2]
    here = iota((3 * rows, lanes), 0) == iota((3 * rows, lanes), 1)
    stat_ref[0, 0:1] = jnp.sum(jnp.where(here, jnp.concatenate(tops, axis=0), 0.0), axis=0, keepdims=True)
    stat_ref[0, 1:2] = jnp.sum(jnp.where(here, jnp.concatenate(sums, axis=0), 0.0), axis=0, keepdims=True)


def attend_kernel(owners_ref, stat_ref, sp_ref, sr_ref, keys_ref, resident_ref, out_ref):
    heads = out_ref.shape[0]
    latent = out_ref.shape[1] // PART * LANES
    seqs = owners_ref.shape[0]
    rows = 2 * heads
    device = lax.axis_index("seq")
    lanes = stat_ref.shape[2]
    my_owner = owners_ref[device]
    my_slot = jnp.int32(0)
    seen = jnp.int32(0)
    first = jnp.int32(0)
    second = jnp.int32(0)
    for s in range(seqs):
        owner = owners_ref[s]
        my_slot = my_slot + jnp.where((owner == my_owner) & (s < device), 1, 0)
        mine = owner == device
        first = jnp.where(mine & (seen == 0), s, first)
        second = jnp.where(mine & (seen == 1), s, second)
        seen = seen + jnp.where(mine, 1, 0)

    def column(row, segment):
        picks = iota((rows, 1), 0) + segment * rows
        hit = iota((rows, lanes), 1) == picks
        return jnp.sum(jnp.where(hit, row, 0.0), axis=1, keepdims=True)

    mine = stat_ref[device]
    others = [(stat_ref[my_owner], 1 + my_slot), (stat_ref[first], 0), (stat_ref[second], 0)]
    for k in range(3):
        other, segment = others[k]
        top0, sum0 = column(mine[0:1], k), column(mine[1:2], k)
        top1, sum1 = column(other[0:1], segment), column(other[1:2], segment)
        top = jnp.maximum(top0, top1)
        total = sum0 * jnp.exp(top0 - top) + sum1 * jnp.exp(top1 - top)
        scores = sp_ref[...] if k == 0 else sr_ref[k - 1]
        keys = keys_ref[:latent, :] if k == 0 else resident_ref[k - 1, :latent, :]
        weights = jnp.exp(scores - top).astype(BF16)
        part = dot(weights, keys, ((1,), (1,))) / total
        for h in range(heads):
            for c in range(latent // LANES):
                at = c * PART + 2 * k
                out_ref[h, at : at + 2, :] = part[2 * h : 2 * h + 2, c * LANES : (c + 1) * LANES]


def encode(x):
    top = jnp.max(jnp.abs(x), axis=1, keepdims=True)
    power = jnp.clip(jnp.floor(jnp.log2(jnp.maximum(top, 1e-35))) + 1.0, -100.0, 100.0)
    coded = jnp.round(x * jnp.exp2(BITS - power)).astype(I32).astype(I16)
    return coded, jnp.broadcast_to(power, (x.shape[0], LANES)).astype(I32).astype(I16)


def decode(ref, n, width):
    power = ref[n, :, width : width + 1].astype(I32).astype(F32)
    return ref[n, :, :width].astype(I32).astype(F32) * jnp.exp2(power - BITS)


def project_kernel(owners_ref, part_ref, uv_ref, wo_ref, *out_refs):
    count, each, lanes = part_ref.shape
    seqs = owners_ref.shape[1]
    cuts = each // PART
    rows = 2 * seqs
    width = wo_ref.shape[2]
    device = lax.axis_index("seq")
    owners = owners_ref[...]
    row = iota((cuts * rows, 1), 0)
    cut = row // rows
    seq, tok = relative(row % rows // 2, device, count), row % 2
    owner = column_of(owners, seq)
    slot = column_of(slots_of(owners), seq)
    first = seq * each + cut * PART + tok
    second = owner * each + cut * PART + 2 + 2 * slot + tok
    at = iota((cuts * rows, count * each), 1)
    hit = jnp.where((at == first) | (at == second), 1.0, 0.0).astype(BF16)
    rest = part_ref[...].reshape(count * each, lanes)
    latent = None
    for _ in range(3):
        piece = rest.astype(BF16)
        rest = rest - piece.astype(F32)
        one = dot(hit, piece)
        latent = one if latent is None else latent + one
    latent = latent.astype(BF16)
    latent = jnp.concatenate([latent[c * rows : (c + 1) * rows] for c in range(cuts)], axis=1)
    head_out = dot(latent, uv_ref[0]).astype(BF16)
    coded, power = encode(dot(head_out, wo_ref[0]))
    far = count // NEAR
    for j in range(NEAR):
        for i in range(far):
            at = 2 * (j * far + i)
            out_refs[j][i, :, :width] = coded[at : at + 2]
            out_refs[j][i, :, width:] = power[at : at + 2]


def middle_kernel(*refs):
    in_refs, own_ref, out_refs = refs[:NEAR], refs[NEAR], refs[NEAR + 1 :]
    width = own_ref.shape[1]
    for i in range(in_refs[0].shape[0]):
        total = None
        for ref in in_refs:
            one = decode(ref, i, width)
            total = one if total is None else total + one
        if i == 0:
            own_ref[...] = total
        else:
            coded, power = encode(total)
            out_refs[i - 1][0, :, :width] = coded
            out_refs[i - 1][0, :, width:] = power


def final_kernel(own_ref, *refs):
    in_refs, out_ref = refs[:-1], refs[-1]
    total = own_ref[...]
    for ref in in_refs:
        total = total + decode(ref, 0, own_ref.shape[1])
    out_ref[0] = total.astype(BF16)


def swap(x):
    return lax.all_to_all(x, "seq", split_axis=0, concat_axis=0, tiled=True)


def trade(x, step):
    count = lax.axis_size("seq")
    return lax.ppermute(x, "seq", [(d, d ^ step) for d in range(count)])


def call(kernel, shapes, specs, scratch=(), cost=None, room=40):
    single = not isinstance(shapes, (list, tuple))
    return pl.pallas_call(
        kernel,
        out_shape=shapes,
        in_specs=specs,
        out_specs=VMEM if single else [VMEM] * len(shapes),
        scratch_shapes=list(scratch),
        cost_estimate=cost,
        compiler_params=pltpu.CompilerParams(vmem_limit_bytes=room * 1024 * 1024),
    )


def on_device(prompt_raw, lengths, owners, resident, new_raw, queries, kv_gain, w_uk, w_uv, w_o):
    count = lax.axis_size("seq")
    seqs = lengths.shape[0]
    most, width = prompt_raw.shape[1:]
    latent = kv_gain.shape[0]
    res_rows = resident.shape[1]
    nope = w_uk.shape[1]
    rope = width - latent
    heads = count
    out_width = w_o.shape[2]
    scale = 1.0 / queries.shape[-1] ** 0.5
    half = np.arange(rope // 2, dtype=np.float32)
    freq = (np.float32(10000.0) ** (-(half * np.float32(2.0)) / np.float32(rope))).astype(np.float32)
    freq_row = jnp.asarray(np.concatenate([freq, freq])[None])
    freq_rows = jnp.asarray(np.broadcast_to(freq[:, None], (rope // 2, LANES)))
    owners_row, lengths_row = owners.reshape(1, seqs), lengths.reshape(1, seqs)
    prompt_raw = prompt_raw.transpose(0, 2, 1)
    resident = resident.transpose(0, 2, 1)
    queries = queries.transpose(0, 2, 1, 3)
    keys_rows = most + LANES

    query = call(
        functools.partial(query_kernel, res_rows),
        jax.ShapeDtypeStruct((count, PACK, latent // 2), BF16),
        [HBM] * 5,
        [
            pltpu.VMEM((1, seqs), I32),
            pltpu.VMEM((1, seqs), I32),
            pltpu.VMEM((1, rope), F32),
            pltpu.VMEM(queries.shape, BF16),
            pltpu.VMEM((nope, latent), BF16),
            pltpu.VMEM((2 * seqs, -(-(nope + rope) // LANES) * LANES), F32),
            pltpu.SemaphoreType.DMA((5,)),
        ],
        room=60,
    )(owners_row, lengths_row, freq_row, queries, w_uk[0])
    received = swap(query)
    keys = call(
        functools.partial(compress_kernel, res_rows),
        jax.ShapeDtypeStruct((width, keys_rows), BF16),
        [SMEM] + [VMEM] * 4,
        cost=pl.CostEstimate(flops=10**7, bytes_accessed=10**7, transcendentals=10**5),
    )(lengths, freq_rows, kv_gain.reshape(1, latent), prompt_raw, new_raw)
    lanes = -(-6 * heads // LANES) * LANES
    scores_p, scores_r, stat = call(
        functools.partial(score_kernel, most, scale),
        [
            jax.ShapeDtypeStruct((2 * heads, keys_rows), F32),
            jax.ShapeDtypeStruct((2, 2 * heads, res_rows), F32),
            jax.ShapeDtypeStruct((1, 2, lanes), F32),
        ],
        [SMEM] + [VMEM] * 3,
    )(lengths, received, keys, resident)
    stats = lax.all_gather(stat, "seq", axis=0, tiled=True)
    part = call(
        attend_kernel,
        jax.ShapeDtypeStruct((heads, PART * (latent // LANES), LANES), F32),
        [SMEM] + [VMEM] * 5,
    )(owners, stats, scores_p, scores_r, keys, resident)
    parts = swap(part)
    far = count // NEAR
    message = jax.ShapeDtypeStruct((far, 2, out_width + LANES), I16)
    sums = call(project_kernel, [message] * NEAR, [VMEM] * 4)(owners_row, parts, w_uv, w_o)
    sums = [sums[0]] + [trade(sums[j], j) for j in range(1, NEAR)]
    message = jax.ShapeDtypeStruct((1, 2, out_width + LANES), I16)
    own, *rest = call(
        middle_kernel,
        [jax.ShapeDtypeStruct((2, out_width), F32)] + [message] * (far - 1),
        [VMEM] * NEAR,
    )(*sums)
    rest = [trade(x, (i + 1) * NEAR) for i, x in enumerate(rest)]
    return call(
        final_kernel, jax.ShapeDtypeStruct((1, 2, out_width), BF16), [VMEM] * far
    )(own, *rest)


def solution(mesh):
    in_specs = (
        P(("group", "seq"), None, None),
        P("group"),
        P("group"),
        P(("group", "seq"), None, None),
        P("group", None, None),
        P("group", None, "seq", None),
        P(),
        P("seq", None, None),
        P("seq", None, None),
        P("seq", None, None),
    )
    out_specs = P(("group", "seq"), None, None)
    return jax.shard_map(
        on_device, mesh=mesh, in_specs=in_specs, out_specs=out_specs, check_vma=False
    )
```

```python
import functools

import jax
import jax.numpy as jnp
import numpy as np
from jax import lax
from jax.experimental import pallas as pl
from jax.experimental.pallas import tpu as pltpu
from jax.sharding import PartitionSpec as P

F32 = jnp.float32
BF16 = jnp.bfloat16
I32 = jnp.int32
I16 = jnp.int16
VMEM = pl.BlockSpec(memory_space=pltpu.VMEM)
SMEM = pl.BlockSpec(memory_space=pltpu.SMEM)
HBM = pl.BlockSpec(memory_space=pltpu.HBM)
LANES = 128
PACK = 16
PART = 6
BITS = 14.0
NEAR = 4


def iota(shape, dim):
    return lax.broadcasted_iota(I32, shape, dim)


def dot(a, b, dims=((1,), (0,))):
    return lax.dot_general(a, b, (dims, ((), ())), preferred_element_type=F32)


def column_of(row, picks):
    n, width = picks.shape[0], row.shape[1]
    hit = iota((n, width), 1) == picks
    return jnp.sum(jnp.where(hit, row, 0), axis=1, keepdims=True)


def slots_of(owners_row):
    seqs = owners_row.shape[1]
    owners_col = column_of(owners_row, iota((seqs, 1), 0))
    earlier = iota((seqs, seqs), 0) < iota((seqs, seqs), 1)
    same = (owners_col == owners_row) & earlier
    return jnp.sum(jnp.where(same, 1, 0), axis=0, keepdims=True)


def doubled(row):
    seqs = row.shape[1]
    col = column_of(row, iota((seqs, 1), 0))
    hit = iota((seqs, 2 * seqs), 1) // 2 == iota((seqs, 2 * seqs), 0)
    return jnp.sum(jnp.where(hit, col, 0), axis=0, keepdims=True)


def query_kernel(
    res_rows, owners_hbm, lengths_hbm, freq_hbm, queries_hbm, uk_hbm, out_ref, owners_ref, lengths_ref, freq_ref, queries_ref, uk_ref, flat, sems
):
    copies = []
    pairs = [
        (owners_hbm, owners_ref),
        (lengths_hbm, lengths_ref),
        (freq_hbm, freq_ref),
        (queries_hbm, queries_ref),
        (uk_hbm, uk_ref),
    ]
    for n, (source, target) in enumerate(pairs):
        copies.append(pltpu.make_async_copy(source, target, sems.at[n]))
        copies[-1].start()
    for copy in copies:
        copy.wait()
    seqs = owners_ref.shape[1]
    nope, latent = uk_ref.shape
    rope = freq_ref.shape[1]
    half = latent // 2
    rows = 2 * seqs
    for s in range(seqs):
        flat[2 * s : 2 * s + 2, : nope + rope] = queries_ref[s, 0].astype(F32)
    values = flat[:, : nope + rope]
    absorbed = dot(values[:, :nope].astype(BF16), uk_ref[...]).astype(BF16)
    row = iota((rows, 1), 0)
    lengths = column_of(lengths_ref[...], row // 2)
    angle = (res_rows + lengths + row % 2).astype(F32) * freq_ref[...]
    x = values[:, nope:]
    swapped = jnp.concatenate([x[:, rope // 2 :], x[:, : rope // 2]], axis=1)
    sine = jnp.sin(angle)
    sine = jnp.where(iota(x.shape, 1) < rope // 2, -sine, sine)
    turned = x * jnp.cos(angle) + swapped * sine
    zero = jnp.zeros((rows, rope), F32)
    pieces = [absorbed[:, :half], absorbed[:, half:]]
    for k in range(3):
        blocks = [turned if j == k else zero for j in range(half // rope)]
        pieces.append(jnp.concatenate(blocks, axis=1).astype(BF16))
    owners = owners_ref[...]
    owner = doubled(owners)
    slot = doubled(slots_of(owners))
    count = out_ref.shape[0]
    total = count * PACK
    shape = (total, rows)
    dest, r = iota(shape, 0) // PACK, iota(shape, 0) % PACK
    seq, tok = iota(shape, 1) // 2, iota(shape, 1) % 2
    here = jnp.where(owner == dest, slot + 1, -1)
    result = None
    for p in range(2):
        q = r - PART * p
        wanted = ((q // 2 == 0) & (seq == dest)) | (here == q // 2)
        hit = (q >= 0) & (q < PART) & (tok == q % 2) & wanted
        one = dot(jnp.where(hit, 1.0, 0.0).astype(BF16), pieces[p])
        result = one if result is None else result + one
    for k in range(3):
        match = (seq == dest) if k == 0 else (here == k)
        hit = (r == 2 * PART + tok) & match
        result = result + dot(jnp.where(hit, 1.0, 0.0).astype(BF16), pieces[2 + k])
    out_ref[...] = result.astype(BF16).reshape(out_ref.shape)


def compress_kernel(
    res_rows, lengths_ref, freq_ref, gain_ref, prompt_ref, new_ref, resident_hbm, out_ref, resident_ref, sem
):
    fetch = pltpu.make_async_copy(resident_hbm, resident_ref, sem)
    fetch.start()
    latent = gain_ref.shape[1]
    width, most = prompt_ref.shape[1:]
    half = (width - latent) // 2
    device = lax.axis_index("seq")
    fresh = new_ref[device].astype(F32)
    fresh = jnp.concatenate([fresh, jnp.zeros((PACK - 2, width), F32)], axis=0).astype(BF16)
    pick = jnp.where(iota((PACK, LANES), 0) == iota((PACK, LANES), 1), 1.0, 0.0).astype(BF16)
    fresh = dot(fresh, pick, ((0,), (0,)))
    gain = jnp.broadcast_to(gain_ref[...].astype(F32), (PACK, latent))
    top = jnp.where(iota((PACK, LANES), 0) == 0, 1.0, 0.0).astype(BF16)
    gain = dot(gain.astype(BF16), top, ((0,), (0,)))
    freq = column_of(freq_ref[...], iota((half, 1), 0))
    for i in range(most // LANES + 1):
        at = slice(i * LANES, (i + 1) * LANES)
        lane = iota((1, LANES), 1)
        if i * LANES < most:
            raw = prompt_ref[0, :, at].astype(F32)
            position = res_rows + i * LANES + lane
        else:
            raw = fresh
            position = res_rows + lengths_ref[device] + lane
        lat = raw[:latent]
        meansq = jnp.sum(lat * lat, axis=0, keepdims=True) * (1.0 / latent)
        out_ref[:latent, at] = (lat * lax.rsqrt(meansq + 1e-06) * gain).astype(BF16)
        angle = position.astype(F32) * freq
        cosine, sine = jnp.cos(angle), jnp.sin(angle)
        x1, x2 = raw[latent : latent + half], raw[latent + half :]
        out_ref[latent : latent + half, at] = (x1 * cosine - x2 * sine).astype(BF16)
        out_ref[latent + half :, at] = (x2 * cosine + x1 * sine).astype(BF16)
    fetch.wait()


def score_kernel(most, scale, lengths_ref, q_ref, keys_ref, resident_ref, sp_ref, sr_ref, stat_ref):
    heads = q_ref.shape[0]
    half = q_ref.shape[2]
    width = keys_ref.shape[0]
    rope = width - 2 * half
    device = lax.axis_index("seq")
    rows = 2 * heads
    total = heads * PACK
    flat = q_ref[...].reshape(total, half)
    shape = (rows, total)
    head, tok = iota(shape, 0) // 2, iota(shape, 0) % 2
    source = iota(shape, 1) - head * PACK

    def picked(r):
        hit = source == r + tok
        return dot(jnp.where(hit, 1.0, 0.0).astype(BF16), flat)

    turned = picked(2 * PART)
    tops, sums = [], []
    for k in range(3):
        query = jnp.concatenate(
            [picked(2 * k), picked(PART + 2 * k), turned[:, k * rope : (k + 1) * rope]], axis=1
        ).astype(BF16)
        keys = keys_ref[...] if k == 0 else resident_ref[k - 1]
        scores = dot(query, keys) * scale
        if k == 0:
            at = iota(scores.shape, 1)
            token = iota(scores.shape, 0) % 2
            seen = (at < lengths_ref[device]) | ((at >= most) & (at <= most + token))
            scores = jnp.where(seen, scores, -1e30)
            sp_ref[...] = scores
        else:
            sr_ref[k - 1] = scores
        top = jnp.max(scores, axis=1, keepdims=True)
        tops.append(top)
        sums.append(jnp.sum(jnp.exp(scores - top), axis=1, keepdims=True))
    lanes = stat_ref.shape[2]
    here = iota((3 * rows, lanes), 0) == iota((3 * rows, lanes), 1)
    top = jnp.sum(jnp.where(here, jnp.concatenate(tops, axis=0), 0.0), axis=0, keepdims=True)
    total = jnp.sum(jnp.where(here, jnp.concatenate(sums, axis=0), 0.0), axis=0, keepdims=True)
    for n in range(stat_ref.shape[0]):
        stat_ref[n, 0:1] = top
        stat_ref[n, 1:2] = total


def attend_kernel(owners_ref, stat_ref, sp_ref, sr_ref, keys_ref, resident_ref, out_ref):
    heads = out_ref.shape[0]
    latent = out_ref.shape[1] // PART * LANES
    seqs = owners_ref.shape[0]
    rows = 2 * heads
    device = lax.axis_index("seq")
    lanes = stat_ref.shape[2]
    my_owner = owners_ref[device]
    my_slot = jnp.int32(0)
    seen = jnp.int32(0)
    first = jnp.int32(0)
    second = jnp.int32(0)
    for s in range(seqs):
        owner = owners_ref[s]
        my_slot = my_slot + jnp.where((owner == my_owner) & (s < device), 1, 0)
        mine = owner == device
        first = jnp.where(mine & (seen == 0), s, first)
        second = jnp.where(mine & (seen == 1), s, second)
        seen = seen + jnp.where(mine, 1, 0)

    def column(row, segment):
        picks = iota((rows, 1), 0) + segment * rows
        hit = iota((rows, lanes), 1) == picks
        return jnp.sum(jnp.where(hit, row, 0.0), axis=1, keepdims=True)

    mine = stat_ref[device]
    others = [(stat_ref[my_owner], 1 + my_slot), (stat_ref[first], 0), (stat_ref[second], 0)]
    for k in range(3):
        other, segment = others[k]
        top0, sum0 = column(mine[0:1], k), column(mine[1:2], k)
        top1, sum1 = column(other[0:1], segment), column(other[1:2], segment)
        top = jnp.maximum(top0, top1)
        total = sum0 * jnp.exp(top0 - top) + sum1 * jnp.exp(top1 - top)
        scores = sp_ref[...] if k == 0 else sr_ref[k - 1]
        keys = keys_ref[:latent, :] if k == 0 else resident_ref[k - 1, :latent, :]
        weights = jnp.exp(scores - top).astype(BF16)
        part = dot(weights, keys, ((1,), (1,))) / total
        for h in range(heads):
            for c in range(latent // LANES):
                at = c * PART + 2 * k
                out_ref[h, at : at + 2, :] = part[2 * h : 2 * h + 2, c * LANES : (c + 1) * LANES]


def encode(x):
    top = jnp.max(jnp.abs(x), axis=1, keepdims=True)
    power = jnp.clip(jnp.floor(jnp.log2(jnp.maximum(top, 1e-35))) + 1.0, -100.0, 100.0)
    coded = jnp.round(x * jnp.exp2(BITS - power)).astype(I32).astype(I16)
    return coded, jnp.broadcast_to(power, (x.shape[0], LANES)).astype(I32).astype(I16)


def decode(ref, n, width):
    power = ref[n, :, width : width + 1].astype(I32).astype(F32)
    return ref[n, :, :width].astype(I32).astype(F32) * jnp.exp2(power - BITS)


def project_kernel(owners_ref, part_ref, uv_ref, wo_ref, out_ref):
    count, each, lanes = part_ref.shape
    seqs = owners_ref.shape[1]
    cuts = each // PART
    rows = 2 * seqs
    width = wo_ref.shape[2]
    far = count // NEAR
    owners = owners_ref[...]
    row = iota((cuts * rows, 1), 0)
    cut = row // rows
    turn = row % rows // 2
    seq, tok = turn % far * NEAR + turn // far, row % 2
    owner = column_of(owners, seq)
    slot = column_of(slots_of(owners), seq)
    first = seq * each + cut * PART + tok
    second = owner * each + cut * PART + 2 + 2 * slot + tok
    at = iota((cuts * rows, count * each), 1)
    hit = jnp.where((at == first) | (at == second), 1.0, 0.0).astype(BF16)
    rest = part_ref[...].reshape(count * each, lanes)
    latent = None
    for _ in range(3):
        piece = rest.astype(BF16)
        rest = rest - piece.astype(F32)
        one = dot(hit, piece)
        latent = one if latent is None else latent + one
    latent = latent.astype(BF16)
    latent = jnp.concatenate([latent[c * rows : (c + 1) * rows] for c in range(cuts)], axis=1)
    head_out = dot(latent, uv_ref[0]).astype(BF16)
    coded, power = encode(dot(head_out, wo_ref[0]))
    for n in range(count):
        out_ref[n, :, :width] = coded[2 * n : 2 * n + 2]
        out_ref[n, :, width:] = power[2 * n : 2 * n + 2]


def added(ref, places, width):
    total = None
    for n in places:
        one = decode(ref, n, width)
        total = one if total is None else total + one
    return total


def middle_kernel(in_ref, out_ref):
    far = out_ref.shape[0]
    width = out_ref.shape[2] - LANES
    for i in range(far):
        coded, power = encode(added(in_ref, range(i, in_ref.shape[0], far), width))
        out_ref[i, :, :width] = coded
        out_ref[i, :, width:] = power


def final_kernel(in_ref, out_ref):
    out_ref[0] = added(in_ref, range(in_ref.shape[0]), out_ref.shape[2]).astype(BF16)


def swap(x):
    return lax.all_to_all(x, "seq", split_axis=0, concat_axis=0, tiled=True)


def swap_near(x):
    count = lax.axis_size("seq")
    groups = [list(range(z, z + NEAR)) for z in range(0, count, NEAR)]
    return lax.all_to_all(x, "seq", split_axis=0, concat_axis=0, axis_index_groups=groups, tiled=True)


def swap_far(x):
    count = lax.axis_size("seq")
    groups = [list(range(q, count, NEAR)) for q in range(NEAR)]
    return lax.all_to_all(x, "seq", split_axis=0, concat_axis=0, axis_index_groups=groups, tiled=True)


def call(kernel, shapes, specs, scratch=(), cost=None, room=40):
    single = not isinstance(shapes, (list, tuple))
    return pl.pallas_call(
        kernel,
        out_shape=shapes,
        in_specs=specs,
        out_specs=VMEM if single else [VMEM] * len(shapes),
        scratch_shapes=list(scratch),
        cost_estimate=cost,
        compiler_params=pltpu.CompilerParams(vmem_limit_bytes=room * 1024 * 1024),
    )


def on_device(prompt_raw, lengths, owners, resident, new_raw, queries, kv_gain, w_uk, w_uv, w_o):
    count = lax.axis_size("seq")
    seqs = lengths.shape[0]
    most, width = prompt_raw.shape[1:]
    latent = kv_gain.shape[0]
    res_rows = resident.shape[1]
    nope = w_uk.shape[1]
    rope = width - latent
    heads = count
    out_width = w_o.shape[2]
    scale = 1.0 / queries.shape[-1] ** 0.5
    half = np.arange(rope // 2, dtype=np.float32)
    freq = (np.float32(10000.0) ** (-(half * np.float32(2.0)) / np.float32(rope))).astype(np.float32)
    freq_row = jnp.asarray(np.concatenate([freq, freq])[None])
    owners_row, lengths_row = owners.reshape(1, seqs), lengths.reshape(1, seqs)
    prompt_raw = prompt_raw.transpose(0, 2, 1)
    resident = resident.transpose(0, 2, 1)
    queries = queries.transpose(0, 2, 1, 3)
    keys_rows = most + LANES

    query = call(
        functools.partial(query_kernel, res_rows),
        jax.ShapeDtypeStruct((count, PACK, latent // 2), BF16),
        [HBM] * 5,
        [
            pltpu.VMEM((1, seqs), I32),
            pltpu.VMEM((1, seqs), I32),
            pltpu.VMEM((1, rope), F32),
            pltpu.VMEM(queries.shape, BF16),
            pltpu.VMEM((nope, latent), BF16),
            pltpu.VMEM((2 * seqs, -(-(nope + rope) // LANES) * LANES), F32),
            pltpu.SemaphoreType.DMA((5,)),
        ],
        room=60,
    )(owners_row, lengths_row, freq_row, queries, w_uk[0])
    received = swap(query)
    keys, resident = call(
        functools.partial(compress_kernel, res_rows),
        [jax.ShapeDtypeStruct((width, keys_rows), BF16), jax.ShapeDtypeStruct(resident.shape, BF16)],
        [SMEM] + [VMEM] * 4 + [HBM],
        [pltpu.SemaphoreType.DMA],
        cost=pl.CostEstimate(flops=10**7, bytes_accessed=10**7, transcendentals=10**5),
    )(lengths, freq_row, kv_gain.reshape(1, latent), prompt_raw, new_raw, resident)
    lanes = -(-6 * heads // LANES) * LANES
    scores_p, scores_r, stat = call(
        functools.partial(score_kernel, most, scale),
        [
            jax.ShapeDtypeStruct((2 * heads, keys_rows), F32),
            jax.ShapeDtypeStruct((2, 2 * heads, res_rows), F32),
            jax.ShapeDtypeStruct((NEAR, 2, lanes), F32),
        ],
        [SMEM] + [VMEM] * 3,
    )(lengths, received, keys, resident)
    far = count // NEAR
    stats = swap_far(jnp.broadcast_to(swap_near(stat)[None], (far, NEAR, 2, lanes)))
    stats = stats.reshape(count, 2, lanes)
    part = call(
        attend_kernel,
        jax.ShapeDtypeStruct((heads, PART * (latent // LANES), LANES), F32),
        [SMEM] + [VMEM] * 5,
    )(owners, stats, scores_p, scores_r, keys, resident)
    parts = swap(part)
    sums = call(
        project_kernel, jax.ShapeDtypeStruct((count, 2, out_width + LANES), I16), [VMEM] * 4
    )(owners_row, parts, w_uv, w_o)
    sums = call(middle_kernel, jax.ShapeDtypeStruct((far, 2, out_width + LANES), I16), [VMEM])(swap_near(sums))
    return call(final_kernel, jax.ShapeDtypeStruct((1, 2, out_width), BF16), [VMEM])(swap_far(sums))


def solution(mesh):
    in_specs = (
        P(("group", "seq"), None, None),
        P("group"),
        P("group"),
        P(("group", "seq"), None, None),
        P("group", None, None),
        P("group", None, "seq", None),
        P(),
        P("seq", None, None),
        P("seq", None, None),
        P("seq", None, None),
    )
    out_specs = P(("group", "seq"), None, None)
    return jax.shard_map(
        on_device, mesh=mesh, in_specs=in_specs, out_specs=out_specs, check_vma=False
    )
```

```python
import functools

import jax
import jax.numpy as jnp
import numpy as np
from jax import lax
from jax.experimental import pallas as pl
from jax.experimental.pallas import tpu as pltpu
from jax.sharding import PartitionSpec as P

F32 = jnp.float32
BF16 = jnp.bfloat16
I32 = jnp.int32
I16 = jnp.int16
VMEM = pl.BlockSpec(memory_space=pltpu.VMEM)
SMEM = pl.BlockSpec(memory_space=pltpu.SMEM)
HBM = pl.BlockSpec(memory_space=pltpu.HBM)
LANES = 128
PACK = 16
PART = 6
BITS = 14.0
NEAR = 4


def iota(shape, dim):
    return lax.broadcasted_iota(I32, shape, dim)


def dot(a, b, dims=((1,), (0,))):
    return lax.dot_general(a, b, (dims, ((), ())), preferred_element_type=F32)


def column_of(row, picks):
    n, width = picks.shape[0], row.shape[1]
    hit = iota((n, width), 1) == picks
    return jnp.sum(jnp.where(hit, row, 0), axis=1, keepdims=True)


def slots_of(owners_row):
    seqs = owners_row.shape[1]
    owners_col = column_of(owners_row, iota((seqs, 1), 0))
    earlier = iota((seqs, seqs), 0) < iota((seqs, seqs), 1)
    same = (owners_col == owners_row) & earlier
    return jnp.sum(jnp.where(same, 1, 0), axis=0, keepdims=True)


def doubled(row):
    seqs = row.shape[1]
    col = column_of(row, iota((seqs, 1), 0))
    hit = iota((seqs, 2 * seqs), 1) // 2 == iota((seqs, 2 * seqs), 0)
    return jnp.sum(jnp.where(hit, col, 0), axis=0, keepdims=True)


def frequencies(half, shape, dim):
    at = iota(shape, dim) % half
    values = np.float32(10000.0) ** (-(np.arange(half, dtype=np.float32) * np.float32(2.0)) / np.float32(2 * half))
    result = jnp.zeros(shape, F32)
    for i in range(half):
        result = jnp.where(at == i, float(values[i]), result)
    return result


def query_kernel(
    res_rows, owners_hbm, lengths_hbm, queries_hbm, uk_hbm, out_ref, owners_ref, lengths_ref, queries_ref, uk_ref, flat, sems
):
    copies = []
    pairs = [
        (owners_hbm, owners_ref),
        (lengths_hbm, lengths_ref),
        (queries_hbm, queries_ref),
        (uk_hbm, uk_ref),
    ]
    for n, (source, target) in enumerate(pairs):
        copies.append(pltpu.make_async_copy(source, target, sems.at[n]))
        copies[-1].start()
    for copy in copies:
        copy.wait()
    seqs = owners_ref.shape[1]
    nope, latent = uk_ref.shape
    rope = queries_ref.shape[3] - nope
    half = latent // 2
    rows = 2 * seqs
    for s in range(seqs):
        flat[2 * s : 2 * s + 2, : nope + rope] = queries_ref[s, 0].astype(F32)
    values = flat[:, : nope + rope]
    absorbed = dot(values[:, :nope].astype(BF16), uk_ref[...]).astype(BF16)
    row = iota((rows, 1), 0)
    lengths = column_of(lengths_ref[...], row // 2)
    angle = (res_rows + lengths + row % 2).astype(F32) * frequencies(rope // 2, (1, rope), 1)
    x = values[:, nope:]
    swapped = jnp.concatenate([x[:, rope // 2 :], x[:, : rope // 2]], axis=1)
    sine = jnp.sin(angle)
    sine = jnp.where(iota(x.shape, 1) < rope // 2, -sine, sine)
    turned = x * jnp.cos(angle) + swapped * sine
    zero = jnp.zeros((rows, rope), F32)
    pieces = [absorbed[:, :half], absorbed[:, half:]]
    for k in range(3):
        blocks = [turned if j == k else zero for j in range(half // rope)]
        pieces.append(jnp.concatenate(blocks, axis=1).astype(BF16))
    owners = owners_ref[...]
    owner = doubled(owners)
    slot = doubled(slots_of(owners))
    count = out_ref.shape[0]
    total = count * PACK
    shape = (total, rows)
    dest, r = iota(shape, 0) // PACK, iota(shape, 0) % PACK
    seq, tok = iota(shape, 1) // 2, iota(shape, 1) % 2
    here = jnp.where(owner == dest, slot + 1, -1)
    result = None
    for p in range(2):
        q = r - PART * p
        wanted = ((q // 2 == 0) & (seq == dest)) | (here == q // 2)
        hit = (q >= 0) & (q < PART) & (tok == q % 2) & wanted
        one = dot(jnp.where(hit, 1.0, 0.0).astype(BF16), pieces[p])
        result = one if result is None else result + one
    for k in range(3):
        match = (seq == dest) if k == 0 else (here == k)
        hit = (r == 2 * PART + tok) & match
        result = result + dot(jnp.where(hit, 1.0, 0.0).astype(BF16), pieces[2 + k])
    out_ref[...] = result.astype(BF16).reshape(out_ref.shape)


def compress_kernel(
    res_rows, lengths_ref, gain_ref, prompt_ref, new_ref, resident_hbm, out_ref, resident_ref, sem
):
    fetch = pltpu.make_async_copy(resident_hbm, resident_ref, sem)
    fetch.start()
    latent = gain_ref.shape[1]
    width, most = prompt_ref.shape[1:]
    half = (width - latent) // 2
    device = lax.axis_index("seq")
    fresh = new_ref[device].astype(F32)
    fresh = jnp.concatenate([fresh, jnp.zeros((PACK - 2, width), F32)], axis=0).astype(BF16)
    pick = jnp.where(iota((PACK, LANES), 0) == iota((PACK, LANES), 1), 1.0, 0.0).astype(BF16)
    fresh = dot(fresh, pick, ((0,), (0,)))
    gain = jnp.broadcast_to(gain_ref[...].astype(F32), (PACK, latent))
    top = jnp.where(iota((PACK, LANES), 0) == 0, 1.0, 0.0).astype(BF16)
    gain = dot(gain.astype(BF16), top, ((0,), (0,)))
    freq = frequencies(half, (half, 1), 0)
    for i in range(most // LANES + 1):
        at = slice(i * LANES, (i + 1) * LANES)
        lane = iota((1, LANES), 1)
        if i * LANES < most:
            raw = prompt_ref[0, :, at].astype(F32)
            position = res_rows + i * LANES + lane
        else:
            raw = fresh
            position = res_rows + lengths_ref[device] + lane
        lat = raw[:latent]
        meansq = jnp.sum(lat * lat, axis=0, keepdims=True) * (1.0 / latent)
        out_ref[:latent, at] = (lat * lax.rsqrt(meansq + 1e-06) * gain).astype(BF16)
        angle = position.astype(F32) * freq
        cosine, sine = jnp.cos(angle), jnp.sin(angle)
        x1, x2 = raw[latent : latent + half], raw[latent + half :]
        out_ref[latent : latent + half, at] = (x1 * cosine - x2 * sine).astype(BF16)
        out_ref[latent + half :, at] = (x2 * cosine + x1 * sine).astype(BF16)
    fetch.wait()


def score_kernel(most, scale, lengths_ref, q_ref, keys_ref, resident_ref, sp_ref, sr_ref, stat_ref):
    heads = q_ref.shape[0]
    half = q_ref.shape[2]
    width = keys_ref.shape[0]
    rope = width - 2 * half
    device = lax.axis_index("seq")
    rows = 2 * heads
    total = heads * PACK
    flat = q_ref[...].reshape(total, half)
    shape = (rows, total)
    head, tok = iota(shape, 0) // 2, iota(shape, 0) % 2
    source = iota(shape, 1) - head * PACK

    def picked(r):
        hit = source == r + tok
        return dot(jnp.where(hit, 1.0, 0.0).astype(BF16), flat)

    turned = picked(2 * PART)
    tops, sums = [], []
    for k in range(3):
        query = jnp.concatenate(
            [picked(2 * k), picked(PART + 2 * k), turned[:, k * rope : (k + 1) * rope]], axis=1
        ).astype(BF16)
        keys = keys_ref[...] if k == 0 else resident_ref[k - 1]
        scores = dot(query, keys) * scale
        if k == 0:
            at = iota(scores.shape, 1)
            token = iota(scores.shape, 0) % 2
            seen = (at < lengths_ref[device]) | ((at >= most) & (at <= most + token))
            scores = jnp.where(seen, scores, -1e30)
            sp_ref[...] = scores
        else:
            sr_ref[k - 1] = scores
        top = jnp.max(scores, axis=1, keepdims=True)
        tops.append(top)
        sums.append(jnp.sum(jnp.exp(scores - top), axis=1, keepdims=True))
    lanes = stat_ref.shape[2]
    here = iota((3 * rows, lanes), 0) == iota((3 * rows, lanes), 1)
    top = jnp.sum(jnp.where(here, jnp.concatenate(tops, axis=0), 0.0), axis=0, keepdims=True)
    total = jnp.sum(jnp.where(here, jnp.concatenate(sums, axis=0), 0.0), axis=0, keepdims=True)
    stat_ref[0, 0:1] = top
    stat_ref[0, 1:2] = total


def attend_kernel(owners_ref, *refs):
    *stat_refs, sp_ref, sr_ref, keys_ref, resident_ref, out_ref = refs
    heads = out_ref.shape[0]
    latent = out_ref.shape[1] // PART * LANES
    seqs = owners_ref.shape[0]
    rows = 2 * heads
    device = lax.axis_index("seq")
    lanes = stat_refs[0].shape[2]
    my_owner = owners_ref[device]
    my_slot = jnp.int32(0)
    seen = jnp.int32(0)
    first = jnp.int32(0)
    second = jnp.int32(0)
    for s in range(seqs):
        owner = owners_ref[s]
        my_slot = my_slot + jnp.where((owner == my_owner) & (s < device), 1, 0)
        mine = owner == device
        first = jnp.where(mine & (seen == 0), s, first)
        second = jnp.where(mine & (seen == 1), s, second)
        seen = seen + jnp.where(mine, 1, 0)

    def column(row, segment):
        picks = iota((rows, 1), 0) + segment * rows
        hit = iota((rows, lanes), 1) == picks
        return jnp.sum(jnp.where(hit, row, 0.0), axis=1, keepdims=True)

    def stat_of(other):
        near = (other % NEAR) ^ (device % NEAR)
        far = (other // NEAR) ^ (device // NEAR)
        result = jnp.zeros((2, lanes), F32)
        for i, ref in enumerate(stat_refs):
            result = jnp.where(far == i, ref[near], result)
        return result

    mine = stat_refs[0][0]
    others = [(stat_of(my_owner), 1 + my_slot), (stat_of(first), 0), (stat_of(second), 0)]
    for k in range(3):
        other, segment = others[k]
        top0, sum0 = column(mine[0:1], k), column(mine[1:2], k)
        top1, sum1 = column(other[0:1], segment), column(other[1:2], segment)
        top = jnp.maximum(top0, top1)
        total = sum0 * jnp.exp(top0 - top) + sum1 * jnp.exp(top1 - top)
        scores = sp_ref[...] if k == 0 else sr_ref[k - 1]
        keys = keys_ref[:latent, :] if k == 0 else resident_ref[k - 1, :latent, :]
        weights = jnp.exp(scores - top).astype(BF16)
        part = dot(weights, keys, ((1,), (1,))) / total
        for h in range(heads):
            for c in range(latent // LANES):
                at = c * PART + 2 * k
                out_ref[h, at : at + 2, :] = part[2 * h : 2 * h + 2, c * LANES : (c + 1) * LANES]


def encode(x):
    top = jnp.max(jnp.abs(x), axis=1, keepdims=True)
    power = jnp.clip(jnp.floor(jnp.log2(jnp.maximum(top, 1e-35))) + 1.0, -100.0, 100.0)
    coded = jnp.round(x * jnp.exp2(BITS - power)).astype(I32).astype(I16)
    return coded, jnp.broadcast_to(power, (x.shape[0], LANES)).astype(I32).astype(I16)


def decode(ref, n, width):
    power = ref[n, :, width : width + 1].astype(I32).astype(F32)
    return ref[n, :, :width].astype(I32).astype(F32) * jnp.exp2(power - BITS)


def project_kernel(owners_ref, part_ref, uv_ref, wo_ref, out_ref):
    count, each, lanes = part_ref.shape
    seqs = owners_ref.shape[1]
    cuts = each // PART
    rows = 2 * seqs
    width = wo_ref.shape[2]
    owners = owners_ref[...]
    row = iota((cuts * rows, 1), 0)
    cut = row // rows
    seq, tok = row % rows // 2, row % 2
    owner = column_of(owners, seq)
    slot = column_of(slots_of(owners), seq)
    first = seq * each + cut * PART + tok
    second = owner * each + cut * PART + 2 + 2 * slot + tok
    at = iota((cuts * rows, count * each), 1)
    hit = jnp.where((at == first) | (at == second), 1.0, 0.0).astype(BF16)
    rest = part_ref[...].reshape(count * each, lanes)
    latent = None
    for _ in range(3):
        piece = rest.astype(BF16)
        rest = rest - piece.astype(F32)
        one = dot(hit, piece)
        latent = one if latent is None else latent + one
    latent = latent.astype(BF16)
    latent = jnp.concatenate([latent[c * rows : (c + 1) * rows] for c in range(cuts)], axis=1)
    head_out = dot(latent, uv_ref[0]).astype(BF16)
    coded, power = encode(dot(head_out, wo_ref[0]))
    for n in range(count):
        out_ref[n, :, :width] = coded[2 * n : 2 * n + 2]
        out_ref[n, :, width:] = power[2 * n : 2 * n + 2]


def added(ref, places, width):
    total = None
    for n in places:
        one = decode(ref, n, width)
        total = one if total is None else total + one
    return total


def final_kernel(in_ref, out_ref):
    out_ref[0] = added(in_ref, range(in_ref.shape[0]), out_ref.shape[2]).astype(BF16)


def swap(x):
    return lax.all_to_all(x, "seq", split_axis=0, concat_axis=0, tiled=True)


def trade(x, step):
    count = lax.axis_size("seq")
    return lax.ppermute(x, "seq", [(d, d ^ step) for d in range(count)])


def call(kernel, shapes, specs, scratch=(), cost=None, room=40):
    single = not isinstance(shapes, (list, tuple))
    return pl.pallas_call(
        kernel,
        out_shape=shapes,
        in_specs=specs,
        out_specs=VMEM if single else [VMEM] * len(shapes),
        scratch_shapes=list(scratch),
        cost_estimate=cost,
        compiler_params=pltpu.CompilerParams(vmem_limit_bytes=room * 1024 * 1024),
    )


def on_device(prompt_raw, lengths, owners, resident, new_raw, queries, kv_gain, w_uk, w_uv, w_o):
    count = lax.axis_size("seq")
    seqs = lengths.shape[0]
    most, width = prompt_raw.shape[1:]
    latent = kv_gain.shape[0]
    res_rows = resident.shape[1]
    nope = w_uk.shape[1]
    rope = width - latent
    heads = count
    out_width = w_o.shape[2]
    scale = 1.0 / queries.shape[-1] ** 0.5
    owners_row, lengths_row = owners.reshape(1, seqs), lengths.reshape(1, seqs)
    prompt_raw = prompt_raw.transpose(0, 2, 1)
    resident = resident.transpose(0, 2, 1)
    queries = queries.transpose(0, 2, 1, 3)
    keys_rows = most + LANES

    query = call(
        functools.partial(query_kernel, res_rows),
        jax.ShapeDtypeStruct((count, PACK, latent // 2), BF16),
        [HBM] * 4,
        [
            pltpu.VMEM((1, seqs), I32),
            pltpu.VMEM((1, seqs), I32),
            pltpu.VMEM(queries.shape, BF16),
            pltpu.VMEM((nope, latent), BF16),
            pltpu.VMEM((2 * seqs, -(-(nope + rope) // LANES) * LANES), F32),
            pltpu.SemaphoreType.DMA((4,)),
        ],
        room=60,
    )(owners_row, lengths_row, queries, w_uk[0])
    received = swap(query)
    keys, resident = call(
        functools.partial(compress_kernel, res_rows),
        [jax.ShapeDtypeStruct((width, keys_rows), BF16), jax.ShapeDtypeStruct(resident.shape, BF16)],
        [SMEM] + [VMEM] * 3 + [HBM],
        [pltpu.SemaphoreType.DMA],
        cost=pl.CostEstimate(flops=10**7, bytes_accessed=10**7, transcendentals=10**5),
    )(lengths, kv_gain.reshape(1, latent), prompt_raw, new_raw, resident)
    lanes = -(-6 * heads // LANES) * LANES
    scores_p, scores_r, stat = call(
        functools.partial(score_kernel, most, scale),
        [
            jax.ShapeDtypeStruct((2 * heads, keys_rows), F32),
            jax.ShapeDtypeStruct((2, 2 * heads, res_rows), F32),
            jax.ShapeDtypeStruct((1, 2, lanes), F32),
        ],
        [SMEM] + [VMEM] * 3,
    )(lengths, received, keys, resident)
    quad = jnp.concatenate([stat] + [trade(stat, j) for j in range(1, NEAR)], axis=0)
    far = count // NEAR
    stats = [quad] + [trade(quad, i * NEAR) for i in range(1, far)]
    part = call(
        attend_kernel,
        jax.ShapeDtypeStruct((heads, PART * (latent // LANES), LANES), F32),
        [SMEM] + [VMEM] * (far + 4),
    )(owners, *stats, scores_p, scores_r, keys, resident)
    parts = swap(part)
    sums = call(
        project_kernel, jax.ShapeDtypeStruct((count, 2, out_width + LANES), I16), [VMEM] * 4
    )(owners_row, parts, w_uv, w_o)
    return call(final_kernel, jax.ShapeDtypeStruct((1, 2, out_width), BF16), [VMEM])(swap(sums))


def solution(mesh):
    in_specs = (
        P(("group", "seq"), None, None),
        P("group"),
        P("group"),
        P(("group", "seq"), None, None),
        P("group", None, None),
        P("group", None, "seq", None),
        P(),
        P("seq", None, None),
        P("seq", None, None),
        P("seq", None, None),
    )
    out_specs = P(("group", "seq"), None, None)
    return jax.shard_map(
        on_device, mesh=mesh, in_specs=in_specs, out_specs=out_specs, check_vma=False
    )
```

```python
import functools

import jax
import jax.numpy as jnp
import numpy as np
from jax import lax
from jax.experimental import pallas as pl
from jax.experimental.pallas import tpu as pltpu
from jax.sharding import PartitionSpec as P

F32 = jnp.float32
BF16 = jnp.bfloat16
I32 = jnp.int32
I16 = jnp.int16
VMEM = pl.BlockSpec(memory_space=pltpu.VMEM)
SMEM = pl.BlockSpec(memory_space=pltpu.SMEM)
HBM = pl.BlockSpec(memory_space=pltpu.HBM)
LANES = 128
PACK = 16
PART = 6
BITS = 14.0
NEAR = 4


def iota(shape, dim):
    return lax.broadcasted_iota(I32, shape, dim)


def dot(a, b, dims=((1,), (0,))):
    return lax.dot_general(a, b, (dims, ((), ())), preferred_element_type=F32)


def column_of(row, picks):
    n, width = picks.shape[0], row.shape[1]
    hit = iota((n, width), 1) == picks
    return jnp.sum(jnp.where(hit, row, 0), axis=1, keepdims=True)


def slots_of(owners_row):
    seqs = owners_row.shape[1]
    owners_col = column_of(owners_row, iota((seqs, 1), 0))
    earlier = iota((seqs, seqs), 0) < iota((seqs, seqs), 1)
    same = (owners_col == owners_row) & earlier
    return jnp.sum(jnp.where(same, 1, 0), axis=0, keepdims=True)


def doubled(row):
    seqs = row.shape[1]
    col = column_of(row, iota((seqs, 1), 0))
    hit = iota((seqs, 2 * seqs), 1) // 2 == iota((seqs, 2 * seqs), 0)
    return jnp.sum(jnp.where(hit, col, 0), axis=0, keepdims=True)


def frequencies(half, shape, dim):
    at = iota(shape, dim) % half
    values = np.float32(10000.0) ** (-(np.arange(half, dtype=np.float32) * np.float32(2.0)) / np.float32(2 * half))
    result = jnp.zeros(shape, F32)
    for i in range(half):
        result = jnp.where(at == i, float(values[i]), result)
    return result


def query_kernel(
    res_rows,
    owners_hbm,
    lengths_hbm,
    queries_hbm,
    uk_hbm,
    new_hbm,
    gain_hbm,
    out_ref,
    aux_ref,
    owners_ref,
    lengths_ref,
    queries_ref,
    uk_ref,
    new_ref,
    gain_ref,
    flat,
    sems,
):
    device = lax.axis_index("seq")
    copies = []
    pairs = [
        (owners_hbm, owners_ref),
        (lengths_hbm, lengths_ref),
        (queries_hbm, queries_ref),
        (uk_hbm, uk_ref),
        (new_hbm.at[device], new_ref),
        (gain_hbm, gain_ref),
    ]
    for n, (source, target) in enumerate(pairs):
        copies.append(pltpu.make_async_copy(source, target, sems.at[n]))
        copies[-1].start()
    for copy in copies:
        copy.wait()
    seqs = owners_ref.shape[1]
    nope, latent = uk_ref.shape
    rope = queries_ref.shape[3] - nope
    half = latent // 2
    rows = 2 * seqs
    for s in range(seqs):
        flat[2 * s : 2 * s + 2, : nope + rope] = queries_ref[s, 0].astype(F32)
    values = flat[:, : nope + rope]
    absorbed = dot(values[:, :nope].astype(BF16), uk_ref[...]).astype(BF16)
    row = iota((rows, 1), 0)
    lengths = column_of(lengths_ref[...], row // 2)
    angle = (res_rows + lengths + row % 2).astype(F32) * frequencies(rope // 2, (1, rope), 1)
    x = values[:, nope:]
    swapped = jnp.concatenate([x[:, rope // 2 :], x[:, : rope // 2]], axis=1)
    sine = jnp.sin(angle)
    sine = jnp.where(iota(x.shape, 1) < rope // 2, -sine, sine)
    turned = x * jnp.cos(angle) + swapped * sine
    zero = jnp.zeros((rows, rope), F32)
    pieces = [absorbed[:, :half], absorbed[:, half:]]
    for k in range(3):
        blocks = [turned if j == k else zero for j in range(half // rope)]
        pieces.append(jnp.concatenate(blocks, axis=1).astype(BF16))
    owners = owners_ref[...]
    owner = doubled(owners)
    slot = doubled(slots_of(owners))
    count = out_ref.shape[0]
    total = count * PACK
    shape = (total, rows)
    dest, r = iota(shape, 0) // PACK, iota(shape, 0) % PACK
    seq, tok = iota(shape, 1) // 2, iota(shape, 1) % 2
    here = jnp.where(owner == dest, slot + 1, -1)
    result = None
    for p in range(2):
        q = r - PART * p
        wanted = ((q // 2 == 0) & (seq == dest)) | (here == q // 2)
        hit = (q >= 0) & (q < PART) & (tok == q % 2) & wanted
        one = dot(jnp.where(hit, 1.0, 0.0).astype(BF16), pieces[p])
        result = one if result is None else result + one
    for k in range(3):
        match = (seq == dest) if k == 0 else (here == k)
        hit = (r == 2 * PART + tok) & match
        result = result + dot(jnp.where(hit, 1.0, 0.0).astype(BF16), pieces[2 + k])
    out_ref[...] = result.astype(BF16).reshape(out_ref.shape)
    width = new_ref.shape[1]
    aux_ref[0:2, :width] = new_ref[...].astype(F32)
    mine = jnp.where(iota(lengths_ref.shape, 1) == device, lengths_ref[...], 0)
    mine = jnp.sum(mine, axis=1, keepdims=True).astype(F32)
    aux_ref[2:3, :] = jnp.broadcast_to(mine, (1, aux_ref.shape[1]))
    aux_ref[3:4, :latent] = gain_ref[...].astype(F32).reshape(1, latent)


def compress_kernel(
    res_rows, latent, aux_ref, prompt_ref, resident_hbm, out_ref, bias_ref, resident_ref, sem
):
    fetch = pltpu.make_async_copy(resident_hbm, resident_ref, sem)
    fetch.start()
    width, most = prompt_ref.shape[1:]
    half = (width - latent) // 2
    fresh = jnp.concatenate([aux_ref[0:2, :width], jnp.zeros((PACK - 2, width), F32)], axis=0)
    pick = jnp.where(iota((PACK, LANES), 0) == iota((PACK, LANES), 1), 1.0, 0.0).astype(BF16)
    fresh = dot(fresh.astype(BF16), pick, ((0,), (0,)))
    gain = jnp.broadcast_to(aux_ref[3:4, :latent], (PACK, latent))
    top = jnp.where(iota((PACK, LANES), 0) == 0, 1.0, 0.0).astype(BF16)
    gain = dot(gain.astype(BF16), top, ((0,), (0,)))
    length = aux_ref[2:3, :LANES].astype(I32)
    at = iota(bias_ref.shape, 1)
    token = iota(bias_ref.shape, 0)
    length_all = jnp.concatenate([length] * (bias_ref.shape[1] // LANES), axis=1)
    seen = (at < length_all) | ((at >= most) & (at <= most + token))
    bias_ref[...] = jnp.where(seen, 1.0, 0.0)
    freq = frequencies(half, (half, 1), 0)
    for i in range(most // LANES + 1):
        at = slice(i * LANES, (i + 1) * LANES)
        lane = iota((1, LANES), 1)
        if i * LANES < most:
            raw = prompt_ref[0, :, at].astype(F32)
            position = res_rows + i * LANES + lane
        else:
            raw = fresh
            position = res_rows + length + lane
        lat = raw[:latent]
        meansq = jnp.sum(lat * lat, axis=0, keepdims=True) * (1.0 / latent)
        out_ref[:latent, at] = (lat * lax.rsqrt(meansq + 1e-06) * gain).astype(BF16)
        angle = position.astype(F32) * freq
        cosine, sine = jnp.cos(angle), jnp.sin(angle)
        x1, x2 = raw[latent : latent + half], raw[latent + half :]
        out_ref[latent : latent + half, at] = (x1 * cosine - x2 * sine).astype(BF16)
        out_ref[latent + half :, at] = (x2 * cosine + x1 * sine).astype(BF16)
    fetch.wait()


def score_kernel(scale, q_ref, keys_ref, seen_ref, resident_ref, sp_ref, sr_ref, stat_ref):
    heads = q_ref.shape[0]
    half = q_ref.shape[2]
    width = keys_ref.shape[0]
    rope = width - 2 * half
    rows = 2 * heads
    total = heads * PACK
    flat = q_ref[...].reshape(total, half)
    shape = (rows, total)
    head, tok = iota(shape, 0) // 4 * 2 + iota(shape, 0) % 2, iota(shape, 0) // 2 % 2
    source = iota(shape, 1) - head * PACK

    def picked(r):
        hit = source == r + tok
        return dot(jnp.where(hit, 1.0, 0.0).astype(BF16), flat)

    turned = picked(2 * PART)
    tops, sums = [], []
    for k in range(3):
        query = jnp.concatenate(
            [picked(2 * k), picked(PART + 2 * k), turned[:, k * rope : (k + 1) * rope]], axis=1
        ).astype(BF16)
        keys = keys_ref[...] if k == 0 else resident_ref[k - 1]
        scores = dot(query, keys) * scale
        if k == 0:
            first, second = seen_ref[0:1, :] > 0.5, seen_ref[1:2, :] > 0.5
            token = iota(scores.shape, 0) // 2 % 2
            seen = (first & (token == 0)) | (second & (token == 1))
            scores = jnp.where(seen, scores, -1e30)
            sp_ref[...] = scores
        else:
            sr_ref[k - 1] = scores
        top = jnp.max(scores, axis=1, keepdims=True)
        tops.append(top)
        sums.append(jnp.sum(jnp.exp(scores - top), axis=1, keepdims=True))
    lanes = stat_ref.shape[2]
    here = iota((3 * rows, lanes), 0) == iota((3 * rows, lanes), 1)
    top = jnp.sum(jnp.where(here, jnp.concatenate(tops, axis=0), 0.0), axis=0, keepdims=True)
    total = jnp.sum(jnp.where(here, jnp.concatenate(sums, axis=0), 0.0), axis=0, keepdims=True)
    both = jnp.concatenate([top, total], axis=0)
    stat_ref[...] = jnp.broadcast_to(both[None], stat_ref.shape)


def attend_kernel(owners_ref, stat_ref, sp_ref, sr_ref, keys_ref, resident_ref, out_ref):
    heads = out_ref.shape[0]
    latent = out_ref.shape[1] // PART * LANES
    seqs = owners_ref.shape[0]
    rows = 2 * heads
    device = lax.axis_index("seq")
    lanes = stat_ref.shape[2]
    my_owner = owners_ref[device]
    my_slot = jnp.int32(0)
    seen = jnp.int32(0)
    first = jnp.int32(0)
    second = jnp.int32(0)
    for s in range(seqs):
        owner = owners_ref[s]
        my_slot = my_slot + jnp.where((owner == my_owner) & (s < device), 1, 0)
        mine = owner == device
        first = jnp.where(mine & (seen == 0), s, first)
        second = jnp.where(mine & (seen == 1), s, second)
        seen = seen + jnp.where(mine, 1, 0)

    def column(row, segment):
        picks = iota((rows, 1), 0) + segment * rows
        hit = iota((rows, lanes), 1) == picks
        return jnp.sum(jnp.where(hit, row, 0.0), axis=1, keepdims=True)

    mine = stat_ref[device]
    others = [(stat_ref[my_owner], 1 + my_slot), (stat_ref[first], 0), (stat_ref[second], 0)]
    for k in range(3):
        other, segment = others[k]
        top0, sum0 = column(mine[0:1], k), column(mine[1:2], k)
        top1, sum1 = column(other[0:1], segment), column(other[1:2], segment)
        top = jnp.maximum(top0, top1)
        total = sum0 * jnp.exp(top0 - top) + sum1 * jnp.exp(top1 - top)
        scores = sp_ref[...] if k == 0 else sr_ref[k - 1]
        keys = keys_ref[:latent, :] if k == 0 else resident_ref[k - 1, :latent, :]
        weights = jnp.exp(scores - top).astype(BF16)
        part = dot(weights, keys, ((1,), (1,))) / total
        for h in range(heads):
            for c in range(latent // LANES):
                at = c * PART + 2 * k
                out_ref[h, at : at + 2, :] = part[2 * h : 2 * h + 2, c * LANES : (c + 1) * LANES]


def project_kernel(
    owners_ref, part_ref, uv_ref, other_uv_ref, wo_ref, other_wo_ref, out_ref, flat
):
    count, each, lanes = part_ref.shape
    seqs = owners_ref.shape[1]
    cuts = each // PART
    rows = 2 * seqs
    core = lax.axis_index("seq") % 2
    owners = owners_ref[...]
    row = iota((cuts * rows, 1), 0)
    cut, other, seq = row // rows, row % rows // seqs, row % seqs
    head = jnp.where(other == 0, core, 1 - core)
    owner = column_of(owners, seq)
    slot = column_of(slots_of(owners), seq)
    first = seq * each + cut * PART + head
    second = owner * each + cut * PART + 2 + 2 * slot + head
    at = iota((cuts * rows, count * each), 1)
    hit = jnp.where((at == first) | (at == second), 1.0, 0.0).astype(BF16)
    rest = part_ref[...].reshape(count * each, lanes)
    latent = None
    for _ in range(3):
        piece = rest.astype(BF16)
        rest = rest - piece.astype(F32)
        one = dot(hit, piece)
        latent = one if latent is None else latent + one
    latent = latent.astype(BF16)
    latent = jnp.concatenate([latent[c * rows : (c + 1) * rows] for c in range(cuts)], axis=1)
    product = dot(dot(latent[:seqs], uv_ref[0]).astype(BF16), wo_ref[0])
    product = product + dot(dot(latent[seqs:], other_uv_ref[0]).astype(BF16), other_wo_ref[0])
    top = jnp.max(jnp.abs(product), axis=1, keepdims=True)
    power = jnp.clip(jnp.floor(jnp.log2(jnp.maximum(top, 1e-35))) + 1.0, -100.0, 100.0)
    coded = jnp.round(product * jnp.exp2(BITS - power))
    span = out_ref.shape[2]
    used = product.shape[1] // span
    for s in range(seqs):
        for j in range(used):
            flat[s, j : j + 1, :] = coded[s : s + 1, j * span : (j + 1) * span]
        flat[s, used:, :] = jnp.broadcast_to(power[s : s + 1], (flat.shape[1] - used, span))
        out_ref[s] = flat[s].astype(I32).astype(I16)


def final_kernel(in_ref, out_ref):
    span = in_ref.shape[2]
    used = out_ref.shape[2] // span
    for t in range(2):
        total = None
        for n in range(t, in_ref.shape[0], 2):
            values = in_ref[n].astype(I32).astype(F32)
            one = values * jnp.exp2(values[used : used + 1] - BITS)
            total = one if total is None else total + one
        for j in range(used):
            out_ref[0, t : t + 1, j * span : (j + 1) * span] = total[j : j + 1].astype(BF16)


def swap(x):
    return lax.all_to_all(x, "seq", split_axis=0, concat_axis=0, tiled=True)


def trade(x, step):
    count = lax.axis_size("seq")
    return lax.ppermute(x, "seq", [(d, d ^ step) for d in range(count)])


def call(kernel, shapes, specs, scratch=(), cost=None, room=40):
    single = not isinstance(shapes, (list, tuple))
    return pl.pallas_call(
        kernel,
        out_shape=shapes,
        in_specs=specs,
        out_specs=VMEM if single else [VMEM] * len(shapes),
        scratch_shapes=list(scratch),
        cost_estimate=cost,
        compiler_params=pltpu.CompilerParams(vmem_limit_bytes=room * 1024 * 1024),
    )


def on_device(prompt_raw, lengths, owners, resident, new_raw, queries, kv_gain, w_uk, w_uv, w_o):
    count = lax.axis_size("seq")
    seqs = lengths.shape[0]
    most, width = prompt_raw.shape[1:]
    latent = kv_gain.shape[0]
    res_rows = resident.shape[1]
    nope = w_uk.shape[1]
    rope = width - latent
    heads = count
    out_width = w_o.shape[2]
    scale = 1.0 / queries.shape[-1] ** 0.5
    owners_row, lengths_row = owners.reshape(1, seqs), lengths.reshape(1, seqs)
    prompt_raw = prompt_raw.transpose(0, 2, 1)
    resident = resident.transpose(0, 2, 1)
    queries = queries.transpose(0, 2, 1, 3)
    keys_rows = most + LANES

    aux_width = -(-width // LANES) * LANES
    query, aux = call(
        functools.partial(query_kernel, res_rows),
        [
            jax.ShapeDtypeStruct((count, PACK, latent // 2), BF16),
            jax.ShapeDtypeStruct((8, aux_width), F32),
        ],
        [HBM] * 6,
        [
            pltpu.VMEM((1, seqs), I32),
            pltpu.VMEM((1, seqs), I32),
            pltpu.VMEM(queries.shape, BF16),
            pltpu.VMEM((nope, latent), BF16),
            pltpu.VMEM((2, width), BF16),
            pltpu.VMEM((latent,), BF16),
            pltpu.VMEM((2 * seqs, -(-(nope + rope) // LANES) * LANES), F32),
            pltpu.SemaphoreType.DMA((6,)),
        ],
        room=60,
    )(owners_row, lengths_row, queries, w_uk[0], new_raw, kv_gain)
    received = swap(query)
    keys, seen, resident = call(
        functools.partial(compress_kernel, res_rows, latent),
        [
            jax.ShapeDtypeStruct((width, keys_rows), BF16),
            jax.ShapeDtypeStruct((8, keys_rows), F32),
            jax.ShapeDtypeStruct(resident.shape, BF16),
        ],
        [VMEM] * 2 + [HBM],
        [pltpu.SemaphoreType.DMA],
        cost=pl.CostEstimate(flops=10**7, bytes_accessed=10**7, transcendentals=10**5),
    )(aux, prompt_raw, resident)
    lanes = -(-6 * heads // LANES) * LANES
    scores_p, scores_r, stat = call(
        functools.partial(score_kernel, scale),
        [
            jax.ShapeDtypeStruct((2 * heads, keys_rows), F32),
            jax.ShapeDtypeStruct((2, 2 * heads, res_rows), F32),
            jax.ShapeDtypeStruct((count, 2, lanes), F32),
        ],
        [VMEM] * 4,
    )(received, keys, seen, resident)
    stats = swap(stat)
    part = call(
        attend_kernel,
        jax.ShapeDtypeStruct((heads, PART * (latent // LANES), LANES), F32),
        [SMEM] + [VMEM] * 5,
    )(owners, stats, scores_p, scores_r, keys, resident)
    parts = swap(part)
    span = out_width // (PACK - 2)
    sums = call(
        project_kernel,
        jax.ShapeDtypeStruct((seqs, PACK, span), I16),
        [VMEM] * 6,
        [pltpu.VMEM((seqs, PACK, span), F32)],
    )(owners_row, parts, w_uv, trade(w_uv, 1), w_o, trade(w_o, 1))
    return call(final_kernel, jax.ShapeDtypeStruct((1, 2, out_width), BF16), [VMEM])(swap(sums))


def solution(mesh):
    in_specs = (
        P(("group", "seq"), None, None),
        P("group"),
        P("group"),
        P(("group", "seq"), None, None),
        P("group", None, None),
        P("group", None, "seq", None),
        P(),
        P("seq", None, None),
        P("seq", None, None),
        P("seq", None, None),
    )
    out_specs = P(("group", "seq"), None, None)
    return jax.shard_map(
        on_device, mesh=mesh, in_specs=in_specs, out_specs=out_specs, check_vma=False
    )
```

```python
import functools

import jax
import jax.numpy as jnp
import numpy as np
from jax import lax
from jax.experimental import pallas as pl
from jax.experimental.pallas import tpu as pltpu
from jax.sharding import PartitionSpec as P

F32 = jnp.float32
BF16 = jnp.bfloat16
I32 = jnp.int32
I16 = jnp.int16
VMEM = pl.BlockSpec(memory_space=pltpu.VMEM)
SMEM = pl.BlockSpec(memory_space=pltpu.SMEM)
HBM = pl.BlockSpec(memory_space=pltpu.HBM)
LANES = 128
PACK = 16
PART = 6
BITS = 14.0
NEAR = 4


def iota(shape, dim):
    return lax.broadcasted_iota(I32, shape, dim)


def dot(a, b, dims=((1,), (0,))):
    return lax.dot_general(a, b, (dims, ((), ())), preferred_element_type=F32)


def column_of(row, picks):
    n, width = picks.shape[0], row.shape[1]
    hit = iota((n, width), 1) == picks
    return jnp.sum(jnp.where(hit, row, 0), axis=1, keepdims=True)


def slots_of(owners_row):
    seqs = owners_row.shape[1]
    owners_col = column_of(owners_row, iota((seqs, 1), 0))
    earlier = iota((seqs, seqs), 0) < iota((seqs, seqs), 1)
    same = (owners_col == owners_row) & earlier
    return jnp.sum(jnp.where(same, 1, 0), axis=0, keepdims=True)


def doubled(row):
    seqs = row.shape[1]
    col = column_of(row, iota((seqs, 1), 0))
    hit = iota((seqs, 2 * seqs), 1) // 2 == iota((seqs, 2 * seqs), 0)
    return jnp.sum(jnp.where(hit, col, 0), axis=0, keepdims=True)


def frequencies(half, shape, dim):
    at = iota(shape, dim) % half
    values = np.float32(10000.0) ** (-(np.arange(half, dtype=np.float32) * np.float32(2.0)) / np.float32(2 * half))
    result = jnp.zeros(shape, F32)
    for i in range(half):
        result = jnp.where(at == i, float(values[i]), result)
    return result


def query_kernel(
    res_rows,
    owners_hbm,
    lengths_hbm,
    queries_hbm,
    uk_hbm,
    new_hbm,
    gain_hbm,
    out_ref,
    aux_ref,
    owners_ref,
    lengths_ref,
    queries_ref,
    uk_ref,
    new_ref,
    gain_ref,
    flat,
    sems,
):
    device = lax.axis_index("seq")
    copies = []
    pairs = [
        (owners_hbm, owners_ref),
        (lengths_hbm, lengths_ref),
        (queries_hbm, queries_ref),
        (uk_hbm, uk_ref),
        (new_hbm.at[device], new_ref),
        (gain_hbm, gain_ref),
    ]
    for n, (source, target) in enumerate(pairs):
        copies.append(pltpu.make_async_copy(source, target, sems.at[n]))
        copies[-1].start()
    for copy in copies:
        copy.wait()
    seqs = owners_ref.shape[1]
    nope, latent = uk_ref.shape
    rope = queries_ref.shape[3] - nope
    half = latent // 2
    rows = 2 * seqs
    for s in range(seqs):
        flat[2 * s : 2 * s + 2, : nope + rope] = queries_ref[s, 0].astype(F32)
    values = flat[:, : nope + rope]
    absorbed = dot(values[:, :nope].astype(BF16), uk_ref[...]).astype(BF16)
    row = iota((rows, 1), 0)
    lengths = column_of(lengths_ref[...], row // 2)
    angle = (res_rows + lengths + row % 2).astype(F32) * frequencies(rope // 2, (1, rope), 1)
    x = values[:, nope:]
    swapped = jnp.concatenate([x[:, rope // 2 :], x[:, : rope // 2]], axis=1)
    sine = jnp.sin(angle)
    sine = jnp.where(iota(x.shape, 1) < rope // 2, -sine, sine)
    turned = x * jnp.cos(angle) + swapped * sine
    zero = jnp.zeros((rows, rope), F32)
    pieces = [absorbed[:, :half], absorbed[:, half:]]
    for k in range(3):
        blocks = [turned if j == k else zero for j in range(half // rope)]
        pieces.append(jnp.concatenate(blocks, axis=1).astype(BF16))
    owners = owners_ref[...]
    owner = doubled(owners)
    slot = doubled(slots_of(owners))
    count = out_ref.shape[0]
    total = count * PACK
    shape = (total, rows)
    dest, r = iota(shape, 0) // PACK, iota(shape, 0) % PACK
    seq, tok = iota(shape, 1) // 2, iota(shape, 1) % 2
    here = jnp.where(owner == dest, slot + 1, -1)
    result = None
    for p in range(2):
        q = r - PART * p
        wanted = ((q // 2 == 0) & (seq == dest)) | (here == q // 2)
        hit = (q >= 0) & (q < PART) & (tok == q % 2) & wanted
        one = dot(jnp.where(hit, 1.0, 0.0).astype(BF16), pieces[p])
        result = one if result is None else result + one
    for k in range(3):
        match = (seq == dest) if k == 0 else (here == k)
        hit = (r == 2 * PART + tok) & match
        result = result + dot(jnp.where(hit, 1.0, 0.0).astype(BF16), pieces[2 + k])
    out_ref[...] = result.astype(BF16).reshape(out_ref.shape)
    width = new_ref.shape[1]
    aux_ref[0:2, :width] = new_ref[...].astype(F32)
    mine = jnp.where(iota(lengths_ref.shape, 1) == device, lengths_ref[...], 0)
    mine = jnp.sum(mine, axis=1, keepdims=True).astype(F32)
    aux_ref[2:3, :] = jnp.broadcast_to(mine, (1, aux_ref.shape[1]))
    aux_ref[3:4, :latent] = gain_ref[...].astype(F32).reshape(1, latent)


def compress_kernel(
    res_rows, latent, aux_ref, prompt_ref, resident_hbm, out_ref, bias_ref, resident_ref, sem
):
    fetch = pltpu.make_async_copy(resident_hbm, resident_ref, sem)
    fetch.start()
    width, most = prompt_ref.shape[1:]
    half = (width - latent) // 2
    fresh = jnp.concatenate([aux_ref[0:2, :width], jnp.zeros((PACK - 2, width), F32)], axis=0)
    pick = jnp.where(iota((PACK, LANES), 0) == iota((PACK, LANES), 1), 1.0, 0.0).astype(BF16)
    fresh = dot(fresh.astype(BF16), pick, ((0,), (0,)))
    gain = jnp.broadcast_to(aux_ref[3:4, :latent], (PACK, latent))
    top = jnp.where(iota((PACK, LANES), 0) == 0, 1.0, 0.0).astype(BF16)
    gain = dot(gain.astype(BF16), top, ((0,), (0,)))
    length = aux_ref[2:3, :LANES].astype(I32)
    at = iota(bias_ref.shape, 1)
    token = iota(bias_ref.shape, 0)
    length_all = jnp.concatenate([length] * (bias_ref.shape[1] // LANES), axis=1)
    seen = (at < length_all) | ((at >= most) & (at <= most + token))
    bias_ref[...] = jnp.where(seen, 1.0, 0.0)
    freq = frequencies(half, (half, 1), 0)
    for i in range(most // LANES + 1):
        at = slice(i * LANES, (i + 1) * LANES)
        lane = iota((1, LANES), 1)
        if i * LANES < most:
            raw = prompt_ref[0, :, at].astype(F32)
            position = res_rows + i * LANES + lane
        else:
            raw = fresh
            position = res_rows + length + lane
        lat = raw[:latent]
        meansq = jnp.sum(lat * lat, axis=0, keepdims=True) * (1.0 / latent)
        out_ref[:latent, at] = (lat * lax.rsqrt(meansq + 1e-06) * gain).astype(BF16)
        angle = position.astype(F32) * freq
        cosine, sine = jnp.cos(angle), jnp.sin(angle)
        x1, x2 = raw[latent : latent + half], raw[latent + half :]
        out_ref[latent : latent + half, at] = (x1 * cosine - x2 * sine).astype(BF16)
        out_ref[latent + half :, at] = (x2 * cosine + x1 * sine).astype(BF16)
    fetch.wait()


def score_kernel(scale, q_ref, keys_ref, seen_ref, resident_ref, sp_ref, sr_ref, stat_ref):
    heads = q_ref.shape[0]
    half = q_ref.shape[2]
    width = keys_ref.shape[0]
    rope = width - 2 * half
    rows = 2 * heads
    total = heads * PACK
    flat = q_ref[...].reshape(total, half)
    shape = (rows, total)
    head, tok = iota(shape, 0) // 4 * 2 + iota(shape, 0) % 2, iota(shape, 0) // 2 % 2
    source = iota(shape, 1) - head * PACK

    def picked(r):
        hit = source == r + tok
        return dot(jnp.where(hit, 1.0, 0.0).astype(BF16), flat)

    turned = picked(2 * PART)
    tops, sums = [], []
    for k in range(3):
        query = jnp.concatenate(
            [picked(2 * k), picked(PART + 2 * k), turned[:, k * rope : (k + 1) * rope]], axis=1
        ).astype(BF16)
        keys = keys_ref[...] if k == 0 else resident_ref[k - 1]
        scores = dot(query, keys) * scale
        if k == 0:
            first, second = seen_ref[0:1, :] > 0.5, seen_ref[1:2, :] > 0.5
            token = iota(scores.shape, 0) // 2 % 2
            seen = (first & (token == 0)) | (second & (token == 1))
            scores = jnp.where(seen, scores, -1e30)
            sp_ref[...] = scores
        else:
            sr_ref[k - 1] = scores
        top = jnp.max(scores, axis=1, keepdims=True)
        tops.append(top)
        sums.append(jnp.sum(jnp.exp(scores - top), axis=1, keepdims=True))
    lanes = stat_ref.shape[2]
    here = iota((3 * rows, lanes), 0) == iota((3 * rows, lanes), 1)
    top = jnp.sum(jnp.where(here, jnp.concatenate(tops, axis=0), 0.0), axis=0, keepdims=True)
    total = jnp.sum(jnp.where(here, jnp.concatenate(sums, axis=0), 0.0), axis=0, keepdims=True)
    both = jnp.concatenate([top, total], axis=0)
    stat_ref[...] = jnp.broadcast_to(both[None], stat_ref.shape)


def attend_kernel(owners_ref, mark_ref, stat_ref, sp_ref, sr_ref, keys_ref, resident_ref, out_ref):
    heads = out_ref.shape[0]
    latent = out_ref.shape[1] // PART * LANES
    seqs = owners_ref.shape[0]
    rows = 2 * heads
    device = lax.axis_index("seq")
    lanes = stat_ref.shape[2]
    my_owner = owners_ref[device]
    my_slot = jnp.int32(0)
    seen = jnp.int32(0)
    first = jnp.int32(0)
    second = jnp.int32(0)
    for s in range(seqs):
        owner = owners_ref[s]
        my_slot = my_slot + jnp.where((owner == my_owner) & (s < device), 1, 0)
        mine = owner == device
        first = jnp.where(mine & (seen == 0), s, first)
        second = jnp.where(mine & (seen == 1), s, second)
        seen = seen + jnp.where(mine, 1, 0)

    def column(row, segment):
        picks = iota((rows, 1), 0) + segment * rows
        hit = iota((rows, lanes), 1) == picks
        return jnp.sum(jnp.where(hit, row, 0.0), axis=1, keepdims=True)

    mine = stat_ref[device]
    others = [(stat_ref[my_owner], 1 + my_slot), (stat_ref[first], 0), (stat_ref[second], 0)]
    for k in range(3):
        other, segment = others[k]
        top0, sum0 = column(mine[0:1], k), column(mine[1:2], k)
        top1, sum1 = column(other[0:1], segment), column(other[1:2], segment)
        top = jnp.maximum(top0, top1)
        total = sum0 * jnp.exp(top0 - top) + sum1 * jnp.exp(top1 - top)
        scores = sp_ref[...] if k == 0 else sr_ref[k - 1]
        keys = keys_ref[:latent, :] if k == 0 else resident_ref[k - 1, :latent, :]
        weights = jnp.exp(scores - top).astype(BF16)
        part = dot(weights, keys, ((1,), (1,))) / total
        for h in range(heads):
            for c in range(latent // LANES):
                at = c * PART + 2 * k
                out_ref[h, at : at + 2, :] = part[2 * h : 2 * h + 2, c * LANES : (c + 1) * LANES]


def stack_kernel(after_ref, wo_hbm, other_hbm, out_ref, mark_ref, sems):
    rows = wo_hbm.shape[1]
    cols = out_ref.shape[1]
    copies = []
    for half in range(2):
        for n, ref in enumerate((wo_hbm, other_hbm)):
            at = 2 * half + n
            copies.append(
                pltpu.make_async_copy(
                    ref.at[0, :, pl.ds(half * cols, cols)], out_ref.at[pl.ds(at * rows, rows), :], sems.at[at]
                )
            )
            copies[-1].start()
    mark_ref[...] = after_ref[: mark_ref.shape[0], : mark_ref.shape[1]]
    for copy in copies:
        copy.wait()


def project_kernel(owners_ref, part_ref, uv_ref, other_uv_ref, wo_ref, out_ref):
    count, each, lanes = part_ref.shape
    seqs = owners_ref.shape[1]
    cuts = each // PART
    rows = 2 * seqs
    core = lax.axis_index("seq") % 2
    owners = owners_ref[...]
    row = iota((cuts * 2 * rows, 1), 0)
    cut, other, seq = row // (2 * rows), row % (2 * rows) // rows, row % rows // 2
    head = jnp.where(other == 0, core, 1 - core)
    owner = column_of(owners, seq)
    slot = column_of(slots_of(owners), seq)
    first = seq * each + cut * PART + head
    second = owner * each + cut * PART + 2 + 2 * slot + head
    at = iota((cuts * 2 * rows, count * each), 1)
    hit = jnp.where((at == first) | (at == second), 1.0, 0.0).astype(BF16)
    rest = part_ref[...].reshape(count * each, lanes)
    latent = None
    for _ in range(3):
        piece = rest.astype(BF16)
        rest = rest - piece.astype(F32)
        one = dot(hit, piece)
        latent = one if latent is None else latent + one
    latent = latent.astype(BF16)
    latent = jnp.concatenate(
        [latent[c * 2 * rows : (c + 1) * 2 * rows] for c in range(cuts)], axis=1
    )
    head_out = jnp.concatenate(
        [dot(latent[:rows], uv_ref[0]), dot(latent[rows:], other_uv_ref[0])], axis=1
    )
    half = iota(head_out.shape, 0) % 2
    split = jnp.concatenate(
        [jnp.where(half == 0, head_out, 0.0), jnp.where(half == 1, head_out, 0.0)], axis=1
    )
    product = dot(split.astype(BF16), wo_ref[...])
    top = jnp.max(jnp.abs(product), axis=1, keepdims=True)
    power = jnp.clip(jnp.floor(jnp.log2(jnp.maximum(top, 1e-35))) + 1.0, -100.0, 100.0)
    coded = jnp.round(product * jnp.exp2(BITS - power)).astype(I32).astype(I16)
    power = jnp.broadcast_to(power, (rows, LANES)).astype(I32).astype(I16)
    cols = product.shape[1]
    for s in range(seqs):
        out_ref[s, :, :cols] = coded[2 * s : 2 * s + 2]
        out_ref[s, :, cols:] = power[2 * s : 2 * s + 2]


def final_kernel(in_ref, out_ref):
    cols = out_ref.shape[2] // 2
    for t in range(2):
        total = None
        for n in range(t, in_ref.shape[0], 2):
            power = in_ref[n, :, cols : cols + 1].astype(I32).astype(F32)
            one = in_ref[n, :, :cols].astype(I32).astype(F32) * jnp.exp2(power - BITS)
            total = one if total is None else total + one
        for j in range(2):
            out_ref[0, t : t + 1, j * cols : (j + 1) * cols] = total[j : j + 1].astype(BF16)


def swap(x):
    return lax.all_to_all(x, "seq", split_axis=0, concat_axis=0, tiled=True)


def trade(x, step):
    count = lax.axis_size("seq")
    return lax.ppermute(x, "seq", [(d, d ^ step) for d in range(count)])


def call(kernel, shapes, specs, scratch=(), cost=None, room=40):
    single = not isinstance(shapes, (list, tuple))
    return pl.pallas_call(
        kernel,
        out_shape=shapes,
        in_specs=specs,
        out_specs=VMEM if single else [VMEM] * len(shapes),
        scratch_shapes=list(scratch),
        cost_estimate=cost,
        compiler_params=pltpu.CompilerParams(vmem_limit_bytes=room * 1024 * 1024),
    )


def on_device(prompt_raw, lengths, owners, resident, new_raw, queries, kv_gain, w_uk, w_uv, w_o):
    count = lax.axis_size("seq")
    seqs = lengths.shape[0]
    most, width = prompt_raw.shape[1:]
    latent = kv_gain.shape[0]
    res_rows = resident.shape[1]
    nope = w_uk.shape[1]
    rope = width - latent
    heads = count
    out_width = w_o.shape[2]
    scale = 1.0 / queries.shape[-1] ** 0.5
    owners_row, lengths_row = owners.reshape(1, seqs), lengths.reshape(1, seqs)
    prompt_raw = prompt_raw.transpose(0, 2, 1)
    resident = resident.transpose(0, 2, 1)
    queries = queries.transpose(0, 2, 1, 3)
    keys_rows = most + LANES

    aux_width = -(-width // LANES) * LANES
    query, aux = call(
        functools.partial(query_kernel, res_rows),
        [
            jax.ShapeDtypeStruct((count, PACK, latent // 2), BF16),
            jax.ShapeDtypeStruct((8, aux_width), F32),
        ],
        [HBM] * 6,
        [
            pltpu.VMEM((1, seqs), I32),
            pltpu.VMEM((1, seqs), I32),
            pltpu.VMEM(queries.shape, BF16),
            pltpu.VMEM((nope, latent), BF16),
            pltpu.VMEM((2, width), BF16),
            pltpu.VMEM((latent,), BF16),
            pltpu.VMEM((2 * seqs, -(-(nope + rope) // LANES) * LANES), F32),
            pltpu.SemaphoreType.DMA((6,)),
        ],
        room=60,
    )(owners_row, lengths_row, queries, w_uk[0], new_raw, kv_gain)
    received = swap(query)
    query, w_uv, w_o = lax.optimization_barrier((query, w_uv, w_o))
    other_uv, other_wo = trade(w_uv, 1), trade(w_o, 1)
    keys, seen, resident = call(
        functools.partial(compress_kernel, res_rows, latent),
        [
            jax.ShapeDtypeStruct((width, keys_rows), BF16),
            jax.ShapeDtypeStruct((8, keys_rows), F32),
            jax.ShapeDtypeStruct(resident.shape, BF16),
        ],
        [VMEM] * 2 + [HBM],
        [pltpu.SemaphoreType.DMA],
        cost=pl.CostEstimate(flops=10**7, bytes_accessed=10**7, transcendentals=10**5),
    )(aux, prompt_raw, resident)
    lanes = -(-6 * heads // LANES) * LANES
    scores_p, scores_r, stat = call(
        functools.partial(score_kernel, scale),
        [
            jax.ShapeDtypeStruct((2 * heads, keys_rows), F32),
            jax.ShapeDtypeStruct((2, 2 * heads, res_rows), F32),
            jax.ShapeDtypeStruct((count, 2, lanes), F32),
        ],
        [VMEM] * 4,
    )(received, keys, seen, resident)
    stats = swap(stat)
    half = out_width // 2
    both_wo, mark = call(
        stack_kernel,
        [
            jax.ShapeDtypeStruct((4 * w_o.shape[1], half), BF16),
            jax.ShapeDtypeStruct((8, LANES), F32),
        ],
        [VMEM, HBM, HBM],
        [pltpu.SemaphoreType.DMA((4,))],
    )(scores_p, w_o, other_wo)
    part = call(
        attend_kernel,
        jax.ShapeDtypeStruct((heads, PART * (latent // LANES), LANES), F32),
        [SMEM] + [VMEM] * 6,
    )(owners, mark, stats, scores_p, scores_r, keys, resident)
    parts = swap(part)
    sums = call(
        project_kernel, jax.ShapeDtypeStruct((seqs, 2, half + LANES), I16), [VMEM] * 5
    )(owners_row, parts, w_uv, other_uv, both_wo)
    return call(final_kernel, jax.ShapeDtypeStruct((1, 2, out_width), BF16), [VMEM])(swap(sums))


def solution(mesh):
    in_specs = (
        P(("group", "seq"), None, None),
        P("group"),
        P("group"),
        P(("group", "seq"), None, None),
        P("group", None, None),
        P("group", None, "seq", None),
        P(),
        P("seq", None, None),
        P("seq", None, None),
        P("seq", None, None),
    )
    out_specs = P(("group", "seq"), None, None)
    return jax.shard_map(
        on_device, mesh=mesh, in_specs=in_specs, out_specs=out_specs, check_vma=False
    )
```

```python
import functools

import jax
import jax.numpy as jnp
import numpy as np
from jax import lax
from jax.experimental import pallas as pl
from jax.experimental.pallas import tpu as pltpu
from jax.sharding import PartitionSpec as P

F32 = jnp.float32
BF16 = jnp.bfloat16
I32 = jnp.int32
I16 = jnp.int16
VMEM = pl.BlockSpec(memory_space=pltpu.VMEM)
SMEM = pl.BlockSpec(memory_space=pltpu.SMEM)
HBM = pl.BlockSpec(memory_space=pltpu.HBM)
LANES = 128
PACK = 16
PART = 6
BITS = 14.0
NEAR = 4


def iota(shape, dim):
    return lax.broadcasted_iota(I32, shape, dim)


def dot(a, b, dims=((1,), (0,))):
    return lax.dot_general(a, b, (dims, ((), ())), preferred_element_type=F32)


def column_of(row, picks):
    n, width = picks.shape[0], row.shape[1]
    hit = iota((n, width), 1) == picks
    return jnp.sum(jnp.where(hit, row, 0), axis=1, keepdims=True)


def slots_of(owners_row):
    seqs = owners_row.shape[1]
    owners_col = column_of(owners_row, iota((seqs, 1), 0))
    earlier = iota((seqs, seqs), 0) < iota((seqs, seqs), 1)
    same = (owners_col == owners_row) & earlier
    return jnp.sum(jnp.where(same, 1, 0), axis=0, keepdims=True)


def doubled(row):
    seqs = row.shape[1]
    col = column_of(row, iota((seqs, 1), 0))
    hit = iota((seqs, 2 * seqs), 1) // 2 == iota((seqs, 2 * seqs), 0)
    return jnp.sum(jnp.where(hit, col, 0), axis=0, keepdims=True)


def frequencies(half, shape, dim):
    at = iota(shape, dim) % half
    values = np.float32(10000.0) ** (-(np.arange(half, dtype=np.float32) * np.float32(2.0)) / np.float32(2 * half))
    result = jnp.zeros(shape, F32)
    for i in range(half):
        result = jnp.where(at == i, float(values[i]), result)
    return result


def query_kernel(
    res_rows,
    owners_hbm,
    lengths_hbm,
    queries_hbm,
    uk_hbm,
    new_hbm,
    gain_hbm,
    out_ref,
    aux_ref,
    owners_ref,
    lengths_ref,
    queries_ref,
    uk_ref,
    new_ref,
    gain_ref,
    flat,
    sems,
):
    device = lax.axis_index("seq")
    copies = []
    pairs = [
        (owners_hbm, owners_ref),
        (lengths_hbm, lengths_ref),
        (queries_hbm, queries_ref),
        (uk_hbm, uk_ref),
        (new_hbm.at[device], new_ref),
        (gain_hbm, gain_ref),
    ]
    for n, (source, target) in enumerate(pairs):
        copies.append(pltpu.make_async_copy(source, target, sems.at[n]))
        copies[-1].start()
    for copy in copies:
        copy.wait()
    seqs = owners_ref.shape[1]
    nope, latent = uk_ref.shape
    rope = queries_ref.shape[3] - nope
    half = latent // 2
    rows = 2 * seqs
    for s in range(seqs):
        flat[2 * s : 2 * s + 2, : nope + rope] = queries_ref[s, 0].astype(F32)
    values = flat[:, : nope + rope]
    absorbed = dot(values[:, :nope].astype(BF16), uk_ref[...]).astype(BF16)
    row = iota((rows, 1), 0)
    lengths = column_of(lengths_ref[...], row // 2)
    angle = (res_rows + lengths + row % 2).astype(F32) * frequencies(rope // 2, (1, rope), 1)
    x = values[:, nope:]
    swapped = jnp.concatenate([x[:, rope // 2 :], x[:, : rope // 2]], axis=1)
    sine = jnp.sin(angle)
    sine = jnp.where(iota(x.shape, 1) < rope // 2, -sine, sine)
    turned = x * jnp.cos(angle) + swapped * sine
    zero = jnp.zeros((rows, rope), F32)
    pieces = [absorbed[:, :half], absorbed[:, half:]]
    for k in range(3):
        blocks = [turned if j == k else zero for j in range(half // rope)]
        pieces.append(jnp.concatenate(blocks, axis=1).astype(BF16))
    owners = owners_ref[...]
    owner = doubled(owners)
    slot = doubled(slots_of(owners))
    count = out_ref.shape[0]
    total = count * PACK
    shape = (total, rows)
    dest, r = iota(shape, 0) // PACK, iota(shape, 0) % PACK
    seq, tok = iota(shape, 1) // 2, iota(shape, 1) % 2
    here = jnp.where(owner == dest, slot + 1, -1)
    result = None
    for p in range(2):
        q = r - PART * p
        wanted = ((q // 2 == 0) & (seq == dest)) | (here == q // 2)
        hit = (q >= 0) & (q < PART) & (tok == q % 2) & wanted
        one = dot(jnp.where(hit, 1.0, 0.0).astype(BF16), pieces[p])
        result = one if result is None else result + one
    for k in range(3):
        match = (seq == dest) if k == 0 else (here == k)
        hit = (r == 2 * PART + tok) & match
        result = result + dot(jnp.where(hit, 1.0, 0.0).astype(BF16), pieces[2 + k])
    out_ref[...] = result.astype(BF16).reshape(out_ref.shape)
    width = new_ref.shape[1]
    aux_ref[0:2, :width] = new_ref[...].astype(F32)
    mine = jnp.where(iota(lengths_ref.shape, 1) == device, lengths_ref[...], 0)
    mine = jnp.sum(mine, axis=1, keepdims=True).astype(F32)
    aux_ref[2:3, :] = jnp.broadcast_to(mine, (1, aux_ref.shape[1]))
    aux_ref[3:4, :latent] = gain_ref[...].astype(F32).reshape(1, latent)


def compress_kernel(
    res_rows, latent, aux_ref, prompt_ref, resident_hbm, out_ref, bias_ref, resident_ref, sem
):
    fetch = pltpu.make_async_copy(resident_hbm, resident_ref, sem)
    fetch.start()
    width, most = prompt_ref.shape[1:]
    half = (width - latent) // 2
    fresh = jnp.concatenate([aux_ref[0:2, :width], jnp.zeros((PACK - 2, width), F32)], axis=0)
    pick = jnp.where(iota((PACK, LANES), 0) == iota((PACK, LANES), 1), 1.0, 0.0).astype(BF16)
    fresh = dot(fresh.astype(BF16), pick, ((0,), (0,)))
    gain = jnp.broadcast_to(aux_ref[3:4, :latent], (PACK, latent))
    top = jnp.where(iota((PACK, LANES), 0) == 0, 1.0, 0.0).astype(BF16)
    gain = dot(gain.astype(BF16), top, ((0,), (0,)))
    length = aux_ref[2:3, :LANES].astype(I32)
    at = iota(bias_ref.shape, 1)
    token = iota(bias_ref.shape, 0)
    length_all = jnp.concatenate([length] * (bias_ref.shape[1] // LANES), axis=1)
    seen = (at < length_all) | ((at >= most) & (at <= most + token))
    bias_ref[...] = jnp.where(seen, 1.0, 0.0)
    freq = frequencies(half, (half, 1), 0)
    for i in range(most // LANES + 1):
        at = slice(i * LANES, (i + 1) * LANES)
        lane = iota((1, LANES), 1)
        if i * LANES < most:
            raw = prompt_ref[0, :, at].astype(F32)
            position = res_rows + i * LANES + lane
        else:
            raw = fresh
            position = res_rows + length + lane
        lat = raw[:latent]
        meansq = jnp.sum(lat * lat, axis=0, keepdims=True) * (1.0 / latent)
        out_ref[:latent, at] = (lat * lax.rsqrt(meansq + 1e-06) * gain).astype(BF16)
        angle = position.astype(F32) * freq
        cosine, sine = jnp.cos(angle), jnp.sin(angle)
        x1, x2 = raw[latent : latent + half], raw[latent + half :]
        out_ref[latent : latent + half, at] = (x1 * cosine - x2 * sine).astype(BF16)
        out_ref[latent + half :, at] = (x2 * cosine + x1 * sine).astype(BF16)
    fetch.wait()


def score_kernel(scale, q_ref, keys_ref, seen_ref, resident_ref, sp_ref, sr_ref, stat_ref):
    heads = q_ref.shape[0]
    half = q_ref.shape[2]
    width = keys_ref.shape[0]
    rope = width - 2 * half
    rows = 2 * heads
    total = heads * PACK
    flat = q_ref[...].reshape(total, half)
    shape = (rows, total)
    head, tok = iota(shape, 0) // 4 * 2 + iota(shape, 0) % 2, iota(shape, 0) // 2 % 2
    source = iota(shape, 1) - head * PACK

    def picked(r):
        hit = source == r + tok
        return dot(jnp.where(hit, 1.0, 0.0).astype(BF16), flat)

    turned = picked(2 * PART)
    tops, sums = [], []
    for k in range(3):
        query = jnp.concatenate(
            [picked(2 * k), picked(PART + 2 * k), turned[:, k * rope : (k + 1) * rope]], axis=1
        ).astype(BF16)
        keys = keys_ref[...] if k == 0 else resident_ref[k - 1]
        scores = dot(query, keys) * scale
        if k == 0:
            first, second = seen_ref[0:1, :] > 0.5, seen_ref[1:2, :] > 0.5
            token = iota(scores.shape, 0) // 2 % 2
            seen = (first & (token == 0)) | (second & (token == 1))
            scores = jnp.where(seen, scores, -1e30)
            sp_ref[...] = scores
        else:
            sr_ref[k - 1] = scores
        top = jnp.max(scores, axis=1, keepdims=True)
        tops.append(top)
        sums.append(jnp.sum(jnp.exp(scores - top), axis=1, keepdims=True))
    lanes = stat_ref.shape[2]
    here = iota((3 * rows, lanes), 0) == iota((3 * rows, lanes), 1)
    top = jnp.sum(jnp.where(here, jnp.concatenate(tops, axis=0), 0.0), axis=0, keepdims=True)
    total = jnp.sum(jnp.where(here, jnp.concatenate(sums, axis=0), 0.0), axis=0, keepdims=True)
    both = jnp.concatenate([top, total], axis=0)
    stat_ref[...] = jnp.broadcast_to(both[None], stat_ref.shape)


def attend_kernel(owners_ref, mark_ref, stat_ref, sp_ref, sr_ref, keys_ref, resident_ref, out_ref):
    heads = out_ref.shape[0]
    latent = out_ref.shape[1] // PART * LANES
    seqs = owners_ref.shape[0]
    rows = 2 * heads
    device = lax.axis_index("seq")
    lanes = stat_ref.shape[2]
    my_owner = owners_ref[device]
    my_slot = jnp.int32(0)
    seen = jnp.int32(0)
    first = jnp.int32(0)
    second = jnp.int32(0)
    for s in range(seqs):
        owner = owners_ref[s]
        my_slot = my_slot + jnp.where((owner == my_owner) & (s < device), 1, 0)
        mine = owner == device
        first = jnp.where(mine & (seen == 0), s, first)
        second = jnp.where(mine & (seen == 1), s, second)
        seen = seen + jnp.where(mine, 1, 0)

    def column(row, segment):
        picks = iota((rows, 1), 0) + segment * rows
        hit = iota((rows, lanes), 1) == picks
        return jnp.sum(jnp.where(hit, row, 0.0), axis=1, keepdims=True)

    mine = stat_ref[device]
    others = [(stat_ref[my_owner], 1 + my_slot), (stat_ref[first], 0), (stat_ref[second], 0)]
    for k in range(3):
        other, segment = others[k]
        top0, sum0 = column(mine[0:1], k), column(mine[1:2], k)
        top1, sum1 = column(other[0:1], segment), column(other[1:2], segment)
        top = jnp.maximum(top0, top1)
        total = sum0 * jnp.exp(top0 - top) + sum1 * jnp.exp(top1 - top)
        scores = sp_ref[...] if k == 0 else sr_ref[k - 1]
        keys = keys_ref[:latent, :] if k == 0 else resident_ref[k - 1, :latent, :]
        weights = jnp.exp(scores - top).astype(BF16)
        part = dot(weights, keys, ((1,), (1,))) / total
        for h in range(heads):
            for c in range(latent // LANES):
                at = c * PART + 2 * k
                out_ref[h, at : at + 2, :] = part[2 * h : 2 * h + 2, c * LANES : (c + 1) * LANES]


def stack_kernel(after_ref, uv_hbm, other_uv_hbm, wo_hbm, other_hbm, uv_ref, out_ref, mark_ref, sems):
    rows = wo_hbm.shape[1]
    cols = out_ref.shape[1]
    copies = [
        pltpu.make_async_copy(uv_hbm.at[0], uv_ref.at[0], sems.at[4]),
        pltpu.make_async_copy(other_uv_hbm.at[0], uv_ref.at[1], sems.at[5]),
    ]
    for copy in copies:
        copy.start()
    for half in range(2):
        for n, ref in enumerate((wo_hbm, other_hbm)):
            at = 2 * half + n
            copies.append(
                pltpu.make_async_copy(
                    ref.at[0, :, pl.ds(half * cols, cols)], out_ref.at[pl.ds(at * rows, rows), :], sems.at[at]
                )
            )
            copies[-1].start()
    mark_ref[...] = after_ref[: mark_ref.shape[0], : mark_ref.shape[1]]
    for copy in copies:
        copy.wait()


def project_kernel(owners_ref, part_ref, uv_ref, wo_ref, out_ref):
    count, each, lanes = part_ref.shape
    seqs = owners_ref.shape[1]
    cuts = each // PART
    rows = 2 * seqs
    core = lax.axis_index("seq") % 2
    owners = owners_ref[...]
    row = iota((cuts * 2 * rows, 1), 0)
    cut, other, seq = row // (2 * rows), row % (2 * rows) // rows, row % rows // 2
    head = jnp.where(other == 0, core, 1 - core)
    owner = column_of(owners, seq)
    slot = column_of(slots_of(owners), seq)
    first = seq * each + cut * PART + head
    second = owner * each + cut * PART + 2 + 2 * slot + head
    at = iota((cuts * 2 * rows, count * each), 1)
    hit = jnp.where((at == first) | (at == second), 1.0, 0.0).astype(BF16)
    rest = part_ref[...].reshape(count * each, lanes)
    latent = None
    for _ in range(3):
        piece = rest.astype(BF16)
        rest = rest - piece.astype(F32)
        one = dot(hit, piece)
        latent = one if latent is None else latent + one
    latent = latent.astype(BF16)
    latent = jnp.concatenate(
        [latent[c * 2 * rows : (c + 1) * 2 * rows] for c in range(cuts)], axis=1
    )
    head_out = jnp.concatenate(
        [dot(latent[:rows], uv_ref[0]), dot(latent[rows:], uv_ref[1])], axis=1
    )
    half = iota(head_out.shape, 0) % 2
    split = jnp.concatenate(
        [jnp.where(half == 0, head_out, 0.0), jnp.where(half == 1, head_out, 0.0)], axis=1
    )
    product = dot(split.astype(BF16), wo_ref[...])
    top = jnp.max(jnp.abs(product), axis=1, keepdims=True)
    power = jnp.clip(jnp.floor(jnp.log2(jnp.maximum(top, 1e-35))) + 1.0, -100.0, 100.0)
    coded = jnp.round(product * jnp.exp2(BITS - power)).astype(I32).astype(I16)
    power = jnp.broadcast_to(power, (rows, LANES)).astype(I32).astype(I16)
    cols = product.shape[1]
    for s in range(seqs):
        out_ref[s, :, :cols] = coded[2 * s : 2 * s + 2]
        out_ref[s, :, cols:] = power[2 * s : 2 * s + 2]


def final_kernel(in_ref, out_ref):
    cols = out_ref.shape[2] // 2
    for t in range(2):
        total = None
        for n in range(t, in_ref.shape[0], 2):
            power = in_ref[n, :, cols : cols + 1].astype(I32).astype(F32)
            one = in_ref[n, :, :cols].astype(I32).astype(F32) * jnp.exp2(power - BITS)
            total = one if total is None else total + one
        for j in range(2):
            out_ref[0, t : t + 1, j * cols : (j + 1) * cols] = total[j : j + 1].astype(BF16)


def swap(x):
    return lax.all_to_all(x, "seq", split_axis=0, concat_axis=0, tiled=True)


def trade(x, step):
    count = lax.axis_size("seq")
    return lax.ppermute(x, "seq", [(d, d ^ step) for d in range(count)])


def call(kernel, shapes, specs, scratch=(), cost=None, room=None):
    single = not isinstance(shapes, (list, tuple))
    if room is None:
        room = 16 if lax.axis_size("seq") <= 32 else 56
    return pl.pallas_call(
        kernel,
        out_shape=shapes,
        in_specs=specs,
        out_specs=VMEM if single else [VMEM] * len(shapes),
        scratch_shapes=list(scratch),
        cost_estimate=cost,
        compiler_params=pltpu.CompilerParams(vmem_limit_bytes=room * 1024 * 1024),
    )


def on_device(prompt_raw, lengths, owners, resident, new_raw, queries, kv_gain, w_uk, w_uv, w_o):
    count = lax.axis_size("seq")
    seqs = lengths.shape[0]
    most, width = prompt_raw.shape[1:]
    latent = kv_gain.shape[0]
    res_rows = resident.shape[1]
    nope = w_uk.shape[1]
    rope = width - latent
    heads = count
    out_width = w_o.shape[2]
    scale = 1.0 / queries.shape[-1] ** 0.5
    owners_row, lengths_row = owners.reshape(1, seqs), lengths.reshape(1, seqs)
    prompt_raw = prompt_raw.transpose(0, 2, 1)
    resident = resident.transpose(0, 2, 1)
    queries = queries.transpose(0, 2, 1, 3)
    keys_rows = most + LANES

    aux_width = -(-width // LANES) * LANES
    query, aux = call(
        functools.partial(query_kernel, res_rows),
        [
            jax.ShapeDtypeStruct((count, PACK, latent // 2), BF16),
            jax.ShapeDtypeStruct((8, aux_width), F32),
        ],
        [HBM] * 6,
        [
            pltpu.VMEM((1, seqs), I32),
            pltpu.VMEM((1, seqs), I32),
            pltpu.VMEM(queries.shape, BF16),
            pltpu.VMEM((nope, latent), BF16),
            pltpu.VMEM((2, width), BF16),
            pltpu.VMEM((latent,), BF16),
            pltpu.VMEM((2 * seqs, -(-(nope + rope) // LANES) * LANES), F32),
            pltpu.SemaphoreType.DMA((6,)),
        ],
        room=60,
    )(owners_row, lengths_row, queries, w_uk[0], new_raw, kv_gain)
    received = swap(query)
    query, w_uv, w_o = lax.optimization_barrier((query, w_uv, w_o))
    other_uv, other_wo = trade(w_uv, 1), trade(w_o, 1)
    keys, seen, resident = call(
        functools.partial(compress_kernel, res_rows, latent),
        [
            jax.ShapeDtypeStruct((width, keys_rows), BF16),
            jax.ShapeDtypeStruct((8, keys_rows), F32),
            jax.ShapeDtypeStruct(resident.shape, BF16),
        ],
        [VMEM] * 2 + [HBM],
        [pltpu.SemaphoreType.DMA],
        cost=pl.CostEstimate(flops=10**7, bytes_accessed=10**7, transcendentals=10**5),
    )(aux, prompt_raw, resident)
    lanes = -(-6 * heads // LANES) * LANES
    scores_p, scores_r, stat = call(
        functools.partial(score_kernel, scale),
        [
            jax.ShapeDtypeStruct((2 * heads, keys_rows), F32),
            jax.ShapeDtypeStruct((2, 2 * heads, res_rows), F32),
            jax.ShapeDtypeStruct((count, 2, lanes), F32),
        ],
        [VMEM] * 4,
    )(received, keys, seen, resident)
    stats = swap(stat)
    half = out_width // 2
    both_uv, both_wo, mark = call(
        stack_kernel,
        [
            jax.ShapeDtypeStruct((2,) + w_uv.shape[1:], BF16),
            jax.ShapeDtypeStruct((4 * w_o.shape[1], half), BF16),
            jax.ShapeDtypeStruct((8, LANES), F32),
        ],
        [VMEM] + [HBM] * 4,
        [pltpu.SemaphoreType.DMA((6,))],
    )(scores_p, w_uv, other_uv, w_o, other_wo)
    part = call(
        attend_kernel,
        jax.ShapeDtypeStruct((heads, PART * (latent // LANES), LANES), F32),
        [SMEM] + [VMEM] * 6,
    )(owners, mark, stats, scores_p, scores_r, keys, resident)
    parts = swap(part)
    sums = call(
        project_kernel, jax.ShapeDtypeStruct((seqs, 2, half + LANES), I16), [VMEM] * 4
    )(owners_row, parts, both_uv, both_wo)
    return call(final_kernel, jax.ShapeDtypeStruct((1, 2, out_width), BF16), [VMEM])(swap(sums))


def solution(mesh):
    in_specs = (
        P(("group", "seq"), None, None),
        P("group"),
        P("group"),
        P(("group", "seq"), None, None),
        P("group", None, None),
        P("group", None, "seq", None),
        P(),
        P("seq", None, None),
        P("seq", None, None),
        P("seq", None, None),
    )
    out_specs = P(("group", "seq"), None, None)
    return jax.shard_map(
        on_device, mesh=mesh, in_specs=in_specs, out_specs=out_specs, check_vma=False
    )
```

```python
import functools

import jax
import jax.numpy as jnp
import numpy as np
from jax import lax
from jax.experimental import pallas as pl
from jax.experimental.pallas import tpu as pltpu
from jax.sharding import PartitionSpec as P

F32 = jnp.float32
BF16 = jnp.bfloat16
I32 = jnp.int32
I16 = jnp.int16
VMEM = pl.BlockSpec(memory_space=pltpu.VMEM)
SMEM = pl.BlockSpec(memory_space=pltpu.SMEM)
HBM = pl.BlockSpec(memory_space=pltpu.HBM)
LANES = 128
PACK = 16
PART = 6
BITS = 14.0
NEAR = 4


def iota(shape, dim):
    return lax.broadcasted_iota(I32, shape, dim)


def dot(a, b, dims=((1,), (0,))):
    return lax.dot_general(a, b, (dims, ((), ())), preferred_element_type=F32)


def column_of(row, picks):
    n, width = picks.shape[0], row.shape[1]
    hit = iota((n, width), 1) == picks
    return jnp.sum(jnp.where(hit, row, 0), axis=1, keepdims=True)


def slots_of(owners_row):
    seqs = owners_row.shape[1]
    owners_col = column_of(owners_row, iota((seqs, 1), 0))
    earlier = iota((seqs, seqs), 0) < iota((seqs, seqs), 1)
    same = (owners_col == owners_row) & earlier
    return jnp.sum(jnp.where(same, 1, 0), axis=0, keepdims=True)


def doubled(row):
    seqs = row.shape[1]
    col = column_of(row, iota((seqs, 1), 0))
    hit = iota((seqs, 2 * seqs), 1) // 2 == iota((seqs, 2 * seqs), 0)
    return jnp.sum(jnp.where(hit, col, 0), axis=0, keepdims=True)


def frequencies(half, shape, dim):
    at = iota(shape, dim) % half
    values = np.float32(10000.0) ** (-(np.arange(half, dtype=np.float32) * np.float32(2.0)) / np.float32(2 * half))
    result = jnp.zeros(shape, F32)
    for i in range(half):
        result = jnp.where(at == i, float(values[i]), result)
    return result


def query_kernel(
    res_rows,
    owners_hbm,
    lengths_hbm,
    queries_hbm,
    uk_hbm,
    new_hbm,
    gain_hbm,
    out_ref,
    aux_ref,
    owners_ref,
    lengths_ref,
    queries_ref,
    uk_ref,
    new_ref,
    gain_ref,
    flat,
    sems,
):
    device = lax.axis_index("seq")
    copies = []
    pairs = [
        (owners_hbm, owners_ref),
        (lengths_hbm, lengths_ref),
        (queries_hbm, queries_ref),
        (uk_hbm, uk_ref),
        (new_hbm.at[device], new_ref),
        (gain_hbm, gain_ref),
    ]
    for n, (source, target) in enumerate(pairs):
        copies.append(pltpu.make_async_copy(source, target, sems.at[n]))
        copies[-1].start()
    for copy in copies:
        copy.wait()
    seqs = owners_ref.shape[1]
    nope, latent = uk_ref.shape
    rope = queries_ref.shape[3] - nope
    half = latent // 2
    rows = 2 * seqs
    for s in range(seqs):
        flat[2 * s : 2 * s + 2, : nope + rope] = queries_ref[s, 0].astype(F32)
    values = flat[:, : nope + rope]
    absorbed = dot(values[:, :nope].astype(BF16), uk_ref[...]).astype(BF16)
    row = iota((rows, 1), 0)
    lengths = column_of(lengths_ref[...], row // 2)
    angle = (res_rows + lengths + row % 2).astype(F32) * frequencies(rope // 2, (1, rope), 1)
    x = values[:, nope:]
    swapped = jnp.concatenate([x[:, rope // 2 :], x[:, : rope // 2]], axis=1)
    sine = jnp.sin(angle)
    sine = jnp.where(iota(x.shape, 1) < rope // 2, -sine, sine)
    turned = x * jnp.cos(angle) + swapped * sine
    zero = jnp.zeros((rows, rope), F32)
    pieces = [absorbed[:, :half], absorbed[:, half:]]
    for k in range(3):
        blocks = [turned if j == k else zero for j in range(half // rope)]
        pieces.append(jnp.concatenate(blocks, axis=1).astype(BF16))
    owners = owners_ref[...]
    owner = doubled(owners)
    slot = doubled(slots_of(owners))
    count = out_ref.shape[0]
    total = count * PACK
    shape = (total, rows)
    dest, r = iota(shape, 0) // PACK, iota(shape, 0) % PACK
    seq, tok = iota(shape, 1) // 2, iota(shape, 1) % 2
    here = jnp.where(owner == dest, slot + 1, -1)
    result = None
    for p in range(2):
        q = r - PART * p
        wanted = ((q // 2 == 0) & (seq == dest)) | (here == q // 2)
        hit = (q >= 0) & (q < PART) & (tok == q % 2) & wanted
        one = dot(jnp.where(hit, 1.0, 0.0).astype(BF16), pieces[p])
        result = one if result is None else result + one
    for k in range(3):
        match = (seq == dest) if k == 0 else (here == k)
        hit = (r == 2 * PART + tok) & match
        result = result + dot(jnp.where(hit, 1.0, 0.0).astype(BF16), pieces[2 + k])
    out_ref[...] = result.astype(BF16).reshape(out_ref.shape)
    width = new_ref.shape[1]
    aux_ref[0:2, :width] = new_ref[...].astype(F32)
    mine = jnp.where(iota(lengths_ref.shape, 1) == device, lengths_ref[...], 0)
    mine = jnp.sum(mine, axis=1, keepdims=True).astype(F32)
    aux_ref[2:3, :] = jnp.broadcast_to(mine, (1, aux_ref.shape[1]))
    aux_ref[3:4, :latent] = gain_ref[...].astype(F32).reshape(1, latent)


def compress_kernel(
    res_rows, latent, aux_ref, prompt_ref, resident_hbm, out_ref, bias_ref, resident_ref, sem
):
    fetch = pltpu.make_async_copy(resident_hbm, resident_ref, sem)
    fetch.start()
    width, most = prompt_ref.shape[1:]
    half = (width - latent) // 2
    fresh = jnp.concatenate([aux_ref[0:2, :width], jnp.zeros((PACK - 2, width), F32)], axis=0)
    pick = jnp.where(iota((PACK, LANES), 0) == iota((PACK, LANES), 1), 1.0, 0.0).astype(BF16)
    fresh = dot(fresh.astype(BF16), pick, ((0,), (0,)))
    gain = jnp.broadcast_to(aux_ref[3:4, :latent], (PACK, latent))
    top = jnp.where(iota((PACK, LANES), 0) == 0, 1.0, 0.0).astype(BF16)
    gain = dot(gain.astype(BF16), top, ((0,), (0,)))
    length = aux_ref[2:3, :LANES].astype(I32)
    at = iota(bias_ref.shape, 1)
    token = iota(bias_ref.shape, 0)
    length_all = jnp.concatenate([length] * (bias_ref.shape[1] // LANES), axis=1)
    seen = (at < length_all) | ((at >= most) & (at <= most + token))
    bias_ref[...] = jnp.where(seen, 1.0, 0.0)
    freq = frequencies(half, (half, 1), 0)
    for i in range(most // LANES + 1):
        at = slice(i * LANES, (i + 1) * LANES)
        lane = iota((1, LANES), 1)
        if i * LANES < most:
            raw = prompt_ref[0, :, at].astype(F32)
            position = res_rows + i * LANES + lane
        else:
            raw = fresh
            position = res_rows + length + lane
        lat = raw[:latent]
        meansq = jnp.sum(lat * lat, axis=0, keepdims=True) * (1.0 / latent)
        out_ref[:latent, at] = (lat * lax.rsqrt(meansq + 1e-06) * gain).astype(BF16)
        angle = position.astype(F32) * freq
        cosine, sine = jnp.cos(angle), jnp.sin(angle)
        x1, x2 = raw[latent : latent + half], raw[latent + half :]
        out_ref[latent : latent + half, at] = (x1 * cosine - x2 * sine).astype(BF16)
        out_ref[latent + half :, at] = (x2 * cosine + x1 * sine).astype(BF16)
    fetch.wait()


def score_kernel(scale, q_ref, keys_ref, seen_ref, resident_ref, sp_ref, sr_ref, stat_ref):
    heads = q_ref.shape[0]
    half = q_ref.shape[2]
    width = keys_ref.shape[0]
    rope = width - 2 * half
    rows = 2 * heads
    total = heads * PACK
    flat = q_ref[...].reshape(total, half)
    shape = (rows, total)
    head, tok = iota(shape, 0) // 4 * 2 + iota(shape, 0) % 2, iota(shape, 0) // 2 % 2
    source = iota(shape, 1) - head * PACK

    def picked(r):
        hit = source == r + tok
        return dot(jnp.where(hit, 1.0, 0.0).astype(BF16), flat)

    turned = picked(2 * PART)
    tops, sums = [], []
    for k in range(3):
        query = jnp.concatenate(
            [picked(2 * k), picked(PART + 2 * k), turned[:, k * rope : (k + 1) * rope]], axis=1
        ).astype(BF16)
        keys = keys_ref[...] if k == 0 else resident_ref[k - 1]
        scores = dot(query, keys) * scale
        if k == 0:
            first, second = seen_ref[0:1, :] > 0.5, seen_ref[1:2, :] > 0.5
            token = iota(scores.shape, 0) // 2 % 2
            seen = (first & (token == 0)) | (second & (token == 1))
            scores = jnp.where(seen, scores, -1e30)
            sp_ref[...] = scores
        else:
            sr_ref[k - 1] = scores
        top = jnp.max(scores, axis=1, keepdims=True)
        tops.append(top)
        sums.append(jnp.sum(jnp.exp(scores - top), axis=1, keepdims=True))
    lanes = stat_ref.shape[2]
    here = iota((3 * rows, lanes), 0) == iota((3 * rows, lanes), 1)
    top = jnp.sum(jnp.where(here, jnp.concatenate(tops, axis=0), 0.0), axis=0, keepdims=True)
    total = jnp.sum(jnp.where(here, jnp.concatenate(sums, axis=0), 0.0), axis=0, keepdims=True)
    both = jnp.concatenate([top, total], axis=0)
    stat_ref[...] = jnp.broadcast_to(both[None], stat_ref.shape)


def attend_kernel(owners_ref, stat_ref, sp_ref, sr_ref, keys_ref, resident_ref, out_ref):
    heads = out_ref.shape[0]
    latent = out_ref.shape[1] // PART * LANES
    seqs = owners_ref.shape[0]
    rows = 2 * heads
    device = lax.axis_index("seq")
    lanes = stat_ref.shape[2]
    my_owner = owners_ref[device]
    my_slot = jnp.int32(0)
    seen = jnp.int32(0)
    first = jnp.int32(0)
    second = jnp.int32(0)
    for s in range(seqs):
        owner = owners_ref[s]
        my_slot = my_slot + jnp.where((owner == my_owner) & (s < device), 1, 0)
        mine = owner == device
        first = jnp.where(mine & (seen == 0), s, first)
        second = jnp.where(mine & (seen == 1), s, second)
        seen = seen + jnp.where(mine, 1, 0)

    def column(row, segment):
        picks = iota((rows, 1), 0) + segment * rows
        hit = iota((rows, lanes), 1) == picks
        return jnp.sum(jnp.where(hit, row, 0.0), axis=1, keepdims=True)

    mine = stat_ref[device]
    others = [(stat_ref[my_owner], 1 + my_slot), (stat_ref[first], 0), (stat_ref[second], 0)]
    for k in range(3):
        other, segment = others[k]
        top0, sum0 = column(mine[0:1], k), column(mine[1:2], k)
        top1, sum1 = column(other[0:1], segment), column(other[1:2], segment)
        top = jnp.maximum(top0, top1)
        total = sum0 * jnp.exp(top0 - top) + sum1 * jnp.exp(top1 - top)
        scores = sp_ref[...] if k == 0 else sr_ref[k - 1]
        keys = keys_ref[:latent, :] if k == 0 else resident_ref[k - 1, :latent, :]
        weights = jnp.exp(scores - top).astype(BF16)
        part = dot(weights, keys, ((1,), (1,))) / total
        for h in range(heads):
            for c in range(latent // LANES):
                at = c * PART + 2 * k
                out_ref[h, at : at + 2, :] = part[2 * h : 2 * h + 2, c * LANES : (c + 1) * LANES]


def project_kernel(
    owners_ref, part_ref, uv_ref, other_uv_ref, wo_hbm, other_wo_hbm, out_ref, wo_ref, sems
):
    inner = wo_hbm.shape[1]
    cols = wo_ref.shape[1]
    copies = []
    for side in range(2):
        for n, ref in enumerate((wo_hbm, other_wo_hbm)):
            at = 2 * side + n
            block = wo_ref.at[pl.ds(at * inner, inner), :]
            copies.append(
                pltpu.make_async_copy(ref.at[0, :, pl.ds(side * cols, cols)], block, sems.at[at])
            )
            copies[-1].start()
    count, each, lanes = part_ref.shape
    seqs = owners_ref.shape[1]
    cuts = each // PART
    rows = 2 * seqs
    core = lax.axis_index("seq") % 2
    owners = owners_ref[...]
    row = iota((cuts * 2 * rows, 1), 0)
    cut, other, seq = row // (2 * rows), row % (2 * rows) // rows, row % rows // 2
    head = jnp.where(other == 0, core, 1 - core)
    owner = column_of(owners, seq)
    slot = column_of(slots_of(owners), seq)
    first = seq * each + cut * PART + head
    second = owner * each + cut * PART + 2 + 2 * slot + head
    at = iota((cuts * 2 * rows, count * each), 1)
    hit = jnp.where((at == first) | (at == second), 1.0, 0.0).astype(BF16)
    rest = part_ref[...].reshape(count * each, lanes)
    latent = None
    for _ in range(3):
        piece = rest.astype(BF16)
        rest = rest - piece.astype(F32)
        one = dot(hit, piece)
        latent = one if latent is None else latent + one
    latent = latent.astype(BF16)
    latent = jnp.concatenate(
        [latent[c * 2 * rows : (c + 1) * 2 * rows] for c in range(cuts)], axis=1
    )
    head_out = jnp.concatenate(
        [dot(latent[:rows], uv_ref[0]), dot(latent[rows:], other_uv_ref[0])], axis=1
    )
    half = iota(head_out.shape, 0) % 2
    split = jnp.concatenate(
        [jnp.where(half == 0, head_out, 0.0), jnp.where(half == 1, head_out, 0.0)], axis=1
    )
    split = split.astype(BF16)
    for copy in copies:
        copy.wait()
    product = dot(split, wo_ref[...])
    top = jnp.max(jnp.abs(product), axis=1, keepdims=True)
    power = jnp.clip(jnp.floor(jnp.log2(jnp.maximum(top, 1e-35))) + 1.0, -100.0, 100.0)
    coded = jnp.round(product * jnp.exp2(BITS - power)).astype(I32).astype(I16)
    power = jnp.broadcast_to(power, (rows, LANES)).astype(I32).astype(I16)
    for s in range(seqs):
        out_ref[s, :, :cols] = coded[2 * s : 2 * s + 2]
        out_ref[s, :, cols:] = power[2 * s : 2 * s + 2]


def final_kernel(in_ref, out_ref):
    cols = out_ref.shape[2] // 2
    for t in range(2):
        total = None
        for n in range(t, in_ref.shape[0], 2):
            power = in_ref[n, :, cols : cols + 1].astype(I32).astype(F32)
            one = in_ref[n, :, :cols].astype(I32).astype(F32) * jnp.exp2(power - BITS)
            total = one if total is None else total + one
        for j in range(2):
            out_ref[0, t : t + 1, j * cols : (j + 1) * cols] = total[j : j + 1].astype(BF16)


def swap(x):
    return lax.all_to_all(x, "seq", split_axis=0, concat_axis=0, tiled=True)


def trade(x, step):
    count = lax.axis_size("seq")
    return lax.ppermute(x, "seq", [(d, d ^ step) for d in range(count)])


def call(kernel, shapes, specs, scratch=(), cost=None, room=None):
    single = not isinstance(shapes, (list, tuple))
    if room is None:
        room = 16 if lax.axis_size("seq") <= 32 else 56
    return pl.pallas_call(
        kernel,
        out_shape=shapes,
        in_specs=specs,
        out_specs=VMEM if single else [VMEM] * len(shapes),
        scratch_shapes=list(scratch),
        cost_estimate=cost,
        compiler_params=pltpu.CompilerParams(vmem_limit_bytes=room * 1024 * 1024),
    )


def on_device(prompt_raw, lengths, owners, resident, new_raw, queries, kv_gain, w_uk, w_uv, w_o):
    count = lax.axis_size("seq")
    seqs = lengths.shape[0]
    most, width = prompt_raw.shape[1:]
    latent = kv_gain.shape[0]
    res_rows = resident.shape[1]
    nope = w_uk.shape[1]
    rope = width - latent
    heads = count
    out_width = w_o.shape[2]
    scale = 1.0 / queries.shape[-1] ** 0.5
    owners_row, lengths_row = owners.reshape(1, seqs), lengths.reshape(1, seqs)
    prompt_raw = prompt_raw.transpose(0, 2, 1)
    resident = resident.transpose(0, 2, 1)
    queries = queries.transpose(0, 2, 1, 3)
    keys_rows = most + LANES

    aux_width = -(-width // LANES) * LANES
    query, aux = call(
        functools.partial(query_kernel, res_rows),
        [
            jax.ShapeDtypeStruct((count, PACK, latent // 2), BF16),
            jax.ShapeDtypeStruct((8, aux_width), F32),
        ],
        [HBM] * 6,
        [
            pltpu.VMEM((1, seqs), I32),
            pltpu.VMEM((1, seqs), I32),
            pltpu.VMEM(queries.shape, BF16),
            pltpu.VMEM((nope, latent), BF16),
            pltpu.VMEM((2, width), BF16),
            pltpu.VMEM((latent,), BF16),
            pltpu.VMEM((2 * seqs, -(-(nope + rope) // LANES) * LANES), F32),
            pltpu.SemaphoreType.DMA((6,)),
        ],
        room=60,
    )(owners_row, lengths_row, queries, w_uk[0], new_raw, kv_gain)
    received = swap(query)
    keys, seen, resident = call(
        functools.partial(compress_kernel, res_rows, latent),
        [
            jax.ShapeDtypeStruct((width, keys_rows), BF16),
            jax.ShapeDtypeStruct((8, keys_rows), F32),
            jax.ShapeDtypeStruct(resident.shape, BF16),
        ],
        [VMEM] * 2 + [HBM],
        [pltpu.SemaphoreType.DMA],
        cost=pl.CostEstimate(flops=10**7, bytes_accessed=10**7, transcendentals=10**5),
    )(aux, prompt_raw, resident)
    seen, w_uv, w_o = lax.optimization_barrier((seen, w_uv, w_o))
    other_uv, other_wo = trade(w_uv, 1), trade(w_o, 1)
    lanes = -(-6 * heads // LANES) * LANES
    scores_p, scores_r, stat = call(
        functools.partial(score_kernel, scale),
        [
            jax.ShapeDtypeStruct((2 * heads, keys_rows), F32),
            jax.ShapeDtypeStruct((2, 2 * heads, res_rows), F32),
            jax.ShapeDtypeStruct((count, 2, lanes), F32),
        ],
        [VMEM] * 4,
    )(received, keys, seen, resident)
    stat, other_uv = lax.optimization_barrier((stat, other_uv))
    stats = swap(stat)
    half = out_width // 2
    part = call(
        attend_kernel,
        jax.ShapeDtypeStruct((heads, PART * (latent // LANES), LANES), F32),
        [SMEM] + [VMEM] * 5,
    )(owners, stats, scores_p, scores_r, keys, resident)
    parts = swap(part)
    sums = call(
        project_kernel,
        jax.ShapeDtypeStruct((seqs, 2, half + LANES), I16),
        [VMEM] * 4 + [HBM] * 2,
        [pltpu.VMEM((4 * w_o.shape[1], half), BF16), pltpu.SemaphoreType.DMA((4,))],
        room=60,
    )(owners_row, parts, w_uv, other_uv, w_o, other_wo)
    return call(final_kernel, jax.ShapeDtypeStruct((1, 2, out_width), BF16), [VMEM])(swap(sums))


def solution(mesh):
    in_specs = (
        P(("group", "seq"), None, None),
        P("group"),
        P("group"),
        P(("group", "seq"), None, None),
        P("group", None, None),
        P("group", None, "seq", None),
        P(),
        P("seq", None, None),
        P("seq", None, None),
        P("seq", None, None),
    )
    out_specs = P(("group", "seq"), None, None)
    return jax.shard_map(
        on_device, mesh=mesh, in_specs=in_specs, out_specs=out_specs, check_vma=False
    )
```

```python
import functools

import jax
import jax.numpy as jnp
import numpy as np
from jax import lax
from jax.experimental import pallas as pl
from jax.experimental.pallas import tpu as pltpu
from jax.sharding import PartitionSpec as P

F32 = jnp.float32
BF16 = jnp.bfloat16
I32 = jnp.int32
I16 = jnp.int16
VMEM = pl.BlockSpec(memory_space=pltpu.VMEM)
SMEM = pl.BlockSpec(memory_space=pltpu.SMEM)
HBM = pl.BlockSpec(memory_space=pltpu.HBM)
LANES = 128
PACK = 16
PART = 6
BITS = 14.0
NEAR = 4


def iota(shape, dim):
    return lax.broadcasted_iota(I32, shape, dim)


def dot(a, b, dims=((1,), (0,))):
    return lax.dot_general(a, b, (dims, ((), ())), preferred_element_type=F32)


def column_of(row, picks):
    n, width = picks.shape[0], row.shape[1]
    hit = iota((n, width), 1) == picks
    return jnp.sum(jnp.where(hit, row, 0), axis=1, keepdims=True)


def slots_of(owners_row):
    seqs = owners_row.shape[1]
    owners_col = column_of(owners_row, iota((seqs, 1), 0))
    earlier = iota((seqs, seqs), 0) < iota((seqs, seqs), 1)
    same = (owners_col == owners_row) & earlier
    return jnp.sum(jnp.where(same, 1, 0), axis=0, keepdims=True)


def doubled(row):
    seqs = row.shape[1]
    col = column_of(row, iota((seqs, 1), 0))
    hit = iota((seqs, 2 * seqs), 1) // 2 == iota((seqs, 2 * seqs), 0)
    return jnp.sum(jnp.where(hit, col, 0), axis=0, keepdims=True)


def frequencies(half, shape, dim):
    at = iota(shape, dim) % half
    values = np.float32(10000.0) ** (-(np.arange(half, dtype=np.float32) * np.float32(2.0)) / np.float32(2 * half))
    result = jnp.zeros(shape, F32)
    for i in range(half):
        result = jnp.where(at == i, float(values[i]), result)
    return result


def query_kernel(
    res_rows,
    owners_hbm,
    lengths_hbm,
    queries_hbm,
    uk_hbm,
    new_hbm,
    gain_hbm,
    out_ref,
    aux_ref,
    owners_ref,
    lengths_ref,
    queries_ref,
    uk_ref,
    new_ref,
    gain_ref,
    flat,
    sems,
):
    device = lax.axis_index("seq")
    copies = []
    pairs = [
        (owners_hbm, owners_ref),
        (lengths_hbm, lengths_ref),
        (queries_hbm, queries_ref),
        (uk_hbm, uk_ref),
        (new_hbm.at[device], new_ref),
        (gain_hbm, gain_ref),
    ]
    for n, (source, target) in enumerate(pairs):
        copies.append(pltpu.make_async_copy(source, target, sems.at[n]))
        copies[-1].start()
    for copy in copies:
        copy.wait()
    seqs = owners_ref.shape[1]
    nope, latent = uk_ref.shape
    rope = queries_ref.shape[3] - nope
    half = latent // 2
    rows = 2 * seqs
    for s in range(seqs):
        flat[2 * s : 2 * s + 2, : nope + rope] = queries_ref[s, 0].astype(F32)
    values = flat[:, : nope + rope]
    absorbed = dot(values[:, :nope].astype(BF16), uk_ref[...]).astype(BF16)
    row = iota((rows, 1), 0)
    lengths = column_of(lengths_ref[...], row // 2)
    angle = (res_rows + lengths + row % 2).astype(F32) * frequencies(rope // 2, (1, rope), 1)
    x = values[:, nope:]
    swapped = jnp.concatenate([x[:, rope // 2 :], x[:, : rope // 2]], axis=1)
    sine = jnp.sin(angle)
    sine = jnp.where(iota(x.shape, 1) < rope // 2, -sine, sine)
    turned = x * jnp.cos(angle) + swapped * sine
    zero = jnp.zeros((rows, rope), F32)
    pieces = [absorbed[:, :half], absorbed[:, half:]]
    for k in range(3):
        blocks = [turned if j == k else zero for j in range(half // rope)]
        pieces.append(jnp.concatenate(blocks, axis=1).astype(BF16))
    owners = owners_ref[...]
    owner = doubled(owners)
    slot = doubled(slots_of(owners))
    count = out_ref.shape[0]
    total = count * PACK
    shape = (total, rows)
    dest, r = iota(shape, 0) // PACK, iota(shape, 0) % PACK
    seq, tok = iota(shape, 1) // 2, iota(shape, 1) % 2
    here = jnp.where(owner == dest, slot + 1, -1)
    result = None
    for p in range(2):
        q = r - PART * p
        wanted = ((q // 2 == 0) & (seq == dest)) | (here == q // 2)
        hit = (q >= 0) & (q < PART) & (tok == q % 2) & wanted
        one = dot(jnp.where(hit, 1.0, 0.0).astype(BF16), pieces[p])
        result = one if result is None else result + one
    for k in range(3):
        match = (seq == dest) if k == 0 else (here == k)
        hit = (r == 2 * PART + tok) & match
        result = result + dot(jnp.where(hit, 1.0, 0.0).astype(BF16), pieces[2 + k])
    out_ref[...] = result.astype(BF16).reshape(out_ref.shape)
    width = new_ref.shape[1]
    aux_ref[0:2, :width] = new_ref[...].astype(F32)
    mine = jnp.where(iota(lengths_ref.shape, 1) == device, lengths_ref[...], 0)
    mine = jnp.sum(mine, axis=1, keepdims=True).astype(F32)
    aux_ref[2:3, :] = jnp.broadcast_to(mine, (1, aux_ref.shape[1]))
    aux_ref[3:4, :latent] = gain_ref[...].astype(F32).reshape(1, latent)


def compress_kernel(
    res_rows, latent, aux_ref, prompt_ref, resident_hbm, out_ref, bias_ref, resident_ref, sem
):
    fetch = pltpu.make_async_copy(resident_hbm, resident_ref, sem)
    fetch.start()
    width, most = prompt_ref.shape[1:]
    half = (width - latent) // 2
    fresh = jnp.concatenate([aux_ref[0:2, :width], jnp.zeros((PACK - 2, width), F32)], axis=0)
    pick = jnp.where(iota((PACK, LANES), 0) == iota((PACK, LANES), 1), 1.0, 0.0).astype(BF16)
    fresh = dot(fresh.astype(BF16), pick, ((0,), (0,)))
    gain = jnp.broadcast_to(aux_ref[3:4, :latent], (PACK, latent))
    top = jnp.where(iota((PACK, LANES), 0) == 0, 1.0, 0.0).astype(BF16)
    gain = dot(gain.astype(BF16), top, ((0,), (0,)))
    length = aux_ref[2:3, :LANES].astype(I32)
    at = iota(bias_ref.shape, 1)
    token = iota(bias_ref.shape, 0)
    length_all = jnp.concatenate([length] * (bias_ref.shape[1] // LANES), axis=1)
    seen = (at < length_all) | ((at >= most) & (at <= most + token))
    bias_ref[...] = jnp.where(seen, 1.0, 0.0)
    freq = frequencies(half, (half, 1), 0)
    for i in range(most // LANES + 1):
        at = slice(i * LANES, (i + 1) * LANES)
        lane = iota((1, LANES), 1)
        if i * LANES < most:
            raw = prompt_ref[0, :, at].astype(F32)
            position = res_rows + i * LANES + lane
        else:
            raw = fresh
            position = res_rows + length + lane
        lat = raw[:latent]
        meansq = jnp.sum(lat * lat, axis=0, keepdims=True) * (1.0 / latent)
        out_ref[:latent, at] = (lat * lax.rsqrt(meansq + 1e-06) * gain).astype(BF16)
        angle = position.astype(F32) * freq
        cosine, sine = jnp.cos(angle), jnp.sin(angle)
        x1, x2 = raw[latent : latent + half], raw[latent + half :]
        out_ref[latent : latent + half, at] = (x1 * cosine - x2 * sine).astype(BF16)
        out_ref[latent + half :, at] = (x2 * cosine + x1 * sine).astype(BF16)
    fetch.wait()


def score_kernel(scale, q_ref, keys_ref, seen_ref, resident_ref, sp_ref, sr_ref, stat_ref):
    heads = q_ref.shape[0]
    half = q_ref.shape[2]
    width = keys_ref.shape[0]
    rope = width - 2 * half
    rows = 2 * heads
    total = heads * PACK
    flat = q_ref[...].reshape(total, half)
    shape = (rows, total)
    head, tok = iota(shape, 0) // 4 * 2 + iota(shape, 0) % 2, iota(shape, 0) // 2 % 2
    source = iota(shape, 1) - head * PACK

    def picked(r):
        hit = source == r + tok
        return dot(jnp.where(hit, 1.0, 0.0).astype(BF16), flat)

    turned = picked(2 * PART)
    tops, sums = [], []
    for k in range(3):
        query = jnp.concatenate(
            [picked(2 * k), picked(PART + 2 * k), turned[:, k * rope : (k + 1) * rope]], axis=1
        ).astype(BF16)
        keys = keys_ref[...] if k == 0 else resident_ref[k - 1]
        scores = dot(query, keys) * scale
        if k == 0:
            first, second = seen_ref[0:1, :] > 0.5, seen_ref[1:2, :] > 0.5
            token = iota(scores.shape, 0) // 2 % 2
            seen = (first & (token == 0)) | (second & (token == 1))
            scores = jnp.where(seen, scores, -1e30)
            sp_ref[...] = scores
        else:
            sr_ref[k - 1] = scores
        top = jnp.max(scores, axis=1, keepdims=True)
        tops.append(top)
        sums.append(jnp.sum(jnp.exp(scores - top), axis=1, keepdims=True))
    lanes = stat_ref.shape[2]
    here = iota((3 * rows, lanes), 0) == iota((3 * rows, lanes), 1)
    top = jnp.sum(jnp.where(here, jnp.concatenate(tops, axis=0), 0.0), axis=0, keepdims=True)
    total = jnp.sum(jnp.where(here, jnp.concatenate(sums, axis=0), 0.0), axis=0, keepdims=True)
    both = jnp.concatenate([top, total], axis=0)
    stat_ref[...] = jnp.broadcast_to(both[None], stat_ref.shape)


def attend_kernel(owners_ref, stat_ref, sp_ref, sr_ref, keys_ref, resident_ref, out_ref, mark_ref):
    heads = out_ref.shape[0]
    latent = out_ref.shape[1] // PART * LANES
    seqs = owners_ref.shape[0]
    rows = 2 * heads
    device = lax.axis_index("seq")
    lanes = stat_ref.shape[2]
    my_owner = owners_ref[device]
    my_slot = jnp.int32(0)
    seen = jnp.int32(0)
    first = jnp.int32(0)
    second = jnp.int32(0)
    for s in range(seqs):
        owner = owners_ref[s]
        my_slot = my_slot + jnp.where((owner == my_owner) & (s < device), 1, 0)
        mine = owner == device
        first = jnp.where(mine & (seen == 0), s, first)
        second = jnp.where(mine & (seen == 1), s, second)
        seen = seen + jnp.where(mine, 1, 0)

    def column(row, segment):
        picks = iota((rows, 1), 0) + segment * rows
        hit = iota((rows, lanes), 1) == picks
        return jnp.sum(jnp.where(hit, row, 0.0), axis=1, keepdims=True)

    mark_ref[...] = jnp.zeros(mark_ref.shape, F32)
    mine = stat_ref[device]
    others = [(stat_ref[my_owner], 1 + my_slot), (stat_ref[first], 0), (stat_ref[second], 0)]
    for k in range(3):
        other, segment = others[k]
        top0, sum0 = column(mine[0:1], k), column(mine[1:2], k)
        top1, sum1 = column(other[0:1], segment), column(other[1:2], segment)
        top = jnp.maximum(top0, top1)
        total = sum0 * jnp.exp(top0 - top) + sum1 * jnp.exp(top1 - top)
        scores = sp_ref[...] if k == 0 else sr_ref[k - 1]
        keys = keys_ref[:latent, :] if k == 0 else resident_ref[k - 1, :latent, :]
        weights = jnp.exp(scores - top).astype(BF16)
        part = dot(weights, keys, ((1,), (1,))) / total
        for h in range(heads):
            for c in range(latent // LANES):
                at = c * PART + 2 * k
                out_ref[h, at : at + 2, :] = part[2 * h : 2 * h + 2, c * LANES : (c + 1) * LANES]


def stack_kernel(after_ref, uv_hbm, other_uv_hbm, wo_hbm, other_hbm, uv_ref, out_ref, sems):
    rows = wo_hbm.shape[1]
    cols = out_ref.shape[1]
    copies = [
        pltpu.make_async_copy(uv_hbm.at[0], uv_ref.at[0], sems.at[4]),
        pltpu.make_async_copy(other_uv_hbm.at[0], uv_ref.at[1], sems.at[5]),
    ]
    for copy in copies:
        copy.start()
    for half in range(2):
        for n, ref in enumerate((wo_hbm, other_hbm)):
            at = 2 * half + n
            copies.append(
                pltpu.make_async_copy(
                    ref.at[0, :, pl.ds(half * cols, cols)], out_ref.at[pl.ds(at * rows, rows), :], sems.at[at]
                )
            )
            copies[-1].start()
    for copy in copies:
        copy.wait()


def project_kernel(owners_ref, part_ref, uv_ref, wo_ref, out_ref):
    count, each, lanes = part_ref.shape
    seqs = owners_ref.shape[1]
    cuts = each // PART
    rows = 2 * seqs
    core = lax.axis_index("seq") % 2
    owners = owners_ref[...]
    row = iota((cuts * 2 * rows, 1), 0)
    cut, other, seq = row // (2 * rows), row % (2 * rows) // rows, row % rows // 2
    head = jnp.where(other == 0, core, 1 - core)
    owner = column_of(owners, seq)
    slot = column_of(slots_of(owners), seq)
    first = seq * each + cut * PART + head
    second = owner * each + cut * PART + 2 + 2 * slot + head
    at = iota((cuts * 2 * rows, count * each), 1)
    hit = jnp.where((at == first) | (at == second), 1.0, 0.0).astype(BF16)
    rest = part_ref[...].reshape(count * each, lanes)
    latent = None
    for _ in range(3):
        piece = rest.astype(BF16)
        rest = rest - piece.astype(F32)
        one = dot(hit, piece)
        latent = one if latent is None else latent + one
    latent = latent.astype(BF16)
    latent = jnp.concatenate(
        [latent[c * 2 * rows : (c + 1) * 2 * rows] for c in range(cuts)], axis=1
    )
    head_out = jnp.concatenate(
        [dot(latent[:rows], uv_ref[0]), dot(latent[rows:], uv_ref[1])], axis=1
    )
    half = iota(head_out.shape, 0) % 2
    split = jnp.concatenate(
        [jnp.where(half == 0, head_out, 0.0), jnp.where(half == 1, head_out, 0.0)], axis=1
    )
    product = dot(split.astype(BF16), wo_ref[...])
    top = jnp.max(jnp.abs(product), axis=1, keepdims=True)
    power = jnp.clip(jnp.floor(jnp.log2(jnp.maximum(top, 1e-35))) + 1.0, -100.0, 100.0)
    coded = jnp.round(product * jnp.exp2(BITS - power)).astype(I32).astype(I16)
    power = jnp.broadcast_to(power, (rows, LANES)).astype(I32).astype(I16)
    cols = product.shape[1]
    for s in range(seqs):
        out_ref[s, :, :cols] = coded[2 * s : 2 * s + 2]
        out_ref[s, :, cols:] = power[2 * s : 2 * s + 2]


def final_kernel(in_ref, out_ref):
    cols = out_ref.shape[2] // 2
    for t in range(2):
        total = None
        for n in range(t, in_ref.shape[0], 2):
            power = in_ref[n, :, cols : cols + 1].astype(I32).astype(F32)
            one = in_ref[n, :, :cols].astype(I32).astype(F32) * jnp.exp2(power - BITS)
            total = one if total is None else total + one
        for j in range(2):
            out_ref[0, t : t + 1, j * cols : (j + 1) * cols] = total[j : j + 1].astype(BF16)


def swap(x):
    return lax.all_to_all(x, "seq", split_axis=0, concat_axis=0, tiled=True)


def trade(x, step):
    count = lax.axis_size("seq")
    return lax.ppermute(x, "seq", [(d, d ^ step) for d in range(count)])


def call(kernel, shapes, specs, scratch=(), cost=None, room=None):
    single = not isinstance(shapes, (list, tuple))
    if room is None:
        room = 16 if lax.axis_size("seq") <= 32 else 56
    return pl.pallas_call(
        kernel,
        out_shape=shapes,
        in_specs=specs,
        out_specs=VMEM if single else [VMEM] * len(shapes),
        scratch_shapes=list(scratch),
        cost_estimate=cost,
        compiler_params=pltpu.CompilerParams(vmem_limit_bytes=room * 1024 * 1024),
    )


def on_device(prompt_raw, lengths, owners, resident, new_raw, queries, kv_gain, w_uk, w_uv, w_o):
    count = lax.axis_size("seq")
    seqs = lengths.shape[0]
    most, width = prompt_raw.shape[1:]
    latent = kv_gain.shape[0]
    res_rows = resident.shape[1]
    nope = w_uk.shape[1]
    rope = width - latent
    heads = count
    out_width = w_o.shape[2]
    scale = 1.0 / queries.shape[-1] ** 0.5
    owners_row, lengths_row = owners.reshape(1, seqs), lengths.reshape(1, seqs)
    prompt_raw = prompt_raw.transpose(0, 2, 1)
    resident = resident.transpose(0, 2, 1)
    queries = queries.transpose(0, 2, 1, 3)
    keys_rows = most + LANES

    aux_width = -(-width // LANES) * LANES
    query, aux = call(
        functools.partial(query_kernel, res_rows),
        [
            jax.ShapeDtypeStruct((count, PACK, latent // 2), BF16),
            jax.ShapeDtypeStruct((8, aux_width), F32),
        ],
        [HBM] * 6,
        [
            pltpu.VMEM((1, seqs), I32),
            pltpu.VMEM((1, seqs), I32),
            pltpu.VMEM(queries.shape, BF16),
            pltpu.VMEM((nope, latent), BF16),
            pltpu.VMEM((2, width), BF16),
            pltpu.VMEM((latent,), BF16),
            pltpu.VMEM((2 * seqs, -(-(nope + rope) // LANES) * LANES), F32),
            pltpu.SemaphoreType.DMA((6,)),
        ],
        room=60,
    )(owners_row, lengths_row, queries, w_uk[0], new_raw, kv_gain)
    received = swap(query)
    query, w_uv, w_o = lax.optimization_barrier((query, w_uv, w_o))
    other_uv, other_wo = trade(w_uv, 1), trade(w_o, 1)
    keys, seen, resident = call(
        functools.partial(compress_kernel, res_rows, latent),
        [
            jax.ShapeDtypeStruct((width, keys_rows), BF16),
            jax.ShapeDtypeStruct((8, keys_rows), F32),
            jax.ShapeDtypeStruct(resident.shape, BF16),
        ],
        [VMEM] * 2 + [HBM],
        [pltpu.SemaphoreType.DMA],
        cost=pl.CostEstimate(flops=10**7, bytes_accessed=10**7, transcendentals=10**5),
    )(aux, prompt_raw, resident)
    lanes = -(-6 * heads // LANES) * LANES
    scores_p, scores_r, stat = call(
        functools.partial(score_kernel, scale),
        [
            jax.ShapeDtypeStruct((2 * heads, keys_rows), F32),
            jax.ShapeDtypeStruct((2, 2 * heads, res_rows), F32),
            jax.ShapeDtypeStruct((count, 2, lanes), F32),
        ],
        [VMEM] * 4,
    )(received, keys, seen, resident)
    stats = swap(stat)
    part, mark = call(
        attend_kernel,
        [
            jax.ShapeDtypeStruct((heads, PART * (latent // LANES), LANES), F32),
            jax.ShapeDtypeStruct((8, LANES), F32),
        ],
        [SMEM] + [VMEM] * 5,
    )(owners, stats, scores_p, scores_r, keys, resident)
    parts = swap(part)
    half = out_width // 2
    both_uv, both_wo = call(
        stack_kernel,
        [
            jax.ShapeDtypeStruct((2,) + w_uv.shape[1:], BF16),
            jax.ShapeDtypeStruct((4 * w_o.shape[1], half), BF16),
        ],
        [VMEM] + [HBM] * 4,
        [pltpu.SemaphoreType.DMA((6,))],
    )(mark, w_uv, other_uv, w_o, other_wo)
    sums = call(
        project_kernel, jax.ShapeDtypeStruct((seqs, 2, half + LANES), I16), [VMEM] * 4
    )(owners_row, parts, both_uv, both_wo)
    return call(final_kernel, jax.ShapeDtypeStruct((1, 2, out_width), BF16), [VMEM])(swap(sums))


def solution(mesh):
    in_specs = (
        P(("group", "seq"), None, None),
        P("group"),
        P("group"),
        P(("group", "seq"), None, None),
        P("group", None, None),
        P("group", None, "seq", None),
        P(),
        P("seq", None, None),
        P("seq", None, None),
        P("seq", None, None),
    )
    out_specs = P(("group", "seq"), None, None)
    return jax.shard_map(
        on_device, mesh=mesh, in_specs=in_specs, out_specs=out_specs, check_vma=False
    )
```

```python
import functools

import jax
import jax.numpy as jnp
import numpy as np
from jax import lax
from jax.experimental import pallas as pl
from jax.experimental.pallas import tpu as pltpu
from jax.sharding import PartitionSpec as P

F32 = jnp.float32
BF16 = jnp.bfloat16
I32 = jnp.int32
I16 = jnp.int16
VMEM = pl.BlockSpec(memory_space=pltpu.VMEM)
SMEM = pl.BlockSpec(memory_space=pltpu.SMEM)
HBM = pl.BlockSpec(memory_space=pltpu.HBM)
LANES = 128
PACK = 16
PART = 6
BITS = 14.0
NEAR = 4


def iota(shape, dim):
    return lax.broadcasted_iota(I32, shape, dim)


def dot(a, b, dims=((1,), (0,))):
    return lax.dot_general(a, b, (dims, ((), ())), preferred_element_type=F32)


def column_of(row, picks):
    n, width = picks.shape[0], row.shape[1]
    hit = iota((n, width), 1) == picks
    return jnp.sum(jnp.where(hit, row, 0), axis=1, keepdims=True)


def slots_of(owners_row):
    seqs = owners_row.shape[1]
    owners_col = column_of(owners_row, iota((seqs, 1), 0))
    earlier = iota((seqs, seqs), 0) < iota((seqs, seqs), 1)
    same = (owners_col == owners_row) & earlier
    return jnp.sum(jnp.where(same, 1, 0), axis=0, keepdims=True)


def doubled(row):
    seqs = row.shape[1]
    col = column_of(row, iota((seqs, 1), 0))
    hit = iota((seqs, 2 * seqs), 1) // 2 == iota((seqs, 2 * seqs), 0)
    return jnp.sum(jnp.where(hit, col, 0), axis=0, keepdims=True)


def frequencies(half, shape, dim):
    at = iota(shape, dim) % half
    values = np.float32(10000.0) ** (-(np.arange(half, dtype=np.float32) * np.float32(2.0)) / np.float32(2 * half))
    result = jnp.zeros(shape, F32)
    for i in range(half):
        result = jnp.where(at == i, float(values[i]), result)
    return result


def query_kernel(
    res_rows,
    owners_hbm,
    lengths_hbm,
    queries_hbm,
    uk_hbm,
    new_hbm,
    gain_hbm,
    out_ref,
    aux_ref,
    owners_ref,
    lengths_ref,
    queries_ref,
    uk_ref,
    new_ref,
    gain_ref,
    flat,
    sems,
):
    device = lax.axis_index("seq")
    copies = []
    pairs = [
        (owners_hbm, owners_ref),
        (lengths_hbm, lengths_ref),
        (queries_hbm, queries_ref),
        (uk_hbm, uk_ref),
        (new_hbm.at[device], new_ref),
        (gain_hbm, gain_ref),
    ]
    for n, (source, target) in enumerate(pairs):
        copies.append(pltpu.make_async_copy(source, target, sems.at[n]))
        copies[-1].start()
    for copy in copies:
        copy.wait()
    seqs = owners_ref.shape[1]
    nope, latent = uk_ref.shape
    rope = queries_ref.shape[3] - nope
    half = latent // 2
    rows = 2 * seqs
    for s in range(seqs):
        flat[2 * s : 2 * s + 2, : nope + rope] = queries_ref[s, 0].astype(F32)
    values = flat[:, : nope + rope]
    absorbed = dot(values[:, :nope].astype(BF16), uk_ref[...]).astype(BF16)
    row = iota((rows, 1), 0)
    lengths = column_of(lengths_ref[...], row // 2)
    angle = (res_rows + lengths + row % 2).astype(F32) * frequencies(rope // 2, (1, rope), 1)
    x = values[:, nope:]
    swapped = jnp.concatenate([x[:, rope // 2 :], x[:, : rope // 2]], axis=1)
    sine = jnp.sin(angle)
    sine = jnp.where(iota(x.shape, 1) < rope // 2, -sine, sine)
    turned = x * jnp.cos(angle) + swapped * sine
    zero = jnp.zeros((rows, rope), F32)
    pieces = [absorbed[:, :half], absorbed[:, half:]]
    for k in range(3):
        blocks = [turned if j == k else zero for j in range(half // rope)]
        pieces.append(jnp.concatenate(blocks, axis=1).astype(BF16))
    owners = owners_ref[...]
    owner = doubled(owners)
    slot = doubled(slots_of(owners))
    count = out_ref.shape[0]
    total = count * PACK
    shape = (total, rows)
    dest, r = iota(shape, 0) // PACK, iota(shape, 0) % PACK
    seq, tok = iota(shape, 1) // 2, iota(shape, 1) % 2
    here = jnp.where(owner == dest, slot + 1, -1)
    result = None
    for p in range(2):
        q = r - PART * p
        wanted = ((q // 2 == 0) & (seq == dest)) | (here == q // 2)
        hit = (q >= 0) & (q < PART) & (tok == q % 2) & wanted
        one = dot(jnp.where(hit, 1.0, 0.0).astype(BF16), pieces[p])
        result = one if result is None else result + one
    for k in range(3):
        match = (seq == dest) if k == 0 else (here == k)
        hit = (r == 2 * PART + tok) & match
        result = result + dot(jnp.where(hit, 1.0, 0.0).astype(BF16), pieces[2 + k])
    out_ref[...] = result.astype(BF16).reshape(out_ref.shape)
    width = new_ref.shape[1]
    aux_ref[0:2, :width] = new_ref[...].astype(F32)
    mine = jnp.where(iota(lengths_ref.shape, 1) == device, lengths_ref[...], 0)
    mine = jnp.sum(mine, axis=1, keepdims=True).astype(F32)
    aux_ref[2:3, :] = jnp.broadcast_to(mine, (1, aux_ref.shape[1]))
    aux_ref[3:4, :latent] = gain_ref[...].astype(F32).reshape(1, latent)


def compress_kernel(
    res_rows, latent, aux_ref, prompt_ref, resident_hbm, out_ref, bias_ref, resident_ref, sem
):
    fetch = pltpu.make_async_copy(resident_hbm, resident_ref, sem)
    fetch.start()
    width, most = prompt_ref.shape[1:]
    half = (width - latent) // 2
    fresh = jnp.concatenate([aux_ref[0:2, :width], jnp.zeros((PACK - 2, width), F32)], axis=0)
    pick = jnp.where(iota((PACK, LANES), 0) == iota((PACK, LANES), 1), 1.0, 0.0).astype(BF16)
    fresh = dot(fresh.astype(BF16), pick, ((0,), (0,)))
    gain = jnp.broadcast_to(aux_ref[3:4, :latent], (PACK, latent))
    top = jnp.where(iota((PACK, LANES), 0) == 0, 1.0, 0.0).astype(BF16)
    gain = dot(gain.astype(BF16), top, ((0,), (0,)))
    length = aux_ref[2:3, :LANES].astype(I32)
    at = iota(bias_ref.shape, 1)
    token = iota(bias_ref.shape, 0)
    length_all = jnp.concatenate([length] * (bias_ref.shape[1] // LANES), axis=1)
    seen = (at < length_all) | ((at >= most) & (at <= most + token))
    bias_ref[...] = jnp.where(seen, 1.0, 0.0)
    freq = frequencies(half, (half, 1), 0)
    for i in range(most // LANES + 1):
        at = slice(i * LANES, (i + 1) * LANES)
        lane = iota((1, LANES), 1)
        if i * LANES < most:
            raw = prompt_ref[0, :, at].astype(F32)
            position = res_rows + i * LANES + lane
        else:
            raw = fresh
            position = res_rows + length + lane
        lat = raw[:latent]
        meansq = jnp.sum(lat * lat, axis=0, keepdims=True) * (1.0 / latent)
        out_ref[:latent, at] = (lat * lax.rsqrt(meansq + 1e-06) * gain).astype(BF16)
        angle = position.astype(F32) * freq
        cosine, sine = jnp.cos(angle), jnp.sin(angle)
        x1, x2 = raw[latent : latent + half], raw[latent + half :]
        out_ref[latent : latent + half, at] = (x1 * cosine - x2 * sine).astype(BF16)
        out_ref[latent + half :, at] = (x2 * cosine + x1 * sine).astype(BF16)
    fetch.wait()


def score_kernel(scale, q_ref, keys_ref, seen_ref, resident_ref, sp_ref, sr_ref, stat_ref):
    heads = q_ref.shape[0]
    half = q_ref.shape[2]
    width = keys_ref.shape[0]
    rope = width - 2 * half
    rows = 2 * heads
    total = heads * PACK
    flat = q_ref[...].reshape(total, half)
    shape = (rows, total)
    head, tok = iota(shape, 0) // 4 * 2 + iota(shape, 0) % 2, iota(shape, 0) // 2 % 2
    source = iota(shape, 1) - head * PACK

    def picked(r):
        hit = source == r + tok
        return dot(jnp.where(hit, 1.0, 0.0).astype(BF16), flat)

    turned = picked(2 * PART)
    tops, sums = [], []
    for k in range(3):
        query = jnp.concatenate(
            [picked(2 * k), picked(PART + 2 * k), turned[:, k * rope : (k + 1) * rope]], axis=1
        ).astype(BF16)
        keys = keys_ref[...] if k == 0 else resident_ref[k - 1]
        scores = dot(query, keys) * scale
        if k == 0:
            first, second = seen_ref[0:1, :] > 0.5, seen_ref[1:2, :] > 0.5
            token = iota(scores.shape, 0) // 2 % 2
            seen = (first & (token == 0)) | (second & (token == 1))
            scores = jnp.where(seen, scores, -1e30)
            sp_ref[...] = scores
        else:
            sr_ref[k - 1] = scores
        top = jnp.max(scores, axis=1, keepdims=True)
        tops.append(top)
        sums.append(jnp.sum(jnp.exp(scores - top), axis=1, keepdims=True))
    lanes = stat_ref.shape[2]
    here = iota((3 * rows, lanes), 0) == iota((3 * rows, lanes), 1)
    top = jnp.sum(jnp.where(here, jnp.concatenate(tops, axis=0), 0.0), axis=0, keepdims=True)
    total = jnp.sum(jnp.where(here, jnp.concatenate(sums, axis=0), 0.0), axis=0, keepdims=True)
    both = jnp.concatenate([top, total], axis=0)
    stat_ref[...] = jnp.broadcast_to(both[None], stat_ref.shape)


def attend_kernel(owners_ref, stat_ref, sp_ref, sr_ref, keys_ref, resident_ref, out_ref):
    heads = out_ref.shape[0]
    latent = out_ref.shape[1] // PART * LANES
    seqs = owners_ref.shape[0]
    rows = 2 * heads
    device = lax.axis_index("seq")
    lanes = stat_ref.shape[2]
    my_owner = owners_ref[device]
    my_slot = jnp.int32(0)
    seen = jnp.int32(0)
    first = jnp.int32(0)
    second = jnp.int32(0)
    for s in range(seqs):
        owner = owners_ref[s]
        my_slot = my_slot + jnp.where((owner == my_owner) & (s < device), 1, 0)
        mine = owner == device
        first = jnp.where(mine & (seen == 0), s, first)
        second = jnp.where(mine & (seen == 1), s, second)
        seen = seen + jnp.where(mine, 1, 0)

    def column(row, segment):
        picks = iota((rows, 1), 0) + segment * rows
        hit = iota((rows, lanes), 1) == picks
        return jnp.sum(jnp.where(hit, row, 0.0), axis=1, keepdims=True)

    mine = stat_ref[device]
    others = [(stat_ref[my_owner], 1 + my_slot), (stat_ref[first], 0), (stat_ref[second], 0)]
    for k in range(3):
        other, segment = others[k]
        top0, sum0 = column(mine[0:1], k), column(mine[1:2], k)
        top1, sum1 = column(other[0:1], segment), column(other[1:2], segment)
        top = jnp.maximum(top0, top1)
        total = sum0 * jnp.exp(top0 - top) + sum1 * jnp.exp(top1 - top)
        scores = sp_ref[...] if k == 0 else sr_ref[k - 1]
        keys = keys_ref[:latent, :] if k == 0 else resident_ref[k - 1, :latent, :]
        weights = jnp.exp(scores - top).astype(BF16)
        part = dot(weights, keys, ((1,), (1,))) / total
        for h in range(heads):
            for c in range(latent // LANES):
                at = c * PART + 2 * k
                out_ref[h, at : at + 2, :] = part[2 * h : 2 * h + 2, c * LANES : (c + 1) * LANES]


def project_kernel(owners_ref, part_ref, uv_ref, other_uv_ref, wo_ref, other_wo_ref, out_ref):
    count, each, lanes = part_ref.shape
    seqs = owners_ref.shape[1]
    cuts = each // PART
    rows = 2 * seqs
    core = lax.axis_index("seq") % 2
    owners = owners_ref[...]
    row = iota((cuts * 2 * rows, 1), 0)
    cut, other, seq = row // (2 * rows), row % (2 * rows) // rows, row % rows // 2
    head = jnp.where(other == 0, core, 1 - core)
    owner = column_of(owners, seq)
    slot = column_of(slots_of(owners), seq)
    first = seq * each + cut * PART + head
    second = owner * each + cut * PART + 2 + 2 * slot + head
    at = iota((cuts * 2 * rows, count * each), 1)
    hit = jnp.where((at == first) | (at == second), 1.0, 0.0).astype(BF16)
    rest = part_ref[...].reshape(count * each, lanes)
    latent = None
    for _ in range(3):
        piece = rest.astype(BF16)
        rest = rest - piece.astype(F32)
        one = dot(hit, piece)
        latent = one if latent is None else latent + one
    latent = latent.astype(BF16)
    latent = jnp.concatenate(
        [latent[c * 2 * rows : (c + 1) * 2 * rows] for c in range(cuts)], axis=1
    )
    half = iota((rows, 1), 0) % 2
    cols = wo_ref.shape[2] // 2
    product = None
    for n, (uv, wo) in enumerate(((uv_ref, wo_ref), (other_uv_ref, other_wo_ref))):
        head_out = dot(latent[n * rows : (n + 1) * rows], uv[0])
        for side in range(2):
            lines = jnp.where(half == side, head_out, 0.0).astype(BF16)
            one = dot(lines, wo[0, :, side * cols : (side + 1) * cols])
            product = one if product is None else product + one
    top = jnp.max(jnp.abs(product), axis=1, keepdims=True)
    power = jnp.clip(jnp.floor(jnp.log2(jnp.maximum(top, 1e-35))) + 1.0, -100.0, 100.0)
    coded = jnp.round(product * jnp.exp2(BITS - power)).astype(I32).astype(I16)
    power = jnp.broadcast_to(power, (rows, LANES)).astype(I32).astype(I16)
    for s in range(seqs):
        out_ref[s, :, :cols] = coded[2 * s : 2 * s + 2]
        out_ref[s, :, cols:] = power[2 * s : 2 * s + 2]


def final_kernel(in_ref, out_ref):
    cols = out_ref.shape[2] // 2
    for t in range(2):
        total = None
        for n in range(t, in_ref.shape[0], 2):
            power = in_ref[n, :, cols : cols + 1].astype(I32).astype(F32)
            one = in_ref[n, :, :cols].astype(I32).astype(F32) * jnp.exp2(power - BITS)
            total = one if total is None else total + one
        for j in range(2):
            out_ref[0, t : t + 1, j * cols : (j + 1) * cols] = total[j : j + 1].astype(BF16)


def swap(x):
    return lax.all_to_all(x, "seq", split_axis=0, concat_axis=0, tiled=True)


def trade(x, step):
    count = lax.axis_size("seq")
    return lax.ppermute(x, "seq", [(d, d ^ step) for d in range(count)])


def call(kernel, shapes, specs, scratch=(), cost=None, room=None):
    single = not isinstance(shapes, (list, tuple))
    if room is None:
        room = 16 if lax.axis_size("seq") <= 32 else 56
    return pl.pallas_call(
        kernel,
        out_shape=shapes,
        in_specs=specs,
        out_specs=VMEM if single else [VMEM] * len(shapes),
        scratch_shapes=list(scratch),
        cost_estimate=cost,
        compiler_params=pltpu.CompilerParams(vmem_limit_bytes=room * 1024 * 1024),
    )


def on_device(prompt_raw, lengths, owners, resident, new_raw, queries, kv_gain, w_uk, w_uv, w_o):
    count = lax.axis_size("seq")
    seqs = lengths.shape[0]
    most, width = prompt_raw.shape[1:]
    latent = kv_gain.shape[0]
    res_rows = resident.shape[1]
    nope = w_uk.shape[1]
    rope = width - latent
    heads = count
    out_width = w_o.shape[2]
    scale = 1.0 / queries.shape[-1] ** 0.5
    owners_row, lengths_row = owners.reshape(1, seqs), lengths.reshape(1, seqs)
    prompt_raw = prompt_raw.transpose(0, 2, 1)
    resident = resident.transpose(0, 2, 1)
    queries = queries.transpose(0, 2, 1, 3)
    keys_rows = most + LANES

    aux_width = -(-width // LANES) * LANES
    query, aux = call(
        functools.partial(query_kernel, res_rows),
        [
            jax.ShapeDtypeStruct((count, PACK, latent // 2), BF16),
            jax.ShapeDtypeStruct((8, aux_width), F32),
        ],
        [HBM] * 6,
        [
            pltpu.VMEM((1, seqs), I32),
            pltpu.VMEM((1, seqs), I32),
            pltpu.VMEM(queries.shape, BF16),
            pltpu.VMEM((nope, latent), BF16),
            pltpu.VMEM((2, width), BF16),
            pltpu.VMEM((latent,), BF16),
            pltpu.VMEM((2 * seqs, -(-(nope + rope) // LANES) * LANES), F32),
            pltpu.SemaphoreType.DMA((6,)),
        ],
        room=60,
    )(owners_row, lengths_row, queries, w_uk[0], new_raw, kv_gain)
    received = swap(query)
    query, w_uv, w_o = lax.optimization_barrier((query, w_uv, w_o))
    other_uv, other_wo = trade(w_uv, 1), trade(w_o, 1)
    keys, seen, resident = call(
        functools.partial(compress_kernel, res_rows, latent),
        [
            jax.ShapeDtypeStruct((width, keys_rows), BF16),
            jax.ShapeDtypeStruct((8, keys_rows), F32),
            jax.ShapeDtypeStruct(resident.shape, BF16),
        ],
        [VMEM] * 2 + [HBM],
        [pltpu.SemaphoreType.DMA],
        cost=pl.CostEstimate(flops=10**7, bytes_accessed=10**7, transcendentals=10**5),
    )(aux, prompt_raw, resident)
    lanes = -(-6 * heads // LANES) * LANES
    scores_p, scores_r, stat = call(
        functools.partial(score_kernel, scale),
        [
            jax.ShapeDtypeStruct((2 * heads, keys_rows), F32),
            jax.ShapeDtypeStruct((2, 2 * heads, res_rows), F32),
            jax.ShapeDtypeStruct((count, 2, lanes), F32),
        ],
        [VMEM] * 4,
    )(received, keys, seen, resident)
    stat, other_uv, other_wo = lax.optimization_barrier((stat, other_uv, other_wo))
    stats = swap(stat)
    part = call(
        attend_kernel,
        jax.ShapeDtypeStruct((heads, PART * (latent // LANES), LANES), F32),
        [SMEM] + [VMEM] * 5,
    )(owners, stats, scores_p, scores_r, keys, resident)
    parts = swap(part)
    half = out_width // 2
    sums = call(
        project_kernel, jax.ShapeDtypeStruct((seqs, 2, half + LANES), I16), [VMEM] * 6
    )(owners_row, parts, w_uv, other_uv, w_o, other_wo)
    return call(final_kernel, jax.ShapeDtypeStruct((1, 2, out_width), BF16), [VMEM])(swap(sums))


def solution(mesh):
    in_specs = (
        P(("group", "seq"), None, None),
        P("group"),
        P("group"),
        P(("group", "seq"), None, None),
        P("group", None, None),
        P("group", None, "seq", None),
        P(),
        P("seq", None, None),
        P("seq", None, None),
        P("seq", None, None),
    )
    out_specs = P(("group", "seq"), None, None)
    return jax.shard_map(
        on_device, mesh=mesh, in_specs=in_specs, out_specs=out_specs, check_vma=False
    )
```

```python
import functools

import jax
import jax.numpy as jnp
import numpy as np
from jax import lax
from jax.experimental import pallas as pl
from jax.experimental.pallas import tpu as pltpu
from jax.sharding import PartitionSpec as P

F32 = jnp.float32
BF16 = jnp.bfloat16
I32 = jnp.int32
I16 = jnp.int16
VMEM = pl.BlockSpec(memory_space=pltpu.VMEM)
SMEM = pl.BlockSpec(memory_space=pltpu.SMEM)
HBM = pl.BlockSpec(memory_space=pltpu.HBM)
LANES = 128
PACK = 16
PART = 6
BITS = 14.0
NEAR = 4


def iota(shape, dim):
    return lax.broadcasted_iota(I32, shape, dim)


def over(x, n):
    return x >> (n.bit_length() - 1)


def rest_of(x, n):
    return x & (n - 1)


def dot(a, b, dims=((1,), (0,))):
    return lax.dot_general(a, b, (dims, ((), ())), preferred_element_type=F32)


def column_of(row, picks):
    n, width = picks.shape[0], row.shape[1]
    hit = iota((n, width), 1) == picks
    return jnp.sum(jnp.where(hit, row, 0), axis=1, keepdims=True)


def slots_of(owners_row):
    seqs = owners_row.shape[1]
    owners_col = column_of(owners_row, iota((seqs, 1), 0))
    earlier = iota((seqs, seqs), 0) < iota((seqs, seqs), 1)
    same = (owners_col == owners_row) & earlier
    return jnp.sum(jnp.where(same, 1, 0), axis=0, keepdims=True)


def doubled(row, times):
    seqs = row.shape[1]
    col = column_of(row, iota((seqs, 1), 0))
    shape = (seqs, 2 * seqs * times)
    hit = over(rest_of(iota(shape, 1), 2 * seqs), 2) == iota(shape, 0)
    return jnp.sum(jnp.where(hit, col, 0), axis=0, keepdims=True)


def frequencies(half, shape, dim):
    at = rest_of(iota(shape, dim), half)
    values = np.float32(10000.0) ** (-(np.arange(half, dtype=np.float32) * np.float32(2.0)) / np.float32(2 * half))
    result = jnp.zeros(shape, F32)
    for i in range(half):
        result = jnp.where(at == i, float(values[i]), result)
    return result


def query_kernel(
    res_rows,
    owners_hbm,
    lengths_hbm,
    queries_hbm,
    uk_hbm,
    new_hbm,
    gain_hbm,
    out_ref,
    aux_ref,
    owners_ref,
    lengths_ref,
    queries_ref,
    uk_ref,
    new_ref,
    gain_ref,
    flat,
    sems,
):
    device = lax.axis_index("seq")
    copies = []
    pairs = [
        (owners_hbm, owners_ref),
        (lengths_hbm, lengths_ref),
        (queries_hbm, queries_ref),
        (uk_hbm, uk_ref),
        (new_hbm.at[device], new_ref),
        (gain_hbm, gain_ref),
    ]
    for n, (source, target) in enumerate(pairs):
        copies.append(pltpu.make_async_copy(source, target, sems.at[n]))
        copies[-1].start()
    for copy in copies:
        copy.wait()
    seqs = owners_ref.shape[1]
    nope, latent = uk_ref.shape
    rope = queries_ref.shape[3] - nope
    half = latent // 2
    rows = 2 * seqs
    for s in range(seqs):
        flat[2 * s : 2 * s + 2, : nope + rope] = queries_ref[s, 0].astype(F32)
    values = flat[:, : nope + rope]
    absorbed = dot(values[:, :nope].astype(BF16), uk_ref[...]).astype(BF16)
    row = iota((rows, 1), 0)
    lengths = column_of(lengths_ref[...], over(row, 2))
    angle = (res_rows + lengths + rest_of(row, 2)).astype(F32) * frequencies(rope // 2, (1, rope), 1)
    x = values[:, nope:]
    swapped = jnp.concatenate([x[:, rope // 2 :], x[:, : rope // 2]], axis=1)
    sine = jnp.sin(angle)
    sine = jnp.where(iota(x.shape, 1) < rope // 2, -sine, sine)
    turned = x * jnp.cos(angle) + swapped * sine
    zero = jnp.zeros((rows, rope), F32)
    pieces = [absorbed[:, :half], absorbed[:, half:]]
    for k in range(3):
        blocks = [turned if j == k else zero for j in range(half // rope)]
        pieces.append(jnp.concatenate(blocks, axis=1).astype(BF16))
    owners = owners_ref[...]
    owner = doubled(owners, 5)
    slot = doubled(slots_of(owners), 5)
    shape = (out_ref.shape[0] * PACK, 5 * rows)
    dest, r = over(iota(shape, 0), PACK), rest_of(iota(shape, 0), PACK)
    lane = iota((1, 5 * rows), 1)
    piece, seq, tok = over(lane, rows), over(rest_of(lane, rows), 2), rest_of(lane, 2)
    start = jnp.where(piece < 2, piece * PART, 2 * PART) + tok
    offset = r - start
    rotary = piece >= 2
    third = piece - 2
    here = jnp.where(owner == dest, slot + 1, jnp.where(seq == dest, 0, -1))
    both = (owner == dest) & (seq == dest)
    wide = (offset == 2 * here) | (both & (offset == 0))
    narrow = (offset == 0) & ((here == third) | (both & (third == 0)))
    hit = (~rotary & (here >= 0) & wide) | (rotary & narrow)
    pieces = jnp.concatenate(pieces, axis=0)
    result = dot(jnp.where(hit, 1.0, 0.0).astype(BF16), pieces)
    out_ref[...] = result.astype(BF16).reshape(out_ref.shape)
    width = new_ref.shape[1]
    aux_ref[0:2, :width] = new_ref[...].astype(F32)
    mine = jnp.where(iota(lengths_ref.shape, 1) == device, lengths_ref[...], 0)
    mine = jnp.sum(mine, axis=1, keepdims=True).astype(F32)
    aux_ref[2:3, :] = jnp.broadcast_to(mine, (1, aux_ref.shape[1]))
    aux_ref[3:4, :latent] = gain_ref[...].astype(F32).reshape(1, latent)


def compress_kernel(
    res_rows, latent, aux_ref, prompt_ref, resident_hbm, out_ref, bias_ref, resident_ref, sem
):
    fetch = pltpu.make_async_copy(resident_hbm, resident_ref, sem)
    fetch.start()
    width, most = prompt_ref.shape[1:]
    half = (width - latent) // 2
    fresh = jnp.concatenate([aux_ref[0:2, :width], jnp.zeros((PACK - 2, width), F32)], axis=0)
    pick = jnp.where(iota((PACK, LANES), 0) == iota((PACK, LANES), 1), 1.0, 0.0).astype(BF16)
    fresh = dot(fresh.astype(BF16), pick, ((0,), (0,)))
    gain = jnp.broadcast_to(aux_ref[3:4, :latent], (PACK, latent))
    top = jnp.where(iota((PACK, LANES), 0) == 0, 1.0, 0.0).astype(BF16)
    gain = dot(gain.astype(BF16), top, ((0,), (0,)))
    length = aux_ref[2:3, :LANES].astype(I32)
    at = iota(bias_ref.shape, 1)
    token = iota(bias_ref.shape, 0)
    length_all = jnp.concatenate([length] * (bias_ref.shape[1] // LANES), axis=1)
    seen = (at < length_all) | ((at >= most) & (at <= most + token))
    bias_ref[...] = jnp.where(seen, 1.0, 0.0)
    freq = frequencies(half, (half, 1), 0)
    for i in range(most // LANES + 1):
        at = slice(i * LANES, (i + 1) * LANES)
        lane = iota((1, LANES), 1)
        if i * LANES < most:
            raw = prompt_ref[0, :, at].astype(F32)
            position = res_rows + i * LANES + lane
        else:
            raw = fresh
            position = res_rows + length + lane
        lat = raw[:latent]
        meansq = jnp.sum(lat * lat, axis=0, keepdims=True) * (1.0 / latent)
        out_ref[:latent, at] = (lat * lax.rsqrt(meansq + 1e-06) * gain).astype(BF16)
        angle = position.astype(F32) * freq
        cosine, sine = jnp.cos(angle), jnp.sin(angle)
        x1, x2 = raw[latent : latent + half], raw[latent + half :]
        out_ref[latent : latent + half, at] = (x1 * cosine - x2 * sine).astype(BF16)
        out_ref[latent + half :, at] = (x2 * cosine + x1 * sine).astype(BF16)
    fetch.wait()


def score_kernel(scale, q_ref, keys_ref, seen_ref, resident_ref, sp_ref, sr_ref, stat_ref):
    heads = q_ref.shape[0]
    half = q_ref.shape[2]
    width = keys_ref.shape[0]
    rope = width - 2 * half
    rows = 2 * heads
    total = heads * PACK
    flat = q_ref[...].reshape(total, half)
    shape = (rows, total)
    line = iota(shape, 0)
    head, tok = over(line, 4) * 2 + rest_of(line, 2), rest_of(over(line, 2), 2)
    source = iota(shape, 1) - head * PACK

    def picked(r):
        hit = source == r + tok
        return dot(jnp.where(hit, 1.0, 0.0).astype(BF16), flat)

    turned = picked(2 * PART)
    tops, sums = [], []
    for k in range(3):
        query = jnp.concatenate(
            [picked(2 * k), picked(PART + 2 * k), turned[:, k * rope : (k + 1) * rope]], axis=1
        ).astype(BF16)
        keys = keys_ref[...] if k == 0 else resident_ref[k - 1]
        scores = dot(query, keys) * scale
        if k == 0:
            first, second = seen_ref[0:1, :] > 0.5, seen_ref[1:2, :] > 0.5
            token = rest_of(over(iota(scores.shape, 0), 2), 2)
            seen = (first & (token == 0)) | (second & (token == 1))
            scores = jnp.where(seen, scores, -1e30)
            sp_ref[...] = scores
        else:
            sr_ref[k - 1] = scores
        top = jnp.max(scores, axis=1, keepdims=True)
        tops.append(top)
        sums.append(jnp.sum(jnp.exp(scores - top), axis=1, keepdims=True))
    lanes = stat_ref.shape[2]
    here = iota((3 * rows, lanes), 0) == iota((3 * rows, lanes), 1)
    top = jnp.sum(jnp.where(here, jnp.concatenate(tops, axis=0), 0.0), axis=0, keepdims=True)
    total = jnp.sum(jnp.where(here, jnp.concatenate(sums, axis=0), 0.0), axis=0, keepdims=True)
    both = jnp.concatenate([top, total], axis=0)
    stat_ref[...] = jnp.broadcast_to(both[None], stat_ref.shape)


def attend_kernel(
    owners_ref, stat_ref, sp_ref, sr_ref, keys_ref, resident_ref, wo_hbm, out_ref, wo_ref, sems
):
    parts = sems.shape[0]
    span = wo_ref.shape[2] // parts
    fetches = []
    for n in range(parts):
        at = pl.ds(n * span, span)
        fetches.append(pltpu.make_async_copy(wo_hbm.at[:, :, at], wo_ref.at[:, :, at], sems.at[n]))
        fetches[-1].start()
    heads = out_ref.shape[0]
    latent = out_ref.shape[1] // PART * LANES
    seqs = owners_ref.shape[0]
    rows = 2 * heads
    device = lax.axis_index("seq")
    lanes = stat_ref.shape[2]
    my_owner = owners_ref[device]
    my_slot = jnp.int32(0)
    seen = jnp.int32(0)
    first = jnp.int32(0)
    second = jnp.int32(0)
    for s in range(seqs):
        owner = owners_ref[s]
        my_slot = my_slot + jnp.where((owner == my_owner) & (s < device), 1, 0)
        mine = owner == device
        first = jnp.where(mine & (seen == 0), s, first)
        second = jnp.where(mine & (seen == 1), s, second)
        seen = seen + jnp.where(mine, 1, 0)

    mine = stat_ref[device]
    place = over(iota((1, lanes), 1), rows)
    other = jnp.zeros((2, lanes), F32)
    pairs = [(stat_ref[my_owner], 1 + my_slot), (stat_ref[first], 0), (stat_ref[second], 0)]
    for k, (theirs, segment) in enumerate(pairs):
        moved = jnp.zeros((2, lanes), F32)
        for n in range(3):
            turned = pltpu.roll(theirs, ((k - n) * rows) % lanes, 1)
            moved = jnp.where(segment == n, turned, moved)
        other = jnp.where(place == k, moved, other)
    top = jnp.maximum(mine[0:1], other[0:1])
    total = mine[1:2] * jnp.exp(mine[0:1] - top) + other[1:2] * jnp.exp(other[0:1] - top)
    hit = iota((3 * rows, lanes), 1) == iota((3 * rows, lanes), 0)
    top = jnp.sum(jnp.where(hit, top, 0.0), axis=1, keepdims=True)
    total = jnp.sum(jnp.where(hit, total, 0.0), axis=1, keepdims=True)
    for k in range(3):
        at = slice(k * rows, (k + 1) * rows)
        scores = sp_ref[...] if k == 0 else sr_ref[k - 1]
        keys = keys_ref[:latent, :] if k == 0 else resident_ref[k - 1, :latent, :]
        weights = jnp.exp(scores - top[at]).astype(BF16)
        part = dot(weights, keys, ((1,), (1,))) / total[at]
        for h in range(heads):
            for c in range(latent // LANES):
                at = c * PART + 2 * k
                out_ref[h, at : at + 2, :] = part[2 * h : 2 * h + 2, c * LANES : (c + 1) * LANES]
    for fetch in fetches:
        fetch.wait()


def project_kernel(owners_ref, part_ref, uv_ref, other_uv_ref, wo_ref, other_wo_ref, out_ref):
    count, each, lanes = part_ref.shape
    seqs = owners_ref.shape[1]
    cuts = each // PART
    rows = 2 * seqs
    core = lax.axis_index("seq") % 2
    owners = owners_ref[...]
    row = iota((cuts * 2 * rows, 1), 0)
    cut, other, seq = over(row, 2 * rows), over(rest_of(row, 2 * rows), rows), over(rest_of(row, rows), 2)
    head = jnp.where(other == 0, core, 1 - core)
    owner = column_of(owners, seq)
    slot = column_of(slots_of(owners), seq)
    first = seq * each + cut * PART + head
    second = owner * each + cut * PART + 2 + 2 * slot + head
    at = iota((cuts * 2 * rows, count * each), 1)
    hit = jnp.where((at == first) | (at == second), 1.0, 0.0).astype(BF16)
    rest = part_ref[...].reshape(count * each, lanes)
    latent = None
    for _ in range(3):
        piece = rest.astype(BF16)
        rest = rest - piece.astype(F32)
        one = dot(hit, piece)
        latent = one if latent is None else latent + one
    latent = latent.astype(BF16)
    latent = jnp.concatenate(
        [latent[c * 2 * rows : (c + 1) * 2 * rows] for c in range(cuts)], axis=1
    )
    half = rest_of(iota((rows, 1), 0), 2)
    cols = wo_ref.shape[2] // 2
    product = None
    for n, (uv, wo) in enumerate(((uv_ref, wo_ref), (other_uv_ref, other_wo_ref))):
        head_out = dot(latent[n * rows : (n + 1) * rows], uv[0])
        for side in range(2):
            lines = jnp.where(half == side, head_out, 0.0).astype(BF16)
            one = dot(lines, wo[0, :, side * cols : (side + 1) * cols])
            product = one if product is None else product + one
    top = jnp.max(jnp.abs(product), axis=1, keepdims=True)
    power = jnp.clip(jnp.floor(jnp.log2(jnp.maximum(top, 1e-35))) + 1.0, -100.0, 100.0)
    coded = jnp.round(product * jnp.exp2(BITS - power)).astype(I32).astype(I16)
    power = jnp.broadcast_to(power, (rows, LANES)).astype(I32).astype(I16)
    for s in range(seqs):
        out_ref[s, :, :cols] = coded[2 * s : 2 * s + 2]
        out_ref[s, :, cols:] = power[2 * s : 2 * s + 2]


def final_kernel(in_ref, out_ref):
    cols = out_ref.shape[2] // 2
    for t in range(2):
        total = None
        for n in range(t, in_ref.shape[0], 2):
            power = in_ref[n, :, cols : cols + 1].astype(I32).astype(F32)
            one = in_ref[n, :, :cols].astype(I32).astype(F32) * jnp.exp2(power - BITS)
            total = one if total is None else total + one
        for j in range(2):
            out_ref[0, t : t + 1, j * cols : (j + 1) * cols] = total[j : j + 1].astype(BF16)


def swap(x):
    return lax.all_to_all(x, "seq", split_axis=0, concat_axis=0, tiled=True)


def trade(x, step):
    count = lax.axis_size("seq")
    return lax.ppermute(x, "seq", [(d, d ^ step) for d in range(count)])


def call(kernel, shapes, specs, scratch=(), cost=None, room=None):
    single = not isinstance(shapes, (list, tuple))
    if room is None:
        room = 16 if lax.axis_size("seq") <= 32 else 56
    return pl.pallas_call(
        kernel,
        out_shape=shapes,
        in_specs=specs,
        out_specs=VMEM if single else [VMEM] * len(shapes),
        scratch_shapes=list(scratch),
        cost_estimate=cost,
        compiler_params=pltpu.CompilerParams(vmem_limit_bytes=room * 1024 * 1024),
    )


def on_device(prompt_raw, lengths, owners, resident, new_raw, queries, kv_gain, w_uk, w_uv, w_o):
    count = lax.axis_size("seq")
    seqs = lengths.shape[0]
    most, width = prompt_raw.shape[1:]
    latent = kv_gain.shape[0]
    res_rows = resident.shape[1]
    nope = w_uk.shape[1]
    rope = width - latent
    heads = count
    out_width = w_o.shape[2]
    scale = 1.0 / queries.shape[-1] ** 0.5
    owners_row, lengths_row = owners.reshape(1, seqs), lengths.reshape(1, seqs)
    prompt_raw = prompt_raw.transpose(0, 2, 1)
    resident = resident.transpose(0, 2, 1)
    queries = queries.transpose(0, 2, 1, 3)
    keys_rows = most + LANES

    aux_width = -(-width // LANES) * LANES
    query, aux = call(
        functools.partial(query_kernel, res_rows),
        [
            jax.ShapeDtypeStruct((count, PACK, latent // 2), BF16),
            jax.ShapeDtypeStruct((8, aux_width), F32),
        ],
        [HBM] * 6,
        [
            pltpu.VMEM((1, seqs), I32),
            pltpu.VMEM((1, seqs), I32),
            pltpu.VMEM(queries.shape, BF16),
            pltpu.VMEM((nope, latent), BF16),
            pltpu.VMEM((2, width), BF16),
            pltpu.VMEM((latent,), BF16),
            pltpu.VMEM((2 * seqs, -(-(nope + rope) // LANES) * LANES), F32),
            pltpu.SemaphoreType.DMA((6,)),
        ],
        room=60,
    )(owners_row, lengths_row, queries, w_uk[0], new_raw, kv_gain)
    received = swap(query)
    query, w_uv, w_o = lax.optimization_barrier((query, w_uv, w_o))
    other_uv, other_wo = trade(w_uv, 1), trade(w_o, 1)
    keys, seen, resident = call(
        functools.partial(compress_kernel, res_rows, latent),
        [
            jax.ShapeDtypeStruct((width, keys_rows), BF16),
            jax.ShapeDtypeStruct((8, keys_rows), F32),
            jax.ShapeDtypeStruct(resident.shape, BF16),
        ],
        [VMEM] * 2 + [HBM],
        [pltpu.SemaphoreType.DMA],
        cost=pl.CostEstimate(flops=10**7, bytes_accessed=10**7, transcendentals=10**5),
    )(aux, prompt_raw, resident)
    lanes = -(-6 * heads // LANES) * LANES
    scores_p, scores_r, stat = call(
        functools.partial(score_kernel, scale),
        [
            jax.ShapeDtypeStruct((2 * heads, keys_rows), F32),
            jax.ShapeDtypeStruct((2, 2 * heads, res_rows), F32),
            jax.ShapeDtypeStruct((count, 2, lanes), F32),
        ],
        [VMEM] * 4,
    )(received, keys, seen, resident)
    stat, other_uv, other_wo = lax.optimization_barrier((stat, other_uv, other_wo))
    stats = swap(stat)
    part, other_wo = call(
        attend_kernel,
        [
            jax.ShapeDtypeStruct((heads, PART * (latent // LANES), LANES), F32),
            jax.ShapeDtypeStruct(other_wo.shape, BF16),
        ],
        [SMEM] + [VMEM] * 5 + [HBM],
        [pltpu.SemaphoreType.DMA((4,))],
    )(owners, stats, scores_p, scores_r, keys, resident, other_wo)
    parts = swap(part)
    half = out_width // 2
    sums = call(
        project_kernel, jax.ShapeDtypeStruct((seqs, 2, half + LANES), I16), [VMEM] * 6
    )(owners_row, parts, w_uv, other_uv, w_o, other_wo)
    return call(final_kernel, jax.ShapeDtypeStruct((1, 2, out_width), BF16), [VMEM])(swap(sums))


def solution(mesh):
    in_specs = (
        P(("group", "seq"), None, None),
        P("group"),
        P("group"),
        P(("group", "seq"), None, None),
        P("group", None, None),
        P("group", None, "seq", None),
        P(),
        P("seq", None, None),
        P("seq", None, None),
        P("seq", None, None),
    )
    out_specs = P(("group", "seq"), None, None)
    return jax.shard_map(
        on_device, mesh=mesh, in_specs=in_specs, out_specs=out_specs, check_vma=False
    )
```

```python
import functools

import jax
import jax.numpy as jnp
import numpy as np
from jax import lax
from jax.experimental import pallas as pl
from jax.experimental.pallas import tpu as pltpu
from jax.sharding import PartitionSpec as P

F32 = jnp.float32
BF16 = jnp.bfloat16
I32 = jnp.int32
I16 = jnp.int16
VMEM = pl.BlockSpec(memory_space=pltpu.VMEM)
SMEM = pl.BlockSpec(memory_space=pltpu.SMEM)
HBM = pl.BlockSpec(memory_space=pltpu.HBM)
LANES = 128
PACK = 16
PART = 6
BITS = 14.0
NEAR = 4


def iota(shape, dim):
    return lax.broadcasted_iota(I32, shape, dim)


def over(x, n):
    return x >> (n.bit_length() - 1)


def rest_of(x, n):
    return x & (n - 1)


def dot(a, b, dims=((1,), (0,))):
    return lax.dot_general(a, b, (dims, ((), ())), preferred_element_type=F32)


def column_of(row, picks):
    n, width = picks.shape[0], row.shape[1]
    hit = iota((n, width), 1) == picks
    return jnp.sum(jnp.where(hit, row, 0), axis=1, keepdims=True)


def slots_of(owners_row):
    seqs = owners_row.shape[1]
    owners_col = column_of(owners_row, iota((seqs, 1), 0))
    earlier = iota((seqs, seqs), 0) < iota((seqs, seqs), 1)
    same = (owners_col == owners_row) & earlier
    return jnp.sum(jnp.where(same, 1, 0), axis=0, keepdims=True)


def doubled(row, times):
    seqs = row.shape[1]
    col = column_of(row, iota((seqs, 1), 0))
    shape = (seqs, 2 * seqs * times)
    hit = over(rest_of(iota(shape, 1), 2 * seqs), 2) == iota(shape, 0)
    return jnp.sum(jnp.where(hit, col, 0), axis=0, keepdims=True)


def frequencies(half, shape, dim):
    at = rest_of(iota(shape, dim), half)
    values = np.float32(10000.0) ** (-(np.arange(half, dtype=np.float32) * np.float32(2.0)) / np.float32(2 * half))
    result = jnp.zeros(shape, F32)
    for i in range(half):
        result = jnp.where(at == i, float(values[i]), result)
    return result


def sine_cosine(angle):
    count = jnp.floor(angle * (2.0 / np.pi) + 0.5)
    x = ((angle - count * 1.5703125) - count * 4.837512969970703125e-4) - count * 7.54978995489188216e-8
    quarter = count.astype(I32)
    y = x * x
    sine = x + x * y * (-1.6666654611e-1 + y * (8.3321608736e-3 - y * 1.9515295891e-4))
    cosine = 1.0 - 0.5 * y + y * y * (4.166664568298827e-2 + y * (-1.388731625493765e-3 + y * 2.443315711809948e-5))
    odd = rest_of(quarter, 2) == 1
    first, second = jnp.where(odd, cosine, sine), jnp.where(odd, sine, cosine)
    first = jnp.where(rest_of(quarter, 4) >= 2, -first, first)
    second = jnp.where(rest_of(quarter + 1, 4) >= 2, -second, second)
    return first, second


def query_kernel(
    res_rows,
    owners_hbm,
    lengths_hbm,
    queries_hbm,
    uk_hbm,
    new_hbm,
    gain_hbm,
    out_ref,
    aux_ref,
    owners_ref,
    lengths_ref,
    queries_ref,
    uk_ref,
    new_ref,
    gain_ref,
    flat,
    sems,
):
    device = lax.axis_index("seq")
    copies = []
    pairs = [
        (owners_hbm, owners_ref),
        (lengths_hbm, lengths_ref),
        (queries_hbm, queries_ref),
        (uk_hbm, uk_ref),
        (new_hbm.at[device], new_ref),
        (gain_hbm, gain_ref),
    ]
    for n, (source, target) in enumerate(pairs):
        copies.append(pltpu.make_async_copy(source, target, sems.at[n]))
        copies[-1].start()
    for copy in copies:
        copy.wait()
    seqs = owners_ref.shape[1]
    nope, latent = uk_ref.shape
    rope = queries_ref.shape[3] - nope
    half = latent // 2
    rows = 2 * seqs
    for s in range(seqs):
        flat[2 * s : 2 * s + 2, : nope + rope] = queries_ref[s, 0].astype(F32)
    values = flat[:, : nope + rope]
    absorbed = dot(values[:, :nope].astype(BF16), uk_ref[...]).astype(BF16)
    row = iota((rows, 1), 0)
    lengths = column_of(lengths_ref[...], over(row, 2))
    angle = (res_rows + lengths + rest_of(row, 2)).astype(F32) * frequencies(rope // 2, (1, rope), 1)
    x = values[:, nope:]
    swapped = jnp.concatenate([x[:, rope // 2 :], x[:, : rope // 2]], axis=1)
    sine, cosine = sine_cosine(angle)
    sine = jnp.where(iota(x.shape, 1) < rope // 2, -sine, sine)
    turned = x * cosine + swapped * sine
    zero = jnp.zeros((rows, rope), F32)
    pieces = [absorbed[:, :half], absorbed[:, half:]]
    for k in range(3):
        blocks = [turned if j == k else zero for j in range(half // rope)]
        pieces.append(jnp.concatenate(blocks, axis=1).astype(BF16))
    owners = owners_ref[...]
    owner = doubled(owners, 5)
    slot = doubled(slots_of(owners), 5)
    shape = (out_ref.shape[0] * PACK, 5 * rows)
    dest, r = over(iota(shape, 0), PACK), rest_of(iota(shape, 0), PACK)
    lane = iota((1, 5 * rows), 1)
    piece, seq, tok = over(lane, rows), over(rest_of(lane, rows), 2), rest_of(lane, 2)
    start = jnp.where(piece < 2, piece * PART, 2 * PART) + tok
    offset = r - start
    rotary = piece >= 2
    third = piece - 2
    here = jnp.where(owner == dest, slot + 1, jnp.where(seq == dest, 0, -1))
    both = (owner == dest) & (seq == dest)
    wide = (offset == 2 * here) | (both & (offset == 0))
    narrow = (offset == 0) & ((here == third) | (both & (third == 0)))
    hit = (~rotary & (here >= 0) & wide) | (rotary & narrow)
    pieces = jnp.concatenate(pieces, axis=0)
    result = dot(jnp.where(hit, 1.0, 0.0).astype(BF16), pieces)
    out_ref[...] = result.astype(BF16).reshape(out_ref.shape)
    width = new_ref.shape[1]
    aux_ref[0:2, :width] = new_ref[...].astype(F32)
    mine = jnp.where(iota(lengths_ref.shape, 1) == device, lengths_ref[...], 0)
    mine = jnp.sum(mine, axis=1, keepdims=True).astype(F32)
    aux_ref[2:3, :] = jnp.broadcast_to(mine, (1, aux_ref.shape[1]))
    aux_ref[3:4, :latent] = gain_ref[...].astype(F32).reshape(1, latent)


def fetch_start(source, target, sems, first):
    span = target.shape[2] // sems.shape[0]
    copies = []
    for n in range(sems.shape[0]):
        copies.append(
            pltpu.make_async_copy(
                source.at[:, :, pl.ds(first + n * span, span)], target.at[:, :, pl.ds(n * span, span)], sems.at[n]
            )
        )
        copies[-1].start()
    return copies


def compress_kernel(
    res_rows, latent, aux_ref, prompt_ref, resident_hbm, out_ref, bias_ref, resident_ref, sem
):
    fetch = pltpu.make_async_copy(resident_hbm, resident_ref, sem)
    fetch.start()
    width, most = prompt_ref.shape[1:]
    half = (width - latent) // 2
    fresh = jnp.concatenate([aux_ref[0:2, :width], jnp.zeros((PACK - 2, width), F32)], axis=0)
    pick = jnp.where(iota((PACK, LANES), 0) == iota((PACK, LANES), 1), 1.0, 0.0).astype(BF16)
    fresh = dot(fresh.astype(BF16), pick, ((0,), (0,)))
    gain = jnp.broadcast_to(aux_ref[3:4, :latent], (PACK, latent))
    top = jnp.where(iota((PACK, LANES), 0) == 0, 1.0, 0.0).astype(BF16)
    gain = dot(gain.astype(BF16), top, ((0,), (0,)))
    length = aux_ref[2:3, :LANES].astype(I32)
    at = iota(bias_ref.shape, 1)
    token = iota(bias_ref.shape, 0)
    length_all = jnp.concatenate([length] * (bias_ref.shape[1] // LANES), axis=1)
    seen = (at < length_all) | ((at >= most) & (at <= most + token))
    bias_ref[...] = jnp.where(seen, 1.0, 0.0)
    freq = frequencies(half, (half, 1), 0)
    for i in range(most // LANES + 1):
        at = slice(i * LANES, (i + 1) * LANES)
        lane = iota((1, LANES), 1)
        if i * LANES < most:
            raw = prompt_ref[0, :, at].astype(F32)
            position = res_rows + i * LANES + lane
        else:
            raw = fresh
            position = res_rows + length + lane
        lat = raw[:latent]
        meansq = jnp.sum(lat * lat, axis=0, keepdims=True) * (1.0 / latent)
        out_ref[:latent, at] = (lat * lax.rsqrt(meansq + 1e-06) * gain).astype(BF16)
        angle = position.astype(F32) * freq
        sine, cosine = sine_cosine(angle)
        x1, x2 = raw[latent : latent + half], raw[latent + half :]
        out_ref[latent : latent + half, at] = (x1 * cosine - x2 * sine).astype(BF16)
        out_ref[latent + half :, at] = (x2 * cosine + x1 * sine).astype(BF16)
    fetch.wait()


def score_kernel(
    scale, q_ref, keys_ref, seen_ref, resident_ref, wo_hbm, sp_ref, sr_ref, stat_ref, wo_ref, sems
):
    fetches = fetch_start(wo_hbm, wo_ref, sems, 0)
    heads = q_ref.shape[0]
    half = q_ref.shape[2]
    width = keys_ref.shape[0]
    rope = width - 2 * half
    rows = 2 * heads
    total = heads * PACK
    flat = q_ref[...].reshape(total, half)
    shape = (rows, total)
    line = iota(shape, 0)
    head, tok = over(line, 4) * 2 + rest_of(line, 2), rest_of(over(line, 2), 2)
    source = iota(shape, 1) - head * PACK

    def picked(r):
        hit = source == r + tok
        return dot(jnp.where(hit, 1.0, 0.0).astype(BF16), flat)

    turned = picked(2 * PART)
    tops, sums = [], []
    for k in range(3):
        query = jnp.concatenate(
            [picked(2 * k), picked(PART + 2 * k), turned[:, k * rope : (k + 1) * rope]], axis=1
        ).astype(BF16)
        keys = keys_ref[...] if k == 0 else resident_ref[k - 1]
        scores = dot(query, keys) * scale
        if k == 0:
            first, second = seen_ref[0:1, :] > 0.5, seen_ref[1:2, :] > 0.5
            token = rest_of(over(iota(scores.shape, 0), 2), 2)
            seen = (first & (token == 0)) | (second & (token == 1))
            scores = jnp.where(seen, scores, -1e30)
            sp_ref[...] = scores
        else:
            sr_ref[k - 1] = scores
        top = jnp.max(scores, axis=1, keepdims=True)
        tops.append(top)
        sums.append(jnp.sum(jnp.exp(scores - top), axis=1, keepdims=True))
    lanes = stat_ref.shape[2]
    here = iota((3 * rows, lanes), 0) == iota((3 * rows, lanes), 1)
    top = jnp.sum(jnp.where(here, jnp.concatenate(tops, axis=0), 0.0), axis=0, keepdims=True)
    total = jnp.sum(jnp.where(here, jnp.concatenate(sums, axis=0), 0.0), axis=0, keepdims=True)
    both = jnp.concatenate([top, total], axis=0)
    stat_ref[...] = jnp.broadcast_to(both[None], stat_ref.shape)
    for fetch in fetches:
        fetch.wait()


def attend_kernel(
    owners_ref, stat_ref, sp_ref, sr_ref, keys_ref, resident_ref, wo_hbm, out_ref, wo_ref, sems
):
    fetches = fetch_start(wo_hbm, wo_ref, sems, wo_ref.shape[2])
    heads = out_ref.shape[0]
    latent = out_ref.shape[1] // PART * LANES
    seqs = owners_ref.shape[0]
    rows = 2 * heads
    device = lax.axis_index("seq")
    lanes = stat_ref.shape[2]
    my_owner = owners_ref[device]
    my_slot = jnp.int32(0)
    seen = jnp.int32(0)
    first = jnp.int32(0)
    second = jnp.int32(0)
    for s in range(seqs):
        owner = owners_ref[s]
        my_slot = my_slot + jnp.where((owner == my_owner) & (s < device), 1, 0)
        mine = owner == device
        first = jnp.where(mine & (seen == 0), s, first)
        second = jnp.where(mine & (seen == 1), s, second)
        seen = seen + jnp.where(mine, 1, 0)

    mine = stat_ref[device]
    place = over(iota((1, lanes), 1), rows)
    other = jnp.zeros((2, lanes), F32)
    pairs = [(stat_ref[my_owner], 1 + my_slot), (stat_ref[first], 0), (stat_ref[second], 0)]
    for k, (theirs, segment) in enumerate(pairs):
        moved = jnp.zeros((2, lanes), F32)
        for n in range(3):
            turned = pltpu.roll(theirs, ((k - n) * rows) % lanes, 1)
            moved = jnp.where(segment == n, turned, moved)
        other = jnp.where(place == k, moved, other)
    top = jnp.maximum(mine[0:1], other[0:1])
    total = mine[1:2] * jnp.exp(mine[0:1] - top) + other[1:2] * jnp.exp(other[0:1] - top)
    hit = iota((3 * rows, lanes), 1) == iota((3 * rows, lanes), 0)
    top = jnp.sum(jnp.where(hit, top, 0.0), axis=1, keepdims=True)
    total = jnp.sum(jnp.where(hit, total, 0.0), axis=1, keepdims=True)
    for k in range(3):
        at = slice(k * rows, (k + 1) * rows)
        scores = sp_ref[...] if k == 0 else sr_ref[k - 1]
        keys = keys_ref[:latent, :] if k == 0 else resident_ref[k - 1, :latent, :]
        weights = jnp.exp(scores - top[at]).astype(BF16)
        part = dot(weights, keys, ((1,), (1,))) / total[at]
        for h in range(heads):
            for c in range(latent // LANES):
                at = c * PART + 2 * k
                out_ref[h, at : at + 2, :] = part[2 * h : 2 * h + 2, c * LANES : (c + 1) * LANES]
    for fetch in fetches:
        fetch.wait()


def project_kernel(
    owners_ref, part_ref, uv_ref, other_uv_ref, wo_ref, other_wo0_ref, other_wo1_ref, out_ref
):
    count, each, lanes = part_ref.shape
    seqs = owners_ref.shape[1]
    cuts = each // PART
    rows = 2 * seqs
    core = lax.axis_index("seq") % 2
    owners = owners_ref[...]
    row = iota((cuts * 2 * rows, 1), 0)
    cut, other, seq = over(row, 2 * rows), over(rest_of(row, 2 * rows), rows), over(rest_of(row, rows), 2)
    head = jnp.where(other == 0, core, 1 - core)
    owner = column_of(owners, seq)
    slot = column_of(slots_of(owners), seq)
    first = seq * each + cut * PART + head
    second = owner * each + cut * PART + 2 + 2 * slot + head
    at = iota((cuts * 2 * rows, count * each), 1)
    hit = jnp.where((at == first) | (at == second), 1.0, 0.0).astype(BF16)
    rest = part_ref[...].reshape(count * each, lanes)
    latent = None
    for _ in range(3):
        piece = rest.astype(BF16)
        rest = rest - piece.astype(F32)
        one = dot(hit, piece)
        latent = one if latent is None else latent + one
    latent = latent.astype(BF16)
    latent = jnp.concatenate(
        [latent[c * 2 * rows : (c + 1) * 2 * rows] for c in range(cuts)], axis=1
    )
    half = rest_of(iota((rows, 1), 0), 2)
    cols = wo_ref.shape[2] // 2
    product = None
    others = (other_wo0_ref[0], other_wo1_ref[0])
    sides = (wo_ref[0, :, :cols], wo_ref[0, :, cols:])
    for n, (uv, wo) in enumerate(((uv_ref, sides), (other_uv_ref, others))):
        head_out = dot(latent[n * rows : (n + 1) * rows], uv[0])
        for side in range(2):
            lines = jnp.where(half == side, head_out, 0.0).astype(BF16)
            one = dot(lines, wo[side])
            product = one if product is None else product + one
    top = jnp.max(jnp.abs(product), axis=1, keepdims=True)
    power = jnp.clip(jnp.floor(jnp.log2(jnp.maximum(top, 1e-35))) + 1.0, -100.0, 100.0)
    coded = jnp.round(product * jnp.exp2(BITS - power)).astype(I32).astype(I16)
    power = jnp.broadcast_to(power, (rows, LANES)).astype(I32).astype(I16)
    for s in range(seqs):
        out_ref[s, :, :cols] = coded[2 * s : 2 * s + 2]
        out_ref[s, :, cols:] = power[2 * s : 2 * s + 2]


def final_kernel(in_ref, out_ref):
    cols = out_ref.shape[2] // 2
    for t in range(2):
        total = None
        for n in range(t, in_ref.shape[0], 2):
            power = in_ref[n, :, cols : cols + 1].astype(I32).astype(F32)
            one = in_ref[n, :, :cols].astype(I32).astype(F32) * jnp.exp2(power - BITS)
            total = one if total is None else total + one
        for j in range(2):
            out_ref[0, t : t + 1, j * cols : (j + 1) * cols] = total[j : j + 1].astype(BF16)


def swap(x):
    return lax.all_to_all(x, "seq", split_axis=0, concat_axis=0, tiled=True)


def trade(x, step):
    count = lax.axis_size("seq")
    return lax.ppermute(x, "seq", [(d, d ^ step) for d in range(count)])


def call(kernel, shapes, specs, scratch=(), cost=None, room=None):
    single = not isinstance(shapes, (list, tuple))
    if room is None:
        room = 16 if lax.axis_size("seq") <= 32 else 56
    return pl.pallas_call(
        kernel,
        out_shape=shapes,
        in_specs=specs,
        out_specs=VMEM if single else [VMEM] * len(shapes),
        scratch_shapes=list(scratch),
        cost_estimate=cost,
        compiler_params=pltpu.CompilerParams(vmem_limit_bytes=room * 1024 * 1024),
    )


def on_device(prompt_raw, lengths, owners, resident, new_raw, queries, kv_gain, w_uk, w_uv, w_o):
    count = lax.axis_size("seq")
    seqs = lengths.shape[0]
    most, width = prompt_raw.shape[1:]
    latent = kv_gain.shape[0]
    res_rows = resident.shape[1]
    nope = w_uk.shape[1]
    rope = width - latent
    heads = count
    out_width = w_o.shape[2]
    scale = 1.0 / queries.shape[-1] ** 0.5
    owners_row, lengths_row = owners.reshape(1, seqs), lengths.reshape(1, seqs)
    prompt_raw = prompt_raw.transpose(0, 2, 1)
    resident = resident.transpose(0, 2, 1)
    queries = queries.transpose(0, 2, 1, 3)
    keys_rows = most + LANES

    aux_width = -(-width // LANES) * LANES
    query, aux = call(
        functools.partial(query_kernel, res_rows),
        [
            jax.ShapeDtypeStruct((count, PACK, latent // 2), BF16),
            jax.ShapeDtypeStruct((8, aux_width), F32),
        ],
        [HBM] * 6,
        [
            pltpu.VMEM((1, seqs), I32),
            pltpu.VMEM((1, seqs), I32),
            pltpu.VMEM(queries.shape, BF16),
            pltpu.VMEM((nope, latent), BF16),
            pltpu.VMEM((2, width), BF16),
            pltpu.VMEM((latent,), BF16),
            pltpu.VMEM((2 * seqs, -(-(nope + rope) // LANES) * LANES), F32),
            pltpu.SemaphoreType.DMA((6,)),
        ],
        room=60,
    )(owners_row, lengths_row, queries, w_uk[0], new_raw, kv_gain)
    received = swap(query)
    query, w_uv, w_o = lax.optimization_barrier((query, w_uv, w_o))
    other_uv, other_wo = trade(w_uv, 1), trade(w_o, 1)
    keys, seen, resident = call(
        functools.partial(compress_kernel, res_rows, latent),
        [
            jax.ShapeDtypeStruct((width, keys_rows), BF16),
            jax.ShapeDtypeStruct((8, keys_rows), F32),
            jax.ShapeDtypeStruct(resident.shape, BF16),
        ],
        [VMEM] * 2 + [HBM],
        [pltpu.SemaphoreType.DMA],
        cost=pl.CostEstimate(flops=10**7, bytes_accessed=10**7, transcendentals=10**5),
    )(aux, prompt_raw, resident)
    lanes = -(-6 * heads // LANES) * LANES
    half = out_width // 2
    half_wo = jax.ShapeDtypeStruct((1, w_o.shape[1], half), BF16)
    scores_p, scores_r, stat, other_wo0 = call(
        functools.partial(score_kernel, scale),
        [
            jax.ShapeDtypeStruct((2 * heads, keys_rows), F32),
            jax.ShapeDtypeStruct((2, 2 * heads, res_rows), F32),
            jax.ShapeDtypeStruct((count, 2, lanes), F32),
            half_wo,
        ],
        [VMEM] * 4 + [HBM],
        [pltpu.SemaphoreType.DMA((2,))],
    )(received, keys, seen, resident, other_wo)
    stat, other_uv = lax.optimization_barrier((stat, other_uv))
    stats = swap(stat)
    part, other_wo1 = call(
        attend_kernel,
        [
            jax.ShapeDtypeStruct((heads, PART * (latent // LANES), LANES), F32),
            half_wo,
        ],
        [SMEM] + [VMEM] * 5 + [HBM],
        [pltpu.SemaphoreType.DMA((2,))],
    )(owners, stats, scores_p, scores_r, keys, resident, other_wo)
    parts = swap(part)
    sums = call(
        project_kernel, jax.ShapeDtypeStruct((seqs, 2, half + LANES), I16), [VMEM] * 7
    )(owners_row, parts, w_uv, other_uv, w_o, other_wo0, other_wo1)
    return call(final_kernel, jax.ShapeDtypeStruct((1, 2, out_width), BF16), [VMEM])(swap(sums))


def solution(mesh):
    in_specs = (
        P(("group", "seq"), None, None),
        P("group"),
        P("group"),
        P(("group", "seq"), None, None),
        P("group", None, None),
        P("group", None, "seq", None),
        P(),
        P("seq", None, None),
        P("seq", None, None),
        P("seq", None, None),
    )
    out_specs = P(("group", "seq"), None, None)
    return jax.shard_map(
        on_device, mesh=mesh, in_specs=in_specs, out_specs=out_specs, check_vma=False
    )
```

```python
import functools

import jax
import jax.numpy as jnp
import numpy as np
from jax import lax
from jax.experimental import pallas as pl
from jax.experimental.pallas import tpu as pltpu
from jax.sharding import PartitionSpec as P

F32 = jnp.float32
BF16 = jnp.bfloat16
I32 = jnp.int32
I16 = jnp.int16
VMEM = pl.BlockSpec(memory_space=pltpu.VMEM)
SMEM = pl.BlockSpec(memory_space=pltpu.SMEM)
HBM = pl.BlockSpec(memory_space=pltpu.HBM)
LANES = 128
PACK = 16
PART = 6
BITS = 14.0
NEAR = 4


def iota(shape, dim):
    return lax.broadcasted_iota(I32, shape, dim)


def over(x, n):
    return x >> (n.bit_length() - 1)


def rest_of(x, n):
    return x & (n - 1)


def dot(a, b, dims=((1,), (0,))):
    return lax.dot_general(a, b, (dims, ((), ())), preferred_element_type=F32)


def column_of(row, picks):
    n, width = picks.shape[0], row.shape[1]
    hit = iota((n, width), 1) == picks
    return jnp.sum(jnp.where(hit, row, 0), axis=1, keepdims=True)


def slots_of(owners_row):
    seqs = owners_row.shape[1]
    owners_col = column_of(owners_row, iota((seqs, 1), 0))
    earlier = iota((seqs, seqs), 0) < iota((seqs, seqs), 1)
    same = (owners_col == owners_row) & earlier
    return jnp.sum(jnp.where(same, 1, 0), axis=0, keepdims=True)


def doubled(row, times):
    seqs = row.shape[1]
    col = column_of(row, iota((seqs, 1), 0))
    shape = (seqs, 2 * seqs * times)
    hit = over(rest_of(iota(shape, 1), 2 * seqs), 2) == iota(shape, 0)
    return jnp.sum(jnp.where(hit, col, 0), axis=0, keepdims=True)


def frequencies(half, shape, dim):
    at = rest_of(iota(shape, dim), half)
    values = np.float32(10000.0) ** (-(np.arange(half, dtype=np.float32) * np.float32(2.0)) / np.float32(2 * half))
    result = jnp.zeros(shape, F32)
    for i in range(half):
        result = jnp.where(at == i, float(values[i]), result)
    return result


def sine_cosine(angle):
    count = jnp.floor(angle * (2.0 / np.pi) + 0.5)
    x = ((angle - count * 1.5703125) - count * 4.837512969970703125e-4) - count * 7.54978995489188216e-8
    quarter = count.astype(I32)
    y = x * x
    sine = x + x * y * (-1.6666654611e-1 + y * (8.3321608736e-3 - y * 1.9515295891e-4))
    cosine = 1.0 - 0.5 * y + y * y * (4.166664568298827e-2 + y * (-1.388731625493765e-3 + y * 2.443315711809948e-5))
    odd = rest_of(quarter, 2) == 1
    first, second = jnp.where(odd, cosine, sine), jnp.where(odd, sine, cosine)
    first = jnp.where(rest_of(quarter, 4) >= 2, -first, first)
    second = jnp.where(rest_of(quarter + 1, 4) >= 2, -second, second)
    return first, second


def query_kernel(
    res_rows,
    owners_hbm,
    lengths_hbm,
    queries_hbm,
    uk_hbm,
    new_hbm,
    gain_hbm,
    out_ref,
    aux_ref,
    owners_ref,
    lengths_ref,
    queries_ref,
    uk_ref,
    new_ref,
    gain_ref,
    flat,
    sems,
):
    device = lax.axis_index("seq")
    copies = []
    pairs = [
        (owners_hbm, owners_ref),
        (lengths_hbm, lengths_ref),
        (queries_hbm, queries_ref),
        (uk_hbm, uk_ref),
        (new_hbm.at[device], new_ref),
        (gain_hbm, gain_ref),
    ]
    for n, (source, target) in enumerate(pairs):
        copies.append(pltpu.make_async_copy(source, target, sems.at[n]))
        copies[-1].start()
    for copy in copies:
        copy.wait()
    seqs = owners_ref.shape[1]
    nope, latent = uk_ref.shape
    rope = queries_ref.shape[3] - nope
    half = latent // 2
    rows = 2 * seqs
    for s in range(seqs):
        flat[2 * s : 2 * s + 2, : nope + rope] = queries_ref[s, 0].astype(F32)
    values = flat[:, : nope + rope]
    absorbed = dot(values[:, :nope].astype(BF16), uk_ref[...]).astype(BF16)
    row = iota((rows, 1), 0)
    lengths = column_of(lengths_ref[...], over(row, 2))
    angle = (res_rows + lengths + rest_of(row, 2)).astype(F32) * frequencies(rope // 2, (1, rope), 1)
    x = values[:, nope:]
    swapped = jnp.concatenate([x[:, rope // 2 :], x[:, : rope // 2]], axis=1)
    sine, cosine = sine_cosine(angle)
    sine = jnp.where(iota(x.shape, 1) < rope // 2, -sine, sine)
    turned = x * cosine + swapped * sine
    zero = jnp.zeros((rows, rope), F32)
    pieces = [absorbed[:, :half], absorbed[:, half:]]
    for k in range(3):
        blocks = [turned if j == k else zero for j in range(half // rope)]
        pieces.append(jnp.concatenate(blocks, axis=1).astype(BF16))
    owners = owners_ref[...]
    owner = doubled(owners, 5)
    slot = doubled(slots_of(owners), 5)
    shape = (out_ref.shape[0] * PACK, 5 * rows)
    dest, r = over(iota(shape, 0), PACK), rest_of(iota(shape, 0), PACK)
    lane = iota((1, 5 * rows), 1)
    piece, seq, tok = over(lane, rows), over(rest_of(lane, rows), 2), rest_of(lane, 2)
    start = jnp.where(piece < 2, piece * PART, 2 * PART) + tok
    offset = r - start
    rotary = piece >= 2
    third = piece - 2
    here = jnp.where(owner == dest, slot + 1, jnp.where(seq == dest, 0, -1))
    both = (owner == dest) & (seq == dest)
    wide = (offset == 2 * here) | (both & (offset == 0))
    narrow = (offset == 0) & ((here == third) | (both & (third == 0)))
    hit = (~rotary & (here >= 0) & wide) | (rotary & narrow)
    pieces = jnp.concatenate(pieces, axis=0)
    result = dot(jnp.where(hit, 1.0, 0.0).astype(BF16), pieces)
    out_ref[...] = result.astype(BF16).reshape(out_ref.shape)
    width = new_ref.shape[1]
    aux_ref[0:2, :width] = new_ref[...].astype(F32)
    mine = jnp.where(iota(lengths_ref.shape, 1) == device, lengths_ref[...], 0)
    mine = jnp.sum(mine, axis=1, keepdims=True).astype(F32)
    aux_ref[2:3, :] = jnp.broadcast_to(mine, (1, aux_ref.shape[1]))
    aux_ref[3:4, :latent] = gain_ref[...].astype(F32).reshape(1, latent)


def fetch_start(source, target, sems, first):
    span = target.shape[2] // sems.shape[0]
    copies = []
    for n in range(sems.shape[0]):
        copies.append(
            pltpu.make_async_copy(
                source.at[:, :, pl.ds(first + n * span, span)], target.at[:, :, pl.ds(n * span, span)], sems.at[n]
            )
        )
        copies[-1].start()
    return copies


def compress_kernel(
    res_rows, latent, aux_ref, prompt_ref, resident_hbm, out_ref, bias_ref, resident_ref, sem
):
    fetch = pltpu.make_async_copy(resident_hbm, resident_ref, sem)
    fetch.start()
    width, most = prompt_ref.shape[1:]
    half = (width - latent) // 2
    fresh = jnp.concatenate([aux_ref[0:2, :width], jnp.zeros((PACK - 2, width), F32)], axis=0)
    pick = jnp.where(iota((PACK, LANES), 0) == iota((PACK, LANES), 1), 1.0, 0.0).astype(BF16)
    fresh = dot(fresh.astype(BF16), pick, ((0,), (0,)))
    gain = jnp.broadcast_to(aux_ref[3:4, :latent], (PACK, latent))
    top = jnp.where(iota((PACK, LANES), 0) == 0, 1.0, 0.0).astype(BF16)
    gain = dot(gain.astype(BF16), top, ((0,), (0,)))
    length = aux_ref[2:3, :LANES].astype(I32)
    at = iota(bias_ref.shape, 1)
    token = iota(bias_ref.shape, 0)
    length_all = jnp.concatenate([length] * (bias_ref.shape[1] // LANES), axis=1)
    seen = (at < length_all) | ((at >= most) & (at <= most + token))
    bias_ref[...] = jnp.where(seen, 1.0, 0.0)
    freq = frequencies(half, (half, 1), 0)
    for i in range(most // LANES + 1):
        at = slice(i * LANES, (i + 1) * LANES)
        lane = iota((1, LANES), 1)
        if i * LANES < most:
            raw = prompt_ref[0, :, at].astype(F32)
            position = res_rows + i * LANES + lane
        else:
            raw = fresh
            position = res_rows + length + lane
        lat = raw[:latent]
        meansq = jnp.sum(lat * lat, axis=0, keepdims=True) * (1.0 / latent)
        out_ref[:latent, at] = (lat * lax.rsqrt(meansq + 1e-06) * gain).astype(BF16)
        angle = position.astype(F32) * freq
        sine, cosine = sine_cosine(angle)
        x1, x2 = raw[latent : latent + half], raw[latent + half :]
        out_ref[latent : latent + half, at] = (x1 * cosine - x2 * sine).astype(BF16)
        out_ref[latent + half :, at] = (x2 * cosine + x1 * sine).astype(BF16)
    fetch.wait()


def score_kernel(
    scale, q_ref, keys_ref, seen_ref, resident_ref, wo_hbm, sp_ref, sr_ref, stat_ref, wo_ref, sems
):
    fetches = fetch_start(wo_hbm, wo_ref, sems, 0)
    heads = q_ref.shape[0]
    half = q_ref.shape[2]
    width = keys_ref.shape[0]
    rope = width - 2 * half
    rows = 2 * heads
    total = heads * PACK
    flat = q_ref[...].reshape(total, half)
    shape = (rows, total)
    line = iota(shape, 0)
    head, tok = over(line, 4) * 2 + rest_of(line, 2), rest_of(over(line, 2), 2)
    source = iota(shape, 1) - head * PACK

    def picked(r):
        hit = source == r + tok
        return dot(jnp.where(hit, 1.0, 0.0).astype(BF16), flat)

    turned = picked(2 * PART)
    tops, sums = [], []
    for k in range(3):
        query = jnp.concatenate(
            [picked(2 * k), picked(PART + 2 * k), turned[:, k * rope : (k + 1) * rope]], axis=1
        ).astype(BF16)
        keys = keys_ref[...] if k == 0 else resident_ref[k - 1]
        scores = dot(query, keys) * scale
        if k == 0:
            first, second = seen_ref[0:1, :] > 0.5, seen_ref[1:2, :] > 0.5
            token = rest_of(over(iota(scores.shape, 0), 2), 2)
            seen = (first & (token == 0)) | (second & (token == 1))
            scores = jnp.where(seen, scores, -1e30)
            sp_ref[...] = scores
        else:
            sr_ref[k - 1] = scores
        top = jnp.max(scores, axis=1, keepdims=True)
        tops.append(top)
        sums.append(jnp.sum(jnp.exp(scores - top), axis=1, keepdims=True))
    lanes = stat_ref.shape[2]
    here = iota((3 * rows, lanes), 0) == iota((3 * rows, lanes), 1)
    top = jnp.sum(jnp.where(here, jnp.concatenate(tops, axis=0), 0.0), axis=0, keepdims=True)
    total = jnp.sum(jnp.where(here, jnp.concatenate(sums, axis=0), 0.0), axis=0, keepdims=True)
    both = jnp.concatenate([top, total], axis=0)
    stat_ref[...] = jnp.zeros(stat_ref.shape, F32)
    stat_ref[lax.axis_index("seq")] = both
    for fetch in fetches:
        fetch.wait()


def attend_kernel(
    owners_ref, stat_ref, sp_ref, sr_ref, keys_ref, resident_ref, wo_hbm, out_ref, wo_ref, sems
):
    fetches = fetch_start(wo_hbm, wo_ref, sems, wo_ref.shape[2])
    heads = out_ref.shape[0]
    latent = out_ref.shape[1] // PART * LANES
    seqs = owners_ref.shape[0]
    rows = 2 * heads
    device = lax.axis_index("seq")
    lanes = stat_ref.shape[2]
    my_owner = owners_ref[device]
    my_slot = jnp.int32(0)
    seen = jnp.int32(0)
    first = jnp.int32(0)
    second = jnp.int32(0)
    for s in range(seqs):
        owner = owners_ref[s]
        my_slot = my_slot + jnp.where((owner == my_owner) & (s < device), 1, 0)
        mine = owner == device
        first = jnp.where(mine & (seen == 0), s, first)
        second = jnp.where(mine & (seen == 1), s, second)
        seen = seen + jnp.where(mine, 1, 0)

    mine = stat_ref[device]
    place = over(iota((1, lanes), 1), rows)
    other = jnp.zeros((2, lanes), F32)
    pairs = [(stat_ref[my_owner], 1 + my_slot), (stat_ref[first], 0), (stat_ref[second], 0)]
    for k, (theirs, segment) in enumerate(pairs):
        moved = jnp.zeros((2, lanes), F32)
        for n in range(3):
            turned = pltpu.roll(theirs, ((k - n) * rows) % lanes, 1)
            moved = jnp.where(segment == n, turned, moved)
        other = jnp.where(place == k, moved, other)
    top = jnp.maximum(mine[0:1], other[0:1])
    total = mine[1:2] * jnp.exp(mine[0:1] - top) + other[1:2] * jnp.exp(other[0:1] - top)
    hit = iota((3 * rows, lanes), 1) == iota((3 * rows, lanes), 0)
    top = jnp.sum(jnp.where(hit, top, 0.0), axis=1, keepdims=True)
    total = jnp.sum(jnp.where(hit, total, 0.0), axis=1, keepdims=True)
    for k in range(3):
        at = slice(k * rows, (k + 1) * rows)
        scores = sp_ref[...] if k == 0 else sr_ref[k - 1]
        keys = keys_ref[:latent, :] if k == 0 else resident_ref[k - 1, :latent, :]
        weights = jnp.exp(scores - top[at]).astype(BF16)
        part = dot(weights, keys, ((1,), (1,))) / total[at]
        for h in range(heads):
            for c in range(latent // LANES):
                at = c * PART + 2 * k
                out_ref[h, at : at + 2, :] = part[2 * h : 2 * h + 2, c * LANES : (c + 1) * LANES]
    for fetch in fetches:
        fetch.wait()


def project_kernel(
    owners_ref, part_ref, uv_ref, other_uv_ref, wo_ref, other_wo0_ref, other_wo1_ref, out_ref
):
    count, each, lanes = part_ref.shape
    seqs = owners_ref.shape[1]
    cuts = each // PART
    rows = 2 * seqs
    core = lax.axis_index("seq") % 2
    owners = owners_ref[...]
    row = iota((cuts * 2 * rows, 1), 0)
    cut, other, seq = over(row, 2 * rows), over(rest_of(row, 2 * rows), rows), over(rest_of(row, rows), 2)
    head = jnp.where(other == 0, core, 1 - core)
    owner = column_of(owners, seq)
    slot = column_of(slots_of(owners), seq)
    first = seq * each + cut * PART + head
    second = owner * each + cut * PART + 2 + 2 * slot + head
    at = iota((cuts * 2 * rows, count * each), 1)
    hit = jnp.where((at == first) | (at == second), 1.0, 0.0).astype(BF16)
    rest = part_ref[...].reshape(count * each, lanes)
    latent = None
    for _ in range(3):
        piece = rest.astype(BF16)
        rest = rest - piece.astype(F32)
        one = dot(hit, piece)
        latent = one if latent is None else latent + one
    latent = latent.astype(BF16)
    latent = jnp.concatenate(
        [latent[c * 2 * rows : (c + 1) * 2 * rows] for c in range(cuts)], axis=1
    )
    half = rest_of(iota((rows, 1), 0), 2)
    cols = wo_ref.shape[2] // 2
    product = None
    others = (other_wo0_ref[0], other_wo1_ref[0])
    sides = (wo_ref[0, :, :cols], wo_ref[0, :, cols:])
    for n, (uv, wo) in enumerate(((uv_ref, sides), (other_uv_ref, others))):
        head_out = dot(latent[n * rows : (n + 1) * rows], uv[0])
        for side in range(2):
            lines = jnp.where(half == side, head_out, 0.0).astype(BF16)
            one = dot(lines, wo[side])
            product = one if product is None else product + one
    top = jnp.max(jnp.abs(product), axis=1, keepdims=True)
    power = jnp.clip(jnp.floor(jnp.log2(jnp.maximum(top, 1e-35))) + 1.0, -100.0, 100.0)
    coded = jnp.round(product * jnp.exp2(BITS - power)).astype(I32).astype(I16)
    power = jnp.broadcast_to(power, (rows, LANES)).astype(I32).astype(I16)
    for s in range(seqs):
        out_ref[s, :, :cols] = coded[2 * s : 2 * s + 2]
        out_ref[s, :, cols:] = power[2 * s : 2 * s + 2]


def final_kernel(in_ref, out_ref):
    cols = out_ref.shape[2] // 2
    for t in range(2):
        total = None
        for n in range(t, in_ref.shape[0], 2):
            power = in_ref[n, :, cols : cols + 1].astype(I32).astype(F32)
            one = in_ref[n, :, :cols].astype(I32).astype(F32) * jnp.exp2(power - BITS)
            total = one if total is None else total + one
        for j in range(2):
            out_ref[0, t : t + 1, j * cols : (j + 1) * cols] = total[j : j + 1].astype(BF16)


def swap(x):
    return lax.all_to_all(x, "seq", split_axis=0, concat_axis=0, tiled=True)


def trade(x, step):
    count = lax.axis_size("seq")
    return lax.ppermute(x, "seq", [(d, d ^ step) for d in range(count)])


def call(kernel, shapes, specs, scratch=(), cost=None, room=None):
    single = not isinstance(shapes, (list, tuple))
    if room is None:
        room = 16 if lax.axis_size("seq") <= 32 else 56
    return pl.pallas_call(
        kernel,
        out_shape=shapes,
        in_specs=specs,
        out_specs=VMEM if single else [VMEM] * len(shapes),
        scratch_shapes=list(scratch),
        cost_estimate=cost,
        compiler_params=pltpu.CompilerParams(vmem_limit_bytes=room * 1024 * 1024),
    )


def on_device(prompt_raw, lengths, owners, resident, new_raw, queries, kv_gain, w_uk, w_uv, w_o):
    count = lax.axis_size("seq")
    seqs = lengths.shape[0]
    most, width = prompt_raw.shape[1:]
    latent = kv_gain.shape[0]
    res_rows = resident.shape[1]
    nope = w_uk.shape[1]
    rope = width - latent
    heads = count
    out_width = w_o.shape[2]
    scale = 1.0 / queries.shape[-1] ** 0.5
    owners_row, lengths_row = owners.reshape(1, seqs), lengths.reshape(1, seqs)
    prompt_raw = prompt_raw.transpose(0, 2, 1)
    resident = resident.transpose(0, 2, 1)
    queries = queries.transpose(0, 2, 1, 3)
    keys_rows = most + LANES

    aux_width = -(-width // LANES) * LANES
    query, aux = call(
        functools.partial(query_kernel, res_rows),
        [
            jax.ShapeDtypeStruct((count, PACK, latent // 2), BF16),
            jax.ShapeDtypeStruct((8, aux_width), F32),
        ],
        [HBM] * 6,
        [
            pltpu.VMEM((1, seqs), I32),
            pltpu.VMEM((1, seqs), I32),
            pltpu.VMEM(queries.shape, BF16),
            pltpu.VMEM((nope, latent), BF16),
            pltpu.VMEM((2, width), BF16),
            pltpu.VMEM((latent,), BF16),
            pltpu.VMEM((2 * seqs, -(-(nope + rope) // LANES) * LANES), F32),
            pltpu.SemaphoreType.DMA((6,)),
        ],
        room=60,
    )(owners_row, lengths_row, queries, w_uk[0], new_raw, kv_gain)
    received = swap(query)
    query, w_uv, w_o = lax.optimization_barrier((query, w_uv, w_o))
    other_uv, other_wo = trade(w_uv, 1), trade(w_o, 1)
    keys, seen, resident = call(
        functools.partial(compress_kernel, res_rows, latent),
        [
            jax.ShapeDtypeStruct((width, keys_rows), BF16),
            jax.ShapeDtypeStruct((8, keys_rows), F32),
            jax.ShapeDtypeStruct(resident.shape, BF16),
        ],
        [VMEM] * 2 + [HBM],
        [pltpu.SemaphoreType.DMA],
        cost=pl.CostEstimate(flops=10**7, bytes_accessed=10**7, transcendentals=10**5),
    )(aux, prompt_raw, resident)
    lanes = -(-6 * heads // LANES) * LANES
    half = out_width // 2
    half_wo = jax.ShapeDtypeStruct((1, w_o.shape[1], half), BF16)
    scores_p, scores_r, stat, other_wo0 = call(
        functools.partial(score_kernel, scale),
        [
            jax.ShapeDtypeStruct((2 * heads, keys_rows), F32),
            jax.ShapeDtypeStruct((2, 2 * heads, res_rows), F32),
            jax.ShapeDtypeStruct((count, 2, lanes), F32),
            half_wo,
        ],
        [VMEM] * 4 + [HBM],
        [pltpu.SemaphoreType.DMA((2,))],
    )(received, keys, seen, resident, other_wo)
    stat, other_uv = lax.optimization_barrier((stat, other_uv))
    stats = lax.psum(stat, "seq")
    part, other_wo1 = call(
        attend_kernel,
        [
            jax.ShapeDtypeStruct((heads, PART * (latent // LANES), LANES), F32),
            half_wo,
        ],
        [SMEM] + [VMEM] * 5 + [HBM],
        [pltpu.SemaphoreType.DMA((2,))],
    )(owners, stats, scores_p, scores_r, keys, resident, other_wo)
    parts = swap(part)
    sums = call(
        project_kernel, jax.ShapeDtypeStruct((seqs, 2, half + LANES), I16), [VMEM] * 7
    )(owners_row, parts, w_uv, other_uv, w_o, other_wo0, other_wo1)
    return call(final_kernel, jax.ShapeDtypeStruct((1, 2, out_width), BF16), [VMEM])(swap(sums))


def solution(mesh):
    in_specs = (
        P(("group", "seq"), None, None),
        P("group"),
        P("group"),
        P(("group", "seq"), None, None),
        P("group", None, None),
        P("group", None, "seq", None),
        P(),
        P("seq", None, None),
        P("seq", None, None),
        P("seq", None, None),
    )
    out_specs = P(("group", "seq"), None, None)
    return jax.shard_map(
        on_device, mesh=mesh, in_specs=in_specs, out_specs=out_specs, check_vma=False
    )
```

```python
import functools

import jax
import jax.numpy as jnp
import numpy as np
from jax import lax
from jax.experimental import pallas as pl
from jax.experimental.pallas import tpu as pltpu
from jax.sharding import PartitionSpec as P

F32 = jnp.float32
BF16 = jnp.bfloat16
I32 = jnp.int32
I16 = jnp.int16
VMEM = pl.BlockSpec(memory_space=pltpu.VMEM)
SMEM = pl.BlockSpec(memory_space=pltpu.SMEM)
HBM = pl.BlockSpec(memory_space=pltpu.HBM)
LANES = 128
PACK = 16
PART = 6
BITS = 14.0
NEAR = 4


def iota(shape, dim):
    return lax.broadcasted_iota(I32, shape, dim)


def shift_of(count):
    return count // 2


def over(x, n):
    return x >> (n.bit_length() - 1)


def rest_of(x, n):
    return x & (n - 1)


def dot(a, b, dims=((1,), (0,))):
    return lax.dot_general(a, b, (dims, ((), ())), preferred_element_type=F32)


def column_of(row, picks):
    n, width = picks.shape[0], row.shape[1]
    hit = iota((n, width), 1) == picks
    return jnp.sum(jnp.where(hit, row, 0), axis=1, keepdims=True)


def slots_of(owners_row):
    seqs = owners_row.shape[1]
    owners_col = column_of(owners_row, iota((seqs, 1), 0))
    earlier = iota((seqs, seqs), 0) < iota((seqs, seqs), 1)
    same = (owners_col == owners_row) & earlier
    return jnp.sum(jnp.where(same, 1, 0), axis=0, keepdims=True)


def doubled(row, times):
    seqs = row.shape[1]
    col = column_of(row, iota((seqs, 1), 0))
    shape = (seqs, 2 * seqs * times)
    hit = over(rest_of(iota(shape, 1), 2 * seqs), 2) == iota(shape, 0)
    return jnp.sum(jnp.where(hit, col, 0), axis=0, keepdims=True)


def frequencies(half, shape, dim):
    at = rest_of(iota(shape, dim), half)
    values = np.float32(10000.0) ** (-(np.arange(half, dtype=np.float32) * np.float32(2.0)) / np.float32(2 * half))
    result = jnp.zeros(shape, F32)
    for i in range(half):
        result = jnp.where(at == i, float(values[i]), result)
    return result


def sine_cosine(angle):
    count = jnp.floor(angle * (2.0 / np.pi) + 0.5)
    x = ((angle - count * 1.5703125) - count * 4.837512969970703125e-4) - count * 7.54978995489188216e-8
    quarter = count.astype(I32)
    y = x * x
    sine = x + x * y * (-1.6666654611e-1 + y * (8.3321608736e-3 - y * 1.9515295891e-4))
    cosine = 1.0 - 0.5 * y + y * y * (4.166664568298827e-2 + y * (-1.388731625493765e-3 + y * 2.443315711809948e-5))
    odd = rest_of(quarter, 2) == 1
    first, second = jnp.where(odd, cosine, sine), jnp.where(odd, sine, cosine)
    first = jnp.where(rest_of(quarter, 4) >= 2, -first, first)
    second = jnp.where(rest_of(quarter + 1, 4) >= 2, -second, second)
    return first, second


def query_kernel(
    res_rows,
    owners_hbm,
    lengths_hbm,
    queries_hbm,
    uk_hbm,
    new_hbm,
    gain_hbm,
    out_ref,
    aux_ref,
    owners_ref,
    lengths_ref,
    queries_ref,
    uk_ref,
    new_ref,
    gain_ref,
    flat,
    sems,
):
    device = lax.axis_index("seq")
    copies = []
    pairs = [
        (owners_hbm, owners_ref),
        (lengths_hbm, lengths_ref),
        (queries_hbm, queries_ref),
        (uk_hbm, uk_ref),
        (new_hbm.at[device], new_ref),
        (gain_hbm, gain_ref),
    ]
    for n, (source, target) in enumerate(pairs):
        copies.append(pltpu.make_async_copy(source, target, sems.at[n]))
        copies[-1].start()
    for copy in copies:
        copy.wait()
    seqs = owners_ref.shape[1]
    nope, latent = uk_ref.shape
    rope = queries_ref.shape[3] - nope
    half = latent // 2
    rows = 2 * seqs
    for s in range(seqs):
        flat[2 * s : 2 * s + 2, : nope + rope] = queries_ref[s, 0].astype(F32)
    values = flat[:, : nope + rope]
    absorbed = dot(values[:, :nope].astype(BF16), uk_ref[...]).astype(BF16)
    row = iota((rows, 1), 0)
    lengths = column_of(lengths_ref[...], over(row, 2))
    angle = (res_rows + lengths + rest_of(row, 2)).astype(F32) * frequencies(rope // 2, (1, rope), 1)
    x = values[:, nope:]
    swapped = jnp.concatenate([x[:, rope // 2 :], x[:, : rope // 2]], axis=1)
    sine, cosine = sine_cosine(angle)
    sine = jnp.where(iota(x.shape, 1) < rope // 2, -sine, sine)
    turned = x * cosine + swapped * sine
    zero = jnp.zeros((rows, rope), F32)
    pieces = [absorbed[:, :half], absorbed[:, half:]]
    for k in range(3):
        blocks = [turned if j == k else zero for j in range(half // rope)]
        pieces.append(jnp.concatenate(blocks, axis=1).astype(BF16))
    owners = owners_ref[...]
    owner = doubled(owners, 5)
    slot = doubled(slots_of(owners), 5)
    shape = (out_ref.shape[0] * PACK, 5 * rows)
    dest, r = over(iota(shape, 0), PACK) ^ shift_of(out_ref.shape[0]), rest_of(iota(shape, 0), PACK)
    lane = iota((1, 5 * rows), 1)
    piece, seq, tok = over(lane, rows), over(rest_of(lane, rows), 2), rest_of(lane, 2)
    start = jnp.where(piece < 2, piece * PART, 2 * PART) + tok
    offset = r - start
    rotary = piece >= 2
    third = piece - 2
    here = jnp.where(owner == dest, slot + 1, jnp.where(seq == dest, 0, -1))
    both = (owner == dest) & (seq == dest)
    wide = (offset == 2 * here) | (both & (offset == 0))
    narrow = (offset == 0) & ((here == third) | (both & (third == 0)))
    hit = (~rotary & (here >= 0) & wide) | (rotary & narrow)
    pieces = jnp.concatenate(pieces, axis=0)
    result = dot(jnp.where(hit, 1.0, 0.0).astype(BF16), pieces)
    out_ref[...] = result.astype(BF16).reshape(out_ref.shape)
    width = new_ref.shape[1]
    aux_ref[0:2, :width] = new_ref[...].astype(F32)
    mine = jnp.where(iota(lengths_ref.shape, 1) == device, lengths_ref[...], 0)
    mine = jnp.sum(mine, axis=1, keepdims=True).astype(F32)
    aux_ref[2:3, :] = jnp.broadcast_to(mine, (1, aux_ref.shape[1]))
    aux_ref[3:4, :latent] = gain_ref[...].astype(F32).reshape(1, latent)


def fetch_start(source, target, sems, first):
    span = target.shape[2] // sems.shape[0]
    copies = []
    for n in range(sems.shape[0]):
        copies.append(
            pltpu.make_async_copy(
                source.at[:, :, pl.ds(first + n * span, span)], target.at[:, :, pl.ds(n * span, span)], sems.at[n]
            )
        )
        copies[-1].start()
    return copies


def compress_kernel(
    res_rows, latent, aux_ref, prompt_ref, resident_hbm, out_ref, bias_ref, resident_ref, sem
):
    fetch = pltpu.make_async_copy(resident_hbm, resident_ref, sem)
    fetch.start()
    width, most = prompt_ref.shape[1:]
    half = (width - latent) // 2
    fresh = jnp.concatenate([aux_ref[0:2, :width], jnp.zeros((PACK - 2, width), F32)], axis=0)
    pick = jnp.where(iota((PACK, LANES), 0) == iota((PACK, LANES), 1), 1.0, 0.0).astype(BF16)
    fresh = dot(fresh.astype(BF16), pick, ((0,), (0,)))
    gain = jnp.broadcast_to(aux_ref[3:4, :latent], (PACK, latent))
    top = jnp.where(iota((PACK, LANES), 0) == 0, 1.0, 0.0).astype(BF16)
    gain = dot(gain.astype(BF16), top, ((0,), (0,)))
    length = aux_ref[2:3, :LANES].astype(I32)
    at = iota(bias_ref.shape, 1)
    token = iota(bias_ref.shape, 0)
    length_all = jnp.concatenate([length] * (bias_ref.shape[1] // LANES), axis=1)
    seen = (at < length_all) | ((at >= most) & (at <= most + token))
    bias_ref[...] = jnp.where(seen, 1.0, 0.0)
    freq = frequencies(half, (half, 1), 0)
    for i in range(most // LANES + 1):
        at = slice(i * LANES, (i + 1) * LANES)
        lane = iota((1, LANES), 1)
        if i * LANES < most:
            raw = prompt_ref[0, :, at].astype(F32)
            position = res_rows + i * LANES + lane
        else:
            raw = fresh
            position = res_rows + length + lane
        lat = raw[:latent]
        meansq = jnp.sum(lat * lat, axis=0, keepdims=True) * (1.0 / latent)
        out_ref[:latent, at] = (lat * lax.rsqrt(meansq + 1e-06) * gain).astype(BF16)
        angle = position.astype(F32) * freq
        sine, cosine = sine_cosine(angle)
        x1, x2 = raw[latent : latent + half], raw[latent + half :]
        out_ref[latent : latent + half, at] = (x1 * cosine - x2 * sine).astype(BF16)
        out_ref[latent + half :, at] = (x2 * cosine + x1 * sine).astype(BF16)
    fetch.wait()


def score_kernel(
    scale, q_ref, keys_ref, seen_ref, resident_ref, wo_hbm, sp_ref, sr_ref, stat_ref, wo_ref, sems
):
    fetches = fetch_start(wo_hbm, wo_ref, sems, 0)
    heads = q_ref.shape[0]
    half = q_ref.shape[2]
    width = keys_ref.shape[0]
    rope = width - 2 * half
    rows = 2 * heads
    total = heads * PACK
    flat = q_ref[...].reshape(total, half)
    shape = (rows, total)
    line = iota(shape, 0)
    head, tok = over(line, 4) * 2 + rest_of(line, 2), rest_of(over(line, 2), 2)
    source = iota(shape, 1) - head * PACK

    def picked(r):
        hit = source == r + tok
        return dot(jnp.where(hit, 1.0, 0.0).astype(BF16), flat)

    turned = picked(2 * PART)
    tops, sums = [], []
    for k in range(3):
        query = jnp.concatenate(
            [picked(2 * k), picked(PART + 2 * k), turned[:, k * rope : (k + 1) * rope]], axis=1
        ).astype(BF16)
        keys = keys_ref[...] if k == 0 else resident_ref[k - 1]
        scores = dot(query, keys) * scale
        if k == 0:
            first, second = seen_ref[0:1, :] > 0.5, seen_ref[1:2, :] > 0.5
            token = rest_of(over(iota(scores.shape, 0), 2), 2)
            seen = (first & (token == 0)) | (second & (token == 1))
            scores = jnp.where(seen, scores, -1e30)
            sp_ref[...] = scores
        else:
            sr_ref[k - 1] = scores
        top = jnp.max(scores, axis=1, keepdims=True)
        tops.append(top)
        sums.append(jnp.sum(jnp.exp(scores - top), axis=1, keepdims=True))
    lanes = stat_ref.shape[2]
    here = iota((3 * rows, lanes), 0) == iota((3 * rows, lanes), 1)
    top = jnp.sum(jnp.where(here, jnp.concatenate(tops, axis=0), 0.0), axis=0, keepdims=True)
    total = jnp.sum(jnp.where(here, jnp.concatenate(sums, axis=0), 0.0), axis=0, keepdims=True)
    both = jnp.concatenate([top, total], axis=0)
    stat_ref[...] = jnp.broadcast_to(both[None], stat_ref.shape)
    for fetch in fetches:
        fetch.wait()


def attend_kernel(
    owners_ref, stat_ref, sp_ref, sr_ref, keys_ref, resident_ref, wo_hbm, out_ref, wo_ref, sems
):
    fetches = fetch_start(wo_hbm, wo_ref, sems, wo_ref.shape[2])
    heads = out_ref.shape[0]
    latent = out_ref.shape[1] // PART * LANES
    seqs = owners_ref.shape[0]
    rows = 2 * heads
    device = lax.axis_index("seq")
    lanes = stat_ref.shape[2]
    my_owner = owners_ref[device]
    my_slot = jnp.int32(0)
    seen = jnp.int32(0)
    first = jnp.int32(0)
    second = jnp.int32(0)
    for s in range(seqs):
        owner = owners_ref[s]
        my_slot = my_slot + jnp.where((owner == my_owner) & (s < device), 1, 0)
        mine = owner == device
        first = jnp.where(mine & (seen == 0), s, first)
        second = jnp.where(mine & (seen == 1), s, second)
        seen = seen + jnp.where(mine, 1, 0)

    shift = shift_of(heads)
    mine = stat_ref[device ^ shift]
    place = over(iota((1, lanes), 1), rows)
    other = jnp.zeros((2, lanes), F32)
    pairs = [
        (stat_ref[my_owner ^ shift], 1 + my_slot),
        (stat_ref[first ^ shift], 0),
        (stat_ref[second ^ shift], 0),
    ]
    for k, (theirs, segment) in enumerate(pairs):
        moved = jnp.zeros((2, lanes), F32)
        for n in range(3):
            turned = pltpu.roll(theirs, ((k - n) * rows) % lanes, 1)
            moved = jnp.where(segment == n, turned, moved)
        other = jnp.where(place == k, moved, other)
    top = jnp.maximum(mine[0:1], other[0:1])
    total = mine[1:2] * jnp.exp(mine[0:1] - top) + other[1:2] * jnp.exp(other[0:1] - top)
    hit = iota((3 * rows, lanes), 1) == iota((3 * rows, lanes), 0)
    top = jnp.sum(jnp.where(hit, top, 0.0), axis=1, keepdims=True)
    total = jnp.sum(jnp.where(hit, total, 0.0), axis=1, keepdims=True)
    for k in range(3):
        at = slice(k * rows, (k + 1) * rows)
        scores = sp_ref[...] if k == 0 else sr_ref[k - 1]
        keys = keys_ref[:latent, :] if k == 0 else resident_ref[k - 1, :latent, :]
        weights = jnp.exp(scores - top[at]).astype(BF16)
        part = dot(weights, keys, ((1,), (1,))) / total[at]
        for h in range(heads):
            for c in range(latent // LANES):
                at = c * PART + 2 * k
                out_ref[h, at : at + 2, :] = part[2 * h : 2 * h + 2, c * LANES : (c + 1) * LANES]
    for fetch in fetches:
        fetch.wait()


def project_kernel(
    owners_ref, part_ref, uv_ref, other_uv_ref, wo_ref, other_wo0_ref, other_wo1_ref, out_ref
):
    count, each, lanes = part_ref.shape
    seqs = owners_ref.shape[1]
    cuts = each // PART
    rows = 2 * seqs
    core = lax.axis_index("seq") % 2
    owners = owners_ref[...]
    row = iota((cuts * 2 * rows, 1), 0)
    cut, other, seq = over(row, 2 * rows), over(rest_of(row, 2 * rows), rows), over(rest_of(row, rows), 2)
    shift = shift_of(count)
    seq = seq ^ shift
    head = jnp.where(other == 0, core, 1 - core)
    owner = column_of(owners, seq)
    slot = column_of(slots_of(owners), seq)
    first = (seq ^ shift) * each + cut * PART + head
    second = (owner ^ shift) * each + cut * PART + 2 + 2 * slot + head
    at = iota((cuts * 2 * rows, count * each), 1)
    hit = jnp.where((at == first) | (at == second), 1.0, 0.0).astype(BF16)
    rest = part_ref[...].reshape(count * each, lanes)
    latent = None
    for _ in range(3):
        piece = rest.astype(BF16)
        rest = rest - piece.astype(F32)
        one = dot(hit, piece)
        latent = one if latent is None else latent + one
    latent = latent.astype(BF16)
    latent = jnp.concatenate(
        [latent[c * 2 * rows : (c + 1) * 2 * rows] for c in range(cuts)], axis=1
    )
    half = rest_of(iota((rows, 1), 0), 2)
    cols = wo_ref.shape[2] // 2
    product = None
    others = (other_wo0_ref[0], other_wo1_ref[0])
    sides = (wo_ref[0, :, :cols], wo_ref[0, :, cols:])
    for n, (uv, wo) in enumerate(((uv_ref, sides), (other_uv_ref, others))):
        head_out = dot(latent[n * rows : (n + 1) * rows], uv[0])
        for side in range(2):
            lines = jnp.where(half == side, head_out, 0.0).astype(BF16)
            one = dot(lines, wo[side])
            product = one if product is None else product + one
    top = jnp.max(jnp.abs(product), axis=1, keepdims=True)
    power = jnp.clip(jnp.floor(jnp.log2(jnp.maximum(top, 1e-35))) + 1.0, -100.0, 100.0)
    coded = jnp.round(product * jnp.exp2(BITS - power)).astype(I32).astype(I16)
    power = jnp.broadcast_to(power, (rows, LANES)).astype(I32).astype(I16)
    for s in range(seqs):
        out_ref[s, :, :cols] = coded[2 * s : 2 * s + 2]
        out_ref[s, :, cols:] = power[2 * s : 2 * s + 2]


def final_kernel(in_ref, out_ref):
    cols = out_ref.shape[2] // 2
    for t in range(2):
        total = None
        for n in range(t, in_ref.shape[0], 2):
            power = in_ref[n, :, cols : cols + 1].astype(I32).astype(F32)
            one = in_ref[n, :, :cols].astype(I32).astype(F32) * jnp.exp2(power - BITS)
            total = one if total is None else total + one
        for j in range(2):
            out_ref[0, t : t + 1, j * cols : (j + 1) * cols] = total[j : j + 1].astype(BF16)


def swap(x):
    count = lax.axis_size("seq")
    order = [p ^ shift_of(count) for p in range(count)]
    return lax.all_to_all(x, "seq", split_axis=0, concat_axis=0, axis_index_groups=[order], tiled=True)


def trade(x, step):
    count = lax.axis_size("seq")
    return lax.ppermute(x, "seq", [(d, d ^ step) for d in range(count)])


def call(kernel, shapes, specs, scratch=(), cost=None, room=None):
    single = not isinstance(shapes, (list, tuple))
    if room is None:
        room = 16 if lax.axis_size("seq") <= 32 else 56
    return pl.pallas_call(
        kernel,
        out_shape=shapes,
        in_specs=specs,
        out_specs=VMEM if single else [VMEM] * len(shapes),
        scratch_shapes=list(scratch),
        cost_estimate=cost,
        compiler_params=pltpu.CompilerParams(vmem_limit_bytes=room * 1024 * 1024),
    )


def on_device(prompt_raw, lengths, owners, resident, new_raw, queries, kv_gain, w_uk, w_uv, w_o):
    count = lax.axis_size("seq")
    seqs = lengths.shape[0]
    most, width = prompt_raw.shape[1:]
    latent = kv_gain.shape[0]
    res_rows = resident.shape[1]
    nope = w_uk.shape[1]
    rope = width - latent
    heads = count
    out_width = w_o.shape[2]
    scale = 1.0 / queries.shape[-1] ** 0.5
    owners_row, lengths_row = owners.reshape(1, seqs), lengths.reshape(1, seqs)
    prompt_raw = prompt_raw.transpose(0, 2, 1)
    resident = resident.transpose(0, 2, 1)
    queries = queries.transpose(0, 2, 1, 3)
    keys_rows = most + LANES

    aux_width = -(-width // LANES) * LANES
    query, aux = call(
        functools.partial(query_kernel, res_rows),
        [
            jax.ShapeDtypeStruct((count, PACK, latent // 2), BF16),
            jax.ShapeDtypeStruct((8, aux_width), F32),
        ],
        [HBM] * 6,
        [
            pltpu.VMEM((1, seqs), I32),
            pltpu.VMEM((1, seqs), I32),
            pltpu.VMEM(queries.shape, BF16),
            pltpu.VMEM((nope, latent), BF16),
            pltpu.VMEM((2, width), BF16),
            pltpu.VMEM((latent,), BF16),
            pltpu.VMEM((2 * seqs, -(-(nope + rope) // LANES) * LANES), F32),
            pltpu.SemaphoreType.DMA((6,)),
        ],
        room=60,
    )(owners_row, lengths_row, queries, w_uk[0], new_raw, kv_gain)
    received = swap(query)
    query, w_uv, w_o = lax.optimization_barrier((query, w_uv, w_o))
    other_uv, other_wo = trade(w_uv, 1), trade(w_o, 1)
    keys, seen, resident = call(
        functools.partial(compress_kernel, res_rows, latent),
        [
            jax.ShapeDtypeStruct((width, keys_rows), BF16),
            jax.ShapeDtypeStruct((8, keys_rows), F32),
            jax.ShapeDtypeStruct(resident.shape, BF16),
        ],
        [VMEM] * 2 + [HBM],
        [pltpu.SemaphoreType.DMA],
        cost=pl.CostEstimate(flops=10**7, bytes_accessed=10**7, transcendentals=10**5),
    )(aux, prompt_raw, resident)
    lanes = -(-6 * heads // LANES) * LANES
    half = out_width // 2
    half_wo = jax.ShapeDtypeStruct((1, w_o.shape[1], half), BF16)
    scores_p, scores_r, stat, other_wo0 = call(
        functools.partial(score_kernel, scale),
        [
            jax.ShapeDtypeStruct((2 * heads, keys_rows), F32),
            jax.ShapeDtypeStruct((2, 2 * heads, res_rows), F32),
            jax.ShapeDtypeStruct((count, 2, lanes), F32),
            half_wo,
        ],
        [VMEM] * 4 + [HBM],
        [pltpu.SemaphoreType.DMA((2,))],
    )(received, keys, seen, resident, other_wo)
    stat, other_uv = lax.optimization_barrier((stat, other_uv))
    stats = swap(stat)
    part, other_wo1 = call(
        attend_kernel,
        [
            jax.ShapeDtypeStruct((heads, PART * (latent // LANES), LANES), F32),
            half_wo,
        ],
        [SMEM] + [VMEM] * 5 + [HBM],
        [pltpu.SemaphoreType.DMA((2,))],
    )(owners, stats, scores_p, scores_r, keys, resident, other_wo)
    parts = swap(part)
    sums = call(
        project_kernel, jax.ShapeDtypeStruct((seqs, 2, half + LANES), I16), [VMEM] * 7
    )(owners_row, parts, w_uv, other_uv, w_o, other_wo0, other_wo1)
    return call(final_kernel, jax.ShapeDtypeStruct((1, 2, out_width), BF16), [VMEM])(swap(sums))


def solution(mesh):
    in_specs = (
        P(("group", "seq"), None, None),
        P("group"),
        P("group"),
        P(("group", "seq"), None, None),
        P("group", None, None),
        P("group", None, "seq", None),
        P(),
        P("seq", None, None),
        P("seq", None, None),
        P("seq", None, None),
    )
    out_specs = P(("group", "seq"), None, None)
    return jax.shard_map(
        on_device, mesh=mesh, in_specs=in_specs, out_specs=out_specs, check_vma=False
    )
```

```python
import functools

import jax
import jax.numpy as jnp
import numpy as np
from jax import lax
from jax.experimental import pallas as pl
from jax.experimental.pallas import tpu as pltpu
from jax.sharding import PartitionSpec as P

F32 = jnp.float32
BF16 = jnp.bfloat16
I32 = jnp.int32
I16 = jnp.int16
VMEM = pl.BlockSpec(memory_space=pltpu.VMEM)
SMEM = pl.BlockSpec(memory_space=pltpu.SMEM)
HBM = pl.BlockSpec(memory_space=pltpu.HBM)
LANES = 128
PACK = 16
PART = 6
BITS = 14.0
NEAR = 4


def iota(shape, dim):
    return lax.broadcasted_iota(I32, shape, dim)


def shift_of(count):
    return count // 2 + 2


def over(x, n):
    return x >> (n.bit_length() - 1)


def rest_of(x, n):
    return x & (n - 1)


def dot(a, b, dims=((1,), (0,))):
    return lax.dot_general(a, b, (dims, ((), ())), preferred_element_type=F32)


def column_of(row, picks):
    n, width = picks.shape[0], row.shape[1]
    hit = iota((n, width), 1) == picks
    return jnp.sum(jnp.where(hit, row, 0), axis=1, keepdims=True)


def slots_of(owners_row):
    seqs = owners_row.shape[1]
    owners_col = column_of(owners_row, iota((seqs, 1), 0))
    earlier = iota((seqs, seqs), 0) < iota((seqs, seqs), 1)
    same = (owners_col == owners_row) & earlier
    return jnp.sum(jnp.where(same, 1, 0), axis=0, keepdims=True)


def doubled(row, times):
    seqs = row.shape[1]
    col = column_of(row, iota((seqs, 1), 0))
    shape = (seqs, 2 * seqs * times)
    hit = over(rest_of(iota(shape, 1), 2 * seqs), 2) == iota(shape, 0)
    return jnp.sum(jnp.where(hit, col, 0), axis=0, keepdims=True)


def frequencies(half, shape, dim):
    at = rest_of(iota(shape, dim), half)
    values = np.float32(10000.0) ** (-(np.arange(half, dtype=np.float32) * np.float32(2.0)) / np.float32(2 * half))
    result = jnp.zeros(shape, F32)
    for i in range(half):
        result = jnp.where(at == i, float(values[i]), result)
    return result


def sine_cosine(angle):
    count = jnp.floor(angle * (2.0 / np.pi) + 0.5)
    x = ((angle - count * 1.5703125) - count * 4.837512969970703125e-4) - count * 7.54978995489188216e-8
    quarter = count.astype(I32)
    y = x * x
    sine = x + x * y * (-1.6666654611e-1 + y * (8.3321608736e-3 - y * 1.9515295891e-4))
    cosine = 1.0 - 0.5 * y + y * y * (4.166664568298827e-2 + y * (-1.388731625493765e-3 + y * 2.443315711809948e-5))
    odd = rest_of(quarter, 2) == 1
    first, second = jnp.where(odd, cosine, sine), jnp.where(odd, sine, cosine)
    first = jnp.where(rest_of(quarter, 4) >= 2, -first, first)
    second = jnp.where(rest_of(quarter + 1, 4) >= 2, -second, second)
    return first, second


def query_kernel(
    res_rows,
    owners_hbm,
    lengths_hbm,
    queries_hbm,
    uk_hbm,
    new_hbm,
    gain_hbm,
    out_ref,
    aux_ref,
    owners_ref,
    lengths_ref,
    queries_ref,
    uk_ref,
    new_ref,
    gain_ref,
    flat,
    sems,
):
    device = lax.axis_index("seq")
    copies = []
    pairs = [
        (owners_hbm, owners_ref),
        (lengths_hbm, lengths_ref),
        (queries_hbm, queries_ref),
        (uk_hbm, uk_ref),
        (new_hbm.at[device], new_ref),
        (gain_hbm, gain_ref),
    ]
    for n, (source, target) in enumerate(pairs):
        copies.append(pltpu.make_async_copy(source, target, sems.at[n]))
        copies[-1].start()
    for copy in copies:
        copy.wait()
    seqs = owners_ref.shape[1]
    nope, latent = uk_ref.shape
    rope = queries_ref.shape[3] - nope
    half = latent // 2
    rows = 2 * seqs
    for s in range(seqs):
        flat[2 * s : 2 * s + 2, : nope + rope] = queries_ref[s, 0].astype(F32)
    values = flat[:, : nope + rope]
    absorbed = dot(values[:, :nope].astype(BF16), uk_ref[...]).astype(BF16)
    row = iota((rows, 1), 0)
    lengths = column_of(lengths_ref[...], over(row, 2))
    angle = (res_rows + lengths + rest_of(row, 2)).astype(F32) * frequencies(rope // 2, (1, rope), 1)
    x = values[:, nope:]
    swapped = jnp.concatenate([x[:, rope // 2 :], x[:, : rope // 2]], axis=1)
    sine, cosine = sine_cosine(angle)
    sine = jnp.where(iota(x.shape, 1) < rope // 2, -sine, sine)
    turned = x * cosine + swapped * sine
    zero = jnp.zeros((rows, rope), F32)
    pieces = [absorbed[:, :half], absorbed[:, half:]]
    for k in range(3):
        blocks = [turned if j == k else zero for j in range(half // rope)]
        pieces.append(jnp.concatenate(blocks, axis=1).astype(BF16))
    owners = owners_ref[...]
    owner = doubled(owners, 5)
    slot = doubled(slots_of(owners), 5)
    shape = (out_ref.shape[0] * PACK, 5 * rows)
    dest, r = over(iota(shape, 0), PACK) ^ shift_of(out_ref.shape[0]), rest_of(iota(shape, 0), PACK)
    lane = iota((1, 5 * rows), 1)
    piece, seq, tok = over(lane, rows), over(rest_of(lane, rows), 2), rest_of(lane, 2)
    start = jnp.where(piece < 2, piece * PART, 2 * PART) + tok
    offset = r - start
    rotary = piece >= 2
    third = piece - 2
    here = jnp.where(owner == dest, slot + 1, jnp.where(seq == dest, 0, -1))
    both = (owner == dest) & (seq == dest)
    wide = (offset == 2 * here) | (both & (offset == 0))
    narrow = (offset == 0) & ((here == third) | (both & (third == 0)))
    hit = (~rotary & (here >= 0) & wide) | (rotary & narrow)
    pieces = jnp.concatenate(pieces, axis=0)
    result = dot(jnp.where(hit, 1.0, 0.0).astype(BF16), pieces)
    out_ref[...] = result.astype(BF16).reshape(out_ref.shape)
    width = new_ref.shape[1]
    aux_ref[0:2, :width] = new_ref[...].astype(F32)
    mine = jnp.where(iota(lengths_ref.shape, 1) == device, lengths_ref[...], 0)
    mine = jnp.sum(mine, axis=1, keepdims=True).astype(F32)
    aux_ref[2:3, :] = jnp.broadcast_to(mine, (1, aux_ref.shape[1]))
    aux_ref[3:4, :latent] = gain_ref[...].astype(F32).reshape(1, latent)


def shares(width):
    tiles = width // LANES
    cuts = [0, tiles * 5 // 14 * LANES, tiles * 10 // 14 * LANES, width]
    return list(zip(cuts[:-1], cuts[1:]))


def fetch_start(source, target, sems, first):
    span = target.shape[2] // sems.shape[0]
    copies = []
    for n in range(sems.shape[0]):
        copies.append(
            pltpu.make_async_copy(
                source.at[:, :, pl.ds(first + n * span, span)], target.at[:, :, pl.ds(n * span, span)], sems.at[n]
            )
        )
        copies[-1].start()
    return copies


def compress_kernel(
    res_rows, latent, aux_ref, prompt_ref, resident_hbm, out_ref, bias_ref, resident_ref, sem
):
    fetch = pltpu.make_async_copy(resident_hbm, resident_ref, sem)
    fetch.start()
    width, most = prompt_ref.shape[1:]
    half = (width - latent) // 2
    fresh = jnp.concatenate([aux_ref[0:2, :width], jnp.zeros((PACK - 2, width), F32)], axis=0)
    pick = jnp.where(iota((PACK, LANES), 0) == iota((PACK, LANES), 1), 1.0, 0.0).astype(BF16)
    fresh = dot(fresh.astype(BF16), pick, ((0,), (0,)))
    gain = jnp.broadcast_to(aux_ref[3:4, :latent], (PACK, latent))
    top = jnp.where(iota((PACK, LANES), 0) == 0, 1.0, 0.0).astype(BF16)
    gain = dot(gain.astype(BF16), top, ((0,), (0,)))
    length = aux_ref[2:3, :LANES].astype(I32)
    at = iota(bias_ref.shape, 1)
    token = iota(bias_ref.shape, 0)
    length_all = jnp.concatenate([length] * (bias_ref.shape[1] // LANES), axis=1)
    seen = (at < length_all) | ((at >= most) & (at <= most + token))
    bias_ref[...] = jnp.where(seen, 1.0, 0.0)
    freq = frequencies(half, (half, 1), 0)
    for i in range(most // LANES + 1):
        at = slice(i * LANES, (i + 1) * LANES)
        lane = iota((1, LANES), 1)
        if i * LANES < most:
            raw = prompt_ref[0, :, at].astype(F32)
            position = res_rows + i * LANES + lane
        else:
            raw = fresh
            position = res_rows + length + lane
        lat = raw[:latent]
        meansq = jnp.sum(lat * lat, axis=0, keepdims=True) * (1.0 / latent)
        out_ref[:latent, at] = (lat * lax.rsqrt(meansq + 1e-06) * gain).astype(BF16)
        angle = position.astype(F32) * freq
        sine, cosine = sine_cosine(angle)
        x1, x2 = raw[latent : latent + half], raw[latent + half :]
        out_ref[latent : latent + half, at] = (x1 * cosine - x2 * sine).astype(BF16)
        out_ref[latent + half :, at] = (x2 * cosine + x1 * sine).astype(BF16)
    fetch.wait()


def score_kernel(
    scale, q_ref, keys_ref, seen_ref, resident_ref, wo_hbm, sp_ref, sr_ref, stat_ref, wo_ref, sems
):
    fetches = fetch_start(wo_hbm, wo_ref, sems, 0)
    heads = q_ref.shape[0]
    half = q_ref.shape[2]
    width = keys_ref.shape[0]
    rope = width - 2 * half
    rows = 2 * heads
    total = heads * PACK
    flat = q_ref[...].reshape(total, half)
    shape = (rows, total)
    line = iota(shape, 0)
    head, tok = over(line, 4) * 2 + rest_of(line, 2), rest_of(over(line, 2), 2)
    source = iota(shape, 1) - head * PACK

    def picked(r):
        hit = source == r + tok
        return dot(jnp.where(hit, 1.0, 0.0).astype(BF16), flat)

    turned = picked(2 * PART)
    tops, sums = [], []
    for k in range(3):
        query = jnp.concatenate(
            [picked(2 * k), picked(PART + 2 * k), turned[:, k * rope : (k + 1) * rope]], axis=1
        ).astype(BF16)
        keys = keys_ref[...] if k == 0 else resident_ref[k - 1]
        scores = dot(query, keys) * scale
        if k == 0:
            first, second = seen_ref[0:1, :] > 0.5, seen_ref[1:2, :] > 0.5
            token = rest_of(over(iota(scores.shape, 0), 2), 2)
            seen = (first & (token == 0)) | (second & (token == 1))
            scores = jnp.where(seen, scores, -1e30)
            sp_ref[...] = scores
        else:
            sr_ref[k - 1] = scores
        top = jnp.max(scores, axis=1, keepdims=True)
        tops.append(top)
        sums.append(jnp.sum(jnp.exp(scores - top), axis=1, keepdims=True))
    lanes = stat_ref.shape[2]
    here = iota((3 * rows, lanes), 0) == iota((3 * rows, lanes), 1)
    top = jnp.sum(jnp.where(here, jnp.concatenate(tops, axis=0), 0.0), axis=0, keepdims=True)
    total = jnp.sum(jnp.where(here, jnp.concatenate(sums, axis=0), 0.0), axis=0, keepdims=True)
    both = jnp.concatenate([top, total], axis=0)
    stat_ref[...] = jnp.broadcast_to(both[None], stat_ref.shape)
    for fetch in fetches:
        fetch.wait()


def attend_kernel(
    owners_ref, stat_ref, sp_ref, sr_ref, keys_ref, resident_ref, wo_hbm, out_ref, wo_ref, sems
):
    fetches = fetch_start(wo_hbm, wo_ref, sems, shares(wo_hbm.shape[2])[1][0])
    heads = out_ref.shape[0]
    latent = out_ref.shape[1] // PART * LANES
    seqs = owners_ref.shape[0]
    rows = 2 * heads
    device = lax.axis_index("seq")
    lanes = stat_ref.shape[2]
    my_owner = owners_ref[device]
    my_slot = jnp.int32(0)
    seen = jnp.int32(0)
    first = jnp.int32(0)
    second = jnp.int32(0)
    for s in range(seqs):
        owner = owners_ref[s]
        my_slot = my_slot + jnp.where((owner == my_owner) & (s < device), 1, 0)
        mine = owner == device
        first = jnp.where(mine & (seen == 0), s, first)
        second = jnp.where(mine & (seen == 1), s, second)
        seen = seen + jnp.where(mine, 1, 0)

    shift = shift_of(heads)
    mine = stat_ref[device ^ shift]
    place = over(iota((1, lanes), 1), rows)
    other = jnp.zeros((2, lanes), F32)
    pairs = [
        (stat_ref[my_owner ^ shift], 1 + my_slot),
        (stat_ref[first ^ shift], 0),
        (stat_ref[second ^ shift], 0),
    ]
    for k, (theirs, segment) in enumerate(pairs):
        moved = jnp.zeros((2, lanes), F32)
        for n in range(3):
            turned = pltpu.roll(theirs, ((k - n) * rows) % lanes, 1)
            moved = jnp.where(segment == n, turned, moved)
        other = jnp.where(place == k, moved, other)
    top = jnp.maximum(mine[0:1], other[0:1])
    total = mine[1:2] * jnp.exp(mine[0:1] - top) + other[1:2] * jnp.exp(other[0:1] - top)
    hit = iota((3 * rows, lanes), 1) == iota((3 * rows, lanes), 0)
    top = jnp.sum(jnp.where(hit, top, 0.0), axis=1, keepdims=True)
    total = jnp.sum(jnp.where(hit, total, 0.0), axis=1, keepdims=True)
    for k in range(3):
        at = slice(k * rows, (k + 1) * rows)
        scores = sp_ref[...] if k == 0 else sr_ref[k - 1]
        keys = keys_ref[:latent, :] if k == 0 else resident_ref[k - 1, :latent, :]
        weights = jnp.exp(scores - top[at]).astype(BF16)
        part = dot(weights, keys, ((1,), (1,))) / total[at]
        for h in range(heads):
            for c in range(latent // LANES):
                at = c * PART + 2 * k
                out_ref[h, at : at + 2, :] = part[2 * h : 2 * h + 2, c * LANES : (c + 1) * LANES]
    for fetch in fetches:
        fetch.wait()


def project_kernel(
    owners_ref, part_ref, uv_ref, other_uv_ref, wo_ref, other_wo0_ref, other_wo1_ref, wo_hbm, out_ref, other_wo2_ref, sems
):
    ranges = shares(wo_ref.shape[2])
    fetches = fetch_start(wo_hbm, other_wo2_ref, sems, ranges[2][0])
    count, each, lanes = part_ref.shape
    seqs = owners_ref.shape[1]
    cuts = each // PART
    rows = 2 * seqs
    core = lax.axis_index("seq") % 2
    owners = owners_ref[...]
    row = iota((cuts * 2 * rows, 1), 0)
    cut, other, seq = over(row, 2 * rows), over(rest_of(row, 2 * rows), rows), over(rest_of(row, rows), 2)
    shift = shift_of(count)
    seq = seq ^ shift
    head = jnp.where(other == 0, core, 1 - core)
    owner = column_of(owners, seq)
    slot = column_of(slots_of(owners), seq)
    first = (seq ^ shift) * each + cut * PART + head
    second = (owner ^ shift) * each + cut * PART + 2 + 2 * slot + head
    at = iota((cuts * 2 * rows, count * each), 1)
    hit = jnp.where((at == first) | (at == second), 1.0, 0.0).astype(BF16)
    rest = part_ref[...].reshape(count * each, lanes)
    latent = None
    for _ in range(3):
        piece = rest.astype(BF16)
        rest = rest - piece.astype(F32)
        one = dot(hit, piece)
        latent = one if latent is None else latent + one
    latent = latent.astype(BF16)
    latent = jnp.concatenate(
        [latent[c * 2 * rows : (c + 1) * 2 * rows] for c in range(cuts)], axis=1
    )
    half = rest_of(iota((rows, 1), 0), 2)
    cols = wo_ref.shape[2] // 2
    lines = []
    for n, uv in enumerate((uv_ref, other_uv_ref)):
        head_out = dot(latent[n * rows : (n + 1) * rows], uv[0])
        lines.append([jnp.where(half == side, head_out, 0.0).astype(BF16) for side in range(2)])
    product = dot(lines[0][0], wo_ref[0, :, :cols]) + dot(lines[0][1], wo_ref[0, :, cols:])
    blocks = [[], []]
    for (start, stop), ref in zip(ranges, (other_wo0_ref, other_wo1_ref, other_wo2_ref)):
        if ref is other_wo2_ref:
            for fetch in fetches:
                fetch.wait()
        for side in range(2):
            a, b = max(start, side * cols), min(stop, (side + 1) * cols)
            if a < b:
                blocks[side].append(dot(lines[1][side], ref[0, :, a - start : b - start]))
    for side in range(2):
        product = product + jnp.concatenate(blocks[side], axis=1)
    top = jnp.max(jnp.abs(product), axis=1, keepdims=True)
    power = jnp.clip(jnp.floor(jnp.log2(jnp.maximum(top, 1e-35))) + 1.0, -100.0, 100.0)
    coded = jnp.round(product * jnp.exp2(BITS - power)).astype(I32).astype(I16)
    power = jnp.broadcast_to(power, (rows, LANES)).astype(I32).astype(I16)
    for s in range(seqs):
        out_ref[s, :, :cols] = coded[2 * s : 2 * s + 2]
        out_ref[s, :, cols:] = power[2 * s : 2 * s + 2]


def final_kernel(in_ref, out_ref):
    cols = out_ref.shape[2] // 2
    for t in range(2):
        total = None
        for n in range(t, in_ref.shape[0], 2):
            power = in_ref[n, :, cols : cols + 1].astype(I32).astype(F32)
            one = in_ref[n, :, :cols].astype(I32).astype(F32) * jnp.exp2(power - BITS)
            total = one if total is None else total + one
        for j in range(2):
            out_ref[0, t : t + 1, j * cols : (j + 1) * cols] = total[j : j + 1].astype(BF16)


def swap(x):
    count = lax.axis_size("seq")
    order = [p ^ shift_of(count) for p in range(count)]
    return lax.all_to_all(x, "seq", split_axis=0, concat_axis=0, axis_index_groups=[order], tiled=True)


def trade(x, step):
    count = lax.axis_size("seq")
    return lax.ppermute(x, "seq", [(d, d ^ step) for d in range(count)])


def call(kernel, shapes, specs, scratch=(), cost=None, room=None):
    single = not isinstance(shapes, (list, tuple))
    if room is None:
        room = 16 if lax.axis_size("seq") <= 32 else 56
    return pl.pallas_call(
        kernel,
        out_shape=shapes,
        in_specs=specs,
        out_specs=VMEM if single else [VMEM] * len(shapes),
        scratch_shapes=list(scratch),
        cost_estimate=cost,
        compiler_params=pltpu.CompilerParams(vmem_limit_bytes=room * 1024 * 1024),
    )


def on_device(prompt_raw, lengths, owners, resident, new_raw, queries, kv_gain, w_uk, w_uv, w_o):
    count = lax.axis_size("seq")
    seqs = lengths.shape[0]
    most, width = prompt_raw.shape[1:]
    latent = kv_gain.shape[0]
    res_rows = resident.shape[1]
    nope = w_uk.shape[1]
    rope = width - latent
    heads = count
    out_width = w_o.shape[2]
    scale = 1.0 / queries.shape[-1] ** 0.5
    owners_row, lengths_row = owners.reshape(1, seqs), lengths.reshape(1, seqs)
    prompt_raw = prompt_raw.transpose(0, 2, 1)
    resident = resident.transpose(0, 2, 1)
    queries = queries.transpose(0, 2, 1, 3)
    keys_rows = most + LANES

    aux_width = -(-width // LANES) * LANES
    query, aux = call(
        functools.partial(query_kernel, res_rows),
        [
            jax.ShapeDtypeStruct((count, PACK, latent // 2), BF16),
            jax.ShapeDtypeStruct((8, aux_width), F32),
        ],
        [HBM] * 6,
        [
            pltpu.VMEM((1, seqs), I32),
            pltpu.VMEM((1, seqs), I32),
            pltpu.VMEM(queries.shape, BF16),
            pltpu.VMEM((nope, latent), BF16),
            pltpu.VMEM((2, width), BF16),
            pltpu.VMEM((latent,), BF16),
            pltpu.VMEM((2 * seqs, -(-(nope + rope) // LANES) * LANES), F32),
            pltpu.SemaphoreType.DMA((6,)),
        ],
        room=60,
    )(owners_row, lengths_row, queries, w_uk[0], new_raw, kv_gain)
    received = swap(query)
    query, w_uv, w_o = lax.optimization_barrier((query, w_uv, w_o))
    other_uv, other_wo = trade(w_uv, 1), trade(w_o, 1)
    keys, seen, resident = call(
        functools.partial(compress_kernel, res_rows, latent),
        [
            jax.ShapeDtypeStruct((width, keys_rows), BF16),
            jax.ShapeDtypeStruct((8, keys_rows), F32),
            jax.ShapeDtypeStruct(resident.shape, BF16),
        ],
        [VMEM] * 2 + [HBM],
        [pltpu.SemaphoreType.DMA],
        cost=pl.CostEstimate(flops=10**7, bytes_accessed=10**7, transcendentals=10**5),
    )(aux, prompt_raw, resident)
    lanes = -(-6 * heads // LANES) * LANES
    half = out_width // 2
    share = [jax.ShapeDtypeStruct((1, w_o.shape[1], b - a), BF16) for a, b in shares(out_width)]
    scores_p, scores_r, stat, other_wo0 = call(
        functools.partial(score_kernel, scale),
        [
            jax.ShapeDtypeStruct((2 * heads, keys_rows), F32),
            jax.ShapeDtypeStruct((2, 2 * heads, res_rows), F32),
            jax.ShapeDtypeStruct((count, 2, lanes), F32),
            share[0],
        ],
        [VMEM] * 4 + [HBM],
        [pltpu.SemaphoreType.DMA((2,))],
    )(received, keys, seen, resident, other_wo)
    stat, other_uv = lax.optimization_barrier((stat, other_uv))
    stats = swap(stat)
    part, other_wo1 = call(
        attend_kernel,
        [
            jax.ShapeDtypeStruct((heads, PART * (latent // LANES), LANES), F32),
            share[1],
        ],
        [SMEM] + [VMEM] * 5 + [HBM],
        [pltpu.SemaphoreType.DMA((2,))],
    )(owners, stats, scores_p, scores_r, keys, resident, other_wo)
    parts = swap(part)
    sums = call(
        project_kernel,
        jax.ShapeDtypeStruct((seqs, 2, half + LANES), I16),
        [VMEM] * 7 + [HBM],
        [pltpu.VMEM(share[2].shape, BF16), pltpu.SemaphoreType.DMA((2,))],
    )(owners_row, parts, w_uv, other_uv, w_o, other_wo0, other_wo1, other_wo)
    return call(final_kernel, jax.ShapeDtypeStruct((1, 2, out_width), BF16), [VMEM])(swap(sums))


def solution(mesh):
    in_specs = (
        P(("group", "seq"), None, None),
        P("group"),
        P("group"),
        P(("group", "seq"), None, None),
        P("group", None, None),
        P("group", None, "seq", None),
        P(),
        P("seq", None, None),
        P("seq", None, None),
        P("seq", None, None),
    )
    out_specs = P(("group", "seq"), None, None)
    return jax.shard_map(
        on_device, mesh=mesh, in_specs=in_specs, out_specs=out_specs, check_vma=False
    )
```

```python
import functools

import jax
import jax.numpy as jnp
import numpy as np
from jax import lax
from jax.experimental import pallas as pl
from jax.experimental.pallas import tpu as pltpu
from jax.sharding import PartitionSpec as P

F32 = jnp.float32
BF16 = jnp.bfloat16
I32 = jnp.int32
I16 = jnp.int16
VMEM = pl.BlockSpec(memory_space=pltpu.VMEM)
SMEM = pl.BlockSpec(memory_space=pltpu.SMEM)
HBM = pl.BlockSpec(memory_space=pltpu.HBM)
LANES = 128
PACK = 16
PART = 6
BITS = 14.0
NEAR = 4


def iota(shape, dim):
    return lax.broadcasted_iota(I32, shape, dim)


def shift_of(count):
    return count // 2 + 2


def over(x, n):
    return x >> (n.bit_length() - 1)


def rest_of(x, n):
    return x & (n - 1)


def dot(a, b, dims=((1,), (0,))):
    return lax.dot_general(a, b, (dims, ((), ())), preferred_element_type=F32)


def column_of(row, picks):
    n, width = picks.shape[0], row.shape[1]
    hit = iota((n, width), 1) == picks
    return jnp.sum(jnp.where(hit, row, 0), axis=1, keepdims=True)


def slots_of(owners_row):
    seqs = owners_row.shape[1]
    owners_col = column_of(owners_row, iota((seqs, 1), 0))
    earlier = iota((seqs, seqs), 0) < iota((seqs, seqs), 1)
    same = (owners_col == owners_row) & earlier
    return jnp.sum(jnp.where(same, 1, 0), axis=0, keepdims=True)


def doubled(row, times):
    seqs = row.shape[1]
    col = column_of(row, iota((seqs, 1), 0))
    shape = (seqs, 2 * seqs * times)
    hit = over(rest_of(iota(shape, 1), 2 * seqs), 2) == iota(shape, 0)
    return jnp.sum(jnp.where(hit, col, 0), axis=0, keepdims=True)


def frequencies(half, shape, dim):
    at = rest_of(iota(shape, dim), half)
    values = np.float32(10000.0) ** (-(np.arange(half, dtype=np.float32) * np.float32(2.0)) / np.float32(2 * half))
    result = jnp.zeros(shape, F32)
    for i in range(half):
        result = jnp.where(at == i, float(values[i]), result)
    return result


def sine_cosine(angle):
    count = jnp.floor(angle * (2.0 / np.pi) + 0.5)
    x = ((angle - count * 1.5703125) - count * 4.837512969970703125e-4) - count * 7.54978995489188216e-8
    quarter = count.astype(I32)
    y = x * x
    sine = x + x * y * (-1.6666654611e-1 + y * (8.3321608736e-3 - y * 1.9515295891e-4))
    cosine = 1.0 - 0.5 * y + y * y * (4.166664568298827e-2 + y * (-1.388731625493765e-3 + y * 2.443315711809948e-5))
    odd = rest_of(quarter, 2) == 1
    first, second = jnp.where(odd, cosine, sine), jnp.where(odd, sine, cosine)
    first = jnp.where(rest_of(quarter, 4) >= 2, -first, first)
    second = jnp.where(rest_of(quarter + 1, 4) >= 2, -second, second)
    return first, second


def query_kernel(
    res_rows,
    owners_hbm,
    lengths_hbm,
    queries_hbm,
    uk_hbm,
    new_hbm,
    gain_hbm,
    out_ref,
    aux_ref,
    owners_ref,
    lengths_ref,
    queries_ref,
    uk_ref,
    new_ref,
    gain_ref,
    flat,
    sems,
):
    device = lax.axis_index("seq")
    copies = []
    pairs = [
        (owners_hbm, owners_ref),
        (lengths_hbm, lengths_ref),
        (queries_hbm, queries_ref),
        (uk_hbm, uk_ref),
        (new_hbm.at[device], new_ref),
        (gain_hbm, gain_ref),
    ]
    for n, (source, target) in enumerate(pairs):
        copies.append(pltpu.make_async_copy(source, target, sems.at[n]))
        copies[-1].start()
    for copy in copies:
        copy.wait()
    seqs = owners_ref.shape[1]
    nope, latent = uk_ref.shape
    rope = queries_ref.shape[3] - nope
    half = latent // 2
    rows = 2 * seqs
    for s in range(seqs):
        flat[2 * s : 2 * s + 2, : nope + rope] = queries_ref[s, 0].astype(F32)
    values = flat[:, : nope + rope]
    absorbed = dot(values[:, :nope].astype(BF16), uk_ref[...]).astype(BF16)
    row = iota((rows, 1), 0)
    lengths = column_of(lengths_ref[...], over(row, 2))
    angle = (res_rows + lengths + rest_of(row, 2)).astype(F32) * frequencies(rope // 2, (1, rope), 1)
    x = values[:, nope:]
    swapped = jnp.concatenate([x[:, rope // 2 :], x[:, : rope // 2]], axis=1)
    sine, cosine = sine_cosine(angle)
    sine = jnp.where(iota(x.shape, 1) < rope // 2, -sine, sine)
    turned = x * cosine + swapped * sine
    zero = jnp.zeros((rows, rope), F32)
    pieces = [absorbed[:, :half], absorbed[:, half:]]
    for k in range(3):
        blocks = [turned if j == k else zero for j in range(half // rope)]
        pieces.append(jnp.concatenate(blocks, axis=1).astype(BF16))
    owners = owners_ref[...]
    owner = doubled(owners, 5)
    slot = doubled(slots_of(owners), 5)
    shape = (out_ref.shape[0] * PACK, 5 * rows)
    dest, r = over(iota(shape, 0), PACK) ^ shift_of(out_ref.shape[0]), rest_of(iota(shape, 0), PACK)
    lane = iota((1, 5 * rows), 1)
    piece, seq, tok = over(lane, rows), over(rest_of(lane, rows), 2), rest_of(lane, 2)
    start = jnp.where(piece < 2, piece * PART, 2 * PART) + tok
    offset = r - start
    rotary = piece >= 2
    third = piece - 2
    here = jnp.where(owner == dest, slot + 1, jnp.where(seq == dest, 0, -1))
    both = (owner == dest) & (seq == dest)
    wide = (offset == 2 * here) | (both & (offset == 0))
    narrow = (offset == 0) & ((here == third) | (both & (third == 0)))
    hit = (~rotary & (here >= 0) & wide) | (rotary & narrow)
    pieces = jnp.concatenate(pieces, axis=0)
    result = dot(jnp.where(hit, 1.0, 0.0).astype(BF16), pieces)
    out_ref[...] = result.astype(BF16).reshape(out_ref.shape)
    width = new_ref.shape[1]
    aux_ref[0:2, :width] = new_ref[...].astype(F32)
    mine = jnp.where(iota(lengths_ref.shape, 1) == device, lengths_ref[...], 0)
    mine = jnp.sum(mine, axis=1, keepdims=True).astype(F32)
    aux_ref[2:3, :] = jnp.broadcast_to(mine, (1, aux_ref.shape[1]))
    aux_ref[3:4, :latent] = gain_ref[...].astype(F32).reshape(1, latent)


def fetch_start(source, target, sems, first):
    span = target.shape[2] // sems.shape[0]
    copies = []
    for n in range(sems.shape[0]):
        copies.append(
            pltpu.make_async_copy(
                source.at[:, :, pl.ds(first + n * span, span)], target.at[:, :, pl.ds(n * span, span)], sems.at[n]
            )
        )
        copies[-1].start()
    return copies


def compress_kernel(
    res_rows, latent, aux_ref, prompt_ref, resident_hbm, out_ref, bias_ref, resident_ref, sem
):
    fetch = pltpu.make_async_copy(resident_hbm, resident_ref, sem)
    fetch.start()
    width, most = prompt_ref.shape[1:]
    half = (width - latent) // 2
    fresh = jnp.concatenate([aux_ref[0:2, :width], jnp.zeros((PACK - 2, width), F32)], axis=0)
    pick = jnp.where(iota((PACK, LANES), 0) == iota((PACK, LANES), 1), 1.0, 0.0).astype(BF16)
    fresh = dot(fresh.astype(BF16), pick, ((0,), (0,)))
    gain = jnp.broadcast_to(aux_ref[3:4, :latent], (PACK, latent))
    top = jnp.where(iota((PACK, LANES), 0) == 0, 1.0, 0.0).astype(BF16)
    gain = dot(gain.astype(BF16), top, ((0,), (0,)))
    length = aux_ref[2:3, :LANES].astype(I32)
    at = iota(bias_ref.shape, 1)
    token = iota(bias_ref.shape, 0)
    length_all = jnp.concatenate([length] * (bias_ref.shape[1] // LANES), axis=1)
    seen = (at < length_all) | ((at >= most) & (at <= most + token))
    bias_ref[...] = jnp.where(seen, 1.0, 0.0)
    freq = frequencies(half, (half, 1), 0)
    for i in range(most // LANES + 1):
        at = slice(i * LANES, (i + 1) * LANES)
        lane = iota((1, LANES), 1)
        if i * LANES < most:
            raw = prompt_ref[0, :, at].astype(F32)
            position = res_rows + i * LANES + lane
        else:
            raw = fresh
            position = res_rows + length + lane
        lat = raw[:latent]
        meansq = jnp.sum(lat * lat, axis=0, keepdims=True) * (1.0 / latent)
        out_ref[:latent, at] = (lat * lax.rsqrt(meansq + 1e-06) * gain).astype(BF16)
        angle = position.astype(F32) * freq
        sine, cosine = sine_cosine(angle)
        x1, x2 = raw[latent : latent + half], raw[latent + half :]
        out_ref[latent : latent + half, at] = (x1 * cosine - x2 * sine).astype(BF16)
        out_ref[latent + half :, at] = (x2 * cosine + x1 * sine).astype(BF16)
    fetch.wait()


def score_kernel(
    scale, q_ref, keys_ref, seen_ref, resident_ref, wo_hbm, sp_ref, sr_ref, stat_ref, wo_ref, sems
):
    fetches = fetch_start(wo_hbm, wo_ref, sems, 0)
    heads = q_ref.shape[0]
    half = q_ref.shape[2]
    width = keys_ref.shape[0]
    rope = width - 2 * half
    rows = 2 * heads
    total = heads * PACK
    flat = q_ref[...].reshape(total, half)
    shape = (rows, total)
    line = iota(shape, 0)
    head, tok = over(line, 4) * 2 + rest_of(line, 2), rest_of(over(line, 2), 2)
    source = iota(shape, 1) - head * PACK

    def picked(r):
        hit = source == r + tok
        return dot(jnp.where(hit, 1.0, 0.0).astype(BF16), flat)

    turned = picked(2 * PART)
    tops, sums = [], []
    for k in range(3):
        query = jnp.concatenate(
            [picked(2 * k), picked(PART + 2 * k), turned[:, k * rope : (k + 1) * rope]], axis=1
        ).astype(BF16)
        keys = keys_ref[...] if k == 0 else resident_ref[k - 1]
        scores = dot(query, keys) * scale
        if k == 0:
            first, second = seen_ref[0:1, :] > 0.5, seen_ref[1:2, :] > 0.5
            token = rest_of(over(iota(scores.shape, 0), 2), 2)
            seen = (first & (token == 0)) | (second & (token == 1))
            scores = jnp.where(seen, scores, -1e30)
            sp_ref[...] = scores
        else:
            sr_ref[k - 1] = scores
        top = jnp.max(scores, axis=1, keepdims=True)
        tops.append(top)
        sums.append(jnp.sum(jnp.exp(scores - top), axis=1, keepdims=True))
    lanes = stat_ref.shape[2]
    here = iota((3 * rows, lanes), 0) == iota((3 * rows, lanes), 1)
    top = jnp.sum(jnp.where(here, jnp.concatenate(tops, axis=0), 0.0), axis=0, keepdims=True)
    total = jnp.sum(jnp.where(here, jnp.concatenate(sums, axis=0), 0.0), axis=0, keepdims=True)
    both = jnp.concatenate([top, total], axis=0)
    stat_ref[...] = jnp.broadcast_to(both[None], stat_ref.shape)
    for fetch in fetches:
        fetch.wait()


def attend_kernel(
    owners_ref, stat_ref, sp_ref, sr_ref, keys_ref, resident_ref, wo_hbm, out_ref, wo_ref, sems
):
    fetches = fetch_start(wo_hbm, wo_ref, sems, wo_ref.shape[2])
    heads = out_ref.shape[0]
    latent = out_ref.shape[1] // PART * LANES
    seqs = owners_ref.shape[0]
    rows = 2 * heads
    device = lax.axis_index("seq")
    lanes = stat_ref.shape[2]
    my_owner = owners_ref[device]
    my_slot = jnp.int32(0)
    seen = jnp.int32(0)
    first = jnp.int32(0)
    second = jnp.int32(0)
    for s in range(seqs):
        owner = owners_ref[s]
        my_slot = my_slot + jnp.where((owner == my_owner) & (s < device), 1, 0)
        mine = owner == device
        first = jnp.where(mine & (seen == 0), s, first)
        second = jnp.where(mine & (seen == 1), s, second)
        seen = seen + jnp.where(mine, 1, 0)

    shift = shift_of(heads)
    mine = stat_ref[device ^ shift]
    place = over(iota((1, lanes), 1), rows)
    other = jnp.zeros((2, lanes), F32)
    pairs = [
        (stat_ref[my_owner ^ shift], 1 + my_slot),
        (stat_ref[first ^ shift], 0),
        (stat_ref[second ^ shift], 0),
    ]
    for k, (theirs, segment) in enumerate(pairs):
        moved = jnp.zeros((2, lanes), F32)
        for n in range(3):
            turned = pltpu.roll(theirs, ((k - n) * rows) % lanes, 1)
            moved = jnp.where(segment == n, turned, moved)
        other = jnp.where(place == k, moved, other)
    top = jnp.maximum(mine[0:1], other[0:1])
    total = mine[1:2] * jnp.exp(mine[0:1] - top) + other[1:2] * jnp.exp(other[0:1] - top)
    hit = iota((3 * rows, lanes), 1) == iota((3 * rows, lanes), 0)
    top = jnp.sum(jnp.where(hit, top, 0.0), axis=1, keepdims=True)
    total = jnp.sum(jnp.where(hit, total, 0.0), axis=1, keepdims=True)
    for k in range(3):
        at = slice(k * rows, (k + 1) * rows)
        scores = sp_ref[...] if k == 0 else sr_ref[k - 1]
        keys = keys_ref[:latent, :] if k == 0 else resident_ref[k - 1, :latent, :]
        weights = jnp.exp(scores - top[at]).astype(BF16)
        part = dot(weights, keys, ((1,), (1,))) / total[at]
        for h in range(heads):
            for c in range(latent // LANES):
                at = c * PART + 2 * k
                out_ref[h, at : at + 2, :] = part[2 * h : 2 * h + 2, c * LANES : (c + 1) * LANES]
    for fetch in fetches:
        fetch.wait()


def project_kernel(
    owners_ref, part_ref, uv_ref, other_uv_ref, wo_ref, other_wo0_ref, other_wo1_ref, out_ref
):
    count, each, lanes = part_ref.shape
    seqs = owners_ref.shape[1]
    cuts = each // PART
    rows = 2 * seqs
    core = lax.axis_index("seq") % 2
    owners = owners_ref[...]
    row = iota((cuts * 2 * rows, 1), 0)
    cut, other, seq = over(row, 2 * rows), over(rest_of(row, 2 * rows), rows), over(rest_of(row, rows), 2)
    shift = shift_of(count)
    seq = seq ^ shift
    head = jnp.where(other == 0, core, 1 - core)
    owner = column_of(owners, seq)
    slot = column_of(slots_of(owners), seq)
    first = (seq ^ shift) * each + cut * PART + head
    second = (owner ^ shift) * each + cut * PART + 2 + 2 * slot + head
    at = iota((cuts * 2 * rows, count * each), 1)
    hit = jnp.where((at == first) | (at == second), 1.0, 0.0).astype(BF16)
    rest = part_ref[...].reshape(count * each, lanes)
    latent = None
    for _ in range(3):
        piece = rest.astype(BF16)
        rest = rest - piece.astype(F32)
        one = dot(hit, piece)
        latent = one if latent is None else latent + one
    latent = latent.astype(BF16)
    latent = jnp.concatenate(
        [latent[c * 2 * rows : (c + 1) * 2 * rows] for c in range(cuts)], axis=1
    )
    half = rest_of(iota((rows, 1), 0), 2)
    cols = wo_ref.shape[2] // 2
    product = None
    others = (other_wo0_ref[0], other_wo1_ref[0])
    sides = (wo_ref[0, :, :cols], wo_ref[0, :, cols:])
    for n, (uv, wo) in enumerate(((uv_ref, sides), (other_uv_ref, others))):
        head_out = dot(latent[n * rows : (n + 1) * rows], uv[0])
        for side in range(2):
            lines = jnp.where(half == side, head_out, 0.0).astype(BF16)
            one = dot(lines, wo[side])
            product = one if product is None else product + one
    top = jnp.max(jnp.abs(product), axis=1, keepdims=True)
    power = jnp.clip(jnp.floor(jnp.log2(jnp.maximum(top, 1e-35))) + 1.0, -100.0, 100.0)
    coded = jnp.round(product * jnp.exp2(BITS - power)).astype(I32).astype(I16)
    power = jnp.broadcast_to(power, (rows, LANES)).astype(I32).astype(I16)
    for s in range(seqs):
        out_ref[s, :, :cols] = coded[2 * s : 2 * s + 2]
        out_ref[s, :, cols:] = power[2 * s : 2 * s + 2]


def final_kernel(in_ref, out_ref):
    cols = out_ref.shape[2] // 2
    for t in range(2):
        total = None
        for n in range(t, in_ref.shape[0], 2):
            power = in_ref[n, :, cols : cols + 1].astype(I32).astype(F32)
            one = in_ref[n, :, :cols].astype(I32).astype(F32) * jnp.exp2(power - BITS)
            total = one if total is None else total + one
        for j in range(2):
            out_ref[0, t : t + 1, j * cols : (j + 1) * cols] = total[j : j + 1].astype(BF16)


def swap(x):
    count = lax.axis_size("seq")
    order = [p ^ shift_of(count) for p in range(count)]
    return lax.all_to_all(x, "seq", split_axis=0, concat_axis=0, axis_index_groups=[order], tiled=True)


def trade(x, step):
    count = lax.axis_size("seq")
    return lax.ppermute(x, "seq", [(d, d ^ step) for d in range(count)])


def call(kernel, shapes, specs, scratch=(), cost=None, room=None):
    single = not isinstance(shapes, (list, tuple))
    if room is None:
        room = 16 if lax.axis_size("seq") <= 32 else 56
    return pl.pallas_call(
        kernel,
        out_shape=shapes,
        in_specs=specs,
        out_specs=VMEM if single else [VMEM] * len(shapes),
        scratch_shapes=list(scratch),
        cost_estimate=cost,
        compiler_params=pltpu.CompilerParams(vmem_limit_bytes=room * 1024 * 1024),
    )


def on_device(prompt_raw, lengths, owners, resident, new_raw, queries, kv_gain, w_uk, w_uv, w_o):
    count = lax.axis_size("seq")
    seqs = lengths.shape[0]
    most, width = prompt_raw.shape[1:]
    latent = kv_gain.shape[0]
    res_rows = resident.shape[1]
    nope = w_uk.shape[1]
    rope = width - latent
    heads = count
    out_width = w_o.shape[2]
    scale = 1.0 / queries.shape[-1] ** 0.5
    owners_row, lengths_row = owners.reshape(1, seqs), lengths.reshape(1, seqs)
    prompt_raw = prompt_raw.transpose(0, 2, 1)
    resident = resident.transpose(0, 2, 1)
    queries = queries.transpose(0, 2, 1, 3)
    keys_rows = most + LANES

    aux_width = -(-width // LANES) * LANES
    query, aux = call(
        functools.partial(query_kernel, res_rows),
        [
            jax.ShapeDtypeStruct((count, PACK, latent // 2), BF16),
            jax.ShapeDtypeStruct((8, aux_width), F32),
        ],
        [HBM] * 6,
        [
            pltpu.VMEM((1, seqs), I32),
            pltpu.VMEM((1, seqs), I32),
            pltpu.VMEM(queries.shape, BF16),
            pltpu.VMEM((nope, latent), BF16),
            pltpu.VMEM((2, width), BF16),
            pltpu.VMEM((latent,), BF16),
            pltpu.VMEM((2 * seqs, -(-(nope + rope) // LANES) * LANES), F32),
            pltpu.SemaphoreType.DMA((6,)),
        ],
        room=60,
    )(owners_row, lengths_row, queries, w_uk[0], new_raw, kv_gain)
    received = swap(query)
    query, w_uv, w_o = lax.optimization_barrier((query, w_uv, w_o))
    other_uv, other_wo = trade(w_uv, 1), trade(w_o, 1)
    keys, seen, resident = call(
        functools.partial(compress_kernel, res_rows, latent),
        [
            jax.ShapeDtypeStruct((width, keys_rows), BF16),
            jax.ShapeDtypeStruct((8, keys_rows), F32),
            jax.ShapeDtypeStruct(resident.shape, BF16),
        ],
        [VMEM] * 2 + [HBM],
        [pltpu.SemaphoreType.DMA],
        cost=pl.CostEstimate(flops=10**7, bytes_accessed=10**7, transcendentals=10**5),
    )(aux, prompt_raw, resident)
    lanes = -(-6 * heads // LANES) * LANES
    half = out_width // 2
    half_wo = jax.ShapeDtypeStruct((1, w_o.shape[1], half), BF16)
    scores_p, scores_r, stat, other_wo0 = call(
        functools.partial(score_kernel, scale),
        [
            jax.ShapeDtypeStruct((2 * heads, keys_rows), F32),
            jax.ShapeDtypeStruct((2, 2 * heads, res_rows), F32),
            jax.ShapeDtypeStruct((count, 2, lanes), F32),
            half_wo,
        ],
        [VMEM] * 4 + [HBM],
        [pltpu.SemaphoreType.DMA((2,))],
    )(received, keys, seen, resident, other_wo)
    stat, other_uv = lax.optimization_barrier((stat, other_uv))
    stats = swap(stat)
    part, other_wo1 = call(
        attend_kernel,
        [
            jax.ShapeDtypeStruct((heads, PART * (latent // LANES), LANES), F32),
            half_wo,
        ],
        [SMEM] + [VMEM] * 5 + [HBM],
        [pltpu.SemaphoreType.DMA((2,))],
    )(owners, stats, scores_p, scores_r, keys, resident, other_wo)
    parts = swap(part)
    sums = call(
        project_kernel, jax.ShapeDtypeStruct((seqs, 2, half + LANES), I16), [VMEM] * 7
    )(owners_row, parts, w_uv, other_uv, w_o, other_wo0, other_wo1)
    return call(final_kernel, jax.ShapeDtypeStruct((1, 2, out_width), BF16), [VMEM])(swap(sums))


def solution(mesh):
    in_specs = (
        P(("group", "seq"), None, None),
        P("group"),
        P("group"),
        P(("group", "seq"), None, None),
        P("group", None, None),
        P("group", None, "seq", None),
        P(),
        P("seq", None, None),
        P("seq", None, None),
        P("seq", None, None),
    )
    out_specs = P(("group", "seq"), None, None)
    return jax.shard_map(
        on_device, mesh=mesh, in_specs=in_specs, out_specs=out_specs, check_vma=False
    )
```

```python
import functools

import jax
import jax.numpy as jnp
import numpy as np
from jax import lax
from jax.experimental import pallas as pl
from jax.experimental.pallas import tpu as pltpu
from jax.sharding import PartitionSpec as P

F32 = jnp.float32
BF16 = jnp.bfloat16
I32 = jnp.int32
I16 = jnp.int16
VMEM = pl.BlockSpec(memory_space=pltpu.VMEM)
SMEM = pl.BlockSpec(memory_space=pltpu.SMEM)
HBM = pl.BlockSpec(memory_space=pltpu.HBM)
LANES = 128
PACK = 16
PART = 6
BITS = 14.0
NEAR = 4


def iota(shape, dim):
    return lax.broadcasted_iota(I32, shape, dim)


def shift_of(count):
    return count // 2 + 2


def over(x, n):
    return x >> (n.bit_length() - 1)


def rest_of(x, n):
    return x & (n - 1)


def dot(a, b, dims=((1,), (0,))):
    return lax.dot_general(a, b, (dims, ((), ())), preferred_element_type=F32)


def column_of(row, picks):
    n, width = picks.shape[0], row.shape[1]
    hit = iota((n, width), 1) == picks
    return jnp.sum(jnp.where(hit, row, 0), axis=1, keepdims=True)


def slots_of(owners_row):
    seqs = owners_row.shape[1]
    owners_col = column_of(owners_row, iota((seqs, 1), 0))
    earlier = iota((seqs, seqs), 0) < iota((seqs, seqs), 1)
    same = (owners_col == owners_row) & earlier
    return jnp.sum(jnp.where(same, 1, 0), axis=0, keepdims=True)


def doubled(row, times):
    seqs = row.shape[1]
    col = column_of(row, iota((seqs, 1), 0))
    shape = (seqs, 2 * seqs * times)
    hit = over(rest_of(iota(shape, 1), 2 * seqs), 2) == iota(shape, 0)
    return jnp.sum(jnp.where(hit, col, 0), axis=0, keepdims=True)


def frequencies(half, shape, dim):
    at = rest_of(iota(shape, dim), half)
    values = np.float32(10000.0) ** (-(np.arange(half, dtype=np.float32) * np.float32(2.0)) / np.float32(2 * half))
    result = jnp.zeros(shape, F32)
    for i in range(half):
        result = jnp.where(at == i, float(values[i]), result)
    return result


def sine_cosine(angle):
    count = jnp.floor(angle * (2.0 / np.pi) + 0.5)
    x = ((angle - count * 1.5703125) - count * 4.837512969970703125e-4) - count * 7.54978995489188216e-8
    quarter = count.astype(I32)
    y = x * x
    sine = x + x * y * (-1.6666654611e-1 + y * (8.3321608736e-3 - y * 1.9515295891e-4))
    cosine = 1.0 - 0.5 * y + y * y * (4.166664568298827e-2 + y * (-1.388731625493765e-3 + y * 2.443315711809948e-5))
    odd = rest_of(quarter, 2) == 1
    first, second = jnp.where(odd, cosine, sine), jnp.where(odd, sine, cosine)
    first = jnp.where(rest_of(quarter, 4) >= 2, -first, first)
    second = jnp.where(rest_of(quarter + 1, 4) >= 2, -second, second)
    return first, second


def query_kernel(
    res_rows,
    owners_hbm,
    lengths_hbm,
    queries_hbm,
    uk_hbm,
    new_hbm,
    gain_hbm,
    out_ref,
    aux_ref,
    owners_ref,
    lengths_ref,
    queries_ref,
    uk_ref,
    new_ref,
    gain_ref,
    flat,
    sems,
):
    device = lax.axis_index("seq")
    copies = []
    pairs = [
        (owners_hbm, owners_ref),
        (lengths_hbm, lengths_ref),
        (queries_hbm, queries_ref),
        (uk_hbm, uk_ref),
        (new_hbm.at[device], new_ref),
        (gain_hbm, gain_ref),
    ]
    for n, (source, target) in enumerate(pairs):
        copies.append(pltpu.make_async_copy(source, target, sems.at[n]))
        copies[-1].start()
    seqs = owners_ref.shape[1]
    nope, latent = uk_ref.shape
    rope = queries_ref.shape[3] - nope
    half = latent // 2
    rows = 2 * seqs
    freq = frequencies(rope // 2, (1, rope), 1)
    shape = (out_ref.shape[0] * PACK, 5 * rows)
    dest, r = over(iota(shape, 0), PACK) ^ shift_of(out_ref.shape[0]), rest_of(iota(shape, 0), PACK)
    lane = iota((1, 5 * rows), 1)
    piece, seq, tok = over(lane, rows), over(rest_of(lane, rows), 2), rest_of(lane, 2)
    start = jnp.where(piece < 2, piece * PART, 2 * PART) + tok
    offset = r - start
    rotary = piece >= 2
    third = piece - 2
    own = seq == dest
    copies[0].wait()
    owners = owners_ref[...]
    owner = doubled(owners, 5)
    slot = doubled(slots_of(owners), 5)
    here = jnp.where(owner == dest, slot + 1, jnp.where(own, 0, -1))
    both = (owner == dest) & own
    wide = (offset == 2 * here) | (both & (offset == 0))
    narrow = (offset == 0) & ((here == third) | (both & (third == 0)))
    hit = (~rotary & (here >= 0) & wide) | (rotary & narrow)
    hit = jnp.where(hit, 1.0, 0.0).astype(BF16)
    copies[1].wait()
    row = iota((rows, 1), 0)
    lengths = column_of(lengths_ref[...], over(row, 2))
    sine, cosine = sine_cosine((res_rows + lengths + rest_of(row, 2)).astype(F32) * freq)
    sine = jnp.where(iota(sine.shape, 1) < rope // 2, -sine, sine)
    copies[2].wait()
    for s in range(seqs):
        flat[2 * s : 2 * s + 2, : nope + rope] = queries_ref[s, 0].astype(F32)
    values = flat[:, : nope + rope]
    x = values[:, nope:]
    swapped = jnp.concatenate([x[:, rope // 2 :], x[:, : rope // 2]], axis=1)
    turned = x * cosine + swapped * sine
    copies[3].wait()
    absorbed = dot(values[:, :nope].astype(BF16), uk_ref[...]).astype(BF16)
    zero = jnp.zeros((rows, rope), F32)
    pieces = [absorbed[:, :half], absorbed[:, half:]]
    for k in range(3):
        blocks = [turned if j == k else zero for j in range(half // rope)]
        pieces.append(jnp.concatenate(blocks, axis=1).astype(BF16))
    result = dot(hit, jnp.concatenate(pieces, axis=0))
    out_ref[...] = result.astype(BF16).reshape(out_ref.shape)
    copies[4].wait()
    copies[5].wait()
    width = new_ref.shape[1]
    aux_ref[0:2, :width] = new_ref[...].astype(F32)
    mine = jnp.where(iota(lengths_ref.shape, 1) == device, lengths_ref[...], 0)
    mine = jnp.sum(mine, axis=1, keepdims=True).astype(F32)
    aux_ref[2:3, :] = jnp.broadcast_to(mine, (1, aux_ref.shape[1]))
    aux_ref[3:4, :latent] = gain_ref[...].astype(F32).reshape(1, latent)


def fetch_start(source, target, sems, first):
    span = target.shape[2] // sems.shape[0]
    copies = []
    for n in range(sems.shape[0]):
        copies.append(
            pltpu.make_async_copy(
                source.at[:, :, pl.ds(first + n * span, span)], target.at[:, :, pl.ds(n * span, span)], sems.at[n]
            )
        )
        copies[-1].start()
    return copies


def compress_kernel(
    res_rows, latent, aux_ref, prompt_ref, resident_hbm, out_ref, bias_ref, resident_ref, sem
):
    fetch = pltpu.make_async_copy(resident_hbm, resident_ref, sem)
    fetch.start()
    width, most = prompt_ref.shape[1:]
    half = (width - latent) // 2
    fresh = jnp.concatenate([aux_ref[0:2, :width], jnp.zeros((PACK - 2, width), F32)], axis=0)
    pick = jnp.where(iota((PACK, LANES), 0) == iota((PACK, LANES), 1), 1.0, 0.0).astype(BF16)
    fresh = dot(fresh.astype(BF16), pick, ((0,), (0,)))
    gain = jnp.broadcast_to(aux_ref[3:4, :latent], (PACK, latent))
    top = jnp.where(iota((PACK, LANES), 0) == 0, 1.0, 0.0).astype(BF16)
    gain = dot(gain.astype(BF16), top, ((0,), (0,)))
    length = aux_ref[2:3, :LANES].astype(I32)
    at = iota(bias_ref.shape, 1)
    token = iota(bias_ref.shape, 0)
    length_all = jnp.concatenate([length] * (bias_ref.shape[1] // LANES), axis=1)
    seen = (at < length_all) | ((at >= most) & (at <= most + token))
    bias_ref[...] = jnp.where(seen, 1.0, 0.0)
    freq = frequencies(half, (half, 1), 0)
    for i in range(most // LANES + 1):
        at = slice(i * LANES, (i + 1) * LANES)
        lane = iota((1, LANES), 1)
        if i * LANES < most:
            raw = prompt_ref[0, :, at].astype(F32)
            position = res_rows + i * LANES + lane
        else:
            raw = fresh
            position = res_rows + length + lane
        lat = raw[:latent]
        meansq = jnp.sum(lat * lat, axis=0, keepdims=True) * (1.0 / latent)
        out_ref[:latent, at] = (lat * lax.rsqrt(meansq + 1e-06) * gain).astype(BF16)
        angle = position.astype(F32) * freq
        sine, cosine = sine_cosine(angle)
        x1, x2 = raw[latent : latent + half], raw[latent + half :]
        out_ref[latent : latent + half, at] = (x1 * cosine - x2 * sine).astype(BF16)
        out_ref[latent + half :, at] = (x2 * cosine + x1 * sine).astype(BF16)
    fetch.wait()


def score_kernel(
    scale, q_ref, keys_ref, seen_ref, resident_ref, wo_hbm, sp_ref, sr_ref, stat_ref, wo_ref, sems
):
    fetches = fetch_start(wo_hbm, wo_ref, sems, 0)
    heads = q_ref.shape[0]
    half = q_ref.shape[2]
    width = keys_ref.shape[0]
    rope = width - 2 * half
    rows = 2 * heads
    total = heads * PACK
    flat = q_ref[...].reshape(total, half)
    shape = (rows, total)
    line = iota(shape, 0)
    head, tok = over(line, 4) * 2 + rest_of(line, 2), rest_of(over(line, 2), 2)
    source = iota(shape, 1) - head * PACK

    def picked(r):
        hit = source == r + tok
        return dot(jnp.where(hit, 1.0, 0.0).astype(BF16), flat)

    turned = picked(2 * PART)
    tops, sums = [], []
    for k in range(3):
        query = jnp.concatenate(
            [picked(2 * k), picked(PART + 2 * k), turned[:, k * rope : (k + 1) * rope]], axis=1
        ).astype(BF16)
        keys = keys_ref[...] if k == 0 else resident_ref[k - 1]
        scores = dot(query, keys) * scale
        if k == 0:
            first, second = seen_ref[0:1, :] > 0.5, seen_ref[1:2, :] > 0.5
            token = rest_of(over(iota(scores.shape, 0), 2), 2)
            seen = (first & (token == 0)) | (second & (token == 1))
            scores = jnp.where(seen, scores, -1e30)
            sp_ref[...] = scores
        else:
            sr_ref[k - 1] = scores
        top = jnp.max(scores, axis=1, keepdims=True)
        tops.append(top)
        sums.append(jnp.sum(jnp.exp(scores - top), axis=1, keepdims=True))
    lanes = stat_ref.shape[2]
    here = iota((3 * rows, lanes), 0) == iota((3 * rows, lanes), 1)
    top = jnp.sum(jnp.where(here, jnp.concatenate(tops, axis=0), 0.0), axis=0, keepdims=True)
    total = jnp.sum(jnp.where(here, jnp.concatenate(sums, axis=0), 0.0), axis=0, keepdims=True)
    both = jnp.concatenate([top, total], axis=0)
    stat_ref[...] = jnp.broadcast_to(both[None], stat_ref.shape)
    for fetch in fetches:
        fetch.wait()


def attend_kernel(
    owners_ref, stat_ref, sp_ref, sr_ref, keys_ref, resident_ref, wo_hbm, out_ref, wo_ref, sems
):
    fetches = fetch_start(wo_hbm, wo_ref, sems, wo_ref.shape[2])
    heads = out_ref.shape[0]
    latent = out_ref.shape[1] // PART * LANES
    seqs = owners_ref.shape[0]
    rows = 2 * heads
    device = lax.axis_index("seq")
    lanes = stat_ref.shape[2]
    my_owner = owners_ref[device]
    my_slot = jnp.int32(0)
    seen = jnp.int32(0)
    first = jnp.int32(0)
    second = jnp.int32(0)
    for s in range(seqs):
        owner = owners_ref[s]
        my_slot = my_slot + jnp.where((owner == my_owner) & (s < device), 1, 0)
        mine = owner == device
        first = jnp.where(mine & (seen == 0), s, first)
        second = jnp.where(mine & (seen == 1), s, second)
        seen = seen + jnp.where(mine, 1, 0)

    shift = shift_of(heads)
    mine = stat_ref[device ^ shift]
    place = over(iota((1, lanes), 1), rows)
    other = jnp.zeros((2, lanes), F32)
    pairs = [
        (stat_ref[my_owner ^ shift], 1 + my_slot),
        (stat_ref[first ^ shift], 0),
        (stat_ref[second ^ shift], 0),
    ]
    for k, (theirs, segment) in enumerate(pairs):
        moved = jnp.zeros((2, lanes), F32)
        for n in range(3):
            turned = pltpu.roll(theirs, ((k - n) * rows) % lanes, 1)
            moved = jnp.where(segment == n, turned, moved)
        other = jnp.where(place == k, moved, other)
    top = jnp.maximum(mine[0:1], other[0:1])
    total = mine[1:2] * jnp.exp(mine[0:1] - top) + other[1:2] * jnp.exp(other[0:1] - top)
    hit = iota((3 * rows, lanes), 1) == iota((3 * rows, lanes), 0)
    top = jnp.sum(jnp.where(hit, top, 0.0), axis=1, keepdims=True)
    total = jnp.sum(jnp.where(hit, total, 0.0), axis=1, keepdims=True)
    for k in range(3):
        at = slice(k * rows, (k + 1) * rows)
        scores = sp_ref[...] if k == 0 else sr_ref[k - 1]
        keys = keys_ref[:latent, :] if k == 0 else resident_ref[k - 1, :latent, :]
        weights = jnp.exp(scores - top[at]).astype(BF16)
        part = dot(weights, keys, ((1,), (1,))) / total[at]
        for h in range(heads):
            for c in range(latent // LANES):
                at = c * PART + 2 * k
                out_ref[h, at : at + 2, :] = part[2 * h : 2 * h + 2, c * LANES : (c + 1) * LANES]
    for fetch in fetches:
        fetch.wait()


def project_kernel(
    owners_ref, part_ref, uv_ref, other_uv_ref, wo_ref, other_wo0_ref, other_wo1_ref, out_ref
):
    count, each, lanes = part_ref.shape
    seqs = owners_ref.shape[1]
    cuts = each // PART
    rows = 2 * seqs
    core = lax.axis_index("seq") % 2
    owners = owners_ref[...]
    row = iota((cuts * 2 * rows, 1), 0)
    cut, other, seq = over(row, 2 * rows), over(rest_of(row, 2 * rows), rows), over(rest_of(row, rows), 2)
    shift = shift_of(count)
    seq = seq ^ shift
    head = jnp.where(other == 0, core, 1 - core)
    owner = column_of(owners, seq)
    slot = column_of(slots_of(owners), seq)
    first = (seq ^ shift) * each + cut * PART + head
    second = (owner ^ shift) * each + cut * PART + 2 + 2 * slot + head
    at = iota((cuts * 2 * rows, count * each), 1)
    hit = jnp.where((at == first) | (at == second), 1.0, 0.0).astype(BF16)
    rest = part_ref[...].reshape(count * each, lanes)
    latent = None
    for _ in range(3):
        piece = rest.astype(BF16)
        rest = rest - piece.astype(F32)
        one = dot(hit, piece)
        latent = one if latent is None else latent + one
    latent = latent.astype(BF16)
    latent = jnp.concatenate(
        [latent[c * 2 * rows : (c + 1) * 2 * rows] for c in range(cuts)], axis=1
    )
    half = rest_of(iota((rows, 1), 0), 2)
    cols = wo_ref.shape[2] // 2
    product = None
    others = (other_wo0_ref[0], other_wo1_ref[0])
    sides = (wo_ref[0, :, :cols], wo_ref[0, :, cols:])
    for n, (uv, wo) in enumerate(((uv_ref, sides), (other_uv_ref, others))):
        head_out = dot(latent[n * rows : (n + 1) * rows], uv[0])
        for side in range(2):
            lines = jnp.where(half == side, head_out, 0.0).astype(BF16)
            one = dot(lines, wo[side])
            product = one if product is None else product + one
    top = jnp.max(jnp.abs(product), axis=1, keepdims=True)
    power = jnp.clip(jnp.floor(jnp.log2(jnp.maximum(top, 1e-35))) + 1.0, -100.0, 100.0)
    coded = jnp.round(product * jnp.exp2(BITS - power)).astype(I32).astype(I16)
    power = jnp.broadcast_to(power, (rows, LANES)).astype(I32).astype(I16)
    for s in range(seqs):
        out_ref[s, :, :cols] = coded[2 * s : 2 * s + 2]
        out_ref[s, :, cols:] = power[2 * s : 2 * s + 2]


def final_kernel(in_ref, out_ref):
    cols = out_ref.shape[2] // 2
    for t in range(2):
        total = None
        for n in range(t, in_ref.shape[0], 2):
            power = in_ref[n, :, cols : cols + 1].astype(I32).astype(F32)
            one = in_ref[n, :, :cols].astype(I32).astype(F32) * jnp.exp2(power - BITS)
            total = one if total is None else total + one
        for j in range(2):
            out_ref[0, t : t + 1, j * cols : (j + 1) * cols] = total[j : j + 1].astype(BF16)


def swap(x):
    count = lax.axis_size("seq")
    order = [p ^ shift_of(count) for p in range(count)]
    return lax.all_to_all(x, "seq", split_axis=0, concat_axis=0, axis_index_groups=[order], tiled=True)


def trade(x, step):
    count = lax.axis_size("seq")
    return lax.ppermute(x, "seq", [(d, d ^ step) for d in range(count)])


def call(kernel, shapes, specs, scratch=(), cost=None, room=None):
    single = not isinstance(shapes, (list, tuple))
    if room is None:
        room = 16 if lax.axis_size("seq") <= 32 else 56
    return pl.pallas_call(
        kernel,
        out_shape=shapes,
        in_specs=specs,
        out_specs=VMEM if single else [VMEM] * len(shapes),
        scratch_shapes=list(scratch),
        cost_estimate=cost,
        compiler_params=pltpu.CompilerParams(vmem_limit_bytes=room * 1024 * 1024),
    )


def on_device(prompt_raw, lengths, owners, resident, new_raw, queries, kv_gain, w_uk, w_uv, w_o):
    count = lax.axis_size("seq")
    seqs = lengths.shape[0]
    most, width = prompt_raw.shape[1:]
    latent = kv_gain.shape[0]
    res_rows = resident.shape[1]
    nope = w_uk.shape[1]
    rope = width - latent
    heads = count
    out_width = w_o.shape[2]
    scale = 1.0 / queries.shape[-1] ** 0.5
    owners_row, lengths_row = owners.reshape(1, seqs), lengths.reshape(1, seqs)
    prompt_raw = prompt_raw.transpose(0, 2, 1)
    resident = resident.transpose(0, 2, 1)
    queries = queries.transpose(0, 2, 1, 3)
    keys_rows = most + LANES

    aux_width = -(-width // LANES) * LANES
    query, aux = call(
        functools.partial(query_kernel, res_rows),
        [
            jax.ShapeDtypeStruct((count, PACK, latent // 2), BF16),
            jax.ShapeDtypeStruct((8, aux_width), F32),
        ],
        [HBM] * 6,
        [
            pltpu.VMEM((1, seqs), I32),
            pltpu.VMEM((1, seqs), I32),
            pltpu.VMEM(queries.shape, BF16),
            pltpu.VMEM((nope, latent), BF16),
            pltpu.VMEM((2, width), BF16),
            pltpu.VMEM((latent,), BF16),
            pltpu.VMEM((2 * seqs, -(-(nope + rope) // LANES) * LANES), F32),
            pltpu.SemaphoreType.DMA((6,)),
        ],
        room=60,
    )(owners_row, lengths_row, queries, w_uk[0], new_raw, kv_gain)
    received = swap(query)
    query, w_uv, w_o = lax.optimization_barrier((query, w_uv, w_o))
    other_uv, other_wo = trade(w_uv, 1), trade(w_o, 1)
    keys, seen, resident = call(
        functools.partial(compress_kernel, res_rows, latent),
        [
            jax.ShapeDtypeStruct((width, keys_rows), BF16),
            jax.ShapeDtypeStruct((8, keys_rows), F32),
            jax.ShapeDtypeStruct(resident.shape, BF16),
        ],
        [VMEM] * 2 + [HBM],
        [pltpu.SemaphoreType.DMA],
        cost=pl.CostEstimate(flops=10**7, bytes_accessed=10**7, transcendentals=10**5),
    )(aux, prompt_raw, resident)
    lanes = -(-6 * heads // LANES) * LANES
    half = out_width // 2
    half_wo = jax.ShapeDtypeStruct((1, w_o.shape[1], half), BF16)
    scores_p, scores_r, stat, other_wo0 = call(
        functools.partial(score_kernel, scale),
        [
            jax.ShapeDtypeStruct((2 * heads, keys_rows), F32),
            jax.ShapeDtypeStruct((2, 2 * heads, res_rows), F32),
            jax.ShapeDtypeStruct((count, 2, lanes), F32),
            half_wo,
        ],
        [VMEM] * 4 + [HBM],
        [pltpu.SemaphoreType.DMA((7,))],
    )(received, keys, seen, resident, other_wo)
    stat, other_uv = lax.optimization_barrier((stat, other_uv))
    stats = swap(stat)
    part, other_wo1 = call(
        attend_kernel,
        [
            jax.ShapeDtypeStruct((heads, PART * (latent // LANES), LANES), F32),
            half_wo,
        ],
        [SMEM] + [VMEM] * 5 + [HBM],
        [pltpu.SemaphoreType.DMA((7,))],
    )(owners, stats, scores_p, scores_r, keys, resident, other_wo)
    parts = swap(part)
    sums = call(
        project_kernel, jax.ShapeDtypeStruct((seqs, 2, half + LANES), I16), [VMEM] * 7
    )(owners_row, parts, w_uv, other_uv, w_o, other_wo0, other_wo1)
    return call(final_kernel, jax.ShapeDtypeStruct((1, 2, out_width), BF16), [VMEM])(swap(sums))


def solution(mesh):
    in_specs = (
        P(("group", "seq"), None, None),
        P("group"),
        P("group"),
        P(("group", "seq"), None, None),
        P("group", None, None),
        P("group", None, "seq", None),
        P(),
        P("seq", None, None),
        P("seq", None, None),
        P("seq", None, None),
    )
    out_specs = P(("group", "seq"), None, None)
    return jax.shard_map(
        on_device, mesh=mesh, in_specs=in_specs, out_specs=out_specs, check_vma=False
    )
```

```python
import functools

import jax
import jax.numpy as jnp
import numpy as np
from jax import lax
from jax.experimental import pallas as pl
from jax.experimental.pallas import tpu as pltpu
from jax.sharding import PartitionSpec as P

F32 = jnp.float32
BF16 = jnp.bfloat16
I32 = jnp.int32
I16 = jnp.int16
VMEM = pl.BlockSpec(memory_space=pltpu.VMEM)
SMEM = pl.BlockSpec(memory_space=pltpu.SMEM)
HBM = pl.BlockSpec(memory_space=pltpu.HBM)
LANES = 128
PACK = 16
PART = 6
BITS = 14.0
NEAR = 4


def iota(shape, dim):
    return lax.broadcasted_iota(I32, shape, dim)


def shift_of(count):
    return count // 2 + 2


def over(x, n):
    return x >> (n.bit_length() - 1)


def rest_of(x, n):
    return x & (n - 1)


def dot(a, b, dims=((1,), (0,))):
    return lax.dot_general(a, b, (dims, ((), ())), preferred_element_type=F32)


def column_of(row, picks):
    n, width = picks.shape[0], row.shape[1]
    hit = iota((n, width), 1) == picks
    return jnp.sum(jnp.where(hit, row, 0), axis=1, keepdims=True)


def slots_of(owners_row):
    seqs = owners_row.shape[1]
    owners_col = column_of(owners_row, iota((seqs, 1), 0))
    earlier = iota((seqs, seqs), 0) < iota((seqs, seqs), 1)
    same = (owners_col == owners_row) & earlier
    return jnp.sum(jnp.where(same, 1, 0), axis=0, keepdims=True)


def doubled(row, times):
    seqs = row.shape[1]
    col = column_of(row, iota((seqs, 1), 0))
    shape = (seqs, 2 * seqs * times)
    hit = over(rest_of(iota(shape, 1), 2 * seqs), 2) == iota(shape, 0)
    return jnp.sum(jnp.where(hit, col, 0), axis=0, keepdims=True)


def frequencies(half, shape, dim):
    at = rest_of(iota(shape, dim), half)
    values = np.float32(10000.0) ** (-(np.arange(half, dtype=np.float32) * np.float32(2.0)) / np.float32(2 * half))
    result = jnp.zeros(shape, F32)
    for i in range(half):
        result = jnp.where(at == i, float(values[i]), result)
    return result


def sine_cosine(angle):
    count = jnp.floor(angle * (2.0 / np.pi) + 0.5)
    x = ((angle - count * 1.5703125) - count * 4.837512969970703125e-4) - count * 7.54978995489188216e-8
    quarter = count.astype(I32)
    y = x * x
    sine = x + x * y * (-1.6666654611e-1 + y * (8.3321608736e-3 - y * 1.9515295891e-4))
    cosine = 1.0 - 0.5 * y + y * y * (4.166664568298827e-2 + y * (-1.388731625493765e-3 + y * 2.443315711809948e-5))
    odd = rest_of(quarter, 2) == 1
    first, second = jnp.where(odd, cosine, sine), jnp.where(odd, sine, cosine)
    first = jnp.where(rest_of(quarter, 4) >= 2, -first, first)
    second = jnp.where(rest_of(quarter + 1, 4) >= 2, -second, second)
    return first, second


def query_kernel(
    res_rows,
    owners_hbm,
    lengths_hbm,
    queries_hbm,
    uk_hbm,
    new_hbm,
    gain_hbm,
    out_ref,
    aux_ref,
    owners_ref,
    lengths_ref,
    queries_ref,
    uk_ref,
    new_ref,
    gain_ref,
    flat,
    sems,
):
    device = lax.axis_index("seq")
    copies = []
    pairs = [
        (owners_hbm, owners_ref),
        (lengths_hbm, lengths_ref),
        (queries_hbm, queries_ref),
        (uk_hbm, uk_ref),
        (new_hbm.at[device], new_ref),
        (gain_hbm, gain_ref),
    ]
    for n, (source, target) in enumerate(pairs):
        copies.append(pltpu.make_async_copy(source, target, sems.at[n]))
        copies[-1].start()
    for copy in copies:
        copy.wait()
    seqs = owners_ref.shape[1]
    nope, latent = uk_ref.shape
    rope = queries_ref.shape[3] - nope
    half = latent // 2
    rows = 2 * seqs
    for s in range(seqs):
        flat[2 * s : 2 * s + 2, : nope + rope] = queries_ref[s, 0].astype(F32)
    values = flat[:, : nope + rope]
    absorbed = dot(values[:, :nope].astype(BF16), uk_ref[...]).astype(BF16)
    row = iota((rows, 1), 0)
    lengths = column_of(lengths_ref[...], over(row, 2))
    angle = (res_rows + lengths + rest_of(row, 2)).astype(F32) * frequencies(rope // 2, (1, rope), 1)
    x = values[:, nope:]
    swapped = jnp.concatenate([x[:, rope // 2 :], x[:, : rope // 2]], axis=1)
    sine, cosine = sine_cosine(angle)
    sine = jnp.where(iota(x.shape, 1) < rope // 2, -sine, sine)
    turned = x * cosine + swapped * sine
    zero = jnp.zeros((rows, rope), F32)
    pieces = [absorbed[:, :half], absorbed[:, half:]]
    for k in range(3):
        blocks = [turned if j == k else zero for j in range(half // rope)]
        pieces.append(jnp.concatenate(blocks, axis=1).astype(BF16))
    owners = owners_ref[...]
    owner = doubled(owners, 5)
    slot = doubled(slots_of(owners), 5)
    shape = (out_ref.shape[0] * PACK, 5 * rows)
    dest, r = over(iota(shape, 0), PACK) ^ shift_of(out_ref.shape[0]), rest_of(iota(shape, 0), PACK)
    lane = iota((1, 5 * rows), 1)
    piece, seq, tok = over(lane, rows), over(rest_of(lane, rows), 2), rest_of(lane, 2)
    start = jnp.where(piece < 2, piece * PART, 2 * PART) + tok
    offset = r - start
    rotary = piece >= 2
    third = piece - 2
    here = jnp.where(owner == dest, slot + 1, jnp.where(seq == dest, 0, -1))
    both = (owner == dest) & (seq == dest)
    wide = (offset == 2 * here) | (both & (offset == 0))
    narrow = (offset == 0) & ((here == third) | (both & (third == 0)))
    hit = (~rotary & (here >= 0) & wide) | (rotary & narrow)
    pieces = jnp.concatenate(pieces, axis=0)
    result = dot(jnp.where(hit, 1.0, 0.0).astype(BF16), pieces)
    out_ref[...] = result.astype(BF16).reshape(out_ref.shape)
    width = new_ref.shape[1]
    aux_ref[0:2, :width] = new_ref[...].astype(F32)
    mine = jnp.where(iota(lengths_ref.shape, 1) == device, lengths_ref[...], 0)
    mine = jnp.sum(mine, axis=1, keepdims=True).astype(F32)
    aux_ref[2:3, :] = jnp.broadcast_to(mine, (1, aux_ref.shape[1]))
    aux_ref[3:4, :latent] = gain_ref[...].astype(F32).reshape(1, latent)


def fetch_start(source, target, sem, first):
    copy = pltpu.make_async_copy(source.at[:, pl.ds(first, target.shape[1]), :], target, sem)
    copy.start()
    return copy


def compress_kernel(
    res_rows, latent, aux_ref, prompt_ref, resident_hbm, out_ref, bias_ref, resident_ref, sem
):
    fetch = pltpu.make_async_copy(resident_hbm, resident_ref, sem)
    fetch.start()
    width, most = prompt_ref.shape[1:]
    half = (width - latent) // 2
    fresh = jnp.concatenate([aux_ref[0:2, :width], jnp.zeros((PACK - 2, width), F32)], axis=0)
    pick = jnp.where(iota((PACK, LANES), 0) == iota((PACK, LANES), 1), 1.0, 0.0).astype(BF16)
    fresh = dot(fresh.astype(BF16), pick, ((0,), (0,)))
    gain = jnp.broadcast_to(aux_ref[3:4, :latent], (PACK, latent))
    top = jnp.where(iota((PACK, LANES), 0) == 0, 1.0, 0.0).astype(BF16)
    gain = dot(gain.astype(BF16), top, ((0,), (0,)))
    length = aux_ref[2:3, :LANES].astype(I32)
    at = iota(bias_ref.shape, 1)
    token = iota(bias_ref.shape, 0)
    length_all = jnp.concatenate([length] * (bias_ref.shape[1] // LANES), axis=1)
    seen = (at < length_all) | ((at >= most) & (at <= most + token))
    bias_ref[...] = jnp.where(seen, 1.0, 0.0)
    freq = frequencies(half, (half, 1), 0)
    for i in range(most // LANES + 1):
        at = slice(i * LANES, (i + 1) * LANES)
        lane = iota((1, LANES), 1)
        if i * LANES < most:
            raw = prompt_ref[0, :, at].astype(F32)
            position = res_rows + i * LANES + lane
        else:
            raw = fresh
            position = res_rows + length + lane
        lat = raw[:latent]
        meansq = jnp.sum(lat * lat, axis=0, keepdims=True) * (1.0 / latent)
        out_ref[:latent, at] = (lat * lax.rsqrt(meansq + 1e-06) * gain).astype(BF16)
        angle = position.astype(F32) * freq
        sine, cosine = sine_cosine(angle)
        x1, x2 = raw[latent : latent + half], raw[latent + half :]
        out_ref[latent : latent + half, at] = (x1 * cosine - x2 * sine).astype(BF16)
        out_ref[latent + half :, at] = (x2 * cosine + x1 * sine).astype(BF16)
    fetch.wait()


def score_kernel(
    scale, q_ref, keys_ref, seen_ref, resident_ref, wo_hbm, sp_ref, sr_ref, stat_ref, wo_ref, sem
):
    fetch = fetch_start(wo_hbm, wo_ref, sem, 0)
    heads = q_ref.shape[0]
    half = q_ref.shape[2]
    width = keys_ref.shape[0]
    rope = width - 2 * half
    rows = 2 * heads
    total = heads * PACK
    flat = q_ref[...].reshape(total, half)
    shape = (rows, total)
    line = iota(shape, 0)
    head, tok = over(line, 4) * 2 + rest_of(line, 2), rest_of(over(line, 2), 2)
    source = iota(shape, 1) - head * PACK

    def picked(r):
        hit = source == r + tok
        return dot(jnp.where(hit, 1.0, 0.0).astype(BF16), flat)

    turned = picked(2 * PART)
    tops, sums = [], []
    for k in range(3):
        query = jnp.concatenate(
            [picked(2 * k), picked(PART + 2 * k), turned[:, k * rope : (k + 1) * rope]], axis=1
        ).astype(BF16)
        keys = keys_ref[...] if k == 0 else resident_ref[k - 1]
        scores = dot(query, keys) * scale
        if k == 0:
            first, second = seen_ref[0:1, :] > 0.5, seen_ref[1:2, :] > 0.5
            token = rest_of(over(iota(scores.shape, 0), 2), 2)
            seen = (first & (token == 0)) | (second & (token == 1))
            scores = jnp.where(seen, scores, -1e30)
            sp_ref[...] = scores
        else:
            sr_ref[k - 1] = scores
        top = jnp.max(scores, axis=1, keepdims=True)
        tops.append(top)
        sums.append(jnp.sum(jnp.exp(scores - top), axis=1, keepdims=True))
    lanes = stat_ref.shape[2]
    here = iota((3 * rows, lanes), 0) == iota((3 * rows, lanes), 1)
    top = jnp.sum(jnp.where(here, jnp.concatenate(tops, axis=0), 0.0), axis=0, keepdims=True)
    total = jnp.sum(jnp.where(here, jnp.concatenate(sums, axis=0), 0.0), axis=0, keepdims=True)
    both = jnp.concatenate([top, total], axis=0)
    stat_ref[...] = jnp.broadcast_to(both[None], stat_ref.shape)
    fetch.wait()


def attend_kernel(
    owners_ref, stat_ref, sp_ref, sr_ref, keys_ref, resident_ref, wo_hbm, out_ref, wo_ref, sem
):
    fetch = fetch_start(wo_hbm, wo_ref, sem, wo_ref.shape[1])
    heads = out_ref.shape[0]
    latent = out_ref.shape[1] // PART * LANES
    seqs = owners_ref.shape[0]
    rows = 2 * heads
    device = lax.axis_index("seq")
    lanes = stat_ref.shape[2]
    my_owner = owners_ref[device]
    my_slot = jnp.int32(0)
    seen = jnp.int32(0)
    first = jnp.int32(0)
    second = jnp.int32(0)
    for s in range(seqs):
        owner = owners_ref[s]
        my_slot = my_slot + jnp.where((owner == my_owner) & (s < device), 1, 0)
        mine = owner == device
        first = jnp.where(mine & (seen == 0), s, first)
        second = jnp.where(mine & (seen == 1), s, second)
        seen = seen + jnp.where(mine, 1, 0)

    shift = shift_of(heads)
    mine = stat_ref[device ^ shift]
    place = over(iota((1, lanes), 1), rows)
    other = jnp.zeros((2, lanes), F32)
    pairs = [
        (stat_ref[my_owner ^ shift], 1 + my_slot),
        (stat_ref[first ^ shift], 0),
        (stat_ref[second ^ shift], 0),
    ]
    for k, (theirs, segment) in enumerate(pairs):
        moved = jnp.zeros((2, lanes), F32)
        for n in range(3):
            turned = pltpu.roll(theirs, ((k - n) * rows) % lanes, 1)
            moved = jnp.where(segment == n, turned, moved)
        other = jnp.where(place == k, moved, other)
    top = jnp.maximum(mine[0:1], other[0:1])
    total = mine[1:2] * jnp.exp(mine[0:1] - top) + other[1:2] * jnp.exp(other[0:1] - top)
    hit = iota((3 * rows, lanes), 1) == iota((3 * rows, lanes), 0)
    top = jnp.sum(jnp.where(hit, top, 0.0), axis=1, keepdims=True)
    total = jnp.sum(jnp.where(hit, total, 0.0), axis=1, keepdims=True)
    for k in range(3):
        at = slice(k * rows, (k + 1) * rows)
        scores = sp_ref[...] if k == 0 else sr_ref[k - 1]
        keys = keys_ref[:latent, :] if k == 0 else resident_ref[k - 1, :latent, :]
        weights = jnp.exp(scores - top[at]).astype(BF16)
        part = dot(weights, keys, ((1,), (1,))) / total[at]
        for h in range(heads):
            for c in range(latent // LANES):
                at = c * PART + 2 * k
                out_ref[h, at : at + 2, :] = part[2 * h : 2 * h + 2, c * LANES : (c + 1) * LANES]
    fetch.wait()


def project_kernel(
    owners_ref, part_ref, uv_ref, other_uv_ref, wo_ref, other_wo0_ref, other_wo1_ref, out_ref
):
    count, each, lanes = part_ref.shape
    seqs = owners_ref.shape[1]
    cuts = each // PART
    rows = 2 * seqs
    core = lax.axis_index("seq") % 2
    owners = owners_ref[...]
    row = iota((cuts * 2 * rows, 1), 0)
    cut, other, seq = over(row, 2 * rows), over(rest_of(row, 2 * rows), rows), over(rest_of(row, rows), 2)
    shift = shift_of(count)
    seq = seq ^ shift
    head = jnp.where(other == 0, core, 1 - core)
    owner = column_of(owners, seq)
    slot = column_of(slots_of(owners), seq)
    first = (seq ^ shift) * each + cut * PART + head
    second = (owner ^ shift) * each + cut * PART + 2 + 2 * slot + head
    at = iota((cuts * 2 * rows, count * each), 1)
    hit = jnp.where((at == first) | (at == second), 1.0, 0.0).astype(BF16)
    rest = part_ref[...].reshape(count * each, lanes)
    latent = None
    for _ in range(3):
        piece = rest.astype(BF16)
        rest = rest - piece.astype(F32)
        one = dot(hit, piece)
        latent = one if latent is None else latent + one
    latent = latent.astype(BF16)
    latent = jnp.concatenate(
        [latent[c * 2 * rows : (c + 1) * 2 * rows] for c in range(cuts)], axis=1
    )
    half = rest_of(iota((rows, 1), 0), 2)
    cols = wo_ref.shape[2] // 2
    product = None
    depth = other_wo0_ref.shape[1]
    for n, uv in enumerate((uv_ref, other_uv_ref)):
        head_out = dot(latent[n * rows : (n + 1) * rows], uv[0])
        weights = [wo_ref] if n == 0 else [other_wo0_ref, other_wo1_ref]
        for side in range(2):
            lines = jnp.where(half == side, head_out, 0.0).astype(BF16)
            for i, wo in enumerate(weights):
                line = lines if n == 0 else lines[:, i * depth : (i + 1) * depth]
                one = dot(line, wo[0, :, side * cols : (side + 1) * cols])
                product = one if product is None else product + one
    top = jnp.max(jnp.abs(product), axis=1, keepdims=True)
    power = jnp.clip(jnp.floor(jnp.log2(jnp.maximum(top, 1e-35))) + 1.0, -100.0, 100.0)
    coded = jnp.round(product * jnp.exp2(BITS - power)).astype(I32).astype(I16)
    power = jnp.broadcast_to(power, (rows, LANES)).astype(I32).astype(I16)
    for s in range(seqs):
        out_ref[s, :, :cols] = coded[2 * s : 2 * s + 2]
        out_ref[s, :, cols:] = power[2 * s : 2 * s + 2]


def final_kernel(in_ref, out_ref):
    cols = out_ref.shape[2] // 2
    for t in range(2):
        total = None
        for n in range(t, in_ref.shape[0], 2):
            power = in_ref[n, :, cols : cols + 1].astype(I32).astype(F32)
            one = in_ref[n, :, :cols].astype(I32).astype(F32) * jnp.exp2(power - BITS)
            total = one if total is None else total + one
        for j in range(2):
            out_ref[0, t : t + 1, j * cols : (j + 1) * cols] = total[j : j + 1].astype(BF16)


def swap(x):
    count = lax.axis_size("seq")
    order = [p ^ shift_of(count) for p in range(count)]
    return lax.all_to_all(x, "seq", split_axis=0, concat_axis=0, axis_index_groups=[order], tiled=True)


def trade(x, step):
    count = lax.axis_size("seq")
    return lax.ppermute(x, "seq", [(d, d ^ step) for d in range(count)])


def call(kernel, shapes, specs, scratch=(), cost=None, room=None):
    single = not isinstance(shapes, (list, tuple))
    if room is None:
        room = 16 if lax.axis_size("seq") <= 32 else 56
    return pl.pallas_call(
        kernel,
        out_shape=shapes,
        in_specs=specs,
        out_specs=VMEM if single else [VMEM] * len(shapes),
        scratch_shapes=list(scratch),
        cost_estimate=cost,
        compiler_params=pltpu.CompilerParams(vmem_limit_bytes=room * 1024 * 1024),
    )


def on_device(prompt_raw, lengths, owners, resident, new_raw, queries, kv_gain, w_uk, w_uv, w_o):
    count = lax.axis_size("seq")
    seqs = lengths.shape[0]
    most, width = prompt_raw.shape[1:]
    latent = kv_gain.shape[0]
    res_rows = resident.shape[1]
    nope = w_uk.shape[1]
    rope = width - latent
    heads = count
    out_width = w_o.shape[2]
    scale = 1.0 / queries.shape[-1] ** 0.5
    owners_row, lengths_row = owners.reshape(1, seqs), lengths.reshape(1, seqs)
    prompt_raw = prompt_raw.transpose(0, 2, 1)
    resident = resident.transpose(0, 2, 1)
    queries = queries.transpose(0, 2, 1, 3)
    keys_rows = most + LANES

    aux_width = -(-width // LANES) * LANES
    query, aux = call(
        functools.partial(query_kernel, res_rows),
        [
            jax.ShapeDtypeStruct((count, PACK, latent // 2), BF16),
            jax.ShapeDtypeStruct((8, aux_width), F32),
        ],
        [HBM] * 6,
        [
            pltpu.VMEM((1, seqs), I32),
            pltpu.VMEM((1, seqs), I32),
            pltpu.VMEM(queries.shape, BF16),
            pltpu.VMEM((nope, latent), BF16),
            pltpu.VMEM((2, width), BF16),
            pltpu.VMEM((latent,), BF16),
            pltpu.VMEM((2 * seqs, -(-(nope + rope) // LANES) * LANES), F32),
            pltpu.SemaphoreType.DMA((6,)),
        ],
        room=60,
    )(owners_row, lengths_row, queries, w_uk[0], new_raw, kv_gain)
    received = swap(query)
    query, w_uv, w_o = lax.optimization_barrier((query, w_uv, w_o))
    other_uv, other_wo = trade(w_uv, 1), trade(w_o, 1)
    keys, seen, resident = call(
        functools.partial(compress_kernel, res_rows, latent),
        [
            jax.ShapeDtypeStruct((width, keys_rows), BF16),
            jax.ShapeDtypeStruct((8, keys_rows), F32),
            jax.ShapeDtypeStruct(resident.shape, BF16),
        ],
        [VMEM] * 2 + [HBM],
        [pltpu.SemaphoreType.DMA],
        cost=pl.CostEstimate(flops=10**7, bytes_accessed=10**7, transcendentals=10**5),
    )(aux, prompt_raw, resident)
    lanes = -(-6 * heads // LANES) * LANES
    half = out_width // 2
    half_wo = jax.ShapeDtypeStruct((1, w_o.shape[1] // 2, out_width), BF16)
    scores_p, scores_r, stat, other_wo0 = call(
        functools.partial(score_kernel, scale),
        [
            jax.ShapeDtypeStruct((2 * heads, keys_rows), F32),
            jax.ShapeDtypeStruct((2, 2 * heads, res_rows), F32),
            jax.ShapeDtypeStruct((count, 2, lanes), F32),
            half_wo,
        ],
        [VMEM] * 4 + [HBM],
        [pltpu.SemaphoreType.DMA],
    )(received, keys, seen, resident, other_wo)
    stat, other_uv = lax.optimization_barrier((stat, other_uv))
    stats = swap(stat)
    part, other_wo1 = call(
        attend_kernel,
        [
            jax.ShapeDtypeStruct((heads, PART * (latent // LANES), LANES), F32),
            half_wo,
        ],
        [SMEM] + [VMEM] * 5 + [HBM],
        [pltpu.SemaphoreType.DMA],
    )(owners, stats, scores_p, scores_r, keys, resident, other_wo)
    parts = swap(part)
    sums = call(
        project_kernel, jax.ShapeDtypeStruct((seqs, 2, half + LANES), I16), [VMEM] * 7
    )(owners_row, parts, w_uv, other_uv, w_o, other_wo0, other_wo1)
    return call(final_kernel, jax.ShapeDtypeStruct((1, 2, out_width), BF16), [VMEM])(swap(sums))


def solution(mesh):
    in_specs = (
        P(("group", "seq"), None, None),
        P("group"),
        P("group"),
        P(("group", "seq"), None, None),
        P("group", None, None),
        P("group", None, "seq", None),
        P(),
        P("seq", None, None),
        P("seq", None, None),
        P("seq", None, None),
    )
    out_specs = P(("group", "seq"), None, None)
    return jax.shard_map(
        on_device, mesh=mesh, in_specs=in_specs, out_specs=out_specs, check_vma=False
    )
```

```python
import functools

import jax
import jax.numpy as jnp
import numpy as np
from jax import lax
from jax.experimental import pallas as pl
from jax.experimental.pallas import tpu as pltpu
from jax.sharding import PartitionSpec as P

F32 = jnp.float32
BF16 = jnp.bfloat16
I32 = jnp.int32
I16 = jnp.int16
VMEM = pl.BlockSpec(memory_space=pltpu.VMEM)
SMEM = pl.BlockSpec(memory_space=pltpu.SMEM)
HBM = pl.BlockSpec(memory_space=pltpu.HBM)
LANES = 128
PACK = 16
PART = 6
BITS = 14.0
NEAR = 4


def iota(shape, dim):
    return lax.broadcasted_iota(I32, shape, dim)


def shift_of(count):
    return count // 2 + 2


def over(x, n):
    return x >> (n.bit_length() - 1)


def rest_of(x, n):
    return x & (n - 1)


def dot(a, b, dims=((1,), (0,))):
    return lax.dot_general(a, b, (dims, ((), ())), preferred_element_type=F32)


def column_of(row, picks):
    n, width = picks.shape[0], row.shape[1]
    hit = iota((n, width), 1) == picks
    return jnp.sum(jnp.where(hit, row, 0), axis=1, keepdims=True)


def slots_of(owners_row):
    seqs = owners_row.shape[1]
    owners_col = column_of(owners_row, iota((seqs, 1), 0))
    earlier = iota((seqs, seqs), 0) < iota((seqs, seqs), 1)
    same = (owners_col == owners_row) & earlier
    return jnp.sum(jnp.where(same, 1, 0), axis=0, keepdims=True)


def doubled(row, times):
    seqs = row.shape[1]
    col = column_of(row, iota((seqs, 1), 0))
    shape = (seqs, 2 * seqs * times)
    hit = over(rest_of(iota(shape, 1), 2 * seqs), 2) == iota(shape, 0)
    return jnp.sum(jnp.where(hit, col, 0), axis=0, keepdims=True)


def frequencies(half, shape, dim):
    at = rest_of(iota(shape, dim), half)
    values = np.float32(10000.0) ** (-(np.arange(half, dtype=np.float32) * np.float32(2.0)) / np.float32(2 * half))
    result = jnp.zeros(shape, F32)
    for i in range(half):
        result = jnp.where(at == i, float(values[i]), result)
    return result


def sine_cosine(angle):
    count = jnp.floor(angle * (2.0 / np.pi) + 0.5)
    x = ((angle - count * 1.5703125) - count * 4.837512969970703125e-4) - count * 7.54978995489188216e-8
    quarter = count.astype(I32)
    y = x * x
    sine = x + x * y * (-1.6666654611e-1 + y * (8.3321608736e-3 - y * 1.9515295891e-4))
    cosine = 1.0 - 0.5 * y + y * y * (4.166664568298827e-2 + y * (-1.388731625493765e-3 + y * 2.443315711809948e-5))
    odd = rest_of(quarter, 2) == 1
    first, second = jnp.where(odd, cosine, sine), jnp.where(odd, sine, cosine)
    first = jnp.where(rest_of(quarter, 4) >= 2, -first, first)
    second = jnp.where(rest_of(quarter + 1, 4) >= 2, -second, second)
    return first, second


def query_kernel(
    res_rows,
    owners_hbm,
    lengths_hbm,
    queries_hbm,
    uk_hbm,
    new_hbm,
    gain_hbm,
    out_ref,
    aux_ref,
    owners_ref,
    lengths_ref,
    queries_ref,
    uk_ref,
    new_ref,
    gain_ref,
    flat,
    sems,
):
    device = lax.axis_index("seq")
    copies = []
    pairs = [
        (owners_hbm, owners_ref),
        (lengths_hbm, lengths_ref),
        (queries_hbm, queries_ref),
        (uk_hbm, uk_ref),
        (new_hbm.at[device], new_ref),
        (gain_hbm, gain_ref),
    ]
    for n, (source, target) in enumerate(pairs):
        copies.append(pltpu.make_async_copy(source, target, sems.at[n]))
        copies[-1].start()
    for copy in copies:
        copy.wait()
    seqs = owners_ref.shape[1]
    nope, latent = uk_ref.shape
    rope = queries_ref.shape[3] - nope
    half = latent // 2
    rows = 2 * seqs
    for s in range(seqs):
        flat[2 * s : 2 * s + 2, : nope + rope] = queries_ref[s, 0].astype(F32)
    values = flat[:, : nope + rope]
    absorbed = dot(values[:, :nope].astype(BF16), uk_ref[...]).astype(BF16)
    row = iota((rows, 1), 0)
    lengths = column_of(lengths_ref[...], over(row, 2))
    angle = (res_rows + lengths + rest_of(row, 2)).astype(F32) * frequencies(rope // 2, (1, rope), 1)
    x = values[:, nope:]
    swapped = jnp.concatenate([x[:, rope // 2 :], x[:, : rope // 2]], axis=1)
    sine, cosine = sine_cosine(angle)
    sine = jnp.where(iota(x.shape, 1) < rope // 2, -sine, sine)
    turned = x * cosine + swapped * sine
    zero = jnp.zeros((rows, rope), F32)
    pieces = [absorbed[:, :half], absorbed[:, half:]]
    for k in range(3):
        blocks = [turned if j == k else zero for j in range(half // rope)]
        pieces.append(jnp.concatenate(blocks, axis=1).astype(BF16))
    owners = owners_ref[...]
    owner = doubled(owners, 5)
    slot = doubled(slots_of(owners), 5)
    shape = (out_ref.shape[0] * PACK, 5 * rows)
    dest, r = over(iota(shape, 0), PACK) ^ shift_of(out_ref.shape[0]), rest_of(iota(shape, 0), PACK)
    lane = iota((1, 5 * rows), 1)
    piece, seq, tok = over(lane, rows), over(rest_of(lane, rows), 2), rest_of(lane, 2)
    start = jnp.where(piece < 2, piece * PART, 2 * PART) + tok
    offset = r - start
    rotary = piece >= 2
    third = piece - 2
    here = jnp.where(owner == dest, slot + 1, jnp.where(seq == dest, 0, -1))
    both = (owner == dest) & (seq == dest)
    wide = (offset == 2 * here) | (both & (offset == 0))
    narrow = (offset == 0) & ((here == third) | (both & (third == 0)))
    hit = (~rotary & (here >= 0) & wide) | (rotary & narrow)
    pieces = jnp.concatenate(pieces, axis=0)
    result = dot(jnp.where(hit, 1.0, 0.0).astype(BF16), pieces)
    out_ref[...] = result.astype(BF16).reshape(out_ref.shape)
    width = new_ref.shape[1]
    aux_ref[0:2, :width] = new_ref[...].astype(F32)
    mine = jnp.where(iota(lengths_ref.shape, 1) == device, lengths_ref[...], 0)
    mine = jnp.sum(mine, axis=1, keepdims=True).astype(F32)
    aux_ref[2:3, :] = jnp.broadcast_to(mine, (1, aux_ref.shape[1]))
    aux_ref[3:4, :latent] = gain_ref[...].astype(F32).reshape(1, latent)


def compress_kernel(
    res_rows, latent, aux_ref, prompt_ref, resident_hbm, out_ref, bias_ref, resident_ref, sem
):
    fetch = pltpu.make_async_copy(resident_hbm, resident_ref, sem)
    fetch.start()
    width, most = prompt_ref.shape[1:]
    half = (width - latent) // 2
    fresh = jnp.concatenate([aux_ref[0:2, :width], jnp.zeros((PACK - 2, width), F32)], axis=0)
    pick = jnp.where(iota((PACK, LANES), 0) == iota((PACK, LANES), 1), 1.0, 0.0).astype(BF16)
    fresh = dot(fresh.astype(BF16), pick, ((0,), (0,)))
    gain = jnp.broadcast_to(aux_ref[3:4, :latent], (PACK, latent))
    top = jnp.where(iota((PACK, LANES), 0) == 0, 1.0, 0.0).astype(BF16)
    gain = dot(gain.astype(BF16), top, ((0,), (0,)))
    length = aux_ref[2:3, :LANES].astype(I32)
    at = iota(bias_ref.shape, 1)
    token = iota(bias_ref.shape, 0)
    length_all = jnp.concatenate([length] * (bias_ref.shape[1] // LANES), axis=1)
    seen = (at < length_all) | ((at >= most) & (at <= most + token))
    bias_ref[...] = jnp.where(seen, 1.0, 0.0)
    freq = frequencies(half, (half, 1), 0)
    for i in range(most // LANES + 1):
        at = slice(i * LANES, (i + 1) * LANES)
        lane = iota((1, LANES), 1)
        if i * LANES < most:
            raw = prompt_ref[0, :, at].astype(F32)
            position = res_rows + i * LANES + lane
        else:
            raw = fresh
            position = res_rows + length + lane
        lat = raw[:latent]
        meansq = jnp.sum(lat * lat, axis=0, keepdims=True) * (1.0 / latent)
        out_ref[:latent, at] = (lat * lax.rsqrt(meansq + 1e-06) * gain).astype(BF16)
        angle = position.astype(F32) * freq
        sine, cosine = sine_cosine(angle)
        x1, x2 = raw[latent : latent + half], raw[latent + half :]
        out_ref[latent : latent + half, at] = (x1 * cosine - x2 * sine).astype(BF16)
        out_ref[latent + half :, at] = (x2 * cosine + x1 * sine).astype(BF16)
    fetch.wait()


def score_kernel(
    scale, q_ref, keys_ref, seen_ref, resident_ref, sp_ref, sr_ref, stat_ref
):
    heads = q_ref.shape[0]
    half = q_ref.shape[2]
    width = keys_ref.shape[0]
    rope = width - 2 * half
    rows = 2 * heads
    total = heads * PACK
    flat = q_ref[...].reshape(total, half)
    shape = (rows, total)
    line = iota(shape, 0)
    head, tok = over(line, 4) * 2 + rest_of(line, 2), rest_of(over(line, 2), 2)
    source = iota(shape, 1) - head * PACK

    def picked(r):
        hit = source == r + tok
        return dot(jnp.where(hit, 1.0, 0.0).astype(BF16), flat)

    turned = picked(2 * PART)
    tops, sums = [], []
    for k in range(3):
        query = jnp.concatenate(
            [picked(2 * k), picked(PART + 2 * k), turned[:, k * rope : (k + 1) * rope]], axis=1
        ).astype(BF16)
        keys = keys_ref[...] if k == 0 else resident_ref[k - 1]
        scores = dot(query, keys) * scale
        if k == 0:
            first, second = seen_ref[0:1, :] > 0.5, seen_ref[1:2, :] > 0.5
            token = rest_of(over(iota(scores.shape, 0), 2), 2)
            seen = (first & (token == 0)) | (second & (token == 1))
            scores = jnp.where(seen, scores, -1e30)
            sp_ref[...] = scores
        else:
            sr_ref[k - 1] = scores
        top = jnp.max(scores, axis=1, keepdims=True)
        tops.append(top)
        sums.append(jnp.sum(jnp.exp(scores - top), axis=1, keepdims=True))
    lanes = stat_ref.shape[2]
    here = iota((3 * rows, lanes), 0) == iota((3 * rows, lanes), 1)
    top = jnp.sum(jnp.where(here, jnp.concatenate(tops, axis=0), 0.0), axis=0, keepdims=True)
    total = jnp.sum(jnp.where(here, jnp.concatenate(sums, axis=0), 0.0), axis=0, keepdims=True)
    both = jnp.concatenate([top, total], axis=0)
    stat_ref[...] = jnp.broadcast_to(both[None], stat_ref.shape)


def attend_kernel(
    owners_ref, stat_ref, sp_ref, sr_ref, keys_ref, resident_ref, _, out_ref, __
):
    heads = out_ref.shape[0]
    latent = out_ref.shape[1] // PART * LANES
    seqs = owners_ref.shape[0]
    rows = 2 * heads
    device = lax.axis_index("seq")
    lanes = stat_ref.shape[2]
    my_owner = owners_ref[device]
    my_slot = jnp.int32(0)
    seen = jnp.int32(0)
    first = jnp.int32(0)
    second = jnp.int32(0)
    for s in range(seqs):
        owner = owners_ref[s]
        my_slot = my_slot + jnp.where((owner == my_owner) & (s < device), 1, 0)
        mine = owner == device
        first = jnp.where(mine & (seen == 0), s, first)
        second = jnp.where(mine & (seen == 1), s, second)
        seen = seen + jnp.where(mine, 1, 0)

    shift = shift_of(heads)
    mine = stat_ref[device ^ shift]
    place = over(iota((1, lanes), 1), rows)
    other = jnp.zeros((2, lanes), F32)
    pairs = [
        (stat_ref[my_owner ^ shift], 1 + my_slot),
        (stat_ref[first ^ shift], 0),
        (stat_ref[second ^ shift], 0),
    ]
    for k, (theirs, segment) in enumerate(pairs):
        moved = jnp.zeros((2, lanes), F32)
        for n in range(3):
            turned = pltpu.roll(theirs, ((k - n) * rows) % lanes, 1)
            moved = jnp.where(segment == n, turned, moved)
        other = jnp.where(place == k, moved, other)
    top = jnp.maximum(mine[0:1], other[0:1])
    total = mine[1:2] * jnp.exp(mine[0:1] - top) + other[1:2] * jnp.exp(other[0:1] - top)
    hit = iota((3 * rows, lanes), 1) == iota((3 * rows, lanes), 0)
    top = jnp.sum(jnp.where(hit, top, 0.0), axis=1, keepdims=True)
    total = jnp.sum(jnp.where(hit, total, 0.0), axis=1, keepdims=True)
    for k in range(3):
        at = slice(k * rows, (k + 1) * rows)
        scores = sp_ref[...] if k == 0 else sr_ref[k - 1]
        keys = keys_ref[:latent, :] if k == 0 else resident_ref[k - 1, :latent, :]
        weights = jnp.exp(scores - top[at]).astype(BF16)
        part = dot(weights, keys, ((1,), (1,))) / total[at]
        for h in range(heads):
            for c in range(latent // LANES):
                at = c * PART + 2 * k
                out_ref[h, at : at + 2, :] = part[2 * h : 2 * h + 2, c * LANES : (c + 1) * LANES]


def project_kernel(
    owners_ref, part_ref, uv_ref, other_uv_ref, wo_ref, other_wo_ref, out_ref
):
    count, each, lanes = part_ref.shape
    seqs = owners_ref.shape[1]
    cuts = each // PART
    rows = 2 * seqs
    core = lax.axis_index("seq") % 2
    owners = owners_ref[...]
    row = iota((cuts * 2 * rows, 1), 0)
    cut, other, seq = over(row, 2 * rows), over(rest_of(row, 2 * rows), rows), over(rest_of(row, rows), 2)
    shift = shift_of(count)
    seq = seq ^ shift
    head = jnp.where(other == 0, core, 1 - core)
    owner = column_of(owners, seq)
    slot = column_of(slots_of(owners), seq)
    first = (seq ^ shift) * each + cut * PART + head
    second = (owner ^ shift) * each + cut * PART + 2 + 2 * slot + head
    at = iota((cuts * 2 * rows, count * each), 1)
    hit = jnp.where((at == first) | (at == second), 1.0, 0.0).astype(BF16)
    rest = part_ref[...].reshape(count * each, lanes)
    latent = None
    for _ in range(3):
        piece = rest.astype(BF16)
        rest = rest - piece.astype(F32)
        one = dot(hit, piece)
        latent = one if latent is None else latent + one
    latent = latent.astype(BF16)
    latent = jnp.concatenate(
        [latent[c * 2 * rows : (c + 1) * 2 * rows] for c in range(cuts)], axis=1
    )
    half = rest_of(iota((rows, 1), 0), 2)
    cols = wo_ref.shape[2] // 2
    product = None
    for n, (uv, wo) in enumerate(((uv_ref, wo_ref), (other_uv_ref, other_wo_ref))):
        head_out = dot(latent[n * rows : (n + 1) * rows], uv[0])
        for side in range(2):
            lines = jnp.where(half == side, head_out, 0.0).astype(BF16)
            one = dot(lines, wo[0, :, side * cols : (side + 1) * cols])
            product = one if product is None else product + one
    top = jnp.max(jnp.abs(product), axis=1, keepdims=True)
    power = jnp.clip(jnp.floor(jnp.log2(jnp.maximum(top, 1e-35))) + 1.0, -100.0, 100.0)
    coded = jnp.round(product * jnp.exp2(BITS - power)).astype(I32).astype(I16)
    power = jnp.broadcast_to(power, (rows, LANES)).astype(I32).astype(I16)
    for s in range(seqs):
        out_ref[s, :, :cols] = coded[2 * s : 2 * s + 2]
        out_ref[s, :, cols:] = power[2 * s : 2 * s + 2]


def final_kernel(in_ref, out_ref):
    cols = out_ref.shape[2] // 2
    for t in range(2):
        total = None
        for n in range(t, in_ref.shape[0], 2):
            power = in_ref[n, :, cols : cols + 1].astype(I32).astype(F32)
            one = in_ref[n, :, :cols].astype(I32).astype(F32) * jnp.exp2(power - BITS)
            total = one if total is None else total + one
        for j in range(2):
            out_ref[0, t : t + 1, j * cols : (j + 1) * cols] = total[j : j + 1].astype(BF16)


def swap(x):
    count = lax.axis_size("seq")
    order = [p ^ shift_of(count) for p in range(count)]
    return lax.all_to_all(x, "seq", split_axis=0, concat_axis=0, axis_index_groups=[order], tiled=True)


def trade(x, step):
    count = lax.axis_size("seq")
    return lax.ppermute(x, "seq", [(d, d ^ step) for d in range(count)])


def call(kernel, shapes, specs, scratch=(), cost=None, room=None, outs=None, aliases={}):
    single = not isinstance(shapes, (list, tuple))
    if room is None:
        room = 16 if lax.axis_size("seq") <= 32 else 56
    return pl.pallas_call(
        kernel,
        out_shape=shapes,
        in_specs=specs,
        out_specs=VMEM if single else outs or [VMEM] * len(shapes),
        input_output_aliases=aliases,
        scratch_shapes=list(scratch),
        cost_estimate=cost,
        compiler_params=pltpu.CompilerParams(vmem_limit_bytes=room * 1024 * 1024),
    )


def on_device(prompt_raw, lengths, owners, resident, new_raw, queries, kv_gain, w_uk, w_uv, w_o):
    count = lax.axis_size("seq")
    seqs = lengths.shape[0]
    most, width = prompt_raw.shape[1:]
    latent = kv_gain.shape[0]
    res_rows = resident.shape[1]
    nope = w_uk.shape[1]
    rope = width - latent
    heads = count
    out_width = w_o.shape[2]
    scale = 1.0 / queries.shape[-1] ** 0.5
    owners_row, lengths_row = owners.reshape(1, seqs), lengths.reshape(1, seqs)
    prompt_raw = prompt_raw.transpose(0, 2, 1)
    resident = resident.transpose(0, 2, 1)
    queries = queries.transpose(0, 2, 1, 3)
    keys_rows = most + LANES

    aux_width = -(-width // LANES) * LANES
    query, aux = call(
        functools.partial(query_kernel, res_rows),
        [
            jax.ShapeDtypeStruct((count, PACK, latent // 2), BF16),
            jax.ShapeDtypeStruct((8, aux_width), F32),
        ],
        [HBM] * 6,
        [
            pltpu.VMEM((1, seqs), I32),
            pltpu.VMEM((1, seqs), I32),
            pltpu.VMEM(queries.shape, BF16),
            pltpu.VMEM((nope, latent), BF16),
            pltpu.VMEM((2, width), BF16),
            pltpu.VMEM((latent,), BF16),
            pltpu.VMEM((2 * seqs, -(-(nope + rope) // LANES) * LANES), F32),
            pltpu.SemaphoreType.DMA((6,)),
        ],
        room=60,
    )(owners_row, lengths_row, queries, w_uk[0], new_raw, kv_gain)
    received = swap(query)
    keys, seen, resident = call(
        functools.partial(compress_kernel, res_rows, latent),
        [
            jax.ShapeDtypeStruct((width, keys_rows), BF16),
            jax.ShapeDtypeStruct((8, keys_rows), F32),
            jax.ShapeDtypeStruct(resident.shape, BF16),
        ],
        [VMEM] * 2 + [HBM],
        [pltpu.SemaphoreType.DMA],
        cost=pl.CostEstimate(flops=10**7, bytes_accessed=10**7, transcendentals=10**5),
    )(aux, prompt_raw, resident)
    lanes = -(-6 * heads // LANES) * LANES
    half = out_width // 2
    scores_p, scores_r, stat = call(
        functools.partial(score_kernel, scale),
        [
            jax.ShapeDtypeStruct((2 * heads, keys_rows), F32),
            jax.ShapeDtypeStruct((2, 2 * heads, res_rows), F32),
            jax.ShapeDtypeStruct((count, 2, lanes), F32),
        ],
        [VMEM] * 4,
    )(received, keys, seen, resident)
    stat, w_uv, w_o = lax.optimization_barrier((stat, w_uv, w_o))
    other_uv, other_wo = trade(w_uv, 1), trade(w_o, 1)
    stats = swap(stat)
    part, other_wo = call(
        attend_kernel,
        [
            jax.ShapeDtypeStruct((heads, PART * (latent // LANES), LANES), F32),
            jax.ShapeDtypeStruct(w_o.shape, BF16),
        ],
        [SMEM] + [VMEM] * 5 + [HBM],
        outs=[VMEM, HBM],
        aliases={6: 1},
    )(owners, stats, scores_p, scores_r, keys, resident, other_wo)
    part, other_uv = lax.optimization_barrier((part, other_uv))
    parts = swap(part)
    sums = call(
        project_kernel, jax.ShapeDtypeStruct((seqs, 2, half + LANES), I16), [VMEM] * 6
    )(owners_row, parts, w_uv, other_uv, w_o, other_wo)
    return call(final_kernel, jax.ShapeDtypeStruct((1, 2, out_width), BF16), [VMEM])(swap(sums))


def solution(mesh):
    in_specs = (
        P(("group", "seq"), None, None),
        P("group"),
        P("group"),
        P(("group", "seq"), None, None),
        P("group", None, None),
        P("group", None, "seq", None),
        P(),
        P("seq", None, None),
        P("seq", None, None),
        P("seq", None, None),
    )
    out_specs = P(("group", "seq"), None, None)
    return jax.shard_map(
        on_device, mesh=mesh, in_specs=in_specs, out_specs=out_specs, check_vma=False
    )
```

```python
import functools

import jax
import jax.numpy as jnp
import numpy as np
from jax import lax
from jax.experimental import pallas as pl
from jax.experimental.pallas import tpu as pltpu
from jax.sharding import PartitionSpec as P

F32 = jnp.float32
BF16 = jnp.bfloat16
I32 = jnp.int32
I16 = jnp.int16
VMEM = pl.BlockSpec(memory_space=pltpu.VMEM)
SMEM = pl.BlockSpec(memory_space=pltpu.SMEM)
HBM = pl.BlockSpec(memory_space=pltpu.HBM)
LANES = 128
PACK = 16
PART = 6
BITS = 14.0
NEAR = 4


def iota(shape, dim):
    return lax.broadcasted_iota(I32, shape, dim)


def shift_of(count):
    return count // 2 + 2


def over(x, n):
    return x >> (n.bit_length() - 1)


def rest_of(x, n):
    return x & (n - 1)


def dot(a, b, dims=((1,), (0,))):
    return lax.dot_general(a, b, (dims, ((), ())), preferred_element_type=F32)


def column_of(row, picks):
    n, width = picks.shape[0], row.shape[1]
    hit = iota((n, width), 1) == picks
    return jnp.sum(jnp.where(hit, row, 0), axis=1, keepdims=True)


def slots_of(owners_row):
    seqs = owners_row.shape[1]
    owners_col = column_of(owners_row, iota((seqs, 1), 0))
    earlier = iota((seqs, seqs), 0) < iota((seqs, seqs), 1)
    same = (owners_col == owners_row) & earlier
    return jnp.sum(jnp.where(same, 1, 0), axis=0, keepdims=True)


def doubled(row, times):
    seqs = row.shape[1]
    col = column_of(row, iota((seqs, 1), 0))
    shape = (seqs, 2 * seqs * times)
    hit = over(rest_of(iota(shape, 1), 2 * seqs), 2) == iota(shape, 0)
    return jnp.sum(jnp.where(hit, col, 0), axis=0, keepdims=True)


def frequencies(half, shape, dim):
    at = rest_of(iota(shape, dim), half)
    values = np.float32(10000.0) ** (-(np.arange(half, dtype=np.float32) * np.float32(2.0)) / np.float32(2 * half))
    result = jnp.zeros(shape, F32)
    for i in range(half):
        result = jnp.where(at == i, float(values[i]), result)
    return result


def sine_cosine(angle):
    count = jnp.floor(angle * (2.0 / np.pi) + 0.5)
    x = ((angle - count * 1.5703125) - count * 4.837512969970703125e-4) - count * 7.54978995489188216e-8
    quarter = count.astype(I32)
    y = x * x
    sine = x + x * y * (-1.6666654611e-1 + y * (8.3321608736e-3 - y * 1.9515295891e-4))
    cosine = 1.0 - 0.5 * y + y * y * (4.166664568298827e-2 + y * (-1.388731625493765e-3 + y * 2.443315711809948e-5))
    odd = rest_of(quarter, 2) == 1
    first, second = jnp.where(odd, cosine, sine), jnp.where(odd, sine, cosine)
    first = jnp.where(rest_of(quarter, 4) >= 2, -first, first)
    second = jnp.where(rest_of(quarter + 1, 4) >= 2, -second, second)
    return first, second


def query_kernel(
    res_rows,
    owners_hbm,
    lengths_hbm,
    queries_hbm,
    uk_hbm,
    new_hbm,
    gain_hbm,
    out_ref,
    aux_ref,
    owners_ref,
    lengths_ref,
    queries_ref,
    uk_ref,
    new_ref,
    gain_ref,
    flat,
    sems,
):
    device = lax.axis_index("seq")
    copies = []
    pairs = [
        (owners_hbm, owners_ref),
        (lengths_hbm, lengths_ref),
        (queries_hbm, queries_ref),
        (uk_hbm, uk_ref),
        (new_hbm.at[device], new_ref),
        (gain_hbm, gain_ref),
    ]
    for n, (source, target) in enumerate(pairs):
        copies.append(pltpu.make_async_copy(source, target, sems.at[n]))
        copies[-1].start()
    for copy in copies:
        copy.wait()
    seqs = owners_ref.shape[1]
    nope, latent = uk_ref.shape
    rope = queries_ref.shape[3] - nope
    half = latent // 2
    rows = 2 * seqs
    for s in range(seqs):
        flat[2 * s : 2 * s + 2, : nope + rope] = queries_ref[s, 0].astype(F32)
    values = flat[:, : nope + rope]
    absorbed = dot(values[:, :nope].astype(BF16), uk_ref[...]).astype(BF16)
    row = iota((rows, 1), 0)
    lengths = column_of(lengths_ref[...], over(row, 2))
    angle = (res_rows + lengths + rest_of(row, 2)).astype(F32) * frequencies(rope // 2, (1, rope), 1)
    x = values[:, nope:]
    swapped = jnp.concatenate([x[:, rope // 2 :], x[:, : rope // 2]], axis=1)
    sine, cosine = sine_cosine(angle)
    sine = jnp.where(iota(x.shape, 1) < rope // 2, -sine, sine)
    turned = x * cosine + swapped * sine
    zero = jnp.zeros((rows, rope), F32)
    pieces = [absorbed[:, :half], absorbed[:, half:]]
    for k in range(3):
        blocks = [turned if j == k else zero for j in range(half // rope)]
        pieces.append(jnp.concatenate(blocks, axis=1).astype(BF16))
    owners = owners_ref[...]
    owner = doubled(owners, 5)
    slot = doubled(slots_of(owners), 5)
    shape = (out_ref.shape[0] * PACK, 5 * rows)
    dest, r = over(iota(shape, 0), PACK) ^ shift_of(out_ref.shape[0]), rest_of(iota(shape, 0), PACK)
    lane = iota((1, 5 * rows), 1)
    piece, seq, tok = over(lane, rows), over(rest_of(lane, rows), 2), rest_of(lane, 2)
    start = jnp.where(piece < 2, piece * PART, 2 * PART) + tok
    offset = r - start
    rotary = piece >= 2
    third = piece - 2
    here = jnp.where(owner == dest, slot + 1, jnp.where(seq == dest, 0, -1))
    both = (owner == dest) & (seq == dest)
    wide = (offset == 2 * here) | (both & (offset == 0))
    narrow = (offset == 0) & ((here == third) | (both & (third == 0)))
    hit = (~rotary & (here >= 0) & wide) | (rotary & narrow)
    pieces = jnp.concatenate(pieces, axis=0)
    result = dot(jnp.where(hit, 1.0, 0.0).astype(BF16), pieces)
    out_ref[...] = result.astype(BF16).reshape(out_ref.shape)
    width = new_ref.shape[1]
    aux_ref[0:2, :width] = new_ref[...].astype(F32)
    mine = jnp.where(iota(lengths_ref.shape, 1) == device, lengths_ref[...], 0)
    mine = jnp.sum(mine, axis=1, keepdims=True).astype(F32)
    aux_ref[2:3, :] = jnp.broadcast_to(mine, (1, aux_ref.shape[1]))
    aux_ref[3:4, :latent] = gain_ref[...].astype(F32).reshape(1, latent)


def compress_kernel(
    res_rows, latent, aux_ref, prompt_ref, resident_hbm, out_ref, bias_ref, resident_ref, sem
):
    fetch = pltpu.make_async_copy(resident_hbm, resident_ref, sem)
    fetch.start()
    width, most = prompt_ref.shape[1:]
    half = (width - latent) // 2
    fresh = jnp.concatenate([aux_ref[0:2, :width], jnp.zeros((PACK - 2, width), F32)], axis=0)
    pick = jnp.where(iota((PACK, LANES), 0) == iota((PACK, LANES), 1), 1.0, 0.0).astype(BF16)
    fresh = dot(fresh.astype(BF16), pick, ((0,), (0,)))
    gain = jnp.broadcast_to(aux_ref[3:4, :latent], (PACK, latent))
    top = jnp.where(iota((PACK, LANES), 0) == 0, 1.0, 0.0).astype(BF16)
    gain = dot(gain.astype(BF16), top, ((0,), (0,)))
    length = aux_ref[2:3, :LANES].astype(I32)
    at = iota(bias_ref.shape, 1)
    token = iota(bias_ref.shape, 0)
    length_all = jnp.concatenate([length] * (bias_ref.shape[1] // LANES), axis=1)
    seen = (at < length_all) | ((at >= most) & (at <= most + token))
    bias_ref[...] = jnp.where(seen, 1.0, 0.0)
    freq = frequencies(half, (half, 1), 0)
    for i in range(most // LANES + 1):
        at = slice(i * LANES, (i + 1) * LANES)
        lane = iota((1, LANES), 1)
        if i * LANES < most:
            raw = prompt_ref[0, :, at].astype(F32)
            position = res_rows + i * LANES + lane
        else:
            raw = fresh
            position = res_rows + length + lane
        lat = raw[:latent]
        meansq = jnp.sum(lat * lat, axis=0, keepdims=True) * (1.0 / latent)
        out_ref[:latent, at] = (lat * lax.rsqrt(meansq + 1e-06) * gain).astype(BF16)
        angle = position.astype(F32) * freq
        sine, cosine = sine_cosine(angle)
        x1, x2 = raw[latent : latent + half], raw[latent + half :]
        out_ref[latent : latent + half, at] = (x1 * cosine - x2 * sine).astype(BF16)
        out_ref[latent + half :, at] = (x2 * cosine + x1 * sine).astype(BF16)
    fetch.wait()


def score_kernel(
    scale, q_ref, keys_ref, seen_ref, resident_ref, _, sp_ref, sr_ref, stat_ref, __
):
    heads = q_ref.shape[0]
    half = q_ref.shape[2]
    width = keys_ref.shape[0]
    rope = width - 2 * half
    rows = 2 * heads
    total = heads * PACK
    flat = q_ref[...].reshape(total, half)
    shape = (rows, total)
    line = iota(shape, 0)
    head, tok = over(line, 4) * 2 + rest_of(line, 2), rest_of(over(line, 2), 2)
    source = iota(shape, 1) - head * PACK

    def picked(r):
        hit = source == r + tok
        return dot(jnp.where(hit, 1.0, 0.0).astype(BF16), flat)

    turned = picked(2 * PART)
    tops, sums = [], []
    for k in range(3):
        query = jnp.concatenate(
            [picked(2 * k), picked(PART + 2 * k), turned[:, k * rope : (k + 1) * rope]], axis=1
        ).astype(BF16)
        keys = keys_ref[...] if k == 0 else resident_ref[k - 1]
        scores = dot(query, keys) * scale
        if k == 0:
            first, second = seen_ref[0:1, :] > 0.5, seen_ref[1:2, :] > 0.5
            token = rest_of(over(iota(scores.shape, 0), 2), 2)
            seen = (first & (token == 0)) | (second & (token == 1))
            scores = jnp.where(seen, scores, -1e30)
            sp_ref[...] = scores
        else:
            sr_ref[k - 1] = scores
        top = jnp.max(scores, axis=1, keepdims=True)
        tops.append(top)
        sums.append(jnp.sum(jnp.exp(scores - top), axis=1, keepdims=True))
    lanes = stat_ref.shape[2]
    here = iota((3 * rows, lanes), 0) == iota((3 * rows, lanes), 1)
    top = jnp.sum(jnp.where(here, jnp.concatenate(tops, axis=0), 0.0), axis=0, keepdims=True)
    total = jnp.sum(jnp.where(here, jnp.concatenate(sums, axis=0), 0.0), axis=0, keepdims=True)
    both = jnp.concatenate([top, total], axis=0)
    stat_ref[...] = jnp.broadcast_to(both[None], stat_ref.shape)


def attend_kernel(
    owners_ref, stat_ref, sp_ref, sr_ref, keys_ref, resident_ref, out_ref
):
    heads = out_ref.shape[0]
    latent = out_ref.shape[1] // PART * LANES
    seqs = owners_ref.shape[0]
    rows = 2 * heads
    device = lax.axis_index("seq")
    lanes = stat_ref.shape[2]
    my_owner = owners_ref[device]
    my_slot = jnp.int32(0)
    seen = jnp.int32(0)
    first = jnp.int32(0)
    second = jnp.int32(0)
    for s in range(seqs):
        owner = owners_ref[s]
        my_slot = my_slot + jnp.where((owner == my_owner) & (s < device), 1, 0)
        mine = owner == device
        first = jnp.where(mine & (seen == 0), s, first)
        second = jnp.where(mine & (seen == 1), s, second)
        seen = seen + jnp.where(mine, 1, 0)

    shift = shift_of(heads)
    mine = stat_ref[device ^ shift]
    place = over(iota((1, lanes), 1), rows)
    other = jnp.zeros((2, lanes), F32)
    pairs = [
        (stat_ref[my_owner ^ shift], 1 + my_slot),
        (stat_ref[first ^ shift], 0),
        (stat_ref[second ^ shift], 0),
    ]
    for k, (theirs, segment) in enumerate(pairs):
        moved = jnp.zeros((2, lanes), F32)
        for n in range(3):
            turned = pltpu.roll(theirs, ((k - n) * rows) % lanes, 1)
            moved = jnp.where(segment == n, turned, moved)
        other = jnp.where(place == k, moved, other)
    top = jnp.maximum(mine[0:1], other[0:1])
    total = mine[1:2] * jnp.exp(mine[0:1] - top) + other[1:2] * jnp.exp(other[0:1] - top)
    hit = iota((3 * rows, lanes), 1) == iota((3 * rows, lanes), 0)
    top = jnp.sum(jnp.where(hit, top, 0.0), axis=1, keepdims=True)
    total = jnp.sum(jnp.where(hit, total, 0.0), axis=1, keepdims=True)
    for k in range(3):
        at = slice(k * rows, (k + 1) * rows)
        scores = sp_ref[...] if k == 0 else sr_ref[k - 1]
        keys = keys_ref[:latent, :] if k == 0 else resident_ref[k - 1, :latent, :]
        weights = jnp.exp(scores - top[at]).astype(BF16)
        part = dot(weights, keys, ((1,), (1,))) / total[at]
        for h in range(heads):
            for c in range(latent // LANES):
                at = c * PART + 2 * k
                out_ref[h, at : at + 2, :] = part[2 * h : 2 * h + 2, c * LANES : (c + 1) * LANES]


def project_kernel(
    owners_ref, part_ref, uv_ref, other_uv_ref, wo_ref, other_wo_ref, out_ref
):
    count, each, lanes = part_ref.shape
    seqs = owners_ref.shape[1]
    cuts = each // PART
    rows = 2 * seqs
    core = lax.axis_index("seq") % 2
    owners = owners_ref[...]
    row = iota((cuts * 2 * rows, 1), 0)
    cut, other, seq = over(row, 2 * rows), over(rest_of(row, 2 * rows), rows), over(rest_of(row, rows), 2)
    shift = shift_of(count)
    seq = seq ^ shift
    head = jnp.where(other == 0, core, 1 - core)
    owner = column_of(owners, seq)
    slot = column_of(slots_of(owners), seq)
    first = (seq ^ shift) * each + cut * PART + head
    second = (owner ^ shift) * each + cut * PART + 2 + 2 * slot + head
    at = iota((cuts * 2 * rows, count * each), 1)
    hit = jnp.where((at == first) | (at == second), 1.0, 0.0).astype(BF16)
    rest = part_ref[...].reshape(count * each, lanes)
    latent = None
    for _ in range(3):
        piece = rest.astype(BF16)
        rest = rest - piece.astype(F32)
        one = dot(hit, piece)
        latent = one if latent is None else latent + one
    latent = latent.astype(BF16)
    latent = jnp.concatenate(
        [latent[c * 2 * rows : (c + 1) * 2 * rows] for c in range(cuts)], axis=1
    )
    half = rest_of(iota((rows, 1), 0), 2)
    cols = wo_ref.shape[2] // 2
    product = None
    for n, (uv, wo) in enumerate(((uv_ref, wo_ref), (other_uv_ref, other_wo_ref))):
        head_out = dot(latent[n * rows : (n + 1) * rows], uv[0])
        for side in range(2):
            lines = jnp.where(half == side, head_out, 0.0).astype(BF16)
            one = dot(lines, wo[0, :, side * cols : (side + 1) * cols])
            product = one if product is None else product + one
    top = jnp.max(jnp.abs(product), axis=1, keepdims=True)
    power = jnp.clip(jnp.floor(jnp.log2(jnp.maximum(top, 1e-35))) + 1.0, -100.0, 100.0)
    coded = jnp.round(product * jnp.exp2(BITS - power)).astype(I32).astype(I16)
    power = jnp.broadcast_to(power, (rows, LANES)).astype(I32).astype(I16)
    for s in range(seqs):
        out_ref[s, :, :cols] = coded[2 * s : 2 * s + 2]
        out_ref[s, :, cols:] = power[2 * s : 2 * s + 2]


def final_kernel(in_ref, out_ref):
    cols = out_ref.shape[2] // 2
    for t in range(2):
        total = None
        for n in range(t, in_ref.shape[0], 2):
            power = in_ref[n, :, cols : cols + 1].astype(I32).astype(F32)
            one = in_ref[n, :, :cols].astype(I32).astype(F32) * jnp.exp2(power - BITS)
            total = one if total is None else total + one
        for j in range(2):
            out_ref[0, t : t + 1, j * cols : (j + 1) * cols] = total[j : j + 1].astype(BF16)


def swap(x):
    count = lax.axis_size("seq")
    order = [p ^ shift_of(count) for p in range(count)]
    return lax.all_to_all(x, "seq", split_axis=0, concat_axis=0, axis_index_groups=[order], tiled=True)


def trade(x, step):
    count = lax.axis_size("seq")
    return lax.ppermute(x, "seq", [(d, d ^ step) for d in range(count)])


def call(kernel, shapes, specs, scratch=(), cost=None, room=None, outs=None, aliases={}):
    single = not isinstance(shapes, (list, tuple))
    if room is None:
        room = 16 if lax.axis_size("seq") <= 32 else 56
    return pl.pallas_call(
        kernel,
        out_shape=shapes,
        in_specs=specs,
        out_specs=VMEM if single else outs or [VMEM] * len(shapes),
        input_output_aliases=aliases,
        scratch_shapes=list(scratch),
        cost_estimate=cost,
        compiler_params=pltpu.CompilerParams(vmem_limit_bytes=room * 1024 * 1024),
    )


def on_device(prompt_raw, lengths, owners, resident, new_raw, queries, kv_gain, w_uk, w_uv, w_o):
    count = lax.axis_size("seq")
    seqs = lengths.shape[0]
    most, width = prompt_raw.shape[1:]
    latent = kv_gain.shape[0]
    res_rows = resident.shape[1]
    nope = w_uk.shape[1]
    rope = width - latent
    heads = count
    out_width = w_o.shape[2]
    scale = 1.0 / queries.shape[-1] ** 0.5
    owners_row, lengths_row = owners.reshape(1, seqs), lengths.reshape(1, seqs)
    prompt_raw = prompt_raw.transpose(0, 2, 1)
    resident = resident.transpose(0, 2, 1)
    queries = queries.transpose(0, 2, 1, 3)
    keys_rows = most + LANES

    aux_width = -(-width // LANES) * LANES
    query, aux = call(
        functools.partial(query_kernel, res_rows),
        [
            jax.ShapeDtypeStruct((count, PACK, latent // 2), BF16),
            jax.ShapeDtypeStruct((8, aux_width), F32),
        ],
        [HBM] * 6,
        [
            pltpu.VMEM((1, seqs), I32),
            pltpu.VMEM((1, seqs), I32),
            pltpu.VMEM(queries.shape, BF16),
            pltpu.VMEM((nope, latent), BF16),
            pltpu.VMEM((2, width), BF16),
            pltpu.VMEM((latent,), BF16),
            pltpu.VMEM((2 * seqs, -(-(nope + rope) // LANES) * LANES), F32),
            pltpu.SemaphoreType.DMA((6,)),
        ],
        room=60,
    )(owners_row, lengths_row, queries, w_uk[0], new_raw, kv_gain)
    received = swap(query)
    query, w_uv, w_o = lax.optimization_barrier((query, w_uv, w_o))
    other_uv, other_wo = trade(w_uv, 1), trade(w_o, 1)
    keys, seen, resident = call(
        functools.partial(compress_kernel, res_rows, latent),
        [
            jax.ShapeDtypeStruct((width, keys_rows), BF16),
            jax.ShapeDtypeStruct((8, keys_rows), F32),
            jax.ShapeDtypeStruct(resident.shape, BF16),
        ],
        [VMEM] * 2 + [HBM],
        [pltpu.SemaphoreType.DMA],
        cost=pl.CostEstimate(flops=10**7, bytes_accessed=10**7, transcendentals=10**5),
    )(aux, prompt_raw, resident)
    lanes = -(-6 * heads // LANES) * LANES
    half = out_width // 2
    scores_p, scores_r, stat, other_wo = call(
        functools.partial(score_kernel, scale),
        [
            jax.ShapeDtypeStruct((2 * heads, keys_rows), F32),
            jax.ShapeDtypeStruct((2, 2 * heads, res_rows), F32),
            jax.ShapeDtypeStruct((count, 2, lanes), F32),
            jax.ShapeDtypeStruct(w_o.shape, BF16),
        ],
        [VMEM] * 4 + [HBM],
        outs=[VMEM] * 3 + [HBM],
        aliases={4: 3},
    )(received, keys, seen, resident, other_wo)
    stat, other_uv = lax.optimization_barrier((stat, other_uv))
    stats = swap(stat)
    part = call(
        attend_kernel,
        jax.ShapeDtypeStruct((heads, PART * (latent // LANES), LANES), F32),
        [SMEM] + [VMEM] * 5,
    )(owners, stats, scores_p, scores_r, keys, resident)
    parts = swap(part)
    sums = call(
        project_kernel, jax.ShapeDtypeStruct((seqs, 2, half + LANES), I16), [VMEM] * 6
    )(owners_row, parts, w_uv, other_uv, w_o, other_wo)
    return call(final_kernel, jax.ShapeDtypeStruct((1, 2, out_width), BF16), [VMEM])(swap(sums))


def solution(mesh):
    in_specs = (
        P(("group", "seq"), None, None),
        P("group"),
        P("group"),
        P(("group", "seq"), None, None),
        P("group", None, None),
        P("group", None, "seq", None),
        P(),
        P("seq", None, None),
        P("seq", None, None),
        P("seq", None, None),
    )
    out_specs = P(("group", "seq"), None, None)
    return jax.shard_map(
        on_device, mesh=mesh, in_specs=in_specs, out_specs=out_specs, check_vma=False
    )
```

```python
import functools

import jax
import jax.numpy as jnp
import numpy as np
from jax import lax
from jax.experimental import pallas as pl
from jax.experimental.pallas import tpu as pltpu
from jax.sharding import PartitionSpec as P

F32 = jnp.float32
BF16 = jnp.bfloat16
I32 = jnp.int32
I16 = jnp.int16
VMEM = pl.BlockSpec(memory_space=pltpu.VMEM)
SMEM = pl.BlockSpec(memory_space=pltpu.SMEM)
HBM = pl.BlockSpec(memory_space=pltpu.HBM)
LANES = 128
PACK = 16
PART = 6
BITS = 14.0
NEAR = 4


def iota(shape, dim):
    return lax.broadcasted_iota(I32, shape, dim)


def shift_of(count):
    return count // 2 + 2


def over(x, n):
    return x >> (n.bit_length() - 1)


def rest_of(x, n):
    return x & (n - 1)


def dot(a, b, dims=((1,), (0,))):
    return lax.dot_general(a, b, (dims, ((), ())), preferred_element_type=F32)


def column_of(row, picks):
    n, width = picks.shape[0], row.shape[1]
    hit = iota((n, width), 1) == picks
    return jnp.sum(jnp.where(hit, row, 0), axis=1, keepdims=True)


def slots_of(owners_row):
    seqs = owners_row.shape[1]
    owners_col = column_of(owners_row, iota((seqs, 1), 0))
    earlier = iota((seqs, seqs), 0) < iota((seqs, seqs), 1)
    same = (owners_col == owners_row) & earlier
    return jnp.sum(jnp.where(same, 1, 0), axis=0, keepdims=True)


def doubled(row, times):
    seqs = row.shape[1]
    col = column_of(row, iota((seqs, 1), 0))
    shape = (seqs, 2 * seqs * times)
    hit = over(rest_of(iota(shape, 1), 2 * seqs), 2) == iota(shape, 0)
    return jnp.sum(jnp.where(hit, col, 0), axis=0, keepdims=True)


def frequencies(half, shape, dim):
    at = rest_of(iota(shape, dim), half)
    values = np.float32(10000.0) ** (-(np.arange(half, dtype=np.float32) * np.float32(2.0)) / np.float32(2 * half))
    result = jnp.zeros(shape, F32)
    for i in range(half):
        result = jnp.where(at == i, float(values[i]), result)
    return result


def sine_cosine(angle):
    count = jnp.floor(angle * (2.0 / np.pi) + 0.5)
    x = ((angle - count * 1.5703125) - count * 4.837512969970703125e-4) - count * 7.54978995489188216e-8
    quarter = count.astype(I32)
    y = x * x
    sine = x + x * y * (-1.6666654611e-1 + y * (8.3321608736e-3 - y * 1.9515295891e-4))
    cosine = 1.0 - 0.5 * y + y * y * (4.166664568298827e-2 + y * (-1.388731625493765e-3 + y * 2.443315711809948e-5))
    odd = rest_of(quarter, 2) == 1
    first, second = jnp.where(odd, cosine, sine), jnp.where(odd, sine, cosine)
    first = jnp.where(rest_of(quarter, 4) >= 2, -first, first)
    second = jnp.where(rest_of(quarter + 1, 4) >= 2, -second, second)
    return first, second


def query_kernel(
    res_rows,
    owners_hbm,
    lengths_hbm,
    queries_hbm,
    uk_hbm,
    new_hbm,
    gain_hbm,
    out_ref,
    aux_ref,
    owners_ref,
    lengths_ref,
    queries_ref,
    uk_ref,
    new_ref,
    gain_ref,
    flat,
    sems,
):
    device = lax.axis_index("seq")
    copies = []
    pairs = [
        (owners_hbm, owners_ref),
        (lengths_hbm, lengths_ref),
        (queries_hbm, queries_ref),
        (uk_hbm, uk_ref),
        (new_hbm.at[device], new_ref),
        (gain_hbm, gain_ref),
    ]
    for n, (source, target) in enumerate(pairs):
        copies.append(pltpu.make_async_copy(source, target, sems.at[n]))
        copies[-1].start()
    for copy in copies:
        copy.wait()
    seqs = owners_ref.shape[1]
    nope, latent = uk_ref.shape
    rope = queries_ref.shape[3] - nope
    half = latent // 2
    rows = 2 * seqs
    for s in range(seqs):
        flat[2 * s : 2 * s + 2, : nope + rope] = queries_ref[s, 0].astype(F32)
    values = flat[:, : nope + rope]
    absorbed = dot(values[:, :nope].astype(BF16), uk_ref[...]).astype(BF16)
    row = iota((rows, 1), 0)
    lengths = column_of(lengths_ref[...], over(row, 2))
    angle = (res_rows + lengths + rest_of(row, 2)).astype(F32) * frequencies(rope // 2, (1, rope), 1)
    x = values[:, nope:]
    swapped = jnp.concatenate([x[:, rope // 2 :], x[:, : rope // 2]], axis=1)
    sine, cosine = sine_cosine(angle)
    sine = jnp.where(iota(x.shape, 1) < rope // 2, -sine, sine)
    turned = x * cosine + swapped * sine
    zero = jnp.zeros((rows, rope), F32)
    pieces = [absorbed[:, :half], absorbed[:, half:]]
    for k in range(3):
        blocks = [turned if j == k else zero for j in range(half // rope)]
        pieces.append(jnp.concatenate(blocks, axis=1).astype(BF16))
    owners = owners_ref[...]
    owner = doubled(owners, 5)
    slot = doubled(slots_of(owners), 5)
    count = out_ref.shape[0]
    shape = (count, 5 * rows)
    dest = iota(shape, 0) ^ shift_of(count)
    lane = iota(shape, 1)
    piece, seq, tok = over(lane, rows), over(rest_of(lane, rows), 2), rest_of(lane, 2)
    third = piece - 2
    first = jnp.where(piece < 2, piece * PART, 2 * PART) + tok
    own = seq == dest
    here = jnp.where(owner == dest, slot + 1, jnp.where(own, 0, -1))
    wide = jnp.where(here >= 0, first + 2 * here, -1)
    target = jnp.where(piece < 2, wide, jnp.where(here == third, first, -1))
    again = jnp.where((owner == dest) & own & ((piece < 2) | (third == 0)), first, -1)
    r = iota((PACK, 5 * rows), 0)
    hits = []
    for d in range(count):
        hit = (r == target[d : d + 1]) | (r == again[d : d + 1])
        hits.append(jnp.where(hit, 1.0, 0.0).astype(BF16))
    hit = jnp.concatenate(hits, axis=0)
    pieces = jnp.concatenate(pieces, axis=0)
    result = dot(hit, pieces)
    out_ref[...] = result.astype(BF16).reshape(out_ref.shape)
    width = new_ref.shape[1]
    aux_ref[0:2, :width] = new_ref[...].astype(F32)
    mine = jnp.where(iota(lengths_ref.shape, 1) == device, lengths_ref[...], 0)
    mine = jnp.sum(mine, axis=1, keepdims=True).astype(F32)
    aux_ref[2:3, :] = jnp.broadcast_to(mine, (1, aux_ref.shape[1]))
    aux_ref[3:4, :latent] = gain_ref[...].astype(F32).reshape(1, latent)


def compress_kernel(
    res_rows, latent, aux_ref, prompt_ref, resident_hbm, out_ref, bias_ref, resident_ref, sem
):
    fetch = pltpu.make_async_copy(resident_hbm, resident_ref, sem)
    fetch.start()
    width, most = prompt_ref.shape[1:]
    half = (width - latent) // 2
    fresh = jnp.concatenate([aux_ref[0:2, :width], jnp.zeros((PACK - 2, width), F32)], axis=0)
    pick = jnp.where(iota((PACK, LANES), 0) == iota((PACK, LANES), 1), 1.0, 0.0).astype(BF16)
    fresh = dot(fresh.astype(BF16), pick, ((0,), (0,)))
    gain = jnp.broadcast_to(aux_ref[3:4, :latent], (PACK, latent))
    top = jnp.where(iota((PACK, LANES), 0) == 0, 1.0, 0.0).astype(BF16)
    gain = dot(gain.astype(BF16), top, ((0,), (0,)))
    length = aux_ref[2:3, :LANES].astype(I32)
    at = iota(bias_ref.shape, 1)
    token = iota(bias_ref.shape, 0)
    length_all = jnp.concatenate([length] * (bias_ref.shape[1] // LANES), axis=1)
    seen = (at < length_all) | ((at >= most) & (at <= most + token))
    bias_ref[...] = jnp.where(seen, 1.0, 0.0)
    freq = frequencies(half, (half, 1), 0)
    for i in range(most // LANES + 1):
        at = slice(i * LANES, (i + 1) * LANES)
        lane = iota((1, LANES), 1)
        if i * LANES < most:
            raw = prompt_ref[0, :, at].astype(F32)
            position = res_rows + i * LANES + lane
        else:
            raw = fresh
            position = res_rows + length + lane
        lat = raw[:latent]
        meansq = jnp.sum(lat * lat, axis=0, keepdims=True) * (1.0 / latent)
        out_ref[:latent, at] = (lat * lax.rsqrt(meansq + 1e-06) * gain).astype(BF16)
        angle = position.astype(F32) * freq
        sine, cosine = sine_cosine(angle)
        x1, x2 = raw[latent : latent + half], raw[latent + half :]
        out_ref[latent : latent + half, at] = (x1 * cosine - x2 * sine).astype(BF16)
        out_ref[latent + half :, at] = (x2 * cosine + x1 * sine).astype(BF16)
    fetch.wait()


def score_kernel(
    scale, q_ref, keys_ref, seen_ref, resident_ref, sp_ref, sr_ref, stat_ref
):
    heads = q_ref.shape[0]
    half = q_ref.shape[2]
    width = keys_ref.shape[0]
    rope = width - 2 * half
    rows = 2 * heads
    total = heads * PACK
    flat = q_ref[...].reshape(total, half)
    shape = (rows, total)
    line = iota(shape, 0)
    head, tok = over(line, 4) * 2 + rest_of(line, 2), rest_of(over(line, 2), 2)
    source = iota(shape, 1) - head * PACK

    def picked(r):
        hit = source == r + tok
        return dot(jnp.where(hit, 1.0, 0.0).astype(BF16), flat)

    turned = picked(2 * PART)
    tops, sums = [], []
    for k in range(3):
        query = jnp.concatenate(
            [picked(2 * k), picked(PART + 2 * k), turned[:, k * rope : (k + 1) * rope]], axis=1
        ).astype(BF16)
        keys = keys_ref[...] if k == 0 else resident_ref[k - 1]
        scores = dot(query, keys) * scale
        if k == 0:
            first, second = seen_ref[0:1, :] > 0.5, seen_ref[1:2, :] > 0.5
            token = rest_of(over(iota(scores.shape, 0), 2), 2)
            seen = (first & (token == 0)) | (second & (token == 1))
            scores = jnp.where(seen, scores, -1e30)
            sp_ref[...] = scores
        else:
            sr_ref[k - 1] = scores
        top = jnp.max(scores, axis=1, keepdims=True)
        tops.append(top)
        sums.append(jnp.sum(jnp.exp(scores - top), axis=1, keepdims=True))
    lanes = stat_ref.shape[2]
    here = iota((3 * rows, lanes), 0) == iota((3 * rows, lanes), 1)
    top = jnp.sum(jnp.where(here, jnp.concatenate(tops, axis=0), 0.0), axis=0, keepdims=True)
    total = jnp.sum(jnp.where(here, jnp.concatenate(sums, axis=0), 0.0), axis=0, keepdims=True)
    both = jnp.concatenate([top, total], axis=0)
    stat_ref[...] = jnp.broadcast_to(both[None], stat_ref.shape)


def attend_kernel(
    owners_ref, stat_ref, sp_ref, sr_ref, keys_ref, resident_ref, _, out_ref, __
):
    heads = out_ref.shape[0]
    latent = out_ref.shape[1] // PART * LANES
    seqs = owners_ref.shape[0]
    rows = 2 * heads
    device = lax.axis_index("seq")
    lanes = stat_ref.shape[2]
    my_owner = owners_ref[device]
    my_slot = jnp.int32(0)
    seen = jnp.int32(0)
    first = jnp.int32(0)
    second = jnp.int32(0)
    for s in range(seqs):
        owner = owners_ref[s]
        my_slot = my_slot + jnp.where((owner == my_owner) & (s < device), 1, 0)
        mine = owner == device
        first = jnp.where(mine & (seen == 0), s, first)
        second = jnp.where(mine & (seen == 1), s, second)
        seen = seen + jnp.where(mine, 1, 0)

    shift = shift_of(heads)
    mine = stat_ref[device ^ shift]
    place = over(iota((1, lanes), 1), rows)
    other = jnp.zeros((2, lanes), F32)
    pairs = [
        (stat_ref[my_owner ^ shift], 1 + my_slot),
        (stat_ref[first ^ shift], 0),
        (stat_ref[second ^ shift], 0),
    ]
    for k, (theirs, segment) in enumerate(pairs):
        moved = jnp.zeros((2, lanes), F32)
        for n in range(3):
            turned = pltpu.roll(theirs, ((k - n) * rows) % lanes, 1)
            moved = jnp.where(segment == n, turned, moved)
        other = jnp.where(place == k, moved, other)
    top = jnp.maximum(mine[0:1], other[0:1])
    total = mine[1:2] * jnp.exp(mine[0:1] - top) + other[1:2] * jnp.exp(other[0:1] - top)
    hit = iota((3 * rows, lanes), 1) == iota((3 * rows, lanes), 0)
    top = jnp.sum(jnp.where(hit, top, 0.0), axis=1, keepdims=True)
    total = jnp.sum(jnp.where(hit, total, 0.0), axis=1, keepdims=True)
    for k in range(3):
        at = slice(k * rows, (k + 1) * rows)
        scores = sp_ref[...] if k == 0 else sr_ref[k - 1]
        keys = keys_ref[:latent, :] if k == 0 else resident_ref[k - 1, :latent, :]
        weights = jnp.exp(scores - top[at]).astype(BF16)
        part = dot(weights, keys, ((1,), (1,))) / total[at]
        for h in range(heads):
            for c in range(latent // LANES):
                at = c * PART + 2 * k
                out_ref[h, at : at + 2, :] = part[2 * h : 2 * h + 2, c * LANES : (c + 1) * LANES]


def project_kernel(
    owners_ref, part_ref, uv_ref, other_uv_ref, wo_ref, other_wo_ref, out_ref
):
    count, each, lanes = part_ref.shape
    seqs = owners_ref.shape[1]
    cuts = each // PART
    rows = 2 * seqs
    core = lax.axis_index("seq") % 2
    owners = owners_ref[...]
    row = iota((cuts * 2 * rows, 1), 0)
    cut, other, seq = over(row, 2 * rows), over(rest_of(row, 2 * rows), rows), over(rest_of(row, rows), 2)
    shift = shift_of(count)
    seq = seq ^ shift
    head = jnp.where(other == 0, core, 1 - core)
    owner = column_of(owners, seq)
    slot = column_of(slots_of(owners), seq)
    first = (seq ^ shift) * each + cut * PART + head
    second = (owner ^ shift) * each + cut * PART + 2 + 2 * slot + head
    at = iota((cuts * 2 * rows, count * each), 1)
    hit = jnp.where((at == first) | (at == second), 1.0, 0.0).astype(BF16)
    rest = part_ref[...].reshape(count * each, lanes)
    latent = None
    for _ in range(3):
        piece = rest.astype(BF16)
        rest = rest - piece.astype(F32)
        one = dot(hit, piece)
        latent = one if latent is None else latent + one
    latent = latent.astype(BF16)
    latent = jnp.concatenate(
        [latent[c * 2 * rows : (c + 1) * 2 * rows] for c in range(cuts)], axis=1
    )
    half = rest_of(iota((rows, 1), 0), 2)
    cols = wo_ref.shape[2] // 2
    product = None
    for n, (uv, wo) in enumerate(((uv_ref, wo_ref), (other_uv_ref, other_wo_ref))):
        head_out = dot(latent[n * rows : (n + 1) * rows], uv[0])
        for side in range(2):
            lines = jnp.where(half == side, head_out, 0.0).astype(BF16)
            one = dot(lines, wo[0, :, side * cols : (side + 1) * cols])
            product = one if product is None else product + one
    top = jnp.max(jnp.abs(product), axis=1, keepdims=True)
    power = jnp.clip(jnp.floor(jnp.log2(jnp.maximum(top, 1e-35))) + 1.0, -100.0, 100.0)
    coded = jnp.round(product * jnp.exp2(BITS - power)).astype(I32).astype(I16)
    power = jnp.broadcast_to(power, (rows, LANES)).astype(I32).astype(I16)
    for s in range(seqs):
        out_ref[s, :, :cols] = coded[2 * s : 2 * s + 2]
        out_ref[s, :, cols:] = power[2 * s : 2 * s + 2]


def final_kernel(in_ref, out_ref):
    cols = out_ref.shape[2] // 2
    for t in range(2):
        total = None
        for n in range(t, in_ref.shape[0], 2):
            power = in_ref[n, :, cols : cols + 1].astype(I32).astype(F32)
            one = in_ref[n, :, :cols].astype(I32).astype(F32) * jnp.exp2(power - BITS)
            total = one if total is None else total + one
        for j in range(2):
            out_ref[0, t : t + 1, j * cols : (j + 1) * cols] = total[j : j + 1].astype(BF16)


def swap(x):
    count = lax.axis_size("seq")
    order = [p ^ shift_of(count) for p in range(count)]
    return lax.all_to_all(x, "seq", split_axis=0, concat_axis=0, axis_index_groups=[order], tiled=True)


def trade(x, step):
    count = lax.axis_size("seq")
    return lax.ppermute(x, "seq", [(d, d ^ step) for d in range(count)])


def call(kernel, shapes, specs, scratch=(), cost=None, room=None, outs=None, aliases={}):
    single = not isinstance(shapes, (list, tuple))
    if room is None:
        room = 16 if lax.axis_size("seq") <= 32 else 56
    return pl.pallas_call(
        kernel,
        out_shape=shapes,
        in_specs=specs,
        out_specs=VMEM if single else outs or [VMEM] * len(shapes),
        input_output_aliases=aliases,
        scratch_shapes=list(scratch),
        cost_estimate=cost,
        compiler_params=pltpu.CompilerParams(vmem_limit_bytes=room * 1024 * 1024),
    )


def on_device(prompt_raw, lengths, owners, resident, new_raw, queries, kv_gain, w_uk, w_uv, w_o):
    count = lax.axis_size("seq")
    seqs = lengths.shape[0]
    most, width = prompt_raw.shape[1:]
    latent = kv_gain.shape[0]
    res_rows = resident.shape[1]
    nope = w_uk.shape[1]
    rope = width - latent
    heads = count
    out_width = w_o.shape[2]
    scale = 1.0 / queries.shape[-1] ** 0.5
    owners_row, lengths_row = owners.reshape(1, seqs), lengths.reshape(1, seqs)
    prompt_raw = prompt_raw.transpose(0, 2, 1)
    resident = resident.transpose(0, 2, 1)
    queries = queries.transpose(0, 2, 1, 3)
    keys_rows = most + LANES

    aux_width = -(-width // LANES) * LANES
    query, aux = call(
        functools.partial(query_kernel, res_rows),
        [
            jax.ShapeDtypeStruct((count, PACK, latent // 2), BF16),
            jax.ShapeDtypeStruct((8, aux_width), F32),
        ],
        [HBM] * 6,
        [
            pltpu.VMEM((1, seqs), I32),
            pltpu.VMEM((1, seqs), I32),
            pltpu.VMEM(queries.shape, BF16),
            pltpu.VMEM((nope, latent), BF16),
            pltpu.VMEM((2, width), BF16),
            pltpu.VMEM((latent,), BF16),
            pltpu.VMEM((2 * seqs, -(-(nope + rope) // LANES) * LANES), F32),
            pltpu.SemaphoreType.DMA((6,)),
        ],
        room=60,
    )(owners_row, lengths_row, queries, w_uk[0], new_raw, kv_gain)
    received = swap(query)
    query, w_uv = lax.optimization_barrier((query, w_uv))
    other_uv = trade(w_uv, 1)
    keys, seen, resident = call(
        functools.partial(compress_kernel, res_rows, latent),
        [
            jax.ShapeDtypeStruct((width, keys_rows), BF16),
            jax.ShapeDtypeStruct((8, keys_rows), F32),
            jax.ShapeDtypeStruct(resident.shape, BF16),
        ],
        [VMEM] * 2 + [HBM],
        [pltpu.SemaphoreType.DMA],
        cost=pl.CostEstimate(flops=10**7, bytes_accessed=10**7, transcendentals=10**5),
    )(aux, prompt_raw, resident)
    lanes = -(-6 * heads // LANES) * LANES
    half = out_width // 2
    scores_p, scores_r, stat = call(
        functools.partial(score_kernel, scale),
        [
            jax.ShapeDtypeStruct((2 * heads, keys_rows), F32),
            jax.ShapeDtypeStruct((2, 2 * heads, res_rows), F32),
            jax.ShapeDtypeStruct((count, 2, lanes), F32),
        ],
        [VMEM] * 4,
    )(received, keys, seen, resident)
    stat, other_uv, w_o = lax.optimization_barrier((stat, other_uv, w_o))
    other_wo = trade(w_o, 1)
    stats = swap(stat)
    part, other_wo = call(
        attend_kernel,
        [
            jax.ShapeDtypeStruct((heads, PART * (latent // LANES), LANES), F32),
            jax.ShapeDtypeStruct(w_o.shape, BF16),
        ],
        [SMEM] + [VMEM] * 5 + [HBM],
        outs=[VMEM, HBM],
        aliases={6: 1},
    )(owners, stats, scores_p, scores_r, keys, resident, other_wo)
    parts = swap(part)
    sums = call(
        project_kernel, jax.ShapeDtypeStruct((seqs, 2, half + LANES), I16), [VMEM] * 6
    )(owners_row, parts, w_uv, other_uv, w_o, other_wo)
    return call(final_kernel, jax.ShapeDtypeStruct((1, 2, out_width), BF16), [VMEM])(swap(sums))


def solution(mesh):
    in_specs = (
        P(("group", "seq"), None, None),
        P("group"),
        P("group"),
        P(("group", "seq"), None, None),
        P("group", None, None),
        P("group", None, "seq", None),
        P(),
        P("seq", None, None),
        P("seq", None, None),
        P("seq", None, None),
    )
    out_specs = P(("group", "seq"), None, None)
    return jax.shard_map(
        on_device, mesh=mesh, in_specs=in_specs, out_specs=out_specs, check_vma=False
    )
```

```python
import functools

import jax
import jax.numpy as jnp
import numpy as np
from jax import lax
from jax.experimental import pallas as pl
from jax.experimental.pallas import tpu as pltpu
from jax.sharding import PartitionSpec as P

F32 = jnp.float32
BF16 = jnp.bfloat16
I32 = jnp.int32
I16 = jnp.int16
VMEM = pl.BlockSpec(memory_space=pltpu.VMEM)
SMEM = pl.BlockSpec(memory_space=pltpu.SMEM)
HBM = pl.BlockSpec(memory_space=pltpu.HBM)
LANES = 128
PACK = 16
PART = 6
BITS = 14.0
NEAR = 4


def iota(shape, dim):
    return lax.broadcasted_iota(I32, shape, dim)


def shift_of(count):
    return count // 2 + 2


def over(x, n):
    return x >> (n.bit_length() - 1)


def rest_of(x, n):
    return x & (n - 1)


def dot(a, b, dims=((1,), (0,))):
    return lax.dot_general(a, b, (dims, ((), ())), preferred_element_type=F32)


def column_of(row, picks):
    n, width = picks.shape[0], row.shape[1]
    hit = iota((n, width), 1) == picks
    return jnp.sum(jnp.where(hit, row, 0), axis=1, keepdims=True)


def slots_of(owners_row):
    seqs = owners_row.shape[1]
    owners_col = column_of(owners_row, iota((seqs, 1), 0))
    earlier = iota((seqs, seqs), 0) < iota((seqs, seqs), 1)
    same = (owners_col == owners_row) & earlier
    return jnp.sum(jnp.where(same, 1, 0), axis=0, keepdims=True)


def doubled(row, times):
    seqs = row.shape[1]
    col = column_of(row, iota((seqs, 1), 0))
    shape = (seqs, 2 * seqs * times)
    hit = over(rest_of(iota(shape, 1), 2 * seqs), 2) == iota(shape, 0)
    return jnp.sum(jnp.where(hit, col, 0), axis=0, keepdims=True)


def frequencies(half, shape, dim):
    at = rest_of(iota(shape, dim), half)
    values = np.float32(10000.0) ** (-(np.arange(half, dtype=np.float32) * np.float32(2.0)) / np.float32(2 * half))
    level = [jnp.full(shape, float(v), F32) for v in values]
    bit = 1
    while len(level) > 1:
        odd = (at & bit) != 0
        level = [jnp.where(odd, b, a) for a, b in zip(level[::2], level[1::2])]
        bit *= 2
    return level[0]


def sine_cosine(angle):
    count = jnp.floor(angle * (2.0 / np.pi) + 0.5)
    x = ((angle - count * 1.5703125) - count * 4.837512969970703125e-4) - count * 7.54978995489188216e-8
    quarter = count.astype(I32)
    y = x * x
    sine = x + x * y * (-1.6666654611e-1 + y * (8.3321608736e-3 - y * 1.9515295891e-4))
    cosine = 1.0 - 0.5 * y + y * y * (4.166664568298827e-2 + y * (-1.388731625493765e-3 + y * 2.443315711809948e-5))
    odd = rest_of(quarter, 2) == 1
    first, second = jnp.where(odd, cosine, sine), jnp.where(odd, sine, cosine)
    first = jnp.where(rest_of(quarter, 4) >= 2, -first, first)
    second = jnp.where(rest_of(quarter + 1, 4) >= 2, -second, second)
    return first, second


def query_kernel(
    res_rows,
    owners_hbm,
    lengths_hbm,
    queries_hbm,
    uk_hbm,
    new_hbm,
    gain_hbm,
    out_ref,
    aux_ref,
    owners_ref,
    lengths_ref,
    queries_ref,
    uk_ref,
    new_ref,
    gain_ref,
    flat,
    sems,
):
    device = lax.axis_index("seq")
    copies = []
    pairs = [
        (owners_hbm, owners_ref),
        (lengths_hbm, lengths_ref),
        (queries_hbm, queries_ref),
        (uk_hbm, uk_ref),
        (new_hbm.at[device], new_ref),
        (gain_hbm, gain_ref),
    ]
    for n, (source, target) in enumerate(pairs):
        copies.append(pltpu.make_async_copy(source, target, sems.at[n]))
        copies[-1].start()
    for copy in copies:
        copy.wait()
    seqs = owners_ref.shape[1]
    nope, latent = uk_ref.shape
    rope = queries_ref.shape[3] - nope
    half = latent // 2
    rows = 2 * seqs
    for s in range(seqs):
        flat[2 * s : 2 * s + 2, : nope + rope] = queries_ref[s, 0].astype(F32)
    values = flat[:, : nope + rope]
    absorbed = dot(values[:, :nope].astype(BF16), uk_ref[...]).astype(BF16)
    row = iota((rows, 1), 0)
    lengths = column_of(lengths_ref[...], over(row, 2))
    angle = (res_rows + lengths + rest_of(row, 2)).astype(F32) * frequencies(rope // 2, (1, rope), 1)
    x = values[:, nope:]
    swapped = jnp.concatenate([x[:, rope // 2 :], x[:, : rope // 2]], axis=1)
    sine, cosine = sine_cosine(angle)
    sine = jnp.where(iota(x.shape, 1) < rope // 2, -sine, sine)
    turned = x * cosine + swapped * sine
    zero = jnp.zeros((rows, rope), F32)
    pieces = [absorbed[:, :half], absorbed[:, half:]]
    for k in range(3):
        blocks = [turned if j == k else zero for j in range(half // rope)]
        pieces.append(jnp.concatenate(blocks, axis=1).astype(BF16))
    owners = owners_ref[...]
    owner = doubled(owners, 5)
    slot = doubled(slots_of(owners), 5)
    count = out_ref.shape[0]
    shape = (count, 5 * rows)
    dest = iota(shape, 0) ^ shift_of(count)
    lane = iota(shape, 1)
    piece, seq, tok = over(lane, rows), over(rest_of(lane, rows), 2), rest_of(lane, 2)
    third = piece - 2
    first = jnp.where(piece < 2, piece * PART, 2 * PART) + tok
    own = seq == dest
    here = jnp.where(owner == dest, slot + 1, jnp.where(own, 0, -1))
    wide = jnp.where(here >= 0, first + 2 * here, -1)
    target = jnp.where(piece < 2, wide, jnp.where(here == third, first, -1))
    again = jnp.where((owner == dest) & own & ((piece < 2) | (third == 0)), first, -1)
    r = iota((PACK, 5 * rows), 0)
    hits = []
    for d in range(count):
        hit = (r == target[d : d + 1]) | (r == again[d : d + 1])
        hits.append(jnp.where(hit, 1.0, 0.0).astype(BF16))
    hit = jnp.concatenate(hits, axis=0)
    pieces = jnp.concatenate(pieces, axis=0)
    result = dot(hit, pieces)
    out_ref[...] = result.astype(BF16).reshape(out_ref.shape)
    width = new_ref.shape[1]
    aux_ref[0:2, :width] = new_ref[...].astype(F32)
    mine = jnp.where(iota(lengths_ref.shape, 1) == device, lengths_ref[...], 0)
    mine = jnp.sum(mine, axis=1, keepdims=True).astype(F32)
    aux_ref[2:3, :] = jnp.broadcast_to(mine, (1, aux_ref.shape[1]))
    aux_ref[3:4, :latent] = gain_ref[...].astype(F32).reshape(1, latent)


def compress_kernel(
    res_rows, latent, aux_ref, prompt_ref, resident_hbm, out_ref, bias_ref, resident_ref, sem
):
    fetch = pltpu.make_async_copy(resident_hbm, resident_ref, sem)
    fetch.start()
    width, most = prompt_ref.shape[1:]
    half = (width - latent) // 2
    fresh = jnp.concatenate([aux_ref[0:2, :width], jnp.zeros((PACK - 2, width), F32)], axis=0)
    pick = jnp.where(iota((PACK, LANES), 0) == iota((PACK, LANES), 1), 1.0, 0.0).astype(BF16)
    fresh = dot(fresh.astype(BF16), pick, ((0,), (0,)))
    gain = jnp.broadcast_to(aux_ref[3:4, :latent], (PACK, latent))
    top = jnp.where(iota((PACK, LANES), 0) == 0, 1.0, 0.0).astype(BF16)
    gain = dot(gain.astype(BF16), top, ((0,), (0,)))
    length = aux_ref[2:3, :LANES].astype(I32)
    at = iota(bias_ref.shape, 1)
    token = iota(bias_ref.shape, 0)
    length_all = jnp.concatenate([length] * (bias_ref.shape[1] // LANES), axis=1)
    seen = (at < length_all) | ((at >= most) & (at <= most + token))
    bias_ref[...] = jnp.where(seen, 1.0, 0.0)
    freq = frequencies(half, (half, 1), 0)
    for i in range(most // LANES + 1):
        at = slice(i * LANES, (i + 1) * LANES)
        lane = iota((1, LANES), 1)
        if i * LANES < most:
            raw = prompt_ref[0, :, at].astype(F32)
            position = res_rows + i * LANES + lane
        else:
            raw = fresh
            position = res_rows + length + lane
        lat = raw[:latent]
        meansq = jnp.sum(lat * lat, axis=0, keepdims=True) * (1.0 / latent)
        out_ref[:latent, at] = (lat * lax.rsqrt(meansq + 1e-06) * gain).astype(BF16)
        angle = position.astype(F32) * freq
        sine, cosine = sine_cosine(angle)
        x1, x2 = raw[latent : latent + half], raw[latent + half :]
        out_ref[latent : latent + half, at] = (x1 * cosine - x2 * sine).astype(BF16)
        out_ref[latent + half :, at] = (x2 * cosine + x1 * sine).astype(BF16)
    fetch.wait()


def score_kernel(
    scale, q_ref, keys_ref, seen_ref, resident_ref, sp_ref, sr_ref, stat_ref
):
    heads = q_ref.shape[0]
    half = q_ref.shape[2]
    width = keys_ref.shape[0]
    rope = width - 2 * half
    rows = 2 * heads
    total = heads * PACK
    flat = q_ref[...].reshape(total, half)
    shape = (rows, total)
    line = iota(shape, 0)
    head, tok = over(line, 4) * 2 + rest_of(line, 2), rest_of(over(line, 2), 2)
    source = iota(shape, 1) - head * PACK

    def picked(r):
        hit = source == r + tok
        return dot(jnp.where(hit, 1.0, 0.0).astype(BF16), flat)

    turned = picked(2 * PART)
    tops, sums = [], []
    for k in range(3):
        query = jnp.concatenate(
            [picked(2 * k), picked(PART + 2 * k), turned[:, k * rope : (k + 1) * rope]], axis=1
        ).astype(BF16)
        keys = keys_ref[...] if k == 0 else resident_ref[k - 1]
        scores = dot(query, keys) * scale
        if k == 0:
            first, second = seen_ref[0:1, :] > 0.5, seen_ref[1:2, :] > 0.5
            token = rest_of(over(iota(scores.shape, 0), 2), 2)
            seen = (first & (token == 0)) | (second & (token == 1))
            scores = jnp.where(seen, scores, -1e30)
            sp_ref[...] = scores
        else:
            sr_ref[k - 1] = scores
        top = jnp.max(scores, axis=1, keepdims=True)
        tops.append(top)
        sums.append(jnp.sum(jnp.exp(scores - top), axis=1, keepdims=True))
    lanes = stat_ref.shape[2]
    here = iota((3 * rows, lanes), 0) == iota((3 * rows, lanes), 1)
    top = jnp.sum(jnp.where(here, jnp.concatenate(tops, axis=0), 0.0), axis=0, keepdims=True)
    total = jnp.sum(jnp.where(here, jnp.concatenate(sums, axis=0), 0.0), axis=0, keepdims=True)
    both = jnp.concatenate([top, total], axis=0)
    stat_ref[...] = jnp.broadcast_to(both[None], stat_ref.shape)


def attend_kernel(
    owners_ref, stat_ref, sp_ref, sr_ref, keys_ref, resident_ref, out_ref
):
    heads = out_ref.shape[0]
    latent = out_ref.shape[1] // PART * LANES
    seqs = owners_ref.shape[0]
    rows = 2 * heads
    device = lax.axis_index("seq")
    lanes = stat_ref.shape[2]
    my_owner = owners_ref[device]
    my_slot = jnp.int32(0)
    seen = jnp.int32(0)
    first = jnp.int32(0)
    second = jnp.int32(0)
    for s in range(seqs):
        owner = owners_ref[s]
        my_slot = my_slot + jnp.where((owner == my_owner) & (s < device), 1, 0)
        mine = owner == device
        first = jnp.where(mine & (seen == 0), s, first)
        second = jnp.where(mine & (seen == 1), s, second)
        seen = seen + jnp.where(mine, 1, 0)

    shift = shift_of(heads)
    mine = stat_ref[device ^ shift]
    place = over(iota((1, lanes), 1), rows)
    other = jnp.zeros((2, lanes), F32)
    pairs = [
        (stat_ref[my_owner ^ shift], 1 + my_slot),
        (stat_ref[first ^ shift], 0),
        (stat_ref[second ^ shift], 0),
    ]
    for k, (theirs, segment) in enumerate(pairs):
        moved = jnp.zeros((2, lanes), F32)
        for n in range(3):
            turned = pltpu.roll(theirs, ((k - n) * rows) % lanes, 1)
            moved = jnp.where(segment == n, turned, moved)
        other = jnp.where(place == k, moved, other)
    top = jnp.maximum(mine[0:1], other[0:1])
    total = mine[1:2] * jnp.exp(mine[0:1] - top) + other[1:2] * jnp.exp(other[0:1] - top)
    hit = iota((3 * rows, lanes), 1) == iota((3 * rows, lanes), 0)
    top = jnp.sum(jnp.where(hit, top, 0.0), axis=1, keepdims=True)
    total = jnp.sum(jnp.where(hit, total, 0.0), axis=1, keepdims=True)
    for k in range(3):
        at = slice(k * rows, (k + 1) * rows)
        scores = sp_ref[...] if k == 0 else sr_ref[k - 1]
        keys = keys_ref[:latent, :] if k == 0 else resident_ref[k - 1, :latent, :]
        weights = jnp.exp(scores - top[at]).astype(BF16)
        part = dot(weights, keys, ((1,), (1,))) / total[at]
        for h in range(heads):
            for c in range(latent // LANES):
                at = c * PART + 2 * k
                out_ref[h, at : at + 2, :] = part[2 * h : 2 * h + 2, c * LANES : (c + 1) * LANES]


def project_kernel(
    owners_ref, part_ref, uv_ref, other_uv_ref, wo_ref, other_wo_ref, out_ref
):
    count, each, lanes = part_ref.shape
    seqs = owners_ref.shape[1]
    cuts = each // PART
    rows = 2 * seqs
    core = lax.axis_index("seq") % 2
    owners = owners_ref[...]
    row = iota((2 * rows, 1), 0)
    shift = shift_of(count)
    other, place = over(row, rows), over(rest_of(row, rows), 2)
    seq = place ^ shift
    head = jnp.where(other == 0, core, 1 - core)
    owner = column_of(owners, seq)
    slot = column_of(slots_of(owners), seq)
    shape = (2 * rows, count * each)
    first = jnp.broadcast_to(place * each + head, shape)
    second = jnp.broadcast_to((owner ^ shift) * each + 2 + 2 * slot + head, shape)
    hits = []
    for cut in range(cuts):
        at = iota(shape, 1) - cut * PART
        hits.append(jnp.where((at == first) | (at == second), 1.0, 0.0).astype(BF16))
    hit = jnp.concatenate(hits, axis=0)
    rest = part_ref[...].reshape(count * each, lanes)
    latent = None
    for _ in range(3):
        piece = rest.astype(BF16)
        rest = rest - piece.astype(F32)
        one = dot(hit, piece)
        latent = one if latent is None else latent + one
    latent = latent.astype(BF16)
    latent = jnp.concatenate(
        [latent[c * 2 * rows : (c + 1) * 2 * rows] for c in range(cuts)], axis=1
    )
    half = rest_of(iota((rows, 1), 0), 2)
    cols = wo_ref.shape[2] // 2
    product = None
    for n, (uv, wo) in enumerate(((uv_ref, wo_ref), (other_uv_ref, other_wo_ref))):
        head_out = dot(latent[n * rows : (n + 1) * rows], uv[0])
        for side in range(2):
            lines = jnp.where(half == side, head_out, 0.0).astype(BF16)
            one = dot(lines, wo[0, :, side * cols : (side + 1) * cols])
            product = one if product is None else product + one
    top = jnp.max(jnp.abs(product), axis=1, keepdims=True)
    power = jnp.clip(jnp.floor(jnp.log2(jnp.maximum(top, 1e-35))) + 1.0, -100.0, 100.0)
    coded = jnp.round(product * jnp.exp2(BITS - power)).astype(I32).astype(I16)
    power = jnp.broadcast_to(power, (rows, LANES)).astype(I32).astype(I16)
    for s in range(seqs):
        out_ref[s, :, :cols] = coded[2 * s : 2 * s + 2]
        out_ref[s, :, cols:] = power[2 * s : 2 * s + 2]


def final_kernel(in_ref, out_ref):
    cols = out_ref.shape[2] // 2
    for t in range(2):
        total = None
        for n in range(t, in_ref.shape[0], 2):
            power = in_ref[n, :, cols : cols + 1].astype(I32).astype(F32)
            one = in_ref[n, :, :cols].astype(I32).astype(F32) * jnp.exp2(power - BITS)
            total = one if total is None else total + one
        for j in range(2):
            out_ref[0, t : t + 1, j * cols : (j + 1) * cols] = total[j : j + 1].astype(BF16)


def swap(x):
    count = lax.axis_size("seq")
    order = [p ^ shift_of(count) for p in range(count)]
    return lax.all_to_all(x, "seq", split_axis=0, concat_axis=0, axis_index_groups=[order], tiled=True)


def trade(x, step):
    count = lax.axis_size("seq")
    return lax.ppermute(x, "seq", [(d, d ^ step) for d in range(count)])


def call(kernel, shapes, specs, scratch=(), cost=None, room=None):
    single = not isinstance(shapes, (list, tuple))
    if room is None:
        room = 16 if lax.axis_size("seq") <= 32 else 56
    return pl.pallas_call(
        kernel,
        out_shape=shapes,
        in_specs=specs,
        out_specs=VMEM if single else [VMEM] * len(shapes),
        scratch_shapes=list(scratch),
        cost_estimate=cost,
        compiler_params=pltpu.CompilerParams(vmem_limit_bytes=room * 1024 * 1024),
    )


def on_device(prompt_raw, lengths, owners, resident, new_raw, queries, kv_gain, w_uk, w_uv, w_o):
    count = lax.axis_size("seq")
    seqs = lengths.shape[0]
    most, width = prompt_raw.shape[1:]
    latent = kv_gain.shape[0]
    res_rows = resident.shape[1]
    nope = w_uk.shape[1]
    rope = width - latent
    heads = count
    out_width = w_o.shape[2]
    scale = 1.0 / queries.shape[-1] ** 0.5
    owners_row, lengths_row = owners.reshape(1, seqs), lengths.reshape(1, seqs)
    prompt_raw = prompt_raw.transpose(0, 2, 1)
    resident = resident.transpose(0, 2, 1)
    queries = queries.transpose(0, 2, 1, 3)
    keys_rows = most + LANES

    aux_width = -(-width // LANES) * LANES
    query, aux = call(
        functools.partial(query_kernel, res_rows),
        [
            jax.ShapeDtypeStruct((count, PACK, latent // 2), BF16),
            jax.ShapeDtypeStruct((8, aux_width), F32),
        ],
        [HBM] * 6,
        [
            pltpu.VMEM((1, seqs), I32),
            pltpu.VMEM((1, seqs), I32),
            pltpu.VMEM(queries.shape, BF16),
            pltpu.VMEM((nope, latent), BF16),
            pltpu.VMEM((2, width), BF16),
            pltpu.VMEM((latent,), BF16),
            pltpu.VMEM((2 * seqs, -(-(nope + rope) // LANES) * LANES), F32),
            pltpu.SemaphoreType.DMA((6,)),
        ],
        room=60,
    )(owners_row, lengths_row, queries, w_uk[0], new_raw, kv_gain)
    received = swap(query)
    query, w_uv = lax.optimization_barrier((query, w_uv))
    other_uv = trade(w_uv, 1)
    keys, seen, resident = call(
        functools.partial(compress_kernel, res_rows, latent),
        [
            jax.ShapeDtypeStruct((width, keys_rows), BF16),
            jax.ShapeDtypeStruct((8, keys_rows), F32),
            jax.ShapeDtypeStruct(resident.shape, BF16),
        ],
        [VMEM] * 2 + [HBM],
        [pltpu.SemaphoreType.DMA],
        cost=pl.CostEstimate(flops=10**7, bytes_accessed=10**7, transcendentals=10**5),
    )(aux, prompt_raw, resident)
    lanes = -(-6 * heads // LANES) * LANES
    half = out_width // 2
    scores_p, scores_r, stat = call(
        functools.partial(score_kernel, scale),
        [
            jax.ShapeDtypeStruct((2 * heads, keys_rows), F32),
            jax.ShapeDtypeStruct((2, 2 * heads, res_rows), F32),
            jax.ShapeDtypeStruct((count, 2, lanes), F32),
        ],
        [VMEM] * 4,
    )(received, keys, seen, resident)
    stat, other_uv = lax.optimization_barrier((stat, other_uv))
    stats = swap(stat)
    part = call(
        attend_kernel,
        jax.ShapeDtypeStruct((heads, PART * (latent // LANES), LANES), F32),
        [SMEM] + [VMEM] * 5,
    )(owners, stats, scores_p, scores_r, keys, resident)
    part, w_o = lax.optimization_barrier((part, w_o))
    other_wo = trade(w_o, 1)
    parts = swap(part)
    sums = call(
        project_kernel, jax.ShapeDtypeStruct((seqs, 2, half + LANES), I16), [VMEM] * 6
    )(owners_row, parts, w_uv, other_uv, w_o, other_wo)
    return call(final_kernel, jax.ShapeDtypeStruct((1, 2, out_width), BF16), [VMEM])(swap(sums))


def solution(mesh):
    in_specs = (
        P(("group", "seq"), None, None),
        P("group"),
        P("group"),
        P(("group", "seq"), None, None),
        P("group", None, None),
        P("group", None, "seq", None),
        P(),
        P("seq", None, None),
        P("seq", None, None),
        P("seq", None, None),
    )
    out_specs = P(("group", "seq"), None, None)
    return jax.shard_map(
        on_device, mesh=mesh, in_specs=in_specs, out_specs=out_specs, check_vma=False
    )
```

```python
import functools

import jax
import jax.numpy as jnp
import numpy as np
from jax import lax
from jax.experimental import pallas as pl
from jax.experimental.pallas import tpu as pltpu
from jax.sharding import PartitionSpec as P

F32 = jnp.float32
BF16 = jnp.bfloat16
I32 = jnp.int32
I16 = jnp.int16
VMEM = pl.BlockSpec(memory_space=pltpu.VMEM)
SMEM = pl.BlockSpec(memory_space=pltpu.SMEM)
HBM = pl.BlockSpec(memory_space=pltpu.HBM)
LANES = 128
PACK = 16
PART = 6
BITS = 14.0
NEAR = 4


def iota(shape, dim):
    return lax.broadcasted_iota(I32, shape, dim)


def place_of(device, count):
    chips = count // 2
    return (((chips // 2 + 1) - (device >> 1)) & (chips - 1)) * 2 + (device & 1)


def over(x, n):
    return x >> (n.bit_length() - 1)


def rest_of(x, n):
    return x & (n - 1)


def dot(a, b, dims=((1,), (0,))):
    return lax.dot_general(a, b, (dims, ((), ())), preferred_element_type=F32)


def column_of(row, picks):
    n, width = picks.shape[0], row.shape[1]
    hit = iota((n, width), 1) == picks
    return jnp.sum(jnp.where(hit, row, 0), axis=1, keepdims=True)


def slots_of(owners_row):
    seqs = owners_row.shape[1]
    owners_col = column_of(owners_row, iota((seqs, 1), 0))
    earlier = iota((seqs, seqs), 0) < iota((seqs, seqs), 1)
    same = (owners_col == owners_row) & earlier
    return jnp.sum(jnp.where(same, 1, 0), axis=0, keepdims=True)


def doubled(row, times):
    seqs = row.shape[1]
    col = column_of(row, iota((seqs, 1), 0))
    shape = (seqs, 2 * seqs * times)
    hit = over(rest_of(iota(shape, 1), 2 * seqs), 2) == iota(shape, 0)
    return jnp.sum(jnp.where(hit, col, 0), axis=0, keepdims=True)


def frequencies(half, shape, dim):
    at = rest_of(iota(shape, dim), half)
    values = np.float32(10000.0) ** (-(np.arange(half, dtype=np.float32) * np.float32(2.0)) / np.float32(2 * half))
    level = [jnp.full(shape, float(v), F32) for v in values]
    bit = 1
    while len(level) > 1:
        odd = (at & bit) != 0
        level = [jnp.where(odd, b, a) for a, b in zip(level[::2], level[1::2])]
        bit *= 2
    return level[0]


def sine_cosine(angle):
    count = jnp.floor(angle * (2.0 / np.pi) + 0.5)
    x = ((angle - count * 1.5703125) - count * 4.837512969970703125e-4) - count * 7.54978995489188216e-8
    quarter = count.astype(I32)
    y = x * x
    sine = x + x * y * (-1.6666654611e-1 + y * (8.3321608736e-3 - y * 1.9515295891e-4))
    cosine = 1.0 - 0.5 * y + y * y * (4.166664568298827e-2 + y * (-1.388731625493765e-3 + y * 2.443315711809948e-5))
    odd = rest_of(quarter, 2) == 1
    first, second = jnp.where(odd, cosine, sine), jnp.where(odd, sine, cosine)
    first = jnp.where(rest_of(quarter, 4) >= 2, -first, first)
    second = jnp.where(rest_of(quarter + 1, 4) >= 2, -second, second)
    return first, second


def query_kernel(
    res_rows,
    owners_hbm,
    lengths_hbm,
    queries_hbm,
    uk_hbm,
    new_hbm,
    gain_hbm,
    out_ref,
    aux_ref,
    owners_ref,
    lengths_ref,
    queries_ref,
    uk_ref,
    new_ref,
    gain_ref,
    flat,
    sems,
):
    device = lax.axis_index("seq")
    copies = []
    pairs = [
        (owners_hbm, owners_ref),
        (lengths_hbm, lengths_ref),
        (queries_hbm, queries_ref),
        (uk_hbm, uk_ref),
        (new_hbm.at[device], new_ref),
        (gain_hbm, gain_ref),
    ]
    for n, (source, target) in enumerate(pairs):
        copies.append(pltpu.make_async_copy(source, target, sems.at[n]))
        copies[-1].start()
    for copy in copies:
        copy.wait()
    seqs = owners_ref.shape[1]
    nope, latent = uk_ref.shape
    rope = queries_ref.shape[3] - nope
    half = latent // 2
    rows = 2 * seqs
    for s in range(seqs):
        flat[2 * s : 2 * s + 2, : nope + rope] = queries_ref[s, 0].astype(F32)
    values = flat[:, : nope + rope]
    absorbed = dot(values[:, :nope].astype(BF16), uk_ref[...]).astype(BF16)
    row = iota((rows, 1), 0)
    lengths = column_of(lengths_ref[...], over(row, 2))
    angle = (res_rows + lengths + rest_of(row, 2)).astype(F32) * frequencies(rope // 2, (1, rope), 1)
    x = values[:, nope:]
    swapped = jnp.concatenate([x[:, rope // 2 :], x[:, : rope // 2]], axis=1)
    sine, cosine = sine_cosine(angle)
    sine = jnp.where(iota(x.shape, 1) < rope // 2, -sine, sine)
    turned = x * cosine + swapped * sine
    zero = jnp.zeros((rows, rope), F32)
    pieces = [absorbed[:, :half], absorbed[:, half:]]
    for k in range(3):
        blocks = [turned if j == k else zero for j in range(half // rope)]
        pieces.append(jnp.concatenate(blocks, axis=1).astype(BF16))
    owners = owners_ref[...]
    owner = doubled(owners, 5)
    slot = doubled(slots_of(owners), 5)
    count = out_ref.shape[0]
    shape = (count, 5 * rows)
    dest = place_of(iota(shape, 0), count)
    lane = iota(shape, 1)
    piece, seq, tok = over(lane, rows), over(rest_of(lane, rows), 2), rest_of(lane, 2)
    third = piece - 2
    first = jnp.where(piece < 2, piece * PART, 2 * PART) + tok
    own = seq == dest
    here = jnp.where(owner == dest, slot + 1, jnp.where(own, 0, -1))
    wide = jnp.where(here >= 0, first + 2 * here, -1)
    target = jnp.where(piece < 2, wide, jnp.where(here == third, first, -1))
    again = jnp.where((owner == dest) & own & ((piece < 2) | (third == 0)), first, -1)
    r = iota((PACK, 5 * rows), 0)
    hits = []
    for d in range(count):
        hit = (r == target[d : d + 1]) | (r == again[d : d + 1])
        hits.append(jnp.where(hit, 1.0, 0.0).astype(BF16))
    hit = jnp.concatenate(hits, axis=0)
    pieces = jnp.concatenate(pieces, axis=0)
    result = dot(hit, pieces)
    out_ref[...] = result.astype(BF16).reshape(out_ref.shape)
    width = new_ref.shape[1]
    aux_ref[0:2, :width] = new_ref[...].astype(F32)
    mine = jnp.where(iota(lengths_ref.shape, 1) == device, lengths_ref[...], 0)
    mine = jnp.sum(mine, axis=1, keepdims=True).astype(F32)
    aux_ref[2:3, :] = jnp.broadcast_to(mine, (1, aux_ref.shape[1]))
    aux_ref[3:4, :latent] = gain_ref[...].astype(F32).reshape(1, latent)


def compress_kernel(
    res_rows, latent, aux_ref, prompt_ref, resident_hbm, out_ref, bias_ref, resident_ref, sem
):
    fetch = pltpu.make_async_copy(resident_hbm, resident_ref, sem)
    fetch.start()
    width, most = prompt_ref.shape[1:]
    half = (width - latent) // 2
    fresh = jnp.concatenate([aux_ref[0:2, :width], jnp.zeros((PACK - 2, width), F32)], axis=0)
    pick = jnp.where(iota((PACK, LANES), 0) == iota((PACK, LANES), 1), 1.0, 0.0).astype(BF16)
    fresh = dot(fresh.astype(BF16), pick, ((0,), (0,)))
    gain = jnp.broadcast_to(aux_ref[3:4, :latent], (PACK, latent))
    top = jnp.where(iota((PACK, LANES), 0) == 0, 1.0, 0.0).astype(BF16)
    gain = dot(gain.astype(BF16), top, ((0,), (0,)))
    length = aux_ref[2:3, :LANES].astype(I32)
    at = iota(bias_ref.shape, 1)
    token = iota(bias_ref.shape, 0)
    length_all = jnp.concatenate([length] * (bias_ref.shape[1] // LANES), axis=1)
    seen = (at < length_all) | ((at >= most) & (at <= most + token))
    bias_ref[...] = jnp.where(seen, 1.0, 0.0)
    freq = frequencies(half, (half, 1), 0)
    for i in range(most // LANES + 1):
        at = slice(i * LANES, (i + 1) * LANES)
        lane = iota((1, LANES), 1)
        if i * LANES < most:
            raw = prompt_ref[0, :, at].astype(F32)
            position = res_rows + i * LANES + lane
        else:
            raw = fresh
            position = res_rows + length + lane
        lat = raw[:latent]
        meansq = jnp.sum(lat * lat, axis=0, keepdims=True) * (1.0 / latent)
        out_ref[:latent, at] = (lat * lax.rsqrt(meansq + 1e-06) * gain).astype(BF16)
        angle = position.astype(F32) * freq
        sine, cosine = sine_cosine(angle)
        x1, x2 = raw[latent : latent + half], raw[latent + half :]
        out_ref[latent : latent + half, at] = (x1 * cosine - x2 * sine).astype(BF16)
        out_ref[latent + half :, at] = (x2 * cosine + x1 * sine).astype(BF16)
    fetch.wait()


def score_kernel(
    scale, q_ref, keys_ref, seen_ref, resident_ref, sp_ref, sr_ref, stat_ref
):
    heads = q_ref.shape[0]
    half = q_ref.shape[2]
    width = keys_ref.shape[0]
    rope = width - 2 * half
    rows = 2 * heads
    total = heads * PACK
    flat = q_ref[...].reshape(total, half)
    shape = (rows, total)
    line = iota(shape, 0)
    head, tok = over(line, 4) * 2 + rest_of(line, 2), rest_of(over(line, 2), 2)
    source = iota(shape, 1) - head * PACK

    def picked(r):
        hit = source == r + tok
        return dot(jnp.where(hit, 1.0, 0.0).astype(BF16), flat)

    turned = picked(2 * PART)
    tops, sums = [], []
    for k in range(3):
        query = jnp.concatenate(
            [picked(2 * k), picked(PART + 2 * k), turned[:, k * rope : (k + 1) * rope]], axis=1
        ).astype(BF16)
        keys = keys_ref[...] if k == 0 else resident_ref[k - 1]
        scores = dot(query, keys) * scale
        if k == 0:
            first, second = seen_ref[0:1, :] > 0.5, seen_ref[1:2, :] > 0.5
            token = rest_of(over(iota(scores.shape, 0), 2), 2)
            seen = (first & (token == 0)) | (second & (token == 1))
            scores = jnp.where(seen, scores, -1e30)
            sp_ref[...] = scores
        else:
            sr_ref[k - 1] = scores
        top = jnp.max(scores, axis=1, keepdims=True)
        tops.append(top)
        sums.append(jnp.sum(jnp.exp(scores - top), axis=1, keepdims=True))
    lanes = stat_ref.shape[2]
    here = iota((3 * rows, lanes), 0) == iota((3 * rows, lanes), 1)
    top = jnp.sum(jnp.where(here, jnp.concatenate(tops, axis=0), 0.0), axis=0, keepdims=True)
    total = jnp.sum(jnp.where(here, jnp.concatenate(sums, axis=0), 0.0), axis=0, keepdims=True)
    both = jnp.concatenate([top, total], axis=0)
    stat_ref[...] = jnp.broadcast_to(both[None], stat_ref.shape)


def attend_kernel(
    owners_ref, stat_ref, sp_ref, sr_ref, keys_ref, resident_ref, out_ref
):
    heads = out_ref.shape[0]
    latent = out_ref.shape[1] // PART * LANES
    seqs = owners_ref.shape[0]
    rows = 2 * heads
    device = lax.axis_index("seq")
    lanes = stat_ref.shape[2]
    my_owner = owners_ref[device]
    my_slot = jnp.int32(0)
    seen = jnp.int32(0)
    first = jnp.int32(0)
    second = jnp.int32(0)
    for s in range(seqs):
        owner = owners_ref[s]
        my_slot = my_slot + jnp.where((owner == my_owner) & (s < device), 1, 0)
        mine = owner == device
        first = jnp.where(mine & (seen == 0), s, first)
        second = jnp.where(mine & (seen == 1), s, second)
        seen = seen + jnp.where(mine, 1, 0)

    mine = stat_ref[place_of(device, heads)]
    place = over(iota((1, lanes), 1), rows)
    other = jnp.zeros((2, lanes), F32)
    pairs = [
        (stat_ref[place_of(my_owner, heads)], 1 + my_slot),
        (stat_ref[place_of(first, heads)], 0),
        (stat_ref[place_of(second, heads)], 0),
    ]
    for k, (theirs, segment) in enumerate(pairs):
        moved = jnp.zeros((2, lanes), F32)
        for n in range(3):
            turned = pltpu.roll(theirs, ((k - n) * rows) % lanes, 1)
            moved = jnp.where(segment == n, turned, moved)
        other = jnp.where(place == k, moved, other)
    top = jnp.maximum(mine[0:1], other[0:1])
    total = mine[1:2] * jnp.exp(mine[0:1] - top) + other[1:2] * jnp.exp(other[0:1] - top)
    hit = iota((3 * rows, lanes), 1) == iota((3 * rows, lanes), 0)
    top = jnp.sum(jnp.where(hit, top, 0.0), axis=1, keepdims=True)
    total = jnp.sum(jnp.where(hit, total, 0.0), axis=1, keepdims=True)
    for k in range(3):
        at = slice(k * rows, (k + 1) * rows)
        scores = sp_ref[...] if k == 0 else sr_ref[k - 1]
        keys = keys_ref[:latent, :] if k == 0 else resident_ref[k - 1, :latent, :]
        weights = jnp.exp(scores - top[at]).astype(BF16)
        part = dot(weights, keys, ((1,), (1,))) / total[at]
        for h in range(heads):
            for c in range(latent // LANES):
                at = c * PART + 2 * k
                out_ref[h, at : at + 2, :] = part[2 * h : 2 * h + 2, c * LANES : (c + 1) * LANES]


def project_kernel(
    owners_ref, part_ref, uv_ref, other_uv_ref, wo_ref, other_wo_ref, out_ref
):
    count, each, lanes = part_ref.shape
    seqs = owners_ref.shape[1]
    cuts = each // PART
    rows = 2 * seqs
    core = lax.axis_index("seq") % 2
    owners = owners_ref[...]
    row = iota((2 * rows, 1), 0)
    other, place = over(row, rows), over(rest_of(row, rows), 2)
    seq = place_of(place, count)
    head = jnp.where(other == 0, core, 1 - core)
    owner = column_of(owners, seq)
    slot = column_of(slots_of(owners), seq)
    shape = (2 * rows, count * each)
    first = jnp.broadcast_to(place * each + head, shape)
    second = jnp.broadcast_to(place_of(owner, count) * each + 2 + 2 * slot + head, shape)
    hits = []
    for cut in range(cuts):
        at = iota(shape, 1) - cut * PART
        hits.append(jnp.where((at == first) | (at == second), 1.0, 0.0).astype(BF16))
    hit = jnp.concatenate(hits, axis=0)
    rest = part_ref[...].reshape(count * each, lanes)
    latent = None
    for _ in range(3):
        piece = rest.astype(BF16)
        rest = rest - piece.astype(F32)
        one = dot(hit, piece)
        latent = one if latent is None else latent + one
    latent = latent.astype(BF16)
    latent = jnp.concatenate(
        [latent[c * 2 * rows : (c + 1) * 2 * rows] for c in range(cuts)], axis=1
    )
    half = rest_of(iota((rows, 1), 0), 2)
    cols = wo_ref.shape[2] // 2
    product = None
    for n, (uv, wo) in enumerate(((uv_ref, wo_ref), (other_uv_ref, other_wo_ref))):
        head_out = dot(latent[n * rows : (n + 1) * rows], uv[0])
        for side in range(2):
            lines = jnp.where(half == side, head_out, 0.0).astype(BF16)
            one = dot(lines, wo[0, :, side * cols : (side + 1) * cols])
            product = one if product is None else product + one
    top = jnp.max(jnp.abs(product), axis=1, keepdims=True)
    power = jnp.clip(jnp.floor(jnp.log2(jnp.maximum(top, 1e-35))) + 1.0, -100.0, 100.0)
    coded = jnp.round(product * jnp.exp2(BITS - power)).astype(I32).astype(I16)
    power = jnp.broadcast_to(power, (rows, LANES)).astype(I32).astype(I16)
    for s in range(seqs):
        out_ref[s, :, :cols] = coded[2 * s : 2 * s + 2]
        out_ref[s, :, cols:] = power[2 * s : 2 * s + 2]


def final_kernel(in_ref, out_ref):
    cols = out_ref.shape[2] // 2
    for t in range(2):
        total = None
        for n in range(t, in_ref.shape[0], 2):
            power = in_ref[n, :, cols : cols + 1].astype(I32).astype(F32)
            one = in_ref[n, :, :cols].astype(I32).astype(F32) * jnp.exp2(power - BITS)
            total = one if total is None else total + one
        for j in range(2):
            out_ref[0, t : t + 1, j * cols : (j + 1) * cols] = total[j : j + 1].astype(BF16)


def swap(x):
    count = lax.axis_size("seq")
    order = [place_of(p, count) for p in range(count)]
    return lax.all_to_all(x, "seq", split_axis=0, concat_axis=0, axis_index_groups=[order], tiled=True)


def trade(x, step):
    count = lax.axis_size("seq")
    return lax.ppermute(x, "seq", [(d, d ^ step) for d in range(count)])


def call(kernel, shapes, specs, scratch=(), cost=None, room=None):
    single = not isinstance(shapes, (list, tuple))
    if room is None:
        room = 16 if lax.axis_size("seq") <= 32 else 56
    return pl.pallas_call(
        kernel,
        out_shape=shapes,
        in_specs=specs,
        out_specs=VMEM if single else [VMEM] * len(shapes),
        scratch_shapes=list(scratch),
        cost_estimate=cost,
        compiler_params=pltpu.CompilerParams(vmem_limit_bytes=room * 1024 * 1024),
    )


def on_device(prompt_raw, lengths, owners, resident, new_raw, queries, kv_gain, w_uk, w_uv, w_o):
    count = lax.axis_size("seq")
    seqs = lengths.shape[0]
    most, width = prompt_raw.shape[1:]
    latent = kv_gain.shape[0]
    res_rows = resident.shape[1]
    nope = w_uk.shape[1]
    rope = width - latent
    heads = count
    out_width = w_o.shape[2]
    scale = 1.0 / queries.shape[-1] ** 0.5
    owners_row, lengths_row = owners.reshape(1, seqs), lengths.reshape(1, seqs)
    prompt_raw = prompt_raw.transpose(0, 2, 1)
    resident = resident.transpose(0, 2, 1)
    queries = queries.transpose(0, 2, 1, 3)
    keys_rows = most + LANES

    aux_width = -(-width // LANES) * LANES
    query, aux = call(
        functools.partial(query_kernel, res_rows),
        [
            jax.ShapeDtypeStruct((count, PACK, latent // 2), BF16),
            jax.ShapeDtypeStruct((8, aux_width), F32),
        ],
        [HBM] * 6,
        [
            pltpu.VMEM((1, seqs), I32),
            pltpu.VMEM((1, seqs), I32),
            pltpu.VMEM(queries.shape, BF16),
            pltpu.VMEM((nope, latent), BF16),
            pltpu.VMEM((2, width), BF16),
            pltpu.VMEM((latent,), BF16),
            pltpu.VMEM((2 * seqs, -(-(nope + rope) // LANES) * LANES), F32),
            pltpu.SemaphoreType.DMA((6,)),
        ],
        room=60,
    )(owners_row, lengths_row, queries, w_uk[0], new_raw, kv_gain)
    received = swap(query)
    query, w_uv = lax.optimization_barrier((query, w_uv))
    other_uv = trade(w_uv, 1)
    keys, seen, resident = call(
        functools.partial(compress_kernel, res_rows, latent),
        [
            jax.ShapeDtypeStruct((width, keys_rows), BF16),
            jax.ShapeDtypeStruct((8, keys_rows), F32),
            jax.ShapeDtypeStruct(resident.shape, BF16),
        ],
        [VMEM] * 2 + [HBM],
        [pltpu.SemaphoreType.DMA],
        cost=pl.CostEstimate(flops=10**7, bytes_accessed=10**7, transcendentals=10**5),
    )(aux, prompt_raw, resident)
    lanes = -(-6 * heads // LANES) * LANES
    half = out_width // 2
    scores_p, scores_r, stat = call(
        functools.partial(score_kernel, scale),
        [
            jax.ShapeDtypeStruct((2 * heads, keys_rows), F32),
            jax.ShapeDtypeStruct((2, 2 * heads, res_rows), F32),
            jax.ShapeDtypeStruct((count, 2, lanes), F32),
        ],
        [VMEM] * 4,
    )(received, keys, seen, resident)
    stat, other_uv = lax.optimization_barrier((stat, other_uv))
    stats = swap(stat)
    part = call(
        attend_kernel,
        jax.ShapeDtypeStruct((heads, PART * (latent // LANES), LANES), F32),
        [SMEM] + [VMEM] * 5,
    )(owners, stats, scores_p, scores_r, keys, resident)
    part, w_o = lax.optimization_barrier((part, w_o))
    other_wo = trade(w_o, 1)
    parts = swap(part)
    sums = call(
        project_kernel, jax.ShapeDtypeStruct((seqs, 2, half + LANES), I16), [VMEM] * 6
    )(owners_row, parts, w_uv, other_uv, w_o, other_wo)
    return call(final_kernel, jax.ShapeDtypeStruct((1, 2, out_width), BF16), [VMEM])(swap(sums))


def solution(mesh):
    in_specs = (
        P(("group", "seq"), None, None),
        P("group"),
        P("group"),
        P(("group", "seq"), None, None),
        P("group", None, None),
        P("group", None, "seq", None),
        P(),
        P("seq", None, None),
        P("seq", None, None),
        P("seq", None, None),
    )
    out_specs = P(("group", "seq"), None, None)
    return jax.shard_map(
        on_device, mesh=mesh, in_specs=in_specs, out_specs=out_specs, check_vma=False
    )
```

```python
import functools

import jax
import jax.numpy as jnp
import numpy as np
from jax import lax
from jax.experimental import pallas as pl
from jax.experimental.pallas import tpu as pltpu
from jax.sharding import PartitionSpec as P

F32 = jnp.float32
BF16 = jnp.bfloat16
I32 = jnp.int32
I16 = jnp.int16
VMEM = pl.BlockSpec(memory_space=pltpu.VMEM)
SMEM = pl.BlockSpec(memory_space=pltpu.SMEM)
HBM = pl.BlockSpec(memory_space=pltpu.HBM)
LANES = 128
PACK = 16
PART = 6
BITS = 14.0
NEAR = 4


def iota(shape, dim):
    return lax.broadcasted_iota(I32, shape, dim)


def place_of(device, count):
    chips = count // 2
    return (((device >> 1) - (chips // 2 + 1)) & (chips - 1)) * 2 + (device & 1)


def device_at(place, count):
    chips = count // 2
    return (((place >> 1) + (chips // 2 + 1)) & (chips - 1)) * 2 + (place & 1)


def over(x, n):
    return x >> (n.bit_length() - 1)


def rest_of(x, n):
    return x & (n - 1)


def dot(a, b, dims=((1,), (0,))):
    return lax.dot_general(a, b, (dims, ((), ())), preferred_element_type=F32)


def column_of(row, picks):
    n, width = picks.shape[0], row.shape[1]
    hit = iota((n, width), 1) == picks
    return jnp.sum(jnp.where(hit, row, 0), axis=1, keepdims=True)


def slots_of(owners_row):
    seqs = owners_row.shape[1]
    owners_col = column_of(owners_row, iota((seqs, 1), 0))
    earlier = iota((seqs, seqs), 0) < iota((seqs, seqs), 1)
    same = (owners_col == owners_row) & earlier
    return jnp.sum(jnp.where(same, 1, 0), axis=0, keepdims=True)


def doubled(row, times):
    seqs = row.shape[1]
    col = column_of(row, iota((seqs, 1), 0))
    shape = (seqs, 2 * seqs * times)
    hit = over(rest_of(iota(shape, 1), 2 * seqs), 2) == iota(shape, 0)
    return jnp.sum(jnp.where(hit, col, 0), axis=0, keepdims=True)


def frequencies(half, shape, dim):
    at = rest_of(iota(shape, dim), half)
    values = np.float32(10000.0) ** (-(np.arange(half, dtype=np.float32) * np.float32(2.0)) / np.float32(2 * half))
    level = [jnp.full(shape, float(v), F32) for v in values]
    bit = 1
    while len(level) > 1:
        odd = (at & bit) != 0
        level = [jnp.where(odd, b, a) for a, b in zip(level[::2], level[1::2])]
        bit *= 2
    return level[0]


def sine_cosine(angle):
    count = jnp.floor(angle * (2.0 / np.pi) + 0.5)
    x = ((angle - count * 1.5703125) - count * 4.837512969970703125e-4) - count * 7.54978995489188216e-8
    quarter = count.astype(I32)
    y = x * x
    sine = x + x * y * (-1.6666654611e-1 + y * (8.3321608736e-3 - y * 1.9515295891e-4))
    cosine = 1.0 - 0.5 * y + y * y * (4.166664568298827e-2 + y * (-1.388731625493765e-3 + y * 2.443315711809948e-5))
    odd = rest_of(quarter, 2) == 1
    first, second = jnp.where(odd, cosine, sine), jnp.where(odd, sine, cosine)
    first = jnp.where(rest_of(quarter, 4) >= 2, -first, first)
    second = jnp.where(rest_of(quarter + 1, 4) >= 2, -second, second)
    return first, second


def query_kernel(
    res_rows,
    owners_hbm,
    lengths_hbm,
    queries_hbm,
    uk_hbm,
    new_hbm,
    gain_hbm,
    out_ref,
    aux_ref,
    owners_ref,
    lengths_ref,
    queries_ref,
    uk_ref,
    new_ref,
    gain_ref,
    flat,
    sems,
):
    device = lax.axis_index("seq")
    copies = []
    pairs = [
        (owners_hbm, owners_ref),
        (lengths_hbm, lengths_ref),
        (queries_hbm, queries_ref),
        (uk_hbm, uk_ref),
        (new_hbm.at[device], new_ref),
        (gain_hbm, gain_ref),
    ]
    for n, (source, target) in enumerate(pairs):
        copies.append(pltpu.make_async_copy(source, target, sems.at[n]))
        copies[-1].start()
    seqs = owners_ref.shape[1]
    nope, latent = uk_ref.shape
    rope = queries_ref.shape[3] - nope
    half = latent // 2
    rows = 2 * seqs
    copies[0].wait()
    owners = owners_ref[...]
    owner = doubled(owners, 5)
    slot = doubled(slots_of(owners), 5)
    count = out_ref.shape[0]
    shape = (count, 5 * rows)
    dest = device_at(iota(shape, 0), count)
    lane = iota(shape, 1)
    piece, seq, tok = over(lane, rows), over(rest_of(lane, rows), 2), rest_of(lane, 2)
    third = piece - 2
    first = jnp.where(piece < 2, piece * PART, 2 * PART) + tok
    own = seq == dest
    here = jnp.where(owner == dest, slot + 1, jnp.where(own, 0, -1))
    wide = jnp.where(here >= 0, first + 2 * here, -1)
    target = jnp.where(piece < 2, wide, jnp.where(here == third, first, -1))
    again = jnp.where((owner == dest) & own & ((piece < 2) | (third == 0)), first, -1)
    r = iota((PACK, 5 * rows), 0)
    hits = []
    for d in range(count):
        hit = (r == target[d : d + 1]) | (r == again[d : d + 1])
        hits.append(jnp.where(hit, 1.0, 0.0).astype(BF16))
    hit = jnp.concatenate(hits, axis=0)
    copies[1].wait()
    copies[2].wait()
    for s in range(seqs):
        flat[2 * s : 2 * s + 2, : nope + rope] = queries_ref[s, 0].astype(F32)
    values = flat[:, : nope + rope]
    copies[3].wait()
    absorbed = dot(values[:, :nope].astype(BF16), uk_ref[...]).astype(BF16)
    row = iota((rows, 1), 0)
    lengths = column_of(lengths_ref[...], over(row, 2))
    angle = (res_rows + lengths + rest_of(row, 2)).astype(F32) * frequencies(rope // 2, (1, rope), 1)
    x = values[:, nope:]
    swapped = jnp.concatenate([x[:, rope // 2 :], x[:, : rope // 2]], axis=1)
    sine, cosine = sine_cosine(angle)
    sine = jnp.where(iota(x.shape, 1) < rope // 2, -sine, sine)
    turned = x * cosine + swapped * sine
    zero = jnp.zeros((rows, rope), F32)
    pieces = [absorbed[:, :half], absorbed[:, half:]]
    for k in range(3):
        blocks = [turned if j == k else zero for j in range(half // rope)]
        pieces.append(jnp.concatenate(blocks, axis=1).astype(BF16))
    pieces = jnp.concatenate(pieces, axis=0)
    result = dot(hit, pieces)
    out_ref[...] = result.astype(BF16).reshape(out_ref.shape)
    copies[4].wait()
    copies[5].wait()
    width = new_ref.shape[1]
    aux_ref[0:2, :width] = new_ref[...].astype(F32)
    mine = jnp.where(iota(lengths_ref.shape, 1) == device, lengths_ref[...], 0)
    mine = jnp.sum(mine, axis=1, keepdims=True).astype(F32)
    aux_ref[2:3, :] = jnp.broadcast_to(mine, (1, aux_ref.shape[1]))
    aux_ref[3:4, :latent] = gain_ref[...].astype(F32).reshape(1, latent)


def compress_kernel(
    res_rows, latent, aux_ref, prompt_ref, resident_hbm, out_ref, bias_ref, resident_ref, sem
):
    fetch = pltpu.make_async_copy(resident_hbm, resident_ref, sem)
    fetch.start()
    width, most = prompt_ref.shape[1:]
    half = (width - latent) // 2
    fresh = jnp.concatenate([aux_ref[0:2, :width], jnp.zeros((PACK - 2, width), F32)], axis=0)
    pick = jnp.where(iota((PACK, LANES), 0) == iota((PACK, LANES), 1), 1.0, 0.0).astype(BF16)
    fresh = dot(fresh.astype(BF16), pick, ((0,), (0,)))
    gain = jnp.broadcast_to(aux_ref[3:4, :latent], (PACK, latent))
    top = jnp.where(iota((PACK, LANES), 0) == 0, 1.0, 0.0).astype(BF16)
    gain = dot(gain.astype(BF16), top, ((0,), (0,)))
    length = aux_ref[2:3, :LANES].astype(I32)
    at = iota(bias_ref.shape, 1)
    token = iota(bias_ref.shape, 0)
    length_all = jnp.concatenate([length] * (bias_ref.shape[1] // LANES), axis=1)
    seen = (at < length_all) | ((at >= most) & (at <= most + token))
    bias_ref[...] = jnp.where(seen, 1.0, 0.0)
    freq = frequencies(half, (half, 1), 0)
    for i in range(most // LANES + 1):
        at = slice(i * LANES, (i + 1) * LANES)
        lane = iota((1, LANES), 1)
        if i * LANES < most:
            raw = prompt_ref[0, :, at].astype(F32)
            position = res_rows + i * LANES + lane
        else:
            raw = fresh
            position = res_rows + length + lane
        lat = raw[:latent]
        meansq = jnp.sum(lat * lat, axis=0, keepdims=True) * (1.0 / latent)
        out_ref[:latent, at] = (lat * lax.rsqrt(meansq + 1e-06) * gain).astype(BF16)
        angle = position.astype(F32) * freq
        sine, cosine = sine_cosine(angle)
        x1, x2 = raw[latent : latent + half], raw[latent + half :]
        out_ref[latent : latent + half, at] = (x1 * cosine - x2 * sine).astype(BF16)
        out_ref[latent + half :, at] = (x2 * cosine + x1 * sine).astype(BF16)
    fetch.wait()


def score_kernel(
    scale, q_ref, keys_ref, seen_ref, resident_ref, sp_ref, sr_ref, stat_ref
):
    heads = q_ref.shape[0]
    half = q_ref.shape[2]
    width = keys_ref.shape[0]
    rope = width - 2 * half
    rows = 2 * heads
    total = heads * PACK
    flat = q_ref[...].reshape(total, half)
    shape = (rows, total)
    line = iota(shape, 0)
    head, tok = over(line, 4) * 2 + rest_of(line, 2), rest_of(over(line, 2), 2)
    source = iota(shape, 1) - head * PACK

    def picked(r):
        hit = source == r + tok
        return dot(jnp.where(hit, 1.0, 0.0).astype(BF16), flat)

    turned = picked(2 * PART)
    tops, sums = [], []
    for k in range(3):
        query = jnp.concatenate(
            [picked(2 * k), picked(PART + 2 * k), turned[:, k * rope : (k + 1) * rope]], axis=1
        ).astype(BF16)
        keys = keys_ref[...] if k == 0 else resident_ref[k - 1]
        scores = dot(query, keys) * scale
        if k == 0:
            first, second = seen_ref[0:1, :] > 0.5, seen_ref[1:2, :] > 0.5
            token = rest_of(over(iota(scores.shape, 0), 2), 2)
            seen = (first & (token == 0)) | (second & (token == 1))
            scores = jnp.where(seen, scores, -1e30)
            sp_ref[...] = scores
        else:
            sr_ref[k - 1] = scores
        top = jnp.max(scores, axis=1, keepdims=True)
        tops.append(top)
        sums.append(jnp.sum(jnp.exp(scores - top), axis=1, keepdims=True))
    lanes = stat_ref.shape[2]
    here = iota((3 * rows, lanes), 0) == iota((3 * rows, lanes), 1)
    top = jnp.sum(jnp.where(here, jnp.concatenate(tops, axis=0), 0.0), axis=0, keepdims=True)
    total = jnp.sum(jnp.where(here, jnp.concatenate(sums, axis=0), 0.0), axis=0, keepdims=True)
    both = jnp.concatenate([top, total], axis=0)
    stat_ref[...] = jnp.broadcast_to(both[None], stat_ref.shape)


def attend_kernel(
    owners_ref, stat_ref, sp_ref, sr_ref, keys_ref, resident_ref, out_ref
):
    heads = out_ref.shape[0]
    latent = out_ref.shape[1] // PART * LANES
    seqs = owners_ref.shape[0]
    rows = 2 * heads
    device = lax.axis_index("seq")
    lanes = stat_ref.shape[2]
    my_owner = owners_ref[device]
    my_slot = jnp.int32(0)
    seen = jnp.int32(0)
    first = jnp.int32(0)
    second = jnp.int32(0)
    for s in range(seqs):
        owner = owners_ref[s]
        my_slot = my_slot + jnp.where((owner == my_owner) & (s < device), 1, 0)
        mine = owner == device
        first = jnp.where(mine & (seen == 0), s, first)
        second = jnp.where(mine & (seen == 1), s, second)
        seen = seen + jnp.where(mine, 1, 0)

    mine = stat_ref[place_of(device, heads)]
    place = over(iota((1, lanes), 1), rows)
    other = jnp.zeros((2, lanes), F32)
    pairs = [
        (stat_ref[place_of(my_owner, heads)], 1 + my_slot),
        (stat_ref[place_of(first, heads)], 0),
        (stat_ref[place_of(second, heads)], 0),
    ]
    for k, (theirs, segment) in enumerate(pairs):
        moved = jnp.zeros((2, lanes), F32)
        for n in range(3):
            turned = pltpu.roll(theirs, ((k - n) * rows) % lanes, 1)
            moved = jnp.where(segment == n, turned, moved)
        other = jnp.where(place == k, moved, other)
    top = jnp.maximum(mine[0:1], other[0:1])
    total = mine[1:2] * jnp.exp(mine[0:1] - top) + other[1:2] * jnp.exp(other[0:1] - top)
    hit = iota((3 * rows, lanes), 1) == iota((3 * rows, lanes), 0)
    top = jnp.sum(jnp.where(hit, top, 0.0), axis=1, keepdims=True)
    total = jnp.sum(jnp.where(hit, total, 0.0), axis=1, keepdims=True)
    for k in range(3):
        at = slice(k * rows, (k + 1) * rows)
        scores = sp_ref[...] if k == 0 else sr_ref[k - 1]
        keys = keys_ref[:latent, :] if k == 0 else resident_ref[k - 1, :latent, :]
        weights = jnp.exp(scores - top[at]).astype(BF16)
        part = dot(weights, keys, ((1,), (1,))) / total[at]
        for h in range(heads):
            for c in range(latent // LANES):
                at = c * PART + 2 * k
                out_ref[h, at : at + 2, :] = part[2 * h : 2 * h + 2, c * LANES : (c + 1) * LANES]


def project_kernel(
    owners_ref, part_ref, uv_ref, other_uv_ref, wo_ref, other_wo_ref, out_ref
):
    count, each, lanes = part_ref.shape
    seqs = owners_ref.shape[1]
    cuts = each // PART
    rows = 2 * seqs
    core = lax.axis_index("seq") % 2
    owners = owners_ref[...]
    row = iota((2 * rows, 1), 0)
    other, place = over(row, rows), over(rest_of(row, rows), 2)
    seq = device_at(place, count)
    head = jnp.where(other == 0, core, 1 - core)
    owner = column_of(owners, seq)
    slot = column_of(slots_of(owners), seq)
    shape = (2 * rows, count * each)
    first = jnp.broadcast_to(place * each + head, shape)
    second = jnp.broadcast_to(place_of(owner, count) * each + 2 + 2 * slot + head, shape)
    hits = []
    for cut in range(cuts):
        at = iota(shape, 1) - cut * PART
        hits.append(jnp.where((at == first) | (at == second), 1.0, 0.0).astype(BF16))
    hit = jnp.concatenate(hits, axis=0)
    rest = part_ref[...].reshape(count * each, lanes)
    latent = None
    for _ in range(3):
        piece = rest.astype(BF16)
        rest = rest - piece.astype(F32)
        one = dot(hit, piece)
        latent = one if latent is None else latent + one
    latent = latent.astype(BF16)
    latent = jnp.concatenate(
        [latent[c * 2 * rows : (c + 1) * 2 * rows] for c in range(cuts)], axis=1
    )
    half = rest_of(iota((rows, 1), 0), 2)
    cols = wo_ref.shape[2] // 2
    product = None
    for n, (uv, wo) in enumerate(((uv_ref, wo_ref), (other_uv_ref, other_wo_ref))):
        head_out = dot(latent[n * rows : (n + 1) * rows], uv[0])
        for side in range(2):
            lines = jnp.where(half == side, head_out, 0.0).astype(BF16)
            one = dot(lines, wo[0, :, side * cols : (side + 1) * cols])
            product = one if product is None else product + one
    top = jnp.max(jnp.abs(product), axis=1, keepdims=True)
    power = jnp.clip(jnp.floor(jnp.log2(jnp.maximum(top, 1e-35))) + 1.0, -100.0, 100.0)
    coded = jnp.round(product * jnp.exp2(BITS - power)).astype(I32).astype(I16)
    power = jnp.broadcast_to(power, (rows, LANES)).astype(I32).astype(I16)
    for s in range(seqs):
        out_ref[s, :, :cols] = coded[2 * s : 2 * s + 2]
        out_ref[s, :, cols:] = power[2 * s : 2 * s + 2]


def final_kernel(in_ref, out_ref):
    cols = out_ref.shape[2] // 2
    for t in range(2):
        total = None
        for n in range(t, in_ref.shape[0], 2):
            power = in_ref[n, :, cols : cols + 1].astype(I32).astype(F32)
            one = in_ref[n, :, :cols].astype(I32).astype(F32) * jnp.exp2(power - BITS)
            total = one if total is None else total + one
        for j in range(2):
            out_ref[0, t : t + 1, j * cols : (j + 1) * cols] = total[j : j + 1].astype(BF16)


def swap(x):
    count = lax.axis_size("seq")
    order = [device_at(p, count) for p in range(count)]
    return lax.all_to_all(x, "seq", split_axis=0, concat_axis=0, axis_index_groups=[order], tiled=True)


def trade(x, step):
    count = lax.axis_size("seq")
    return lax.ppermute(x, "seq", [(d, d ^ step) for d in range(count)])


def call(kernel, shapes, specs, scratch=(), cost=None, room=None):
    single = not isinstance(shapes, (list, tuple))
    if room is None:
        room = 16 if lax.axis_size("seq") <= 32 else 56
    return pl.pallas_call(
        kernel,
        out_shape=shapes,
        in_specs=specs,
        out_specs=VMEM if single else [VMEM] * len(shapes),
        scratch_shapes=list(scratch),
        cost_estimate=cost,
        compiler_params=pltpu.CompilerParams(vmem_limit_bytes=room * 1024 * 1024),
    )


def on_device(prompt_raw, lengths, owners, resident, new_raw, queries, kv_gain, w_uk, w_uv, w_o):
    count = lax.axis_size("seq")
    seqs = lengths.shape[0]
    most, width = prompt_raw.shape[1:]
    latent = kv_gain.shape[0]
    res_rows = resident.shape[1]
    nope = w_uk.shape[1]
    rope = width - latent
    heads = count
    out_width = w_o.shape[2]
    scale = 1.0 / queries.shape[-1] ** 0.5
    owners_row, lengths_row = owners.reshape(1, seqs), lengths.reshape(1, seqs)
    prompt_raw = prompt_raw.transpose(0, 2, 1)
    resident = resident.transpose(0, 2, 1)
    queries = queries.transpose(0, 2, 1, 3)
    keys_rows = most + LANES

    aux_width = -(-width // LANES) * LANES
    query, aux = call(
        functools.partial(query_kernel, res_rows),
        [
            jax.ShapeDtypeStruct((count, PACK, latent // 2), BF16),
            jax.ShapeDtypeStruct((8, aux_width), F32),
        ],
        [HBM] * 6,
        [
            pltpu.VMEM((1, seqs), I32),
            pltpu.VMEM((1, seqs), I32),
            pltpu.VMEM(queries.shape, BF16),
            pltpu.VMEM((nope, latent), BF16),
            pltpu.VMEM((2, width), BF16),
            pltpu.VMEM((latent,), BF16),
            pltpu.VMEM((2 * seqs, -(-(nope + rope) // LANES) * LANES), F32),
            pltpu.SemaphoreType.DMA((6,)),
        ],
        room=60,
    )(owners_row, lengths_row, queries, w_uk[0], new_raw, kv_gain)
    received = swap(query)
    query, w_uv = lax.optimization_barrier((query, w_uv))
    other_uv = trade(w_uv, 1)
    keys, seen, resident = call(
        functools.partial(compress_kernel, res_rows, latent),
        [
            jax.ShapeDtypeStruct((width, keys_rows), BF16),
            jax.ShapeDtypeStruct((8, keys_rows), F32),
            jax.ShapeDtypeStruct(resident.shape, BF16),
        ],
        [VMEM] * 2 + [HBM],
        [pltpu.SemaphoreType.DMA],
        cost=pl.CostEstimate(flops=10**7, bytes_accessed=10**7, transcendentals=10**5),
    )(aux, prompt_raw, resident)
    lanes = -(-6 * heads // LANES) * LANES
    half = out_width // 2
    scores_p, scores_r, stat = call(
        functools.partial(score_kernel, scale),
        [
            jax.ShapeDtypeStruct((2 * heads, keys_rows), F32),
            jax.ShapeDtypeStruct((2, 2 * heads, res_rows), F32),
            jax.ShapeDtypeStruct((count, 2, lanes), F32),
        ],
        [VMEM] * 4,
    )(received, keys, seen, resident)
    stat, other_uv = lax.optimization_barrier((stat, other_uv))
    stats = swap(stat)
    part = call(
        attend_kernel,
        jax.ShapeDtypeStruct((heads, PART * (latent // LANES), LANES), F32),
        [SMEM] + [VMEM] * 5,
    )(owners, stats, scores_p, scores_r, keys, resident)
    part, w_o = lax.optimization_barrier((part, w_o))
    other_wo = trade(w_o, 1)
    parts = swap(part)
    sums = call(
        project_kernel, jax.ShapeDtypeStruct((seqs, 2, half + LANES), I16), [VMEM] * 6
    )(owners_row, parts, w_uv, other_uv, w_o, other_wo)
    return call(final_kernel, jax.ShapeDtypeStruct((1, 2, out_width), BF16), [VMEM])(swap(sums))


def solution(mesh):
    in_specs = (
        P(("group", "seq"), None, None),
        P("group"),
        P("group"),
        P(("group", "seq"), None, None),
        P("group", None, None),
        P("group", None, "seq", None),
        P(),
        P("seq", None, None),
        P("seq", None, None),
        P("seq", None, None),
    )
    out_specs = P(("group", "seq"), None, None)
    return jax.shard_map(
        on_device, mesh=mesh, in_specs=in_specs, out_specs=out_specs, check_vma=False
    )
```

```python
import functools

import jax
import jax.numpy as jnp
import numpy as np
from jax import lax
from jax.experimental import pallas as pl
from jax.experimental.pallas import tpu as pltpu
from jax.sharding import PartitionSpec as P

F32 = jnp.float32
BF16 = jnp.bfloat16
I32 = jnp.int32
I16 = jnp.int16
VMEM = pl.BlockSpec(memory_space=pltpu.VMEM)
SMEM = pl.BlockSpec(memory_space=pltpu.SMEM)
HBM = pl.BlockSpec(memory_space=pltpu.HBM)
LANES = 128
PACK = 16
PART = 6
BITS = 14.0
NEAR = 4


def iota(shape, dim):
    return lax.broadcasted_iota(I32, shape, dim)


def place_of(device, count):
    chips = count // 2
    return (((chips // 2 + 1) - (device >> 1)) & (chips - 1)) * 2 + (device & 1)


def over(x, n):
    return x >> (n.bit_length() - 1)


def rest_of(x, n):
    return x & (n - 1)


def dot(a, b, dims=((1,), (0,))):
    return lax.dot_general(a, b, (dims, ((), ())), preferred_element_type=F32)


def column_of(row, picks):
    n, width = picks.shape[0], row.shape[1]
    hit = iota((n, width), 1) == picks
    return jnp.sum(jnp.where(hit, row, 0), axis=1, keepdims=True)


def slots_of(owners_row):
    seqs = owners_row.shape[1]
    owners_col = column_of(owners_row, iota((seqs, 1), 0))
    earlier = iota((seqs, seqs), 0) < iota((seqs, seqs), 1)
    same = (owners_col == owners_row) & earlier
    return jnp.sum(jnp.where(same, 1, 0), axis=0, keepdims=True)


def doubled(row, times):
    seqs = row.shape[1]
    col = column_of(row, iota((seqs, 1), 0))
    shape = (seqs, 2 * seqs * times)
    hit = over(rest_of(iota(shape, 1), 2 * seqs), 2) == iota(shape, 0)
    return jnp.sum(jnp.where(hit, col, 0), axis=0, keepdims=True)


def frequencies(half, shape, dim):
    at = rest_of(iota(shape, dim), half)
    values = np.float32(10000.0) ** (-(np.arange(half, dtype=np.float32) * np.float32(2.0)) / np.float32(2 * half))
    level = [jnp.full(shape, float(v), F32) for v in values]
    bit = 1
    while len(level) > 1:
        odd = (at & bit) != 0
        level = [jnp.where(odd, b, a) for a, b in zip(level[::2], level[1::2])]
        bit *= 2
    return level[0]


def sine_cosine(angle):
    count = jnp.floor(angle * (2.0 / np.pi) + 0.5)
    x = ((angle - count * 1.5703125) - count * 4.837512969970703125e-4) - count * 7.54978995489188216e-8
    quarter = count.astype(I32)
    y = x * x
    sine = x + x * y * (-1.6666654611e-1 + y * (8.3321608736e-3 - y * 1.9515295891e-4))
    cosine = 1.0 - 0.5 * y + y * y * (4.166664568298827e-2 + y * (-1.388731625493765e-3 + y * 2.443315711809948e-5))
    odd = rest_of(quarter, 2) == 1
    first, second = jnp.where(odd, cosine, sine), jnp.where(odd, sine, cosine)
    first = jnp.where(rest_of(quarter, 4) >= 2, -first, first)
    second = jnp.where(rest_of(quarter + 1, 4) >= 2, -second, second)
    return first, second


def query_kernel(
    res_rows,
    owners_hbm,
    lengths_hbm,
    queries_hbm,
    uk_hbm,
    new_hbm,
    gain_hbm,
    out_ref,
    aux_ref,
    owners_ref,
    lengths_ref,
    queries_ref,
    uk_ref,
    new_ref,
    gain_ref,
    flat,
    sems,
):
    device = lax.axis_index("seq")
    copies = []
    pairs = [
        (owners_hbm, owners_ref),
        (lengths_hbm, lengths_ref),
        (queries_hbm, queries_ref),
        (uk_hbm, uk_ref),
        (new_hbm.at[device], new_ref),
        (gain_hbm, gain_ref),
    ]
    for n, (source, target) in enumerate(pairs):
        copies.append(pltpu.make_async_copy(source, target, sems.at[n]))
        copies[-1].start()
    for copy in copies:
        copy.wait()
    seqs = owners_ref.shape[1]
    nope, latent = uk_ref.shape
    rope = queries_ref.shape[3] - nope
    half = latent // 2
    rows = 2 * seqs
    for s in range(seqs):
        flat[2 * s : 2 * s + 2, : nope + rope] = queries_ref[s, 0].astype(F32)
    values = flat[:, : nope + rope]
    absorbed = dot(values[:, :nope].astype(BF16), uk_ref[...]).astype(BF16)
    row = iota((rows, 1), 0)
    lengths = column_of(lengths_ref[...], over(row, 2))
    angle = (res_rows + lengths + rest_of(row, 2)).astype(F32) * frequencies(rope // 2, (1, rope), 1)
    x = values[:, nope:]
    swapped = jnp.concatenate([x[:, rope // 2 :], x[:, : rope // 2]], axis=1)
    sine, cosine = sine_cosine(angle)
    sine = jnp.where(iota(x.shape, 1) < rope // 2, -sine, sine)
    turned = x * cosine + swapped * sine
    zero = jnp.zeros((rows, rope), F32)
    pieces = [absorbed[:, :half], absorbed[:, half:]]
    for k in range(3):
        blocks = [turned if j == k else zero for j in range(half // rope)]
        pieces.append(jnp.concatenate(blocks, axis=1).astype(BF16))
    owners = owners_ref[...]
    owner = doubled(owners, 5)
    slot = doubled(slots_of(owners), 5)
    count = out_ref.shape[0]
    shape = (count, 5 * rows)
    dest = place_of(iota(shape, 0), count)
    lane = iota(shape, 1)
    piece, seq, tok = over(lane, rows), over(rest_of(lane, rows), 2), rest_of(lane, 2)
    third = piece - 2
    first = jnp.where(piece < 2, piece * PART, 2 * PART) + tok
    own = seq == dest
    here = jnp.where(owner == dest, slot + 1, jnp.where(own, 0, -1))
    wide = jnp.where(here >= 0, first + 2 * here, -1)
    target = jnp.where(piece < 2, wide, jnp.where(here == third, first, -1))
    again = jnp.where((owner == dest) & own & ((piece < 2) | (third == 0)), first, -1)
    r = iota((PACK, 5 * rows), 0)
    hits = []
    for d in range(count):
        hit = (r == target[d : d + 1]) | (r == again[d : d + 1])
        hits.append(jnp.where(hit, 1.0, 0.0).astype(BF16))
    hit = jnp.concatenate(hits, axis=0)
    pieces = jnp.concatenate(pieces, axis=0)
    result = dot(hit, pieces)
    out_ref[...] = result.astype(BF16).reshape(out_ref.shape)
    width = new_ref.shape[1]
    aux_ref[0:2, :width] = new_ref[...].astype(F32)
    mine = jnp.where(iota(lengths_ref.shape, 1) == device, lengths_ref[...], 0)
    mine = jnp.sum(mine, axis=1, keepdims=True).astype(F32)
    aux_ref[2:3, :] = jnp.broadcast_to(mine, (1, aux_ref.shape[1]))
    aux_ref[3:4, :latent] = gain_ref[...].astype(F32).reshape(1, latent)


def compress_kernel(
    res_rows, latent, aux_ref, prompt_ref, resident_hbm, out_ref, bias_ref, resident_ref, sem
):
    fetch = pltpu.make_async_copy(resident_hbm, resident_ref, sem)
    fetch.start()
    width, most = prompt_ref.shape[1:]
    half = (width - latent) // 2
    fresh = jnp.concatenate([aux_ref[0:2, :width], jnp.zeros((PACK - 2, width), F32)], axis=0)
    pick = jnp.where(iota((PACK, LANES), 0) == iota((PACK, LANES), 1), 1.0, 0.0).astype(BF16)
    fresh = dot(fresh.astype(BF16), pick, ((0,), (0,)))
    gain = jnp.broadcast_to(aux_ref[3:4, :latent], (PACK, latent))
    top = jnp.where(iota((PACK, LANES), 0) == 0, 1.0, 0.0).astype(BF16)
    gain = dot(gain.astype(BF16), top, ((0,), (0,)))
    length = aux_ref[2:3, :LANES].astype(I32)
    at = iota(bias_ref.shape, 1)
    token = iota(bias_ref.shape, 0)
    length_all = jnp.concatenate([length] * (bias_ref.shape[1] // LANES), axis=1)
    seen = (at < length_all) | ((at >= most) & (at <= most + token))
    bias_ref[...] = jnp.where(seen, 1.0, 0.0)
    freq = frequencies(half, (half, 1), 0)
    for i in range(most // LANES + 1):
        at = slice(i * LANES, (i + 1) * LANES)
        lane = iota((1, LANES), 1)
        if i * LANES < most:
            raw = prompt_ref[0, :, at].astype(F32)
            position = res_rows + i * LANES + lane
        else:
            raw = fresh
            position = res_rows + length + lane
        lat = raw[:latent]
        meansq = jnp.sum(lat * lat, axis=0, keepdims=True) * (1.0 / latent)
        out_ref[:latent, at] = (lat * lax.rsqrt(meansq + 1e-06) * gain).astype(BF16)
        angle = position.astype(F32) * freq
        sine, cosine = sine_cosine(angle)
        x1, x2 = raw[latent : latent + half], raw[latent + half :]
        out_ref[latent : latent + half, at] = (x1 * cosine - x2 * sine).astype(BF16)
        out_ref[latent + half :, at] = (x2 * cosine + x1 * sine).astype(BF16)
    fetch.wait()


def score_kernel(
    scale, q_ref, keys_ref, seen_ref, resident_ref, sp_ref, sr_ref, stat_ref
):
    heads = q_ref.shape[0]
    half = q_ref.shape[2]
    width = keys_ref.shape[0]
    rope = width - 2 * half
    rows = 2 * heads
    total = heads * PACK
    flat = q_ref[...].reshape(total, half)
    shape = (rows, total)
    line = iota(shape, 0)
    head, tok = over(line, 4) * 2 + rest_of(line, 2), rest_of(over(line, 2), 2)
    source = iota(shape, 1) - head * PACK

    def picked(r):
        hit = source == r + tok
        return dot(jnp.where(hit, 1.0, 0.0).astype(BF16), flat)

    turned = picked(2 * PART)
    tops, sums = [], []
    for k in range(3):
        query = jnp.concatenate(
            [picked(2 * k), picked(PART + 2 * k), turned[:, k * rope : (k + 1) * rope]], axis=1
        ).astype(BF16)
        keys = keys_ref[...] if k == 0 else resident_ref[k - 1]
        scores = dot(query, keys) * scale
        if k == 0:
            first, second = seen_ref[0:1, :] > 0.5, seen_ref[1:2, :] > 0.5
            token = rest_of(over(iota(scores.shape, 0), 2), 2)
            seen = (first & (token == 0)) | (second & (token == 1))
            scores = jnp.where(seen, scores, -1e30)
            sp_ref[...] = scores
        else:
            sr_ref[k - 1] = scores
        top = jnp.max(scores, axis=1, keepdims=True)
        tops.append(top)
        sums.append(jnp.sum(jnp.exp(scores - top), axis=1, keepdims=True))
    lanes = stat_ref.shape[2]
    here = iota((3 * rows, lanes), 0) == iota((3 * rows, lanes), 1)
    top = jnp.sum(jnp.where(here, jnp.concatenate(tops, axis=0), 0.0), axis=0, keepdims=True)
    total = jnp.sum(jnp.where(here, jnp.concatenate(sums, axis=0), 0.0), axis=0, keepdims=True)
    both = jnp.concatenate([top, total], axis=0)
    stat_ref[...] = jnp.broadcast_to(both[None], stat_ref.shape)


def attend_kernel(
    owners_ref, stat_ref, sp_ref, sr_ref, keys_ref, resident_ref, out_ref
):
    heads = out_ref.shape[0]
    latent = out_ref.shape[1] // PART * LANES
    seqs = owners_ref.shape[0]
    rows = 2 * heads
    device = lax.axis_index("seq")
    lanes = stat_ref.shape[2]
    my_owner = owners_ref[device]
    my_slot = jnp.int32(0)
    seen = jnp.int32(0)
    first = jnp.int32(0)
    second = jnp.int32(0)
    for s in range(seqs):
        owner = owners_ref[s]
        my_slot = my_slot + jnp.where((owner == my_owner) & (s < device), 1, 0)
        mine = owner == device
        first = jnp.where(mine & (seen == 0), s, first)
        second = jnp.where(mine & (seen == 1), s, second)
        seen = seen + jnp.where(mine, 1, 0)

    mine = stat_ref[place_of(device, heads)]
    place = over(iota((1, lanes), 1), rows)
    other = jnp.zeros((2, lanes), F32)
    pairs = [
        (stat_ref[place_of(my_owner, heads)], 1 + my_slot),
        (stat_ref[place_of(first, heads)], 0),
        (stat_ref[place_of(second, heads)], 0),
    ]
    for k, (theirs, segment) in enumerate(pairs):
        moved = jnp.zeros((2, lanes), F32)
        for n in range(3):
            turned = pltpu.roll(theirs, ((k - n) * rows) % lanes, 1)
            moved = jnp.where(segment == n, turned, moved)
        other = jnp.where(place == k, moved, other)
    top = jnp.maximum(mine[0:1], other[0:1])
    total = mine[1:2] * jnp.exp(mine[0:1] - top) + other[1:2] * jnp.exp(other[0:1] - top)
    hit = iota((3 * rows, lanes), 1) == iota((3 * rows, lanes), 0)
    top = jnp.sum(jnp.where(hit, top, 0.0), axis=1, keepdims=True)
    total = jnp.sum(jnp.where(hit, total, 0.0), axis=1, keepdims=True)
    result = None
    for k in range(3):
        scores = sp_ref[...] if k == 0 else sr_ref[k - 1]
        keys = keys_ref[:latent, :] if k == 0 else resident_ref[k - 1, :latent, :]
        weights = jnp.exp(scores - top[k * rows : (k + 1) * rows]).astype(BF16)
        zero = jnp.zeros(weights.shape, BF16)
        blocks = [weights if j == k else zero for j in range(lanes // rows)]
        one = dot(keys, jnp.concatenate(blocks, axis=0), ((1,), (1,)))
        result = one if result is None else result + one
    result = result.T[: 3 * rows] / total
    for k in range(3):
        for h in range(heads):
            for c in range(latent // LANES):
                at = c * PART + 2 * k
                line = k * rows + 2 * h
                out_ref[h, at : at + 2, :] = result[line : line + 2, c * LANES : (c + 1) * LANES]


def project_kernel(
    owners_ref, part_ref, uv_ref, other_uv_ref, wo_ref, other_wo_ref, out_ref
):
    count, each, lanes = part_ref.shape
    seqs = owners_ref.shape[1]
    cuts = each // PART
    rows = 2 * seqs
    core = lax.axis_index("seq") % 2
    owners = owners_ref[...]
    row = iota((2 * rows, 1), 0)
    other, place = over(row, rows), over(rest_of(row, rows), 2)
    seq = place_of(place, count)
    head = jnp.where(other == 0, core, 1 - core)
    owner = column_of(owners, seq)
    slot = column_of(slots_of(owners), seq)
    shape = (2 * rows, count * each)
    first = jnp.broadcast_to(place * each + head, shape)
    second = jnp.broadcast_to(place_of(owner, count) * each + 2 + 2 * slot + head, shape)
    hits = []
    for cut in range(cuts):
        at = iota(shape, 1) - cut * PART
        hits.append(jnp.where((at == first) | (at == second), 1.0, 0.0).astype(BF16))
    hit = jnp.concatenate(hits, axis=0)
    rest = part_ref[...].reshape(count * each, lanes)
    latent = None
    for _ in range(3):
        piece = rest.astype(BF16)
        rest = rest - piece.astype(F32)
        one = dot(hit, piece)
        latent = one if latent is None else latent + one
    latent = latent.astype(BF16)
    latent = jnp.concatenate(
        [latent[c * 2 * rows : (c + 1) * 2 * rows] for c in range(cuts)], axis=1
    )
    half = rest_of(iota((rows, 1), 0), 2)
    cols = wo_ref.shape[2] // 2
    product = None
    for n, (uv, wo) in enumerate(((uv_ref, wo_ref), (other_uv_ref, other_wo_ref))):
        head_out = dot(latent[n * rows : (n + 1) * rows], uv[0])
        for side in range(2):
            lines = jnp.where(half == side, head_out, 0.0).astype(BF16)
            one = dot(lines, wo[0, :, side * cols : (side + 1) * cols])
            product = one if product is None else product + one
    top = jnp.max(jnp.abs(product), axis=1, keepdims=True)
    power = jnp.clip(jnp.floor(jnp.log2(jnp.maximum(top, 1e-35))) + 1.0, -100.0, 100.0)
    coded = jnp.round(product * jnp.exp2(BITS - power)).astype(I32).astype(I16)
    power = jnp.broadcast_to(power, (rows, LANES)).astype(I32).astype(I16)
    for s in range(seqs):
        out_ref[s, :, :cols] = coded[2 * s : 2 * s + 2]
        out_ref[s, :, cols:] = power[2 * s : 2 * s + 2]


def final_kernel(in_ref, out_ref):
    cols = out_ref.shape[2] // 2
    for t in range(2):
        total = None
        for n in range(t, in_ref.shape[0], 2):
            power = in_ref[n, :, cols : cols + 1].astype(I32).astype(F32)
            one = in_ref[n, :, :cols].astype(I32).astype(F32) * jnp.exp2(power - BITS)
            total = one if total is None else total + one
        for j in range(2):
            out_ref[0, t : t + 1, j * cols : (j + 1) * cols] = total[j : j + 1].astype(BF16)


def swap(x):
    count = lax.axis_size("seq")
    order = [place_of(p, count) for p in range(count)]
    return lax.all_to_all(x, "seq", split_axis=0, concat_axis=0, axis_index_groups=[order], tiled=True)


def trade(x, step):
    count = lax.axis_size("seq")
    return lax.ppermute(x, "seq", [(d, d ^ step) for d in range(count)])


def call(kernel, shapes, specs, scratch=(), cost=None, room=None):
    single = not isinstance(shapes, (list, tuple))
    if room is None:
        room = 16 if lax.axis_size("seq") <= 32 else 56
    return pl.pallas_call(
        kernel,
        out_shape=shapes,
        in_specs=specs,
        out_specs=VMEM if single else [VMEM] * len(shapes),
        scratch_shapes=list(scratch),
        cost_estimate=cost,
        compiler_params=pltpu.CompilerParams(vmem_limit_bytes=room * 1024 * 1024),
    )


def on_device(prompt_raw, lengths, owners, resident, new_raw, queries, kv_gain, w_uk, w_uv, w_o):
    count = lax.axis_size("seq")
    seqs = lengths.shape[0]
    most, width = prompt_raw.shape[1:]
    latent = kv_gain.shape[0]
    res_rows = resident.shape[1]
    nope = w_uk.shape[1]
    rope = width - latent
    heads = count
    out_width = w_o.shape[2]
    scale = 1.0 / queries.shape[-1] ** 0.5
    owners_row, lengths_row = owners.reshape(1, seqs), lengths.reshape(1, seqs)
    prompt_raw = prompt_raw.transpose(0, 2, 1)
    resident = resident.transpose(0, 2, 1)
    queries = queries.transpose(0, 2, 1, 3)
    keys_rows = most + LANES

    aux_width = -(-width // LANES) * LANES
    query, aux = call(
        functools.partial(query_kernel, res_rows),
        [
            jax.ShapeDtypeStruct((count, PACK, latent // 2), BF16),
            jax.ShapeDtypeStruct((8, aux_width), F32),
        ],
        [HBM] * 6,
        [
            pltpu.VMEM((1, seqs), I32),
            pltpu.VMEM((1, seqs), I32),
            pltpu.VMEM(queries.shape, BF16),
            pltpu.VMEM((nope, latent), BF16),
            pltpu.VMEM((2, width), BF16),
            pltpu.VMEM((latent,), BF16),
            pltpu.VMEM((2 * seqs, -(-(nope + rope) // LANES) * LANES), F32),
            pltpu.SemaphoreType.DMA((6,)),
        ],
        room=60,
    )(owners_row, lengths_row, queries, w_uk[0], new_raw, kv_gain)
    received = swap(query)
    query, w_uv = lax.optimization_barrier((query, w_uv))
    other_uv = trade(w_uv, 1)
    keys, seen, resident = call(
        functools.partial(compress_kernel, res_rows, latent),
        [
            jax.ShapeDtypeStruct((width, keys_rows), BF16),
            jax.ShapeDtypeStruct((8, keys_rows), F32),
            jax.ShapeDtypeStruct(resident.shape, BF16),
        ],
        [VMEM] * 2 + [HBM],
        [pltpu.SemaphoreType.DMA],
        cost=pl.CostEstimate(flops=10**7, bytes_accessed=10**7, transcendentals=10**5),
    )(aux, prompt_raw, resident)
    lanes = -(-6 * heads // LANES) * LANES
    half = out_width // 2
    scores_p, scores_r, stat = call(
        functools.partial(score_kernel, scale),
        [
            jax.ShapeDtypeStruct((2 * heads, keys_rows), F32),
            jax.ShapeDtypeStruct((2, 2 * heads, res_rows), F32),
            jax.ShapeDtypeStruct((count, 2, lanes), F32),
        ],
        [VMEM] * 4,
    )(received, keys, seen, resident)
    stat, other_uv = lax.optimization_barrier((stat, other_uv))
    stats = swap(stat)
    part = call(
        attend_kernel,
        jax.ShapeDtypeStruct((heads, PART * (latent // LANES), LANES), F32),
        [SMEM] + [VMEM] * 5,
    )(owners, stats, scores_p, scores_r, keys, resident)
    part, w_o = lax.optimization_barrier((part, w_o))
    other_wo = trade(w_o, 1)
    parts = swap(part)
    sums = call(
        project_kernel, jax.ShapeDtypeStruct((seqs, 2, half + LANES), I16), [VMEM] * 6
    )(owners_row, parts, w_uv, other_uv, w_o, other_wo)
    return call(final_kernel, jax.ShapeDtypeStruct((1, 2, out_width), BF16), [VMEM])(swap(sums))


def solution(mesh):
    in_specs = (
        P(("group", "seq"), None, None),
        P("group"),
        P("group"),
        P(("group", "seq"), None, None),
        P("group", None, None),
        P("group", None, "seq", None),
        P(),
        P("seq", None, None),
        P("seq", None, None),
        P("seq", None, None),
    )
    out_specs = P(("group", "seq"), None, None)
    return jax.shard_map(
        on_device, mesh=mesh, in_specs=in_specs, out_specs=out_specs, check_vma=False
    )
```

```python
import functools

import jax
import jax.numpy as jnp
import numpy as np
from jax import lax
from jax.experimental import pallas as pl
from jax.experimental.pallas import tpu as pltpu
from jax.sharding import PartitionSpec as P

F32 = jnp.float32
BF16 = jnp.bfloat16
I32 = jnp.int32
I16 = jnp.int16
VMEM = pl.BlockSpec(memory_space=pltpu.VMEM)
SMEM = pl.BlockSpec(memory_space=pltpu.SMEM)
HBM = pl.BlockSpec(memory_space=pltpu.HBM)
LANES = 128
PACK = 16
PART = 6
BITS = 14.0
NEAR = 4


def iota(shape, dim):
    return lax.broadcasted_iota(I32, shape, dim)


def place_of(device, count):
    chips = count // 2
    return (((chips // 2 + 1) - (device >> 1)) & (chips - 1)) * 2 + (device & 1)


def over(x, n):
    return x >> (n.bit_length() - 1)


def rest_of(x, n):
    return x & (n - 1)


def dot(a, b, dims=((1,), (0,))):
    return lax.dot_general(a, b, (dims, ((), ())), preferred_element_type=F32)


def column_of(row, picks):
    n, width = picks.shape[0], row.shape[1]
    hit = iota((n, width), 1) == picks
    return jnp.sum(jnp.where(hit, row, 0), axis=1, keepdims=True)


def slots_of(owners_row):
    seqs = owners_row.shape[1]
    owners_col = column_of(owners_row, iota((seqs, 1), 0))
    earlier = iota((seqs, seqs), 0) < iota((seqs, seqs), 1)
    same = (owners_col == owners_row) & earlier
    return jnp.sum(jnp.where(same, 1, 0), axis=0, keepdims=True)


def doubled(row, times):
    seqs = row.shape[1]
    col = column_of(row, iota((seqs, 1), 0))
    shape = (seqs, 2 * seqs * times)
    hit = over(rest_of(iota(shape, 1), 2 * seqs), 2) == iota(shape, 0)
    return jnp.sum(jnp.where(hit, col, 0), axis=0, keepdims=True)


def frequencies(half, shape, dim):
    at = rest_of(iota(shape, dim), half)
    values = np.float32(10000.0) ** (-(np.arange(half, dtype=np.float32) * np.float32(2.0)) / np.float32(2 * half))
    level = [jnp.full(shape, float(v), F32) for v in values]
    bit = 1
    while len(level) > 1:
        odd = (at & bit) != 0
        level = [jnp.where(odd, b, a) for a, b in zip(level[::2], level[1::2])]
        bit *= 2
    return level[0]


def sine_cosine(angle):
    count = jnp.floor(angle * (2.0 / np.pi) + 0.5)
    x = ((angle - count * 1.5703125) - count * 4.837512969970703125e-4) - count * 7.54978995489188216e-8
    quarter = count.astype(I32)
    y = x * x
    sine = x + x * y * (-1.6666654611e-1 + y * (8.3321608736e-3 - y * 1.9515295891e-4))
    cosine = 1.0 - 0.5 * y + y * y * (4.166664568298827e-2 + y * (-1.388731625493765e-3 + y * 2.443315711809948e-5))
    odd = rest_of(quarter, 2) == 1
    first, second = jnp.where(odd, cosine, sine), jnp.where(odd, sine, cosine)
    first = jnp.where(rest_of(quarter, 4) >= 2, -first, first)
    second = jnp.where(rest_of(quarter + 1, 4) >= 2, -second, second)
    return first, second


def query_kernel(
    res_rows,
    owners_hbm,
    lengths_hbm,
    queries_hbm,
    uk_hbm,
    new_hbm,
    gain_hbm,
    out_ref,
    aux_ref,
    owners_ref,
    lengths_ref,
    queries_ref,
    uk_ref,
    new_ref,
    gain_ref,
    flat,
    sems,
):
    device = lax.axis_index("seq")
    copies = []
    pairs = [
        (owners_hbm, owners_ref),
        (lengths_hbm, lengths_ref),
        (queries_hbm, queries_ref),
        (uk_hbm, uk_ref),
        (new_hbm.at[device], new_ref),
        (gain_hbm, gain_ref),
    ]
    for n, (source, target) in enumerate(pairs):
        copies.append(pltpu.make_async_copy(source, target, sems.at[n]))
        copies[-1].start()
    for copy in copies:
        copy.wait()
    seqs = owners_ref.shape[1]
    nope, latent = uk_ref.shape
    rope = queries_ref.shape[3] - nope
    half = latent // 2
    rows = 2 * seqs
    for s in range(seqs):
        flat[2 * s : 2 * s + 2, : nope + rope] = queries_ref[s, 0].astype(F32)
    values = flat[:, : nope + rope]
    absorbed = dot(values[:, :nope].astype(BF16), uk_ref[...]).astype(BF16)
    row = iota((rows, 1), 0)
    lengths = column_of(lengths_ref[...], over(row, 2))
    angle = (res_rows + lengths + rest_of(row, 2)).astype(F32) * frequencies(rope // 2, (1, rope), 1)
    x = values[:, nope:]
    swapped = jnp.concatenate([x[:, rope // 2 :], x[:, : rope // 2]], axis=1)
    sine, cosine = sine_cosine(angle)
    sine = jnp.where(iota(x.shape, 1) < rope // 2, -sine, sine)
    turned = x * cosine + swapped * sine
    zero = jnp.zeros((rows, rope), F32)
    pieces = [absorbed[:, :half], absorbed[:, half:]]
    for k in range(3):
        blocks = [turned if j == k else zero for j in range(half // rope)]
        pieces.append(jnp.concatenate(blocks, axis=1).astype(BF16))
    owners = owners_ref[...]
    packed = doubled(owners * 4 + slots_of(owners), 5)
    owner, slot = over(packed, 4), rest_of(packed, 4)
    count = out_ref.shape[0]
    shape = (count, 5 * rows)
    dest = place_of(iota(shape, 0), count)
    lane = iota(shape, 1)
    piece, seq, tok = over(lane, rows), over(rest_of(lane, rows), 2), rest_of(lane, 2)
    third = piece - 2
    first = jnp.where(piece < 2, piece * PART, 2 * PART) + tok
    own = seq == dest
    here = jnp.where(owner == dest, slot + 1, jnp.where(own, 0, -1))
    wide = jnp.where(here >= 0, first + 2 * here, -1)
    target = jnp.where(piece < 2, wide, jnp.where(here == third, first, -1))
    again = jnp.where((owner == dest) & own & ((piece < 2) | (third == 0)), first, -1)
    r = iota((PACK, 5 * rows), 0)
    hits = []
    for d in range(count):
        hit = (r == target[d : d + 1]) | (r == again[d : d + 1])
        hits.append(jnp.where(hit, 1.0, 0.0).astype(BF16))
    hit = jnp.concatenate(hits, axis=0)
    pieces = jnp.concatenate(pieces, axis=0)
    result = dot(hit, pieces)
    out_ref[...] = result.astype(BF16).reshape(out_ref.shape)
    width = new_ref.shape[1]
    aux_ref[0:2, :width] = new_ref[...].astype(F32)
    mine = jnp.where(iota(lengths_ref.shape, 1) == device, lengths_ref[...], 0)
    mine = jnp.sum(mine, axis=1, keepdims=True).astype(F32)
    aux_ref[2:3, :] = jnp.broadcast_to(mine, (1, aux_ref.shape[1]))
    aux_ref[3:4, :latent] = gain_ref[...].astype(F32).reshape(1, latent)


def compress_kernel(
    res_rows, latent, aux_ref, prompt_ref, resident_hbm, out_ref, bias_ref, resident_ref, sem
):
    fetch = pltpu.make_async_copy(resident_hbm, resident_ref, sem)
    fetch.start()
    width, most = prompt_ref.shape[1:]
    half = (width - latent) // 2
    fresh = jnp.concatenate([aux_ref[0:2, :width], jnp.zeros((PACK - 2, width), F32)], axis=0)
    pick = jnp.where(iota((PACK, LANES), 0) == iota((PACK, LANES), 1), 1.0, 0.0).astype(BF16)
    fresh = dot(fresh.astype(BF16), pick, ((0,), (0,)))
    gain = jnp.broadcast_to(aux_ref[3:4, :latent], (PACK, latent))
    top = jnp.where(iota((PACK, LANES), 0) == 0, 1.0, 0.0).astype(BF16)
    gain = dot(gain.astype(BF16), top, ((0,), (0,)))
    length = aux_ref[2:3, :LANES].astype(I32)
    at = iota(bias_ref.shape, 1)
    token = iota(bias_ref.shape, 0)
    length_all = jnp.concatenate([length] * (bias_ref.shape[1] // LANES), axis=1)
    seen = (at < length_all) | ((at >= most) & (at <= most + token))
    bias_ref[...] = jnp.where(seen, 1.0, 0.0)
    freq = frequencies(half, (half, 1), 0)
    for i in range(most // LANES + 1):
        at = slice(i * LANES, (i + 1) * LANES)
        lane = iota((1, LANES), 1)
        if i * LANES < most:
            raw = prompt_ref[0, :, at].astype(F32)
            position = res_rows + i * LANES + lane
        else:
            raw = fresh
            position = res_rows + length + lane
        lat = raw[:latent]
        meansq = jnp.sum(lat * lat, axis=0, keepdims=True) * (1.0 / latent)
        out_ref[:latent, at] = (lat * lax.rsqrt(meansq + 1e-06) * gain).astype(BF16)
        angle = position.astype(F32) * freq
        sine, cosine = sine_cosine(angle)
        x1, x2 = raw[latent : latent + half], raw[latent + half :]
        out_ref[latent : latent + half, at] = (x1 * cosine - x2 * sine).astype(BF16)
        out_ref[latent + half :, at] = (x2 * cosine + x1 * sine).astype(BF16)
    fetch.wait()


def score_kernel(
    scale, q_ref, keys_ref, seen_ref, resident_ref, sp_ref, sr_ref, stat_ref
):
    heads = q_ref.shape[0]
    half = q_ref.shape[2]
    width = keys_ref.shape[0]
    rope = width - 2 * half
    rows = 2 * heads
    total = heads * PACK
    flat = q_ref[...].reshape(total, half)
    shape = (rows, total)
    line = iota(shape, 0)
    head, tok = over(line, 4) * 2 + rest_of(line, 2), rest_of(over(line, 2), 2)
    source = iota(shape, 1) - head * PACK

    def picked(r):
        hit = source == r + tok
        return dot(jnp.where(hit, 1.0, 0.0).astype(BF16), flat)

    turned = picked(2 * PART)
    tops, sums = [], []
    for k in range(3):
        query = jnp.concatenate(
            [picked(2 * k), picked(PART + 2 * k), turned[:, k * rope : (k + 1) * rope]], axis=1
        ).astype(BF16)
        keys = keys_ref[...] if k == 0 else resident_ref[k - 1]
        scores = dot(query, keys) * scale
        if k == 0:
            first, second = seen_ref[0:1, :] > 0.5, seen_ref[1:2, :] > 0.5
            token = rest_of(over(iota(scores.shape, 0), 2), 2)
            seen = (first & (token == 0)) | (second & (token == 1))
            scores = jnp.where(seen, scores, -1e30)
            sp_ref[...] = scores
        else:
            sr_ref[k - 1] = scores
        top = jnp.max(scores, axis=1, keepdims=True)
        tops.append(top)
        sums.append(jnp.sum(jnp.exp(scores - top), axis=1, keepdims=True))
    lanes = stat_ref.shape[2]
    here = iota((3 * rows, lanes), 0) == iota((3 * rows, lanes), 1)
    top = jnp.sum(jnp.where(here, jnp.concatenate(tops, axis=0), 0.0), axis=0, keepdims=True)
    total = jnp.sum(jnp.where(here, jnp.concatenate(sums, axis=0), 0.0), axis=0, keepdims=True)
    both = jnp.concatenate([top, total], axis=0)
    stat_ref[...] = jnp.broadcast_to(both[None], stat_ref.shape)


def attend_kernel(
    owners_ref, stat_ref, sp_ref, sr_ref, keys_ref, resident_ref, _, out_ref, __
):
    heads = out_ref.shape[0]
    latent = out_ref.shape[1] // PART * LANES
    seqs = owners_ref.shape[0]
    rows = 2 * heads
    device = lax.axis_index("seq")
    lanes = stat_ref.shape[2]
    my_owner = owners_ref[device]
    my_slot = jnp.int32(0)
    seen = jnp.int32(0)
    first = jnp.int32(0)
    second = jnp.int32(0)
    for s in range(seqs):
        owner = owners_ref[s]
        my_slot = my_slot + jnp.where((owner == my_owner) & (s < device), 1, 0)
        mine = owner == device
        first = jnp.where(mine & (seen == 0), s, first)
        second = jnp.where(mine & (seen == 1), s, second)
        seen = seen + jnp.where(mine, 1, 0)

    mine = stat_ref[place_of(device, heads)]
    place = over(iota((1, lanes), 1), rows)
    other = jnp.zeros((2, lanes), F32)
    pairs = [
        (stat_ref[place_of(my_owner, heads)], 1 + my_slot),
        (stat_ref[place_of(first, heads)], 0),
        (stat_ref[place_of(second, heads)], 0),
    ]
    for k, (theirs, segment) in enumerate(pairs):
        moved = jnp.zeros((2, lanes), F32)
        for n in range(3):
            turned = pltpu.roll(theirs, ((k - n) * rows) % lanes, 1)
            moved = jnp.where(segment == n, turned, moved)
        other = jnp.where(place == k, moved, other)
    top = jnp.maximum(mine[0:1], other[0:1])
    total = mine[1:2] * jnp.exp(mine[0:1] - top) + other[1:2] * jnp.exp(other[0:1] - top)
    hit = iota((3 * rows, lanes), 1) == iota((3 * rows, lanes), 0)
    top = jnp.sum(jnp.where(hit, top, 0.0), axis=1, keepdims=True)
    total = jnp.sum(jnp.where(hit, total, 0.0), axis=1, keepdims=True)
    for k in range(3):
        at = slice(k * rows, (k + 1) * rows)
        scores = sp_ref[...] if k == 0 else sr_ref[k - 1]
        keys = keys_ref[:latent, :] if k == 0 else resident_ref[k - 1, :latent, :]
        weights = jnp.exp(scores - top[at]).astype(BF16)
        part = dot(weights, keys, ((1,), (1,))) / total[at]
        for h in range(heads):
            for c in range(latent // LANES):
                at = c * PART + 2 * k
                out_ref[h, at : at + 2, :] = part[2 * h : 2 * h + 2, c * LANES : (c + 1) * LANES]


def project_kernel(
    owners_ref, part_ref, uv_ref, other_uv_ref, wo_ref, other_wo_ref, out_ref
):
    count, each, lanes = part_ref.shape
    seqs = owners_ref.shape[1]
    cuts = each // PART
    rows = 2 * seqs
    core = lax.axis_index("seq") % 2
    owners = owners_ref[...]
    row = iota((2 * rows, 1), 0)
    other, place = over(row, rows), over(rest_of(row, rows), 2)
    seq = place_of(place, count)
    head = jnp.where(other == 0, core, 1 - core)
    packed = column_of(owners * 4 + slots_of(owners), seq)
    owner, slot = over(packed, 4), rest_of(packed, 4)
    shape = (2 * rows, count * each)
    first = jnp.broadcast_to(place * each + head, shape)
    second = jnp.broadcast_to(place_of(owner, count) * each + 2 + 2 * slot + head, shape)
    hits = []
    for cut in range(cuts):
        at = iota(shape, 1) - cut * PART
        hits.append(jnp.where((at == first) | (at == second), 1.0, 0.0).astype(BF16))
    hit = jnp.concatenate(hits, axis=0)
    rest = part_ref[...].reshape(count * each, lanes)
    latent = None
    for _ in range(3):
        piece = rest.astype(BF16)
        rest = rest - piece.astype(F32)
        one = dot(hit, piece)
        latent = one if latent is None else latent + one
    latent = latent.astype(BF16)
    latent = jnp.concatenate(
        [latent[c * 2 * rows : (c + 1) * 2 * rows] for c in range(cuts)], axis=1
    )
    half = rest_of(iota((rows, 1), 0), 2)
    cols = wo_ref.shape[2] // 2
    product = None
    for n, (uv, wo) in enumerate(((uv_ref, wo_ref), (other_uv_ref, other_wo_ref))):
        head_out = dot(latent[n * rows : (n + 1) * rows], uv[0])
        for side in range(2):
            lines = jnp.where(half == side, head_out, 0.0).astype(BF16)
            one = dot(lines, wo[0, :, side * cols : (side + 1) * cols])
            product = one if product is None else product + one
    top = jnp.max(jnp.abs(product), axis=1, keepdims=True)
    power = jnp.clip(jnp.floor(jnp.log2(jnp.maximum(top, 1e-35))) + 1.0, -100.0, 100.0)
    coded = jnp.round(product * jnp.exp2(BITS - power)).astype(I32).astype(I16)
    power = jnp.broadcast_to(power, (rows, LANES)).astype(I32).astype(I16)
    for s in range(seqs):
        out_ref[s, :, :cols] = coded[2 * s : 2 * s + 2]
        out_ref[s, :, cols:] = power[2 * s : 2 * s + 2]


def final_kernel(in_ref, out_ref):
    cols = out_ref.shape[2] // 2
    for t in range(2):
        total = None
        for n in range(t, in_ref.shape[0], 2):
            power = in_ref[n, :, cols : cols + 1].astype(I32).astype(F32)
            one = in_ref[n, :, :cols].astype(I32).astype(F32) * jnp.exp2(power - BITS)
            total = one if total is None else total + one
        for j in range(2):
            out_ref[0, t : t + 1, j * cols : (j + 1) * cols] = total[j : j + 1].astype(BF16)


def swap(x):
    count = lax.axis_size("seq")
    order = [place_of(p, count) for p in range(count)]
    return lax.all_to_all(x, "seq", split_axis=0, concat_axis=0, axis_index_groups=[order], tiled=True)


def trade(x, step):
    count = lax.axis_size("seq")
    return lax.ppermute(x, "seq", [(d, d ^ step) for d in range(count)])


def call(kernel, shapes, specs, scratch=(), cost=None, room=None, outs=None, aliases={}):
    single = not isinstance(shapes, (list, tuple))
    if room is None:
        room = 16 if lax.axis_size("seq") <= 32 else 56
    return pl.pallas_call(
        kernel,
        out_shape=shapes,
        in_specs=specs,
        out_specs=VMEM if single else outs or [VMEM] * len(shapes),
        input_output_aliases=aliases,
        scratch_shapes=list(scratch),
        cost_estimate=cost,
        compiler_params=pltpu.CompilerParams(vmem_limit_bytes=room * 1024 * 1024),
    )


def on_device(prompt_raw, lengths, owners, resident, new_raw, queries, kv_gain, w_uk, w_uv, w_o):
    count = lax.axis_size("seq")
    seqs = lengths.shape[0]
    most, width = prompt_raw.shape[1:]
    latent = kv_gain.shape[0]
    res_rows = resident.shape[1]
    nope = w_uk.shape[1]
    rope = width - latent
    heads = count
    out_width = w_o.shape[2]
    scale = 1.0 / queries.shape[-1] ** 0.5
    owners_row, lengths_row = owners.reshape(1, seqs), lengths.reshape(1, seqs)
    prompt_raw = prompt_raw.transpose(0, 2, 1)
    resident = resident.transpose(0, 2, 1)
    queries = queries.transpose(0, 2, 1, 3)
    keys_rows = most + LANES

    aux_width = -(-width // LANES) * LANES
    query, aux = call(
        functools.partial(query_kernel, res_rows),
        [
            jax.ShapeDtypeStruct((count, PACK, latent // 2), BF16),
            jax.ShapeDtypeStruct((8, aux_width), F32),
        ],
        [HBM] * 6,
        [
            pltpu.VMEM((1, seqs), I32),
            pltpu.VMEM((1, seqs), I32),
            pltpu.VMEM(queries.shape, BF16),
            pltpu.VMEM((nope, latent), BF16),
            pltpu.VMEM((2, width), BF16),
            pltpu.VMEM((latent,), BF16),
            pltpu.VMEM((2 * seqs, -(-(nope + rope) // LANES) * LANES), F32),
            pltpu.SemaphoreType.DMA((6,)),
        ],
        room=60,
    )(owners_row, lengths_row, queries, w_uk[0], new_raw, kv_gain)
    received = swap(query)
    query, w_uv = lax.optimization_barrier((query, w_uv))
    other_uv = trade(w_uv, 1)
    keys, seen, resident = call(
        functools.partial(compress_kernel, res_rows, latent),
        [
            jax.ShapeDtypeStruct((width, keys_rows), BF16),
            jax.ShapeDtypeStruct((8, keys_rows), F32),
            jax.ShapeDtypeStruct(resident.shape, BF16),
        ],
        [VMEM] * 2 + [HBM],
        [pltpu.SemaphoreType.DMA],
        cost=pl.CostEstimate(flops=10**7, bytes_accessed=10**7, transcendentals=10**5),
    )(aux, prompt_raw, resident)
    lanes = -(-6 * heads // LANES) * LANES
    half = out_width // 2
    scores_p, scores_r, stat = call(
        functools.partial(score_kernel, scale),
        [
            jax.ShapeDtypeStruct((2 * heads, keys_rows), F32),
            jax.ShapeDtypeStruct((2, 2 * heads, res_rows), F32),
            jax.ShapeDtypeStruct((count, 2, lanes), F32),
        ],
        [VMEM] * 4,
    )(received, keys, seen, resident)
    stat, other_uv, w_o = lax.optimization_barrier((stat, other_uv, w_o))
    other_wo = trade(w_o, 1)
    stats = swap(stat)
    part, other_wo = call(
        attend_kernel,
        [
            jax.ShapeDtypeStruct((heads, PART * (latent // LANES), LANES), F32),
            jax.ShapeDtypeStruct(w_o.shape, BF16),
        ],
        [SMEM] + [VMEM] * 5 + [HBM],
        outs=[VMEM, HBM],
        aliases={6: 1},
    )(owners, stats, scores_p, scores_r, keys, resident, other_wo)
    parts = swap(part)
    sums = call(
        project_kernel, jax.ShapeDtypeStruct((seqs, 2, half + LANES), I16), [VMEM] * 6
    )(owners_row, parts, w_uv, other_uv, w_o, other_wo)
    return call(final_kernel, jax.ShapeDtypeStruct((1, 2, out_width), BF16), [VMEM])(swap(sums))


def solution(mesh):
    in_specs = (
        P(("group", "seq"), None, None),
        P("group"),
        P("group"),
        P(("group", "seq"), None, None),
        P("group", None, None),
        P("group", None, "seq", None),
        P(),
        P("seq", None, None),
        P("seq", None, None),
        P("seq", None, None),
    )
    out_specs = P(("group", "seq"), None, None)
    return jax.shard_map(
        on_device, mesh=mesh, in_specs=in_specs, out_specs=out_specs, check_vma=False
    )
```
